32 devices in a mesh: depth: 8 (over y, x, core), chan: 4 (over z).
Axes of the slice: x: 2, y: 2, z: 4, core: 2. Of those that a mesh axis runs over, the one named last changes fastest.
Arguments:
- grad_out: bfloat16 [128, 8, 32, 128], P('chan', 'depth'), may hold values from -6 to 6
- volume: bfloat16 [64, 16, 64, 256], P('chan', 'depth'), may hold values from -6 to 6
- weight: bfloat16 [27, 64, 128], replicated, may hold values from -0.15625 to 0.15625
Outputs:
- input_grad: bfloat16 [64, 16, 64, 256], P('chan', 'depth')
- weight_grad: float32 [27, 64, 128], P(None, 'chan', 'depth')
The draws below stay inside these ranges and needn't reach their ends.
All inputs are finite; a program needn't handle non-finite values.
Results may differ from the reference program's by a relative error of at most 0.001.
Values may be sent and summed in bfloat16 or wider, within the bound.
No kernel may reach another device: no remote copies, remote signals or barrier semaphores. Data moves between devices by JAX's collectives and lax.ppermute only.
A program may use at most 192 MiB of HBM per device.

```python
import math
import jax
import jax.numpy as jnp
from jax import lax

CI = 64
CO = 128
OD_DEV = 1
OH = 32
OW = 128
OD = 8
ID = 16
IH = 64
IW = 256
N_DEPTH = 8


def raised(result, rng, source, target, blocks, factor):
    def block_of(axis_at):
        return (jnp.arange(result.shape[axis_at]) // (result.shape[axis_at] // blocks)).reshape((-1,) + (1,) * (result.ndim - 1 - axis_at))

    one_side = jax.random.permutation(rng, blocks)[block_of(target)]
    second = (block_of(target) + blocks // 2) % blocks
    return jnp.where((block_of(source) == one_side) | (block_of(source) == second), factor * result, result)


def levels(rng, shape, shards, least, largest):
    def one(position, blocks):
        draws = jax.random.uniform(jax.random.fold_in(jax.random.fold_in(rng, 6), position), (blocks,), jnp.float32, least / len(shards), largest / len(shards))
        return jnp.repeat(jnp.exp(draws), shape[position] // blocks).reshape((-1,) + (1,) * (len(shape) - position - 1))

    level = one(*shards[0])
    for cut in shards[1:]:
        level = level * one(*cut)
    return level


def noise(own_key, extent, deviation, bound, shards=(), kind=jnp.bfloat16):
    factor_of = levels(own_key, extent, shards, -0.22, 0.18) if shards else 1.0
    values = jax.random.normal(own_key, extent, jnp.float32) * deviation * factor_of
    return jnp.minimum(jnp.maximum(values, -bound), bound).astype(kind)


def bell_draw_with(key, shape, spread, bound, cuts, heavy, kind=jnp.bfloat16):
    array = spread * jax.random.normal(key, shape, jnp.float32)
    if cuts:
        array = array * levels(key, shape, cuts, -0.22, 0.18)
    return jnp.clip(raised(array, jax.random.fold_in(key, 3), *heavy), -bound, bound).astype(kind)


def setup_inputs(seed: int = 0) -> dict:
    streams_of = jax.random.split(jax.random.key(seed), 4)
    grad_out = bell_draw_with(streams_of[0], (CO, OD, OH, OW), 1.0, 6.0, ((0, 4), (1, 8)), (1, 0, 8, 2.0))
    volume = noise(streams_of[1], (CI, ID, IH, IW), 1.0, 6.0, ((0, 4), (1, 8)))
    weight = noise(streams_of[2], (27, CI, CO), (27 * CI) ** -0.5, 0.15625)
    return dict(grad_out=grad_out, volume=volume, weight=weight)


def upsample(stacked, axis, extended):
    tap_zero, tap_one, tap_two = (stacked[0], stacked[1], stacked[2])
    coord_axis = axis - 1
    length = tap_zero.shape[coord_axis]
    if extended:
        outer = length - 1
        even_cells = lax.slice_in_dim(tap_one, 0, outer, axis=coord_axis)
        odd_cells = lax.slice_in_dim(tap_zero, 1, length, axis=coord_axis) + lax.slice_in_dim(tap_two, 0, outer, axis=coord_axis)
    else:
        outer = length
        shifted = lax.slice_in_dim(tap_zero, 1, length, axis=coord_axis)
        shifted = jnp.concatenate([shifted, jnp.zeros_like(lax.slice_in_dim(tap_zero, 0, 1, axis=coord_axis))], axis=coord_axis)
        even_cells = tap_one
        odd_cells = shifted + tap_two
    paired = jnp.stack([even_cells, odd_cells], axis=coord_axis + 1)
    new_shape = list(even_cells.shape)
    new_shape[coord_axis] = 2 * outer
    return paired.reshape(new_shape)

def tap_views(padded, axis, half):
    return jnp.stack([lax.slice_in_dim(padded, k, k + 2 * half - 1, stride=2, axis=axis) for k in range(3)], axis=0)

def reference(grad_out, volume, weight):
    channels_in = volume.shape[0]
    channels_out = grad_out.shape[0]
    rows_out = grad_out.shape[2]
    cols_out = grad_out.shape[3]
    weight_flat = weight.astype(jnp.float32).reshape(27 * channels_in, channels_out)
    grad_tail = jnp.concatenate([grad_out, jnp.zeros((channels_out, 1, rows_out, cols_out), grad_out.dtype)], axis=1)
    volume_head = jnp.concatenate([jnp.zeros((channels_in, 1) + volume.shape[2:], volume.dtype), volume], axis=1)

    def one_block(running, block_index):
        plane_start = block_index * OD_DEV
        grads = lax.dynamic_slice_in_dim(grad_tail, plane_start, OD_DEV + 1, 1).astype(jnp.float32)
        inputs = lax.dynamic_slice_in_dim(volume_head, 2 * plane_start, 2 * OD_DEV + 1, 1).astype(jnp.float32)
        taps_out = jnp.dot(weight_flat, grads.reshape(channels_out, -1), precision=lax.Precision.HIGHEST, preferred_element_type=jnp.float32)
        taps_out = taps_out.reshape(3, 3, 3, channels_in, OD_DEV + 1, rows_out, cols_out)
        along_w = upsample(jnp.moveaxis(taps_out, 2, 0), 6, False)
        along_h = upsample(jnp.moveaxis(along_w, 1, 0), 4, False)
        along_d = upsample(along_h, 2, True)
        views = jnp.pad(inputs, ((0, 0), (0, 0), (1, 0), (1, 0)))
        views = tap_views(views, 3, cols_out)
        views = tap_views(views, 3, rows_out)
        views = tap_views(views, 3, OD_DEV)
        grads_own = grads[:, :OD_DEV].reshape(channels_out, -1)
        block_weight = jnp.dot(views.reshape(27 * channels_in, -1), grads_own.T, precision=lax.Precision.HIGHEST, preferred_element_type=jnp.float32)
        return (running + block_weight, along_d.astype(jnp.bfloat16))
    total, pieces = lax.scan(one_block, jnp.zeros((27 * channels_in, channels_out), jnp.float32), jnp.arange(N_DEPTH, dtype=jnp.int32))
    input_grad = jnp.moveaxis(pieces, 0, 1).reshape(volume.shape)
    weight_grad = total.reshape(27, channels_in, channels_out) * (1.0 / math.sqrt(OD * OH * OW))
    return (input_grad, weight_grad)
```

```python
import math

import jax
import jax.numpy as jnp
from jax import lax
from jax.experimental import pallas as pl
from jax.experimental.pallas import tpu as pltpu
from jax.sharding import PartitionSpec as P

F32 = jnp.float32
BF16 = jnp.bfloat16
VMEM = pl.BlockSpec(memory_space=pltpu.VMEM)
SMEM = pl.BlockSpec(memory_space=pltpu.SMEM)
LIMIT = 48 * 1024 * 1024


def ring_order(count):
    return [0] + list(range(1, count, 2)) + list(range(2, count, 2))[::-1]


def matmul(left, right):
    return jnp.dot(left, right, preferred_element_type=F32)


def one_hot(rows, cols, source):
    row = lax.broadcasted_iota(jnp.int32, (rows, cols), 0)
    col = lax.broadcasted_iota(jnp.int32, (rows, cols), 1)
    return jnp.where(source(row, col), 1.0, 0.0).astype(BF16)


def swap_rows(major, minor):
    bits = minor.bit_length() - 1
    return one_hot(
        major * minor,
        major * minor,
        lambda row, col: col == (row & (minor - 1)) * major + (row >> bits),
    )


def volume_kernel(v_ref, m_ref):
    chans, _, rows, cols = v_ref.shape
    half = cols // 2
    group = 256 // chans
    swap = swap_rows(group, chans)
    split = one_hot(cols, 3 * half, lambda row, col: row == 2 * (col & (half - 1)) + col // half - 1)
    for plane in range(2):
        base = plane * 9 * chans
        for start in range(0, rows, group):
            block = v_ref[:, plane, start : start + group, :].reshape(chans * group, cols)
            by_row = matmul(swap, block).astype(BF16)
            views = matmul(by_row, split).astype(BF16)
            for at in range(group):
                row = start + at
                for e in range(3):
                    piece = views[at * chans : (at + 1) * chans, e * half : (e + 1) * half]
                    if row % 2 == 0:
                        places = [(1, row // 2)]
                    else:
                        places = [(2, row // 2), (0, row // 2 + 1)]
                    for b, r in places:
                        if r < rows // 2:
                            lo = base + (3 * b + e) * chans
                            m_ref[lo : lo + chans, r * half : (r + 1) * half] = piece
        m_ref[base : base + 3 * chans, :half] = jnp.zeros((3 * chans, half), BF16)


def grads_kernel(at_ref, *refs):
    parts = len(refs) // 2 - 1
    m_ref, stack_ref, wt_ref = refs[2 * parts], refs[2 * parts + 1], refs[2 * parts + 2]
    _, _, rows, cols = refs[0].shape
    channels = stack_ref.shape[0] // 4
    swap = swap_rows(16, 16)
    ahead = one_hot(cols, cols, lambda row, col: row == col + 1)
    for index in range(2 * parts):
        ref = refs[index]
        own = index < parts
        plain_base = 2 * channels if own else channels
        ahead_base = 3 * channels if own else 0
        for o in range(0, ref.shape[0], 16):
            place = pl.multiple_of(at_ref[index % parts] + o, 16)
            for h in range(0, rows, 16):
                block = ref[o : o + 16, 0, h : h + 16, :].reshape(256, cols)
                by_row = matmul(swap, block).astype(BF16)
                moved = matmul(by_row, ahead).astype(BF16)
                for k in range(16):
                    lanes = slice((h + k) * cols, (h + k + 1) * cols)
                    stack_ref[pl.ds(plain_base + place, 16), lanes] = by_row[16 * k : 16 * k + 16]
                    stack_ref[pl.ds(ahead_base + place, 16), lanes] = moved[16 * k : 16 * k + 16]
    third = m_ref.shape[0] // 2
    contract = (((1,), (1,)), ((), ()))
    wt_ref[:, :third] = lax.dot_general(
        stack_ref[channels : 2 * channels, :], m_ref[third:, :], contract, preferred_element_type=F32
    )
    wt_ref[:, third:] = lax.dot_general(
        stack_ref[2 * channels : 3 * channels, :], m_ref[...], contract, preferred_element_type=F32
    )


def input_kernel(w_ref, stack_ref, out_ref, lhs_ref, taps_ref):
    chans, _, rows, cols = out_ref.shape
    channels = w_ref.shape[2]
    half = cols // 2
    zero = jnp.zeros((chans, channels), BF16)
    tap = lambda a, b, e: w_ref[9 * a + 3 * b + e]
    for b in range(3):
        for k, line in enumerate(
            (
                (zero, zero, tap(1, b, 1), zero),
                (zero, zero, tap(1, b, 2), tap(1, b, 0)),
                (zero, tap(0, b, 1), tap(2, b, 1), zero),
                (tap(0, b, 0), tap(0, b, 2), tap(2, b, 2), tap(2, b, 0)),
            )
        ):
            lo = (3 * k + b) * chans
            for q, block in enumerate(line):
                lhs_ref[lo : lo + chans, q * channels : (q + 1) * channels] = block
    grid_cells = stack_ref.shape[1]
    taps_ref[:, :grid_cells] = matmul(lhs_ref[...], stack_ref[...])
    taps_ref[:, grid_cells:] = jnp.zeros((taps_ref.shape[0], half), F32)
    group = 256 // chans
    swap = swap_rows(chans, group)
    weave = one_hot(cols, cols, lambda row, col: col == 2 * (row & (half - 1)) + row // half)

    def cells(plane, side, b, r):
        lo = ((plane * 2 + side) * 3 + b) * chans
        return taps_ref[lo : lo + chans, r * half : (r + 1) * half]

    for plane in range(2):
        for start in range(0, rows, group):
            pieces = []
            for row in range(start, start + group):
                r = row // 2
                if row % 2 == 0:
                    both = [cells(plane, side, 1, r) for side in range(2)]
                else:
                    both = [cells(plane, side, 0, r + 1) + cells(plane, side, 2, r) for side in range(2)]
                pieces.append(jnp.concatenate(both, axis=1).astype(BF16))
            block = jnp.concatenate(pieces, axis=0)
            woven = matmul(block, weave).astype(BF16)
            placed = matmul(swap, woven).astype(BF16)
            out_ref[:, plane, start : start + group, :] = placed.reshape(chans, group, cols)


def total_kernel(scale, r_ref, out_ref):
    chans, outs, taps = out_ref.shape
    total = r_ref[0]
    for source in range(1, r_ref.shape[0]):
        total = total + r_ref[source]
    total = total * scale
    bits = chans.bit_length() - 1
    order = one_hot(
        taps * chans, 32 * chans, lambda row, col: row == (col & 31) * chans + (col >> 5)
    ).astype(F32)
    by_chan = jnp.dot(total, order, precision=lax.Precision.HIGHEST, preferred_element_type=F32)
    for c in range(chans):
        out_ref[c] = by_chan[:, 32 * c : 32 * c + taps]


def from_behind(shard, axis, by):
    count = lax.axis_size(axis)
    pairs = [(i, i + by) for i in range(count) if 0 <= i + by < count]
    return lax.ppermute(shard, axis, pairs)


def upsample(stacked, axis, extended):
    tap_zero, tap_one, tap_two = (stacked[0], stacked[1], stacked[2])
    coord_axis = axis - 1
    length = tap_zero.shape[coord_axis]
    if extended:
        outer = length - 1
        even_cells = lax.slice_in_dim(tap_one, 0, outer, axis=coord_axis)
        odd_cells = lax.slice_in_dim(tap_zero, 1, length, axis=coord_axis) + lax.slice_in_dim(
            tap_two, 0, outer, axis=coord_axis
        )
    else:
        outer = length
        shifted = lax.slice_in_dim(tap_zero, 1, length, axis=coord_axis)
        shifted = jnp.concatenate(
            [shifted, jnp.zeros_like(lax.slice_in_dim(tap_zero, 0, 1, axis=coord_axis))],
            axis=coord_axis,
        )
        even_cells = tap_one
        odd_cells = shifted + tap_two
    paired = jnp.stack([even_cells, odd_cells], axis=coord_axis + 1)
    new_shape = list(even_cells.shape)
    new_shape[coord_axis] = 2 * outer
    return paired.reshape(new_shape)


def phase_grads(weight_rows, grads_ext):
    local_in = weight_rows.shape[0] // 27
    channels_out, planes, rows, cols = grads_ext.shape
    taps_out = jnp.dot(
        weight_rows, grads_ext.reshape(channels_out, -1), preferred_element_type=jnp.float32
    )
    taps_out = taps_out.reshape(3, 3, 3, local_in, planes, rows, cols)
    along_w = upsample(jnp.moveaxis(taps_out, 2, 0), 6, False)
    along_h = upsample(jnp.moveaxis(along_w, 1, 0), 4, False)
    return upsample(along_h, 2, True)


def weight_terms(inputs, grads_ext):
    row_extra = 0
    weight_cube = lax.conv_general_dilated(
        inputs[None],
        grads_ext[:, None],
        (1, 1, 1),
        ((1, 2), (1, row_extra), (1, 0)),
        rhs_dilation=(2, 2, 2),
        dimension_numbers=("CNDHW", "OIDHW", "NCDHW"),
        preferred_element_type=jnp.float32,
    )
    return jnp.transpose(weight_cube, (2, 3, 4, 0, 1)).reshape(
        27, weight_cube.shape[0], weight_cube.shape[1]
    )


def plain_shards(grad_out, volume, weight):
    plane_next = from_behind(grad_out, "depth", -1)
    grads_ext = jnp.concatenate([grad_out, plane_next], axis=1)
    channels_out = weight.shape[2]
    local_in = volume.shape[0]
    every_channel = lax.all_gather(grads_ext, "chan", axis=0, tiled=True)
    own_weight = lax.dynamic_slice_in_dim(weight, lax.axis_index("chan") * local_in, local_in, 1)
    input_part = phase_grads(own_weight.reshape(27 * local_in, channels_out), every_channel)
    weight_part = weight_terms(volume, every_channel)
    input_grad = input_part.astype(jnp.bfloat16)
    summed = lax.psum_scatter(weight_part, "depth", scatter_dimension=2, tiled=True)
    cell_count = grad_out.shape[1] * lax.axis_size("depth") * grad_out.shape[2] * grad_out.shape[3]
    return (input_grad, summed * (1.0 / math.sqrt(cell_count)))


def call(kernel, out_shape, *args, specs=None, scratch=(), cost=None):
    flops, moved = cost
    return pl.pallas_call(
        kernel,
        out_shape=out_shape,
        in_specs=specs or [VMEM] * len(args),
        out_specs=jax.tree.map(lambda _: VMEM, out_shape),
        scratch_shapes=scratch,
        compiler_params=pltpu.CompilerParams(vmem_limit_bytes=LIMIT),
        cost_estimate=pl.CostEstimate(flops=flops, bytes_accessed=moved, transcendentals=0),
    )(*args)


def shards(grad_out, volume, weight):
    count = lax.axis_size("chan")
    depth = lax.axis_size("depth")
    own_outs, _, rows, cols = grad_out.shape
    chans = volume.shape[0]
    channels = weight.shape[2]
    cells = rows * cols
    order = ring_order(count)
    ahead = [(order[i], order[(i + 1) % count]) for i in range(count)]
    back = [(b, a) for a, b in ahead]
    nearer = [(i, i - 1) for i in range(1, depth)]
    mine = lax.axis_index("chan")
    seats = [order.index(i) for i in range(count)]
    holders = lambda shift, extra=0: [order[(seat + shift) % count] * own_outs + extra for seat in seats]

    parts = [grad_out]
    places = [holders(0)]
    up = down = grad_out
    for step in range(1, (count - 1) // 2 + 1):
        up = lax.ppermute(up, "chan", ahead)
        down = lax.ppermute(down, "chan", back)
        parts += [up, down]
        places += [holders(-step), holders(step)]
    if count % 2 == 0:
        middle = own_outs // 2
        parts += [lax.ppermute(up[:middle], "chan", ahead), lax.ppermute(down[middle:], "chan", back)]
        places += [holders(count // 2), holders(count // 2, middle)]
    nexts = [lax.ppermute(part, "depth", nearer) for part in parts]

    unfolded = call(
        volume_kernel,
        jax.ShapeDtypeStruct((18 * chans, cells), BF16),
        volume,
        cost=(2 * 2 * 64 * 256 * 640 * chans, 4 << 20),
    )
    own_weight = lax.dynamic_slice_in_dim(weight, mine * chans, chans, 1)
    stack, partial = call(
        grads_kernel,
        (
            jax.ShapeDtypeStruct((4 * channels, cells), BF16),
            jax.ShapeDtypeStruct((channels, 27 * chans), F32),
        ),
        lax.dynamic_index_in_dim(jnp.asarray(places, jnp.int32).T, mine, 0, keepdims=False),
        *parts,
        *nexts,
        unfolded,
        specs=[SMEM] + [VMEM] * (2 * len(parts) + 1),
        cost=(2 * 27 * chans * channels * cells * 4, 8 << 20),
    )
    terms = lax.all_to_all(partial, "depth", split_axis=0, concat_axis=0, tiled=True)
    input_grad = call(
        input_kernel,
        jax.ShapeDtypeStruct(volume.shape, BF16),
        own_weight,
        stack,
        scratch=(
            pltpu.VMEM((12 * chans, 4 * channels), BF16),
            pltpu.VMEM((12 * chans, cells + cols), F32),
        ),
        cost=(2 * 12 * chans * 4 * channels * cells, 8 << 20),
    )
    scale = 1.0 / math.sqrt(depth * cells)
    outs = channels // depth
    weight_grad = call(
        lambda r, o: total_kernel(scale, r, o),
        jax.ShapeDtypeStruct((chans, outs, 27), F32),
        terms.reshape(depth, outs, 27 * chans),
        cost=(1 << 20, 1 << 20),
    )
    return input_grad, jnp.transpose(weight_grad, (2, 0, 1))


def solution(mesh):
    in_specs = (P("chan", "depth", None, None), P("chan", "depth", None, None), P())
    out_specs = (P("chan", "depth", None, None), P(None, "chan", "depth"))
    def either(grad_out, volume, weight):
        fits = grad_out.shape[0] % 32 == 0 and volume.shape[0] == 16 and grad_out.shape[1] == 1
        return (shards if fits else plain_shards)(grad_out, volume, weight)

    return jax.shard_map(either, mesh=mesh, in_specs=in_specs, out_specs=out_specs, check_vma=False)
```

```python
import math

import jax
import jax.numpy as jnp
from jax import lax
from jax.experimental import pallas as pl
from jax.experimental.pallas import tpu as pltpu
from jax.sharding import PartitionSpec as P

F32 = jnp.float32
BF16 = jnp.bfloat16
VMEM = pl.BlockSpec(memory_space=pltpu.VMEM)
SMEM = pl.BlockSpec(memory_space=pltpu.SMEM)
LIMIT = 48 * 1024 * 1024


def ring_order(count):
    return [0] + list(range(1, count, 2)) + list(range(2, count, 2))[::-1]


def matmul(left, right):
    return jnp.dot(left, right, preferred_element_type=F32)


def one_hot(rows, cols, source):
    row = lax.broadcasted_iota(jnp.int32, (rows, cols), 0)
    col = lax.broadcasted_iota(jnp.int32, (rows, cols), 1)
    return jnp.where(source(row, col), 1.0, 0.0).astype(BF16)


def views_kernel(seats, behind_ref, volume_ref, weight_ref, views_ref, taps_ref, lines_ref):
    chans, _, rows, cols = volume_ref.shape
    channels = weight_ref.shape[2]
    half = cols // 2
    split = one_hot(cols, 3 * half, lambda row, col: row == 2 * (col & (half - 1)) + col // half - 1)
    planes = [behind_ref.at[:, 0], volume_ref.at[:, 0], volume_ref.at[:, 1]]
    for a, plane in enumerate(planes):
        parted = matmul(plane[...].reshape(chans * rows, cols), split)
        for e in range(3):
            lines_ref[e] = parted[:, e * half : (e + 1) * half]
        for row in range(rows):
            places = [(1, row // 2)] if row % 2 == 0 else [(2, row // 2), (0, row // 2 + 1)]
            for e in range(3):
                line = lines_ref[e, pl.ds(row, chans, stride=rows), :].astype(BF16)
                for b, r in places:
                    if r < rows // 2:
                        lo = (9 * a + 3 * b + e) * chans
                        views_ref[lo : lo + chans, r * half : (r + 1) * half] = line
        base = 9 * a * chans
        views_ref[base : base + 3 * chans, :half] = jnp.zeros((3 * chans, half), BF16)
    here = lax.axis_index("chan")
    part = channels // len(seats)
    row = lax.broadcasted_iota(jnp.int32, (channels, channels), 0)
    col = lax.broadcasted_iota(jnp.int32, (channels, channels), 1)
    order = jnp.zeros((channels, channels), jnp.bool_)
    for slot in range(len(seats)):
        owner = jnp.int32(0)
        for chip in range(len(seats)):
            owner = jnp.where(here == chip, seats[chip][slot], owner)
        inside = (col >= slot * part) & (col < (slot + 1) * part)
        order = order | (inside & (row == col + (owner - slot) * part))
    order = jnp.where(order, 1.0, 0.0).astype(BF16)
    ordered = matmul(weight_ref[...].reshape(27 * chans, channels), order).astype(BF16)
    zero = jnp.zeros((chans, channels), BF16)
    for k, e in enumerate((1, 2, 0)):
        for b in range(3):
            pick = lambda a: ordered[(9 * a + 3 * b + e) * chans : (9 * a + 3 * b + e + 1) * chans]
            for plane, line in enumerate(((zero, pick(1)), (pick(0), pick(2)))):
                lo = ((3 * plane + k) * 3 + b) * chans
                taps_ref[lo : lo + chans, :] = jnp.concatenate(line, axis=1)


def lines_kernel(*refs):
    *parts, out_ref, wide_ref = refs
    at = 0
    for part in parts:
        outs, _, rows, cols = part.shape
        wide_ref[...] = part[...].reshape(outs * rows, cols).astype(F32)
        for row in range(rows):
            line = wide_ref[pl.ds(row, outs, stride=rows), :].astype(BF16)
            out_ref[at : at + outs, row * cols : (row + 1) * cols] = line
        at += outs


def weight_kernel(seats, chans, *refs):
    views_ref, *part_refs, out_ref, terms_ref, placed_ref = refs
    channels = out_ref.shape[0]
    grads = jnp.concatenate([ref[...] for ref in part_refs], axis=0)
    terms_ref[: 27 * chans, :] = lax.dot_general(
        views_ref[...], grads, (((1,), (1,)), ((), ())), preferred_element_type=F32
    )
    terms_ref[27 * chans :, :] = jnp.zeros((5 * chans, channels), F32)
    for c in range(chans):
        placed_ref[32 * c : 32 * c + 32, :] = terms_ref[pl.ds(c, 32, stride=chans), :]
    turned = placed_ref[...].T
    here = lax.axis_index("chan")
    part = channels // len(seats)
    for slot in range(len(seats)):
        owner = jnp.int32(0)
        for chip in range(len(seats)):
            owner = jnp.where(here == chip, seats[chip][slot], owner)
        place = pl.multiple_of(owner * part, part)
        out_ref[pl.ds(place, part), :] = turned[slot * part : (slot + 1) * part]


def input_kernel(parts, *refs):
    taps_ref, *grad_refs, out_ref, cells_ref, lines_ref = refs
    chans, _, rows, cols = out_ref.shape
    half = cols // 2
    grid_cells = half * rows // 2
    grads = jnp.concatenate([ref[...] for ref in grad_refs], axis=0)
    cells_ref[:, :grid_cells] = matmul(taps_ref[...], grads)
    cells_ref[:, grid_cells:] = jnp.zeros((cells_ref.shape[0], half), F32)
    group = 256 // chans
    weave = one_hot(cols, cols, lambda row, col: col == 2 * (row & (half - 1)) + row // half)
    inner = lax.broadcasted_iota(jnp.int32, (chans, half), 1) < half - 1

    def cells(plane, kind, b, r):
        lo = ((3 * plane + kind) * 3 + b) * chans
        return cells_ref[lo : lo + chans, r * half : (r + 1) * half]

    for plane in range(2):
        for start in range(0, rows, group):
            pieces = []
            for row in range(start, start + group):
                r = row // 2
                if row % 2 == 0:
                    even, odd, next_odd = [cells(plane, kind, 1, r) for kind in range(3)]
                else:
                    even, odd, next_odd = [
                        cells(plane, kind, 0, r + 1) + cells(plane, kind, 2, r) for kind in range(3)
                    ]
                odd = odd + jnp.where(inner, pltpu.roll(next_odd, half - 1, 1), 0.0)
                pieces.append(jnp.concatenate([even, odd], axis=1).astype(BF16))
            woven = matmul(jnp.concatenate(pieces, axis=0), weave)
            for side in range(2):
                lanes = slice(side * half, (side + 1) * half)
                lines_ref[side] = woven[:, lanes]
                for c in range(chans):
                    line = lines_ref[side, pl.ds(c, group, stride=chans), :].astype(BF16)
                    out_ref[c, plane, start : start + group, lanes] = line


def total_kernel(scale, terms_ref, out_ref):
    chans, outs, taps = out_ref.shape
    total = terms_ref[0]
    for source in range(1, terms_ref.shape[0]):
        total = total + terms_ref[source]
    total = total * scale
    for c in range(chans):
        out_ref[c] = total[:, 32 * c : 32 * c + taps]


def from_behind(shard, axis, by):
    count = lax.axis_size(axis)
    pairs = [(i, i + by) for i in range(count) if 0 <= i + by < count]
    return lax.ppermute(shard, axis, pairs)


def upsample(stacked, axis, extended):
    tap_zero, tap_one, tap_two = (stacked[0], stacked[1], stacked[2])
    coord_axis = axis - 1
    length = tap_zero.shape[coord_axis]
    if extended:
        outer = length - 1
        even_cells = lax.slice_in_dim(tap_one, 0, outer, axis=coord_axis)
        odd_cells = lax.slice_in_dim(tap_zero, 1, length, axis=coord_axis) + lax.slice_in_dim(
            tap_two, 0, outer, axis=coord_axis
        )
    else:
        outer = length
        shifted = lax.slice_in_dim(tap_zero, 1, length, axis=coord_axis)
        shifted = jnp.concatenate(
            [shifted, jnp.zeros_like(lax.slice_in_dim(tap_zero, 0, 1, axis=coord_axis))],
            axis=coord_axis,
        )
        even_cells = tap_one
        odd_cells = shifted + tap_two
    paired = jnp.stack([even_cells, odd_cells], axis=coord_axis + 1)
    new_shape = list(even_cells.shape)
    new_shape[coord_axis] = 2 * outer
    return paired.reshape(new_shape)


def phase_grads(weight_rows, grads_ext):
    local_in = weight_rows.shape[0] // 27
    channels_out, planes, rows, cols = grads_ext.shape
    taps_out = jnp.dot(
        weight_rows, grads_ext.reshape(channels_out, -1), preferred_element_type=jnp.float32
    )
    taps_out = taps_out.reshape(3, 3, 3, local_in, planes, rows, cols)
    along_w = upsample(jnp.moveaxis(taps_out, 2, 0), 6, False)
    along_h = upsample(jnp.moveaxis(along_w, 1, 0), 4, False)
    return upsample(along_h, 2, True)


def weight_terms(inputs, grads_ext):
    row_extra = 0
    weight_cube = lax.conv_general_dilated(
        inputs[None],
        grads_ext[:, None],
        (1, 1, 1),
        ((1, 2), (1, row_extra), (1, 0)),
        rhs_dilation=(2, 2, 2),
        dimension_numbers=("CNDHW", "OIDHW", "NCDHW"),
        preferred_element_type=jnp.float32,
    )
    return jnp.transpose(weight_cube, (2, 3, 4, 0, 1)).reshape(
        27, weight_cube.shape[0], weight_cube.shape[1]
    )


def plain_shards(grad_out, volume, weight):
    plane_next = from_behind(grad_out, "depth", -1)
    grads_ext = jnp.concatenate([grad_out, plane_next], axis=1)
    channels_out = weight.shape[2]
    local_in = volume.shape[0]
    every_channel = lax.all_gather(grads_ext, "chan", axis=0, tiled=True)
    own_weight = lax.dynamic_slice_in_dim(weight, lax.axis_index("chan") * local_in, local_in, 1)
    input_part = phase_grads(own_weight.reshape(27 * local_in, channels_out), every_channel)
    weight_part = weight_terms(volume, every_channel)
    input_grad = input_part.astype(jnp.bfloat16)
    summed = lax.psum_scatter(weight_part, "depth", scatter_dimension=2, tiled=True)
    cell_count = grad_out.shape[1] * lax.axis_size("depth") * grad_out.shape[2] * grad_out.shape[3]
    return (input_grad, summed * (1.0 / math.sqrt(cell_count)))


def call(kernel, out_shape, *args, specs=None, scratch=(), cost=None):
    flops, moved = cost
    return pl.pallas_call(
        kernel,
        out_shape=out_shape,
        in_specs=specs or [VMEM] * len(args),
        out_specs=jax.tree.map(lambda _: VMEM, out_shape),
        scratch_shapes=scratch,
        compiler_params=pltpu.CompilerParams(vmem_limit_bytes=LIMIT),
        cost_estimate=pl.CostEstimate(flops=flops, bytes_accessed=moved, transcendentals=0),
    )(*args)


def shards(grad_out, volume, weight):
    count = lax.axis_size("chan")
    depth = lax.axis_size("depth")
    own_outs, _, rows, cols = grad_out.shape
    chans = volume.shape[0]
    channels = weight.shape[2]
    cells = rows * cols
    order = ring_order(count)
    ahead = [(order[i], order[(i + 1) % count]) for i in range(count)]
    back = [(b, a) for a, b in ahead]
    farther = [(i, i + 1) for i in range(depth - 1)]
    nearer = [(i, i - 1) for i in range(1, depth)]
    shifts = [0]

    near = []
    up = down = grad_out
    for step in range(1, (count - 1) // 2 + 1):
        up = lax.ppermute(up, "chan", ahead)
        down = lax.ppermute(down, "chan", back)
        near += [up, down]
        shifts += [-step, step]
    last = lax.ppermute(up, "chan", ahead)
    shifts += [count // 2]
    seats = [[order[(order.index(chip) + s) % count] for s in shifts] for chip in range(count)]

    next_own = lax.ppermute(grad_out, "depth", nearer)
    behind = lax.ppermute(volume[:, 1:], "depth", farther)

    own_weight = lax.dynamic_slice_in_dim(weight, lax.axis_index("chan") * chans, chans, 1)
    views, taps = call(
        lambda *refs: views_kernel(seats, *refs),
        (
            jax.ShapeDtypeStruct((27 * chans, cells), BF16),
            jax.ShapeDtypeStruct((18 * chans, 2 * channels), BF16),
        ),
        behind,
        volume,
        own_weight,
        scratch=(pltpu.VMEM((3, chans * 2 * rows, cols), F32),),
        cost=(2 * 3 * 2 * cells * chans * 6 * cols, 6 << 20),
    )

    def lines(*parts):
        return call(
            lines_kernel,
            jax.ShapeDtypeStruct((own_outs * len(parts), cells), BF16),
            *parts,
            scratch=(pltpu.VMEM((own_outs * rows, cols), F32),),
            cost=(1 << 20, (len(parts) * own_outs * cells) << 2),
        )

    *near, views = lax.optimization_barrier((*near, views))
    near_lines = lines(*near)
    own_lines = lines(grad_out)
    next_own_lines = lines(next_own)
    next_near_lines = lax.ppermute(near_lines, "depth", nearer)
    last_lines = lines(last)
    next_last_lines = lax.ppermute(last_lines, "depth", nearer)
    partial = call(
        lambda *refs: weight_kernel(seats, chans, *refs),
        jax.ShapeDtypeStruct((channels, 32 * chans), F32),
        views,
        own_lines,
        near_lines,
        last_lines,
        scratch=(pltpu.VMEM((32 * chans, channels), F32), pltpu.VMEM((32 * chans, channels), F32)),
        cost=(2 * 27 * chans * channels * cells, 8 << 20),
    )
    terms = lax.all_to_all(partial, "depth", split_axis=0, concat_axis=0, tiled=True)
    input_grad = call(
        lambda *refs: input_kernel(count, *refs),
        jax.ShapeDtypeStruct(volume.shape, BF16),
        taps,
        next_own_lines,
        next_near_lines,
        next_last_lines,
        own_lines,
        near_lines,
        last_lines,
        scratch=(
            pltpu.VMEM((18 * chans, cells + cols), F32),
            pltpu.VMEM((2, 256, cols), F32),
        ),
        cost=(2 * 18 * chans * 2 * channels * cells, 8 << 20),
    )
    scale = 1.0 / math.sqrt(depth * cells)
    outs = channels // depth
    weight_grad = call(
        lambda *refs: total_kernel(scale, *refs),
        jax.ShapeDtypeStruct((chans, outs, 27), F32),
        terms.reshape(depth, outs, 32 * chans),
        cost=(1 << 20, 1 << 20),
    )
    return input_grad, jnp.transpose(weight_grad, (2, 0, 1))


def solution(mesh):
    in_specs = (P("chan", "depth", None, None), P("chan", "depth", None, None), P())
    out_specs = (P("chan", "depth", None, None), P(None, "chan", "depth"))
    ring = mesh.shape["chan"]

    def either(grad_out, volume, weight):
        fits = (
            grad_out.shape[0] % 16 == 0
            and volume.shape[0] == 16
            and grad_out.shape[1] == 1
            and ring % 2 == 0
            and ring >= 4
        )
        return (shards if fits else plain_shards)(grad_out, volume, weight)

    return jax.shard_map(either, mesh=mesh, in_specs=in_specs, out_specs=out_specs, check_vma=False)
```

```python
import math

import jax
import jax.numpy as jnp
from jax import lax
from jax.experimental import pallas as pl
from jax.experimental.pallas import tpu as pltpu
from jax.sharding import PartitionSpec as P

F32 = jnp.float32
BF16 = jnp.bfloat16
VMEM = pl.BlockSpec(memory_space=pltpu.VMEM)
SMEM = pl.BlockSpec(memory_space=pltpu.SMEM)
LIMIT = 48 * 1024 * 1024


def ring_order(count):
    return [0] + list(range(1, count, 2)) + list(range(2, count, 2))[::-1]


def matmul(left, right):
    return jnp.dot(left, right, preferred_element_type=F32)


def one_hot(rows, cols, source):
    row = lax.broadcasted_iota(jnp.int32, (rows, cols), 0)
    col = lax.broadcasted_iota(jnp.int32, (rows, cols), 1)
    return jnp.where(source(row, col), 1.0, 0.0).astype(BF16)


def swap_rows(major, minor):
    bits = minor.bit_length() - 1
    return one_hot(
        major * minor,
        major * minor,
        lambda row, col: col == (row & (minor - 1)) * major + (row >> bits),
    )


def place_views(plane, views_ref, base):
    chans, rows, cols = plane.shape
    half = cols // 2
    group = 256 // chans
    swap = swap_rows(group, chans)
    split = one_hot(cols, cols, lambda row, col: row == 2 * (col & (half - 1)) + col // half)
    inner = lax.broadcasted_iota(jnp.int32, (group * chans, half), 1) > 0
    for start in range(0, rows, group):
        block = plane[:, start : start + group, :].reshape(chans * group, cols)
        parted = matmul(matmul(swap, block).astype(BF16), split)
        odd = parted[:, half:]
        before = jnp.where(inner, pltpu.roll(odd, 1, 1), 0.0)
        views = [view.astype(BF16) for view in (before, parted[:, :half], odd)]
        for at in range(group):
            row = start + at
            lanes = slice(row // 2 * half, (row // 2 + 1) * half)
            for e in range(3):
                lo = base + (3 * (row % 2) + e) * chans
                views_ref[lo : lo + chans, lanes] = views[e][at * chans : (at + 1) * chans]


def owner_of(seats, slot):
    here = lax.axis_index("chan")
    owner = jnp.int32(seats[0][slot])
    for chip in range(1, len(seats)):
        owner = jnp.where(here == chip, seats[chip][slot], owner)
    return owner


def own_views_kernel(seats, volume_ref, weight_ref, views_ref, taps_ref, odd_ref):
    chans = volume_ref.shape[0]
    channels = weight_ref.shape[2]
    odd_ref[...] = volume_ref[:, 1:]
    place_views(volume_ref.at[:, 0], views_ref, 0)
    place_views(volume_ref.at[:, 1], views_ref, 6 * chans)
    part = channels // len(seats)
    row = lax.broadcasted_iota(jnp.int32, (channels, channels), 0)
    col = lax.broadcasted_iota(jnp.int32, (channels, channels), 1)
    order = jnp.zeros((channels, channels), F32)
    for slot in range(len(seats)):
        moved = (owner_of(seats, slot) - slot) * part
        inside = (col >= slot * part) & (col < (slot + 1) * part)
        order = jnp.where(inside & (row == col + moved), 1.0, order)
    ordered = matmul(weight_ref[...].reshape(27 * chans, channels), order.astype(BF16)).astype(BF16)
    zero = jnp.zeros((chans, channels), BF16)
    for k, e in enumerate((1, 2, 0)):
        for b in range(3):
            pick = lambda a: ordered[(9 * a + 3 * b + e) * chans : (9 * a + 3 * b + e + 1) * chans]
            for plane, line in enumerate(((zero, pick(1)), (pick(0), pick(2)))):
                lo = ((3 * plane + k) * 3 + b) * chans
                taps_ref[lo : lo + chans, :] = jnp.concatenate(line, axis=1)


def behind_views_kernel(behind_ref, views_ref):
    place_views(behind_ref.at[:, 0], views_ref, 0)


def place_lines(part, out_ref, at, wide_ref):
    outs, _, rows, cols = part.shape
    wide_ref[...] = part[...].reshape(outs * rows, cols).astype(F32)
    for row in range(rows):
        line = wide_ref[pl.ds(row, outs, stride=rows), :].astype(BF16)
        out_ref[at : at + outs, row * cols : (row + 1) * cols] = line


def lines_kernel(*refs):
    *parts, out_ref, wide_ref = refs
    at = 0
    for part in parts:
        place_lines(part, out_ref, at, wide_ref)
        at += part.shape[0]


def weight_kernel(seats, own_ref, behind_ref, near_ref, far_ref, out_ref, grads_ref, terms_ref, placed_ref):
    channels = out_ref.shape[0]
    chans = behind_ref.shape[0] // 6
    cells = own_ref.shape[1]
    cols = grads_ref.shape[1] - cells
    known = near_ref.shape[0]
    grads_ref[:known, :cells] = near_ref[...]
    grads_ref[known:, :cells] = far_ref[...]
    grads_ref[:, cells:] = jnp.zeros((channels, cols), BF16)
    both = jnp.concatenate([grads_ref[:, :cells], grads_ref[:, cols:]], axis=0)
    contract = (((1,), (1,)), ((), ()))
    for a, (ref, at) in enumerate(((behind_ref, 0), (own_ref, 0), (own_ref, 6 * chans))):
        terms = lax.dot_general(ref[at : at + 6 * chans], both, contract, preferred_element_type=F32)
        even, odd = terms[: 3 * chans, :channels], terms[3 * chans :]
        for b, block in enumerate((odd[:, channels:], even, odd[:, :channels])):
            lo = (9 * a + 3 * b) * chans
            terms_ref[lo : lo + 3 * chans, :] = block
    terms_ref[27 * chans :, :] = jnp.zeros((5 * chans, channels), F32)
    for c in range(chans):
        placed_ref[32 * c : 32 * c + 32, :] = terms_ref[pl.ds(c, 32, stride=chans), :]
    turned = placed_ref[...].T
    part = channels // len(seats)
    for slot in range(len(seats)):
        place = pl.multiple_of(owner_of(seats, slot) * part, part)
        out_ref[pl.ds(place, part), :] = turned[slot * part : (slot + 1) * part]


def input_kernel(taps_ref, next_near_ref, next_far_ref, near_ref, far_ref, out_ref, cells_ref, lines_ref):
    chans, _, rows, cols = out_ref.shape
    half = cols // 2
    grid_cells = half * rows // 2
    grads = [ref[...] for ref in (next_near_ref, next_far_ref, near_ref, far_ref)]
    cells_ref[:, :grid_cells] = matmul(taps_ref[...], jnp.concatenate(grads, axis=0))
    cells_ref[:, grid_cells:] = jnp.zeros((cells_ref.shape[0], half), F32)
    group = 256 // chans
    weave = one_hot(cols, cols, lambda row, col: col == 2 * (row & (half - 1)) + row // half)
    inner = lax.broadcasted_iota(jnp.int32, (chans, half), 1) < half - 1

    def cells(plane, kind, b, r):
        lo = ((3 * plane + kind) * 3 + b) * chans
        return cells_ref[lo : lo + chans, r * half : (r + 1) * half]

    for plane in range(2):
        for start in range(0, rows, group):
            pieces = []
            for row in range(start, start + group):
                r = row // 2
                if row % 2 == 0:
                    even, odd, next_odd = [cells(plane, kind, 1, r) for kind in range(3)]
                else:
                    even, odd, next_odd = [
                        cells(plane, kind, 0, r + 1) + cells(plane, kind, 2, r) for kind in range(3)
                    ]
                odd = odd + jnp.where(inner, pltpu.roll(next_odd, half - 1, 1), 0.0)
                pieces.append(jnp.concatenate([even, odd], axis=1).astype(BF16))
            woven = matmul(jnp.concatenate(pieces, axis=0), weave)
            for side in range(2):
                lanes = slice(side * half, (side + 1) * half)
                lines_ref[side] = woven[:, lanes]
                for c in range(chans):
                    line = lines_ref[side, pl.ds(c, group, stride=chans), :].astype(BF16)
                    out_ref[c, plane, start : start + group, lanes] = line


def total_kernel(scale, terms_ref, out_ref):
    chans, outs, taps = out_ref.shape
    total = terms_ref[0]
    for source in range(1, terms_ref.shape[0]):
        total = total + terms_ref[source]
    total = total * scale
    for c in range(chans):
        out_ref[c] = total[:, 32 * c : 32 * c + taps]


def from_behind(shard, axis, by):
    count = lax.axis_size(axis)
    pairs = [(i, i + by) for i in range(count) if 0 <= i + by < count]
    return lax.ppermute(shard, axis, pairs)


def upsample(stacked, axis, extended):
    tap_zero, tap_one, tap_two = (stacked[0], stacked[1], stacked[2])
    coord_axis = axis - 1
    length = tap_zero.shape[coord_axis]
    if extended:
        outer = length - 1
        even_cells = lax.slice_in_dim(tap_one, 0, outer, axis=coord_axis)
        odd_cells = lax.slice_in_dim(tap_zero, 1, length, axis=coord_axis) + lax.slice_in_dim(
            tap_two, 0, outer, axis=coord_axis
        )
    else:
        outer = length
        shifted = lax.slice_in_dim(tap_zero, 1, length, axis=coord_axis)
        shifted = jnp.concatenate(
            [shifted, jnp.zeros_like(lax.slice_in_dim(tap_zero, 0, 1, axis=coord_axis))],
            axis=coord_axis,
        )
        even_cells = tap_one
        odd_cells = shifted + tap_two
    paired = jnp.stack([even_cells, odd_cells], axis=coord_axis + 1)
    new_shape = list(even_cells.shape)
    new_shape[coord_axis] = 2 * outer
    return paired.reshape(new_shape)


def phase_grads(weight_rows, grads_ext):
    local_in = weight_rows.shape[0] // 27
    channels_out, planes, rows, cols = grads_ext.shape
    taps_out = jnp.dot(
        weight_rows, grads_ext.reshape(channels_out, -1), preferred_element_type=jnp.float32
    )
    taps_out = taps_out.reshape(3, 3, 3, local_in, planes, rows, cols)
    along_w = upsample(jnp.moveaxis(taps_out, 2, 0), 6, False)
    along_h = upsample(jnp.moveaxis(along_w, 1, 0), 4, False)
    return upsample(along_h, 2, True)


def weight_terms(inputs, grads_ext):
    row_extra = 0
    weight_cube = lax.conv_general_dilated(
        inputs[None],
        grads_ext[:, None],
        (1, 1, 1),
        ((1, 2), (1, row_extra), (1, 0)),
        rhs_dilation=(2, 2, 2),
        dimension_numbers=("CNDHW", "OIDHW", "NCDHW"),
        preferred_element_type=jnp.float32,
    )
    return jnp.transpose(weight_cube, (2, 3, 4, 0, 1)).reshape(
        27, weight_cube.shape[0], weight_cube.shape[1]
    )


def plain_shards(grad_out, volume, weight):
    plane_next = from_behind(grad_out, "depth", -1)
    grads_ext = jnp.concatenate([grad_out, plane_next], axis=1)
    channels_out = weight.shape[2]
    local_in = volume.shape[0]
    every_channel = lax.all_gather(grads_ext, "chan", axis=0, tiled=True)
    own_weight = lax.dynamic_slice_in_dim(weight, lax.axis_index("chan") * local_in, local_in, 1)
    input_part = phase_grads(own_weight.reshape(27 * local_in, channels_out), every_channel)
    weight_part = weight_terms(volume, every_channel)
    input_grad = input_part.astype(jnp.bfloat16)
    summed = lax.psum_scatter(weight_part, "depth", scatter_dimension=2, tiled=True)
    cell_count = grad_out.shape[1] * lax.axis_size("depth") * grad_out.shape[2] * grad_out.shape[3]
    return (input_grad, summed * (1.0 / math.sqrt(cell_count)))


def call(kernel, out_shape, *args, specs=None, scratch=(), cost=None):
    flops, moved = cost
    return pl.pallas_call(
        kernel,
        out_shape=out_shape,
        in_specs=specs or [VMEM] * len(args),
        out_specs=jax.tree.map(lambda _: VMEM, out_shape),
        scratch_shapes=scratch,
        compiler_params=pltpu.CompilerParams(vmem_limit_bytes=LIMIT),
        cost_estimate=pl.CostEstimate(flops=flops, bytes_accessed=moved, transcendentals=0),
    )(*args)


def shards(grad_out, volume, weight):
    count = lax.axis_size("chan")
    depth = lax.axis_size("depth")
    own_outs, _, rows, cols = grad_out.shape
    chans = volume.shape[0]
    channels = weight.shape[2]
    cells = rows * cols
    order = ring_order(count)
    ahead = [(order[i], order[(i + 1) % count]) for i in range(count)]
    back = [(b, a) for a, b in ahead]
    farther = [(i, i + 1) for i in range(depth - 1)]
    nearer = [(i, i - 1) for i in range(1, depth)]
    shifts = [0, -1]
    for step in range(1, count // 2):
        shifts += [step, -step - 1]
    seats = [[order[(order.index(chip) + s) % count] for s in shifts] for chip in range(count)]

    own_weight = lax.dynamic_slice_in_dim(weight, lax.axis_index("chan") * local_in, local_in, 1)
    input_part = phase_grads(own_weight.reshape(27 * local_in, channels_out), every_channel)
    weight_part = weight_terms(volume, every_channel)
    input_grad = input_part.astype(jnp.bfloat16)
    summed = lax.psum_scatter(weight_part, "depth", scatter_dimension=2, tiled=True)
    cell_count = grad_out.shape[1] * lax.axis_size("depth") * grad_out.shape[2] * grad_out.shape[3]
    return (input_grad, summed * (1.0 / math.sqrt(cell_count)))


def call(kernel, out_shape, *args, specs=None, scratch=(), cost=None):
    flops, moved = cost
    return pl.pallas_call(
        kernel,
        out_shape=out_shape,
        in_specs=specs or [VMEM] * len(args),
        out_specs=jax.tree.map(lambda _: VMEM, out_shape),
        scratch_shapes=scratch,
        compiler_params=pltpu.CompilerParams(vmem_limit_bytes=LIMIT),
        cost_estimate=pl.CostEstimate(flops=flops, bytes_accessed=moved, transcendentals=0),
    )(*args)


def shards(grad_out, volume, weight):
    count = lax.axis_size("chan")
    depth = lax.axis_size("depth")
    own_outs, _, rows, cols = grad_out.shape
    chans = volume.shape[0]
    channels = weight.shape[2]
    cells = rows * cols
    order = ring_order(count)
    ahead = [(order[i], order[(i + 1) % count]) for i in range(count)]
    back = [(b, a) for a, b in ahead]
    farther = [(i, i + 1) for i in range(depth - 1)]
    nearer = [(i, i - 1) for i in range(1, depth)]
    shifts = [0, -1]
    for step in range(1, count // 2):
        shifts += [step, -step - 1]
    seats = [[order[(order.index(chip) + s) % count] for s in shifts] for chip in range(count)]

    own_weight = lax.dynamic_slice_in_dim(weight, lax.axis_index("chan") * local_in, local_in, 1)
    input_part = phase_grads(own_weight.reshape(27 * local_in, channels_out), every_channel)
    weight_part = weight_terms(volume, every_channel)
    input_grad = input_part.astype(jnp.bfloat16)
    summed = lax.psum_scatter(weight_part, "depth", scatter_dimension=2, tiled=True)
    cell_count = grad_out.shape[1] * lax.axis_size("depth") * grad_out.shape[2] * grad_out.shape[3]
    return (input_grad, summed * (1.0 / math.sqrt(cell_count)))


def call(kernel, out_shape, *args, specs=None, scratch=(), cost=None):
    flops, moved = cost
    return pl.pallas_call(
        kernel,
        out_shape=out_shape,
        in_specs=specs or [VMEM] * len(args),
        out_specs=jax.tree.map(lambda _: VMEM, out_shape),
        scratch_shapes=scratch,
        compiler_params=pltpu.CompilerParams(vmem_limit_bytes=LIMIT),
        cost_estimate=pl.CostEstimate(flops=flops, bytes_accessed=moved, transcendentals=0),
    )(*args)


def shards(grad_out, volume, weight):
    count = lax.axis_size("chan")
    depth = lax.axis_size("depth")
    own_outs, _, rows, cols = grad_out.shape
    chans = volume.shape[0]
    channels = weight.shape[2]
    cells = rows * cols
    order = ring_order(count)
    ahead = [(order[i], order[(i + 1) % count]) for i in range(count)]
    back = [(b, a) for a, b in ahead]
    farther = [(i, i + 1) for i in range(depth - 1)]
    nearer = [(i, i - 1) for i in range(1, depth)]
    shifts = [0, -1]
    for step in range(1, count // 2):
        shifts += [step, -step - 1]
    seats = [[order[(order.index(chip) + s) % count] for s in shifts] for chip in range(count)]

    own_weight = lax.dynamic_slice_in_dim(weight, lax.axis_index("chan") * local_in, local_in, 1)
    input_part = phase_grads(own_weight.reshape(27 * local_in, channels_out), every_channel)
    weight_part = weight_terms(volume, every_channel)
    input_grad = input_part.astype(jnp.bfloat16)
    summed = lax.psum_scatter(weight_part, "depth", scatter_dimension=2, tiled=True)
    cell_count = grad_out.shape[1] * lax.axis_size("depth") * grad_out.shape[2] * grad_out.shape[3]
    return (input_grad, summed * (1.0 / math.sqrt(cell_count)))


def call(kernel, out_shape, *args, specs=None, scratch=(), cost=None):
    flops, moved = cost
    return pl.pallas_call(
        kernel,
        out_shape=out_shape,
        in_specs=specs or [VMEM] * len(args),
        out_specs=jax.tree.map(lambda _: VMEM, out_shape),
        scratch_shapes=scratch,
        compiler_params=pltpu.CompilerParams(vmem_limit_bytes=LIMIT),
        cost_estimate=pl.CostEstimate(flops=flops, bytes_accessed=moved, transcendentals=0),
    )(*args)


def shards(grad_out, volume, weight):
    count = lax.axis_size("chan")
    depth = lax.axis_size("depth")
    own_outs, _, rows, cols = grad_out.shape
    chans = volume.shape[0]
    channels = weight.shape[2]
    cells = rows * cols
    order = ring_order(count)
    ahead = [(order[i], order[(i + 1) % count]) for i in range(count)]
    back = [(b, a) for a, b in ahead]
    farther = [(i, i + 1) for i in range(depth - 1)]
    nearer = [(i, i - 1) for i in range(1, depth)]
    shifts = [0]

    near = []
    up = down = grad_out
    for step in range(1, (count - 1) // 2 + 1):
        up = lax.ppermute(up, "chan", ahead)
        down = lax.ppermute(down, "chan", back)
        near += [up, down]
        shifts += [-step, step]
    last = lax.ppermute(up, "chan", ahead)
    shifts += [count // 2]
    seats = [[order[(order.index(chip) + s) % count] for s in shifts] for chip in range(count)]

    shifts = [0, -1]
    for step in range(1, count // 2):
        shifts += [step, -step - 1]
    seats = [[order[(order.index(chip) + s) % count] for s in shifts] for chip in range(count)]

    own_weight = lax.dynamic_slice_in_dim(weight, lax.axis_index("chan") * chans, chans, 1)
    views, taps, odd = call(
        lambda *refs: own_views_kernel(seats, *refs),
        (
            jax.ShapeDtypeStruct((12 * chans, cells), BF16),
            jax.ShapeDtypeStruct((18 * chans, 2 * channels), BF16),
            jax.ShapeDtypeStruct((chans, 1, 2 * rows, 2 * cols), BF16),
        ),
        volume,
        own_weight,
        cost=(2 * 2 * 2 * cells * chans * 8 * cols, 4 << 20),
    )
    first = lax.ppermute(grad_out, "chan", ahead)
    up, down, odd = lax.optimization_barrier((first, grad_out, odd))
    far = []
    for step in range(1, count // 2):
        down = lax.ppermute(down, "chan", back)
        up = lax.ppermute(up, "chan", ahead)
        far += [down, up]
    behind = lax.ppermute(odd, "depth", farther)
    behind_views = call(
        behind_views_kernel,
        jax.ShapeDtypeStruct((6 * chans, cells), BF16),
        behind,
        cost=(2 * 2 * cells * chans * 8 * cols, 2 << 20),
    )
    lines = lambda *parts: call(
        lines_kernel,
        jax.ShapeDtypeStruct((len(parts) * own_outs, cells), BF16),
        *parts,
        scratch=(pltpu.VMEM((own_outs * rows, cols), F32),),
        cost=(1 << 20, 2 << 20),
    )
    near_lines = lines(grad_out, first)
    next_near_lines = lax.ppermute(near_lines, "depth", nearer)
    *far, behind_views = lax.optimization_barrier((*far, behind_views))
    far_lines = lines(*far)
    next_far_lines = lax.ppermute(far_lines, "depth", nearer)
    partial = call(
        lambda *refs: weight_kernel(seats, *refs),
        jax.ShapeDtypeStruct((channels, 32 * chans), F32),
        views,
        behind_views,
        near_lines,
        far_lines,
        scratch=(
            pltpu.VMEM((channels, cells + cols), BF16),
            pltpu.VMEM((32 * chans, channels), F32),
            pltpu.VMEM((32 * chans, channels), F32),
        ),
        cost=(2 * 27 * chans * channels * cells, 8 << 20),
    )
    terms = lax.all_to_all(partial, "depth", split_axis=0, concat_axis=0, tiled=True)
    input_grad = call(
        input_kernel,
        jax.ShapeDtypeStruct(volume.shape, BF16),
        taps,
        next_near_lines,
        next_far_lines,
        near_lines,
        far_lines,
        scratch=(
            pltpu.VMEM((18 * chans, cells + cols), F32),
            pltpu.VMEM((2, 256, cols), F32),
        ),
        cost=(2 * 18 * chans * 2 * channels * cells, 8 << 20),
    )
    terms, input_grad = lax.optimization_barrier((terms, input_grad))
    scale = 1.0 / math.sqrt(depth * cells)
    outs = channels // depth
    weight_grad = call(
        lambda *refs: total_kernel(scale, *refs),
        jax.ShapeDtypeStruct((chans, outs, 27), F32),
        terms.reshape(depth, outs, 32 * chans),
        cost=(1 << 20, 1 << 20),
    )
    return input_grad, jnp.transpose(weight_grad, (2, 0, 1))


def solution(mesh):
    in_specs = (P("chan", "depth", None, None), P("chan", "depth", None, None), P())
    out_specs = (P("chan", "depth", None, None), P(None, "chan", "depth"))
    ring = mesh.shape["chan"]

    def either(grad_out, volume, weight):
        fits = (
            grad_out.shape[0] % 16 == 0
            and volume.shape[0] == 16
            and grad_out.shape[1] == 1
            and ring % 2 == 0
            and ring >= 4
        )
        return (shards if fits else plain_shards)(grad_out, volume, weight)

    return jax.shard_map(either, mesh=mesh, in_specs=in_specs, out_specs=out_specs, check_vma=False)
```

```python
import math

import jax
import jax.numpy as jnp
from jax import lax
from jax.experimental import pallas as pl
from jax.experimental.pallas import tpu as pltpu
from jax.sharding import PartitionSpec as P

F32 = jnp.float32
BF16 = jnp.bfloat16
VMEM = pl.BlockSpec(memory_space=pltpu.VMEM)
SMEM = pl.BlockSpec(memory_space=pltpu.SMEM)
LIMIT = 48 * 1024 * 1024


def ring_order(count):
    return [0] + list(range(1, count, 2)) + list(range(2, count, 2))[::-1]


def matmul(left, right):
    return jnp.dot(left, right, preferred_element_type=F32)


def one_hot(rows, cols, source):
    row = lax.broadcasted_iota(jnp.int32, (rows, cols), 0)
    col = lax.broadcasted_iota(jnp.int32, (rows, cols), 1)
    return jnp.where(source(row, col), 1.0, 0.0).astype(BF16)


def swap_rows(major, minor):
    bits = minor.bit_length() - 1
    return one_hot(
        major * minor,
        major * minor,
        lambda row, col: col == (row & (minor - 1)) * major + (row >> bits),
    )


def place_views(plane, views_ref, base):
    chans, rows, cols = plane.shape
    half = cols // 2
    group = 256 // chans
    swap = swap_rows(group, chans)
    split = one_hot(cols, cols, lambda row, col: row == 2 * (col & (half - 1)) + col // half)
    inner = lax.broadcasted_iota(jnp.int32, (group * chans, half), 1) > 0
    for start in range(0, rows, group):
        block = plane[:, start : start + group, :].reshape(chans * group, cols)
        parted = matmul(matmul(swap, block).astype(BF16), split)
        odd = parted[:, half:]
        before = jnp.where(inner, pltpu.roll(odd, 1, 1), 0.0)
        views = [view.astype(BF16) for view in (before, parted[:, :half], odd)]
        for at in range(group):
            row = start + at
            lanes = slice(row // 2 * half, (row // 2 + 1) * half)
            for e in range(3):
                lo = base + (3 * (row % 2) + e) * chans
                views_ref[lo : lo + chans, lanes] = views[e][at * chans : (at + 1) * chans]


def owner_of(seats, slot):
    here = lax.axis_index("chan")
    owner = jnp.int32(seats[0][slot])
    for chip in range(1, len(seats)):
        owner = jnp.where(here == chip, seats[chip][slot], owner)
    return owner


def own_views_kernel(seats, depth, volume_ref, weight_ref, views_ref, taps_ref, odd_ref):
    chans = volume_ref.shape[0]
    channels = weight_ref.shape[2]
    odd_ref[...] = volume_ref[:, 1:]
    place_views(volume_ref.at[:, 0], views_ref, 0)
    place_views(volume_ref.at[:, 1], views_ref, 6 * chans)
    part = channels // len(seats)
    row = lax.broadcasted_iota(jnp.int32, (channels, channels), 0)
    col = lax.broadcasted_iota(jnp.int32, (channels, channels), 1)
    order = jnp.zeros((channels, channels), F32)
    for slot in range(len(seats)):
        moved = (owner_of(seats, slot) - slot) * part
        inside = (col >= slot * part) & (col < (slot + 1) * part)
        order = jnp.where(inside & (row == col + moved), 1.0, order)
    ordered = matmul(weight_ref[...].reshape(27 * chans, channels), order.astype(BF16)).astype(BF16)
    beyond = jnp.where(lax.axis_index("depth") == depth - 1, 0.0, 1.0).astype(BF16)
    zero = jnp.zeros((chans, channels), BF16)
    for k, e in enumerate((1, 2, 0)):
        for b in range(3):
            pick = lambda a: ordered[(9 * a + 3 * b + e) * chans : (9 * a + 3 * b + e + 1) * chans]
            for plane, line in enumerate(((zero, pick(1)), (pick(0) * beyond, pick(2)))):
                lo = ((3 * plane + k) * 3 + b) * chans
                taps_ref[lo : lo + chans, :] = jnp.concatenate(line, axis=1)


def behind_views_kernel(behind_ref, views_ref):
    first = lax.axis_index("depth") == 0

    @pl.when(jnp.logical_not(first))
    def _():
        place_views(behind_ref.at[:, 0], views_ref, 0)

    @pl.when(first)
    def _():
        views_ref[...] = jnp.zeros(views_ref.shape, BF16)


def place_lines(part, out_ref, at, wide_ref):
    outs, _, rows, cols = part.shape
    wide_ref[...] = part[...].reshape(outs * rows, cols).astype(F32)
    for row in range(rows):
        line = wide_ref[pl.ds(row, outs, stride=rows), :].astype(BF16)
        out_ref[at : at + outs, row * cols : (row + 1) * cols] = line


def lines_kernel(*refs):
    *parts, out_ref, wide_ref = refs
    at = 0
    for part in parts:
        place_lines(part, out_ref, at, wide_ref)
        at += part.shape[0]


def weight_kernel(seats, own_ref, behind_ref, near_ref, far_ref, out_ref, grads_ref, terms_ref, placed_ref):
    channels = out_ref.shape[0]
    chans = behind_ref.shape[0] // 6
    cells = own_ref.shape[1]
    cols = grads_ref.shape[1] - cells
    known = near_ref.shape[0]
    grads_ref[:known, :cells] = near_ref[...]
    grads_ref[known:, :cells] = far_ref[...]
    grads_ref[:, cells:] = jnp.zeros((channels, cols), BF16)
    both = jnp.concatenate([grads_ref[:, :cells], grads_ref[:, cols:]], axis=0)
    contract = (((1,), (1,)), ((), ()))
    for a, (ref, at) in enumerate(((behind_ref, 0), (own_ref, 0), (own_ref, 6 * chans))):
        terms = lax.dot_general(ref[at : at + 6 * chans], both, contract, preferred_element_type=F32)
        even, odd = terms[: 3 * chans, :channels], terms[3 * chans :]
        for b, block in enumerate((odd[:, channels:], even, odd[:, :channels])):
            lo = (9 * a + 3 * b) * chans
            terms_ref[lo : lo + 3 * chans, :] = block
    terms_ref[27 * chans :, :] = jnp.zeros((5 * chans, channels), F32)
    for c in range(chans):
        placed_ref[32 * c : 32 * c + 32, :] = terms_ref[pl.ds(c, 32, stride=chans), :]
    turned = placed_ref[...].T
    part = channels // len(seats)
    for slot in range(len(seats)):
        place = pl.multiple_of(owner_of(seats, slot) * part, part)
        out_ref[pl.ds(place, part), :] = turned[slot * part : (slot + 1) * part]


def input_kernel(taps_ref, next_near_ref, next_far_ref, near_ref, far_ref, out_ref, cells_ref, lines_ref):
    chans, _, rows, cols = out_ref.shape
    half = cols // 2
    grid_cells = half * rows // 2
    grads = [ref[...] for ref in (next_near_ref, next_far_ref, near_ref, far_ref)]
    cells_ref[:, :grid_cells] = matmul(taps_ref[...], jnp.concatenate(grads, axis=0))
    cells_ref[:, grid_cells:] = jnp.zeros((cells_ref.shape[0], half), F32)
    group = 256 // chans
    weave = one_hot(cols, cols, lambda row, col: col == 2 * (row & (half - 1)) + row // half)
    inner = lax.broadcasted_iota(jnp.int32, (chans, half), 1) < half - 1

    def cells(plane, kind, b, r):
        lo = ((3 * plane + kind) * 3 + b) * chans
        return cells_ref[lo : lo + chans, r * half : (r + 1) * half]

    for plane in range(2):
        for start in range(0, rows, group):
            pieces = []
            for row in range(start, start + group):
                r = row // 2
                if row % 2 == 0:
                    even, odd, next_odd = [cells(plane, kind, 1, r) for kind in range(3)]
                else:
                    even, odd, next_odd = [
                        cells(plane, kind, 0, r + 1) + cells(plane, kind, 2, r) for kind in range(3)
                    ]
                odd = odd + jnp.where(inner, pltpu.roll(next_odd, half - 1, 1), 0.0)
                pieces.append(jnp.concatenate([even, odd], axis=1).astype(BF16))
            woven = matmul(jnp.concatenate(pieces, axis=0), weave)
            for side in range(2):
                lanes = slice(side * half, (side + 1) * half)
                lines_ref[side] = woven[:, lanes]
                for c in range(chans):
                    line = lines_ref[side, pl.ds(c, group, stride=chans), :].astype(BF16)
                    out_ref[c, plane, start : start + group, lanes] = line


def total_kernel(scale, terms_ref, out_ref):
    chans, outs, taps = out_ref.shape
    total = terms_ref[0]
    for source in range(1, terms_ref.shape[0]):
        total = total + terms_ref[source]
    total = total * scale
    for c in range(chans):
        out_ref[c] = total[:, 32 * c : 32 * c + taps]


def from_behind(shard, axis, by):
    count = lax.axis_size(axis)
    pairs = [(i, i + by) for i in range(count) if 0 <= i + by < count]
    return lax.ppermute(shard, axis, pairs)


def upsample(stacked, axis, extended):
    tap_zero, tap_one, tap_two = (stacked[0], stacked[1], stacked[2])
    coord_axis = axis - 1
    length = tap_zero.shape[coord_axis]
    if extended:
        outer = length - 1
        even_cells = lax.slice_in_dim(tap_one, 0, outer, axis=coord_axis)
        odd_cells = lax.slice_in_dim(tap_zero, 1, length, axis=coord_axis) + lax.slice_in_dim(
            tap_two, 0, outer, axis=coord_axis
        )
    else:
        outer = length
        shifted = lax.slice_in_dim(tap_zero, 1, length, axis=coord_axis)
        shifted = jnp.concatenate(
            [shifted, jnp.zeros_like(lax.slice_in_dim(tap_zero, 0, 1, axis=coord_axis))],
            axis=coord_axis,
        )
        even_cells = tap_one
        odd_cells = shifted + tap_two
    paired = jnp.stack([even_cells, odd_cells], axis=coord_axis + 1)
    new_shape = list(even_cells.shape)
    new_shape[coord_axis] = 2 * outer
    return paired.reshape(new_shape)


def phase_grads(weight_rows, grads_ext):
    local_in = weight_rows.shape[0] // 27
    channels_out, planes, rows, cols = grads_ext.shape
    taps_out = jnp.dot(
        weight_rows, grads_ext.reshape(channels_out, -1), preferred_element_type=jnp.float32
    )
    taps_out = taps_out.reshape(3, 3, 3, local_in, planes, rows, cols)
    along_w = upsample(jnp.moveaxis(taps_out, 2, 0), 6, False)
    along_h = upsample(jnp.moveaxis(along_w, 1, 0), 4, False)
    return upsample(along_h, 2, True)


def weight_terms(inputs, grads_ext):
    row_extra = 0
    weight_cube = lax.conv_general_dilated(
        inputs[None],
        grads_ext[:, None],
        (1, 1, 1),
        ((1, 2), (1, row_extra), (1, 0)),
        rhs_dilation=(2, 2, 2),
        dimension_numbers=("CNDHW", "OIDHW", "NCDHW"),
        preferred_element_type=jnp.float32,
    )
    return jnp.transpose(weight_cube, (2, 3, 4, 0, 1)).reshape(
        27, weight_cube.shape[0], weight_cube.shape[1]
    )


def plain_shards(grad_out, volume, weight):
    plane_next = from_behind(grad_out, "depth", -1)
    grads_ext = jnp.concatenate([grad_out, plane_next], axis=1)
    channels_out = weight.shape[2]
    local_in = volume.shape[0]
    every_channel = lax.all_gather(grads_ext, "chan", axis=0, tiled=True)
    own_weight = lax.dynamic_slice_in_dim(weight, lax.axis_index("chan") * local_in, local_in, 1)
    input_part = phase_grads(own_weight.reshape(27 * local_in, channels_out), every_channel)
    weight_part = weight_terms(volume, every_channel)
    input_grad = input_part.astype(jnp.bfloat16)
    summed = lax.psum_scatter(weight_part, "depth", scatter_dimension=2, tiled=True)
    cell_count = grad_out.shape[1] * lax.axis_size("depth") * grad_out.shape[2] * grad_out.shape[3]
    return (input_grad, summed * (1.0 / math.sqrt(cell_count)))


def call(kernel, out_shape, *args, specs=None, scratch=(), cost=None):
    flops, moved = cost
    return pl.pallas_call(
        kernel,
        out_shape=out_shape,
        in_specs=specs or [VMEM] * len(args),
        out_specs=jax.tree.map(lambda _: VMEM, out_shape),
        scratch_shapes=scratch,
        compiler_params=pltpu.CompilerParams(vmem_limit_bytes=LIMIT),
        cost_estimate=pl.CostEstimate(flops=flops, bytes_accessed=moved, transcendentals=0),
    )(*args)


def shards(grad_out, volume, weight):
    count = lax.axis_size("chan")
    depth = lax.axis_size("depth")
    own_outs, _, rows, cols = grad_out.shape
    chans = volume.shape[0]
    channels = weight.shape[2]
    cells = rows * cols
    order = ring_order(count)
    ahead = [(order[i], order[(i + 1) % count]) for i in range(count)]
    back = [(b, a) for a, b in ahead]
    farther = [(i, (i + 1) % depth) for i in range(depth)]
    nearer = [(b, a) for a, b in farther]
    own_weight = lax.dynamic_slice_in_dim(weight, lax.axis_index("chan") * local_in, local_in, 1)
    input_part = phase_grads(own_weight.reshape(27 * local_in, channels_out), every_channel)
    weight_part = weight_terms(volume, every_channel)
    input_grad = input_part.astype(jnp.bfloat16)
    summed = lax.psum_scatter(weight_part, "depth", scatter_dimension=2, tiled=True)
    cell_count = grad_out.shape[1] * lax.axis_size("depth") * grad_out.shape[2] * grad_out.shape[3]
    return (input_grad, summed * (1.0 / math.sqrt(cell_count)))


def call(kernel, out_shape, *args, specs=None, scratch=(), cost=None):
    flops, moved = cost
    return pl.pallas_call(
        kernel,
        out_shape=out_shape,
        in_specs=specs or [VMEM] * len(args),
        out_specs=jax.tree.map(lambda _: VMEM, out_shape),
        scratch_shapes=scratch,
        compiler_params=pltpu.CompilerParams(vmem_limit_bytes=LIMIT),
        cost_estimate=pl.CostEstimate(flops=flops, bytes_accessed=moved, transcendentals=0),
    )(*args)


def shards(grad_out, volume, weight):
    count = lax.axis_size("chan")
    depth = lax.axis_size("depth")
    own_outs, _, rows, cols = grad_out.shape
    chans = volume.shape[0]
    channels = weight.shape[2]
    cells = rows * cols
    order = ring_order(count)
    ahead = [(order[i], order[(i + 1) % count]) for i in range(count)]
    back = [(b, a) for a, b in ahead]
    farther = [(i, (i + 1) % depth) for i in range(depth)]
    nearer = [(b, a) for a, b in farther]
    own_weight = lax.dynamic_slice_in_dim(weight, lax.axis_index("chan") * local_in, local_in, 1)
    input_part = phase_grads(own_weight.reshape(27 * local_in, channels_out), every_channel)
    weight_part = weight_terms(volume, every_channel)
    input_grad = input_part.astype(jnp.bfloat16)
    summed = lax.psum_scatter(weight_part, "depth", scatter_dimension=2, tiled=True)
    cell_count = grad_out.shape[1] * lax.axis_size("depth") * grad_out.shape[2] * grad_out.shape[3]
    return (input_grad, summed * (1.0 / math.sqrt(cell_count)))


def call(kernel, out_shape, *args, specs=None, scratch=(), cost=None):
    flops, moved = cost
    return pl.pallas_call(
        kernel,
        out_shape=out_shape,
        in_specs=specs or [VMEM] * len(args),
        out_specs=jax.tree.map(lambda _: VMEM, out_shape),
        scratch_shapes=scratch,
        compiler_params=pltpu.CompilerParams(vmem_limit_bytes=LIMIT),
        cost_estimate=pl.CostEstimate(flops=flops, bytes_accessed=moved, transcendentals=0),
    )(*args)


def shards(grad_out, volume, weight):
    count = lax.axis_size("chan")
    depth = lax.axis_size("depth")
    own_outs, _, rows, cols = grad_out.shape
    chans = volume.shape[0]
    channels = weight.shape[2]
    cells = rows * cols
    order = ring_order(count)
    ahead = [(order[i], order[(i + 1) % count]) for i in range(count)]
    back = [(b, a) for a, b in ahead]
    farther = [(i, (i + 1) % depth) for i in range(depth)]
    nearer = [(b, a) for a, b in farther]
    own_weight = lax.dynamic_slice_in_dim(weight, lax.axis_index("chan") * local_in, local_in, 1)
    input_part = phase_grads(own_weight.reshape(27 * local_in, channels_out), every_channel)
    weight_part = weight_terms(volume, every_channel)
    input_grad = input_part.astype(jnp.bfloat16)
    summed = lax.psum_scatter(weight_part, "depth", scatter_dimension=2, tiled=True)
    cell_count = grad_out.shape[1] * lax.axis_size("depth") * grad_out.shape[2] * grad_out.shape[3]
    return (input_grad, summed * (1.0 / math.sqrt(cell_count)))


def call(kernel, out_shape, *args, specs=None, scratch=(), cost=None):
    flops, moved = cost
    return pl.pallas_call(
        kernel,
        out_shape=out_shape,
        in_specs=specs or [VMEM] * len(args),
        out_specs=jax.tree.map(lambda _: VMEM, out_shape),
        scratch_shapes=scratch,
        compiler_params=pltpu.CompilerParams(vmem_limit_bytes=LIMIT),
        cost_estimate=pl.CostEstimate(flops=flops, bytes_accessed=moved, transcendentals=0),
    )(*args)


def shards(grad_out, volume, weight):
    count = lax.axis_size("chan")
    depth = lax.axis_size("depth")
    own_outs, _, rows, cols = grad_out.shape
    chans = volume.shape[0]
    channels = weight.shape[2]
    cells = rows * cols
    order = ring_order(count)
    ahead = [(order[i], order[(i + 1) % count]) for i in range(count)]
    back = [(b, a) for a, b in ahead]
    farther = [(i, (i + 1) % depth) for i in range(depth)]
    nearer = [(b, a) for a, b in farther]
    shifts = [0]

    near = []
    up = down = grad_out
    for step in range(1, (count - 1) // 2 + 1):
        up = lax.ppermute(up, "chan", ahead)
        down = lax.ppermute(down, "chan", back)
        near += [up, down]
        shifts += [-step, step]
    last = lax.ppermute(up, "chan", ahead)
    shifts += [count // 2]
    seats = [[order[(order.index(chip) + s) % count] for s in shifts] for chip in range(count)]

    shifts = [0, -1]
    for step in range(1, count // 2):
        shifts += [step, -step - 1]
    seats = [[order[(order.index(chip) + s) % count] for s in shifts] for chip in range(count)]

    own_weight = lax.dynamic_slice_in_dim(weight, lax.axis_index("chan") * chans, chans, 1)
    views, taps, odd = call(
        lambda *refs: own_views_kernel(seats, depth, *refs),
        (
            jax.ShapeDtypeStruct((12 * chans, cells), BF16),
            jax.ShapeDtypeStruct((18 * chans, 2 * channels), BF16),
            jax.ShapeDtypeStruct((chans, 1, 2 * rows, 2 * cols), BF16),
        ),
        volume,
        own_weight,
        cost=(2 * 2 * 2 * cells * chans * 8 * cols, 4 << 20),
    )
    first = lax.ppermute(grad_out, "chan", ahead)
    first, views = lax.optimization_barrier((first, views))
    up, down, far = first, grad_out, []
    for step in range(1, count // 2):
        down = lax.ppermute(down, "chan", back)
        up = lax.ppermute(up, "chan", ahead)
        far += [down, up]
    lines = lambda *parts: call(
        lines_kernel,
        jax.ShapeDtypeStruct((len(parts) * own_outs, cells), BF16),
        *parts,
        scratch=(pltpu.VMEM((own_outs * rows, cols), F32),),
        cost=(1 << 20, 2 << 20),
    )
    near_lines = lines(grad_out, first)
    far[0], odd = lax.optimization_barrier((far[0], odd))
    next_near_lines = lax.ppermute(near_lines, "depth", nearer)
    behind = lax.ppermute(odd, "depth", farther)
    behind_views = call(
        behind_views_kernel,
        jax.ShapeDtypeStruct((6 * chans, cells), BF16),
        behind,
        cost=(2 * 2 * cells * chans * 8 * cols, 2 << 20),
    )
    far_lines = lines(*far)
    next_far_lines = lax.ppermute(far_lines, "depth", nearer)
    partial = call(
        lambda *refs: weight_kernel(seats, *refs),
        jax.ShapeDtypeStruct((channels, 32 * chans), F32),
        views,
        behind_views,
        near_lines,
        far_lines,
        scratch=(
            pltpu.VMEM((channels, cells + cols), BF16),
            pltpu.VMEM((32 * chans, channels), F32),
            pltpu.VMEM((32 * chans, channels), F32),
        ),
        cost=(2 * 27 * chans * channels * cells, 8 << 20),
    )
    terms = lax.all_to_all(partial, "depth", split_axis=0, concat_axis=0, tiled=True)
    input_grad = call(
        input_kernel,
        jax.ShapeDtypeStruct(volume.shape, BF16),
        taps,
        next_near_lines,
        next_far_lines,
        near_lines,
        far_lines,
        scratch=(
            pltpu.VMEM((18 * chans, cells + cols), F32),
            pltpu.VMEM((2, 256, cols), F32),
        ),
        cost=(2 * 18 * chans * 2 * channels * cells, 8 << 20),
    )
    terms, input_grad = lax.optimization_barrier((terms, input_grad))
    scale = 1.0 / math.sqrt(depth * cells)
    outs = channels // depth
    weight_grad = call(
        lambda *refs: total_kernel(scale, *refs),
        jax.ShapeDtypeStruct((chans, outs, 27), F32),
        terms.reshape(depth, outs, 32 * chans),
        cost=(1 << 20, 1 << 20),
    )
    return input_grad, jnp.transpose(weight_grad, (2, 0, 1))


def solution(mesh):
    in_specs = (P("chan", "depth", None, None), P("chan", "depth", None, None), P())
    out_specs = (P("chan", "depth", None, None), P(None, "chan", "depth"))
    ring = mesh.shape["chan"]

    def either(grad_out, volume, weight):
        fits = (
            grad_out.shape[0] % 16 == 0
            and volume.shape[0] == 16
            and grad_out.shape[1] == 1
            and ring % 2 == 0
            and ring >= 4
        )
        return (shards if fits else plain_shards)(grad_out, volume, weight)

    return jax.shard_map(either, mesh=mesh, in_specs=in_specs, out_specs=out_specs, check_vma=False)
```

```python
import math

import jax
import jax.numpy as jnp
from jax import lax
from jax.experimental import pallas as pl
from jax.experimental.pallas import tpu as pltpu
from jax.sharding import PartitionSpec as P

F32 = jnp.float32
BF16 = jnp.bfloat16
VMEM = pl.BlockSpec(memory_space=pltpu.VMEM)
SMEM = pl.BlockSpec(memory_space=pltpu.SMEM)
LIMIT = 48 * 1024 * 1024


def ring_order(count):
    return [0] + list(range(1, count, 2)) + list(range(2, count, 2))[::-1]


def matmul(left, right):
    return jnp.dot(left, right, preferred_element_type=F32)


def one_hot(rows, cols, source):
    row = lax.broadcasted_iota(jnp.int32, (rows, cols), 0)
    col = lax.broadcasted_iota(jnp.int32, (rows, cols), 1)
    return jnp.where(source(row, col), 1.0, 0.0).astype(BF16)


def swap_rows(major, minor):
    bits = minor.bit_length() - 1
    return one_hot(
        major * minor,
        major * minor,
        lambda row, col: col == (row & (minor - 1)) * major + (row >> bits),
    )


def place_views(plane, views_ref, base):
    chans, rows, cols = plane.shape
    half = cols // 2
    group = 256 // chans
    swap = swap_rows(group, chans)
    split = one_hot(cols, cols, lambda row, col: row == 2 * (col & (half - 1)) + col // half)
    inner = lax.broadcasted_iota(jnp.int32, (group * chans, half), 1) > 0
    for start in range(0, rows, group):
        block = plane[:, start : start + group, :].reshape(chans * group, cols)
        parted = matmul(matmul(swap, block).astype(BF16), split)
        odd = parted[:, half:]
        before = jnp.where(inner, pltpu.roll(odd, 1, 1), 0.0)
        views = [view.astype(BF16) for view in (before, parted[:, :half], odd)]
        for at in range(group):
            row = start + at
            lanes = slice(row // 2 * half, (row // 2 + 1) * half)
            for e in range(3):
                lo = base + (3 * (row % 2) + e) * chans
                views_ref[lo : lo + chans, lanes] = views[e][at * chans : (at + 1) * chans]


def owner_of(seats, slot):
    here = lax.axis_index("chan")
    owner = jnp.int32(seats[0][slot])
    for chip in range(1, len(seats)):
        owner = jnp.where(here == chip, seats[chip][slot], owner)
    return owner


def own_views_kernel(seats, depth, volume_ref, weight_ref, views_ref, taps_ref, odd_ref):
    chans = volume_ref.shape[0]
    channels = weight_ref.shape[2]
    odd_ref[...] = volume_ref[:, 1:]
    place_views(volume_ref.at[:, 0], views_ref, 0)
    place_views(volume_ref.at[:, 1], views_ref, 6 * chans)
    part = channels // len(seats)
    row = lax.broadcasted_iota(jnp.int32, (channels, channels), 0)
    col = lax.broadcasted_iota(jnp.int32, (channels, channels), 1)
    order = jnp.zeros((channels, channels), F32)
    for slot in range(len(seats)):
        moved = (owner_of(seats, slot) - slot) * part
        inside = (col >= slot * part) & (col < (slot + 1) * part)
        order = jnp.where(inside & (row == col + moved), 1.0, order)
    ordered = matmul(weight_ref[...].reshape(27 * chans, channels), order.astype(BF16)).astype(BF16)
    beyond = jnp.where(lax.axis_index("depth") == depth - 1, 0.0, 1.0).astype(BF16)
    zero = jnp.zeros((chans, channels), BF16)
    for k, e in enumerate((1, 2, 0)):
        for b in range(3):
            pick = lambda a: ordered[(9 * a + 3 * b + e) * chans : (9 * a + 3 * b + e + 1) * chans]
            for plane, line in enumerate(((zero, pick(1)), (pick(0) * beyond, pick(2)))):
                lo = ((3 * plane + k) * 3 + b) * chans
                taps_ref[lo : lo + chans, :] = jnp.concatenate(line, axis=1)


def behind_views_kernel(behind_ref, views_ref):
    first = lax.axis_index("depth") == 0

    @pl.when(jnp.logical_not(first))
    def _():
        place_views(behind_ref.at[:, 0], views_ref, 0)

    @pl.when(first)
    def _():
        views_ref[...] = jnp.zeros(views_ref.shape, BF16)


def place_lines(part, out_ref, at, wide_ref):
    outs, _, rows, cols = part.shape
    wide_ref[...] = part[...].reshape(outs * rows, cols).astype(F32)
    for row in range(rows):
        line = wide_ref[pl.ds(row, outs, stride=rows), :].astype(BF16)
        out_ref[at : at + outs, row * cols : (row + 1) * cols] = line


def lines_kernel(*refs):
    *parts, out_ref, wide_ref = refs
    at = 0
    for part in parts:
        place_lines(part, out_ref, at, wide_ref)
        at += part.shape[0]


def weight_kernel(
    seats, outs, own_ref, behind_ref, near_ref, far_ref, keep_ref, send_ref, grads_ref, terms_ref, placed_ref
):
    channels = grads_ref.shape[0]
    chans = behind_ref.shape[0] // 6
    cells = own_ref.shape[1]
    cols = grads_ref.shape[1] - cells
    known = near_ref.shape[0]
    grads_ref[:known, :cells] = near_ref[...]
    grads_ref[known:, :cells] = far_ref[...]
    grads_ref[:, cells:] = jnp.zeros((channels, cols), BF16)
    both = jnp.concatenate([grads_ref[:, :cells], grads_ref[:, cols:]], axis=0)
    contract = (((1,), (1,)), ((), ()))
    for a, (ref, at) in enumerate(((behind_ref, 0), (own_ref, 0), (own_ref, 6 * chans))):
        terms = lax.dot_general(ref[at : at + 6 * chans], both, contract, preferred_element_type=F32)
        even, odd = terms[: 3 * chans, :channels], terms[3 * chans :]
        for b, block in enumerate((odd[:, channels:], even, odd[:, :channels])):
            lo = (9 * a + 3 * b) * chans
            terms_ref[lo : lo + 3 * chans, :] = block
    terms_ref[27 * chans :, :] = jnp.zeros((5 * chans, channels), F32)
    for c in range(chans):
        placed_ref[32 * c : 32 * c + 32, :] = terms_ref[pl.ds(c, 32, stride=chans), :]
    turned = placed_ref[...].T
    part = channels // len(seats)
    odd_core = lax.axis_index("depth") % 2 == 1
    for slot in range(len(seats)):
        start = owner_of(seats, slot) * (part // 2)
        for at in range(0, part // 2, outs):
            lo = slot * part + 2 * at
            even, odd = turned[lo : lo + outs], turned[lo + outs : lo + 2 * outs]
            place = pl.ds(pl.multiple_of(start + at, outs), outs)
            keep_ref[place, :] = jnp.where(odd_core, odd, even)
            send_ref[place, :] = jnp.where(odd_core, even, odd)


def pair_kernel(keep_ref, other_ref, *out_refs):
    chip = lax.axis_index("depth") // 2
    outs = out_refs[0].shape[0]
    for k, out_ref in enumerate(out_refs):
        place = pl.ds(pl.multiple_of((chip ^ k) * outs, outs), outs)
        out_ref[...] = keep_ref[place, :] + other_ref[place, :]


def input_kernel(taps_ref, next_near_ref, next_far_ref, near_ref, far_ref, out_ref, cells_ref, lines_ref):
    chans, _, rows, cols = out_ref.shape
    half = cols // 2
    grid_cells = half * rows // 2
    grads = [ref[...] for ref in (next_near_ref, next_far_ref, near_ref, far_ref)]
    cells_ref[:, :grid_cells] = matmul(taps_ref[...], jnp.concatenate(grads, axis=0))
    cells_ref[:, grid_cells:] = jnp.zeros((cells_ref.shape[0], half), F32)
    group = 256 // chans
    weave = one_hot(cols, cols, lambda row, col: col == 2 * (row & (half - 1)) + row // half)
    inner = lax.broadcasted_iota(jnp.int32, (chans, half), 1) < half - 1

    def cells(plane, kind, b, r):
        lo = ((3 * plane + kind) * 3 + b) * chans
        return cells_ref[lo : lo + chans, r * half : (r + 1) * half]

    for plane in range(2):
        for start in range(0, rows, group):
            pieces = []
            for row in range(start, start + group):
                r = row // 2
                if row % 2 == 0:
                    even, odd, next_odd = [cells(plane, kind, 1, r) for kind in range(3)]
                else:
                    even, odd, next_odd = [
                        cells(plane, kind, 0, r + 1) + cells(plane, kind, 2, r) for kind in range(3)
                    ]
                odd = odd + jnp.where(inner, pltpu.roll(next_odd, half - 1, 1), 0.0)
                pieces.append(jnp.concatenate([even, odd], axis=1).astype(BF16))
            woven = matmul(jnp.concatenate(pieces, axis=0), weave)
            for side in range(2):
                lanes = slice(side * half, (side + 1) * half)
                lines_ref[side] = woven[:, lanes]
                for c in range(chans):
                    line = lines_ref[side, pl.ds(c, group, stride=chans), :].astype(BF16)
                    out_ref[c, plane, start : start + group, lanes] = line


def total_kernel(scale, *refs):
    *term_refs, out_ref = refs
    chans, outs, taps = out_ref.shape
    total = term_refs[0][...]
    for ref in term_refs[1:]:
        total = total + ref[...]
    total = total * scale
    for c in range(chans):
        out_ref[c] = total[:, 32 * c : 32 * c + taps]


def from_behind(shard, axis, by):
    count = lax.axis_size(axis)
    pairs = [(i, i + by) for i in range(count) if 0 <= i + by < count]
    return lax.ppermute(shard, axis, pairs)


def upsample(stacked, axis, extended):
    tap_zero, tap_one, tap_two = (stacked[0], stacked[1], stacked[2])
    coord_axis = axis - 1
    length = tap_zero.shape[coord_axis]
    if extended:
        outer = length - 1
        even_cells = lax.slice_in_dim(tap_one, 0, outer, axis=coord_axis)
        odd_cells = lax.slice_in_dim(tap_zero, 1, length, axis=coord_axis) + lax.slice_in_dim(
            tap_two, 0, outer, axis=coord_axis
        )
    else:
        outer = length
        shifted = lax.slice_in_dim(tap_zero, 1, length, axis=coord_axis)
        shifted = jnp.concatenate(
            [shifted, jnp.zeros_like(lax.slice_in_dim(tap_zero, 0, 1, axis=coord_axis))],
            axis=coord_axis,
        )
        even_cells = tap_one
        odd_cells = shifted + tap_two
    paired = jnp.stack([even_cells, odd_cells], axis=coord_axis + 1)
    new_shape = list(even_cells.shape)
    new_shape[coord_axis] = 2 * outer
    return paired.reshape(new_shape)


def phase_grads(weight_rows, grads_ext):
    local_in = weight_rows.shape[0] // 27
    channels_out, planes, rows, cols = grads_ext.shape
    taps_out = jnp.dot(
        weight_rows, grads_ext.reshape(channels_out, -1), preferred_element_type=jnp.float32
    )
    taps_out = taps_out.reshape(3, 3, 3, local_in, planes, rows, cols)
    along_w = upsample(jnp.moveaxis(taps_out, 2, 0), 6, False)
    along_h = upsample(jnp.moveaxis(along_w, 1, 0), 4, False)
    return upsample(along_h, 2, True)


def weight_terms(inputs, grads_ext):
    row_extra = 0
    weight_cube = lax.conv_general_dilated(
        inputs[None],
        grads_ext[:, None],
        (1, 1, 1),
        ((1, 2), (1, row_extra), (1, 0)),
        rhs_dilation=(2, 2, 2),
        dimension_numbers=("CNDHW", "OIDHW", "NCDHW"),
        preferred_element_type=jnp.float32,
    )
    return jnp.transpose(weight_cube, (2, 3, 4, 0, 1)).reshape(
        27, weight_cube.shape[0], weight_cube.shape[1]
    )


def plain_shards(grad_out, volume, weight):
    plane_next = from_behind(grad_out, "depth", -1)
    grads_ext = jnp.concatenate([grad_out, plane_next], axis=1)
    channels_out = weight.shape[2]
    local_in = volume.shape[0]
    every_channel = lax.all_gather(grads_ext, "chan", axis=0, tiled=True)
    own_weight = lax.dynamic_slice_in_dim(weight, lax.axis_index("chan") * local_in, local_in, 1)
    input_part = phase_grads(own_weight.reshape(27 * local_in, channels_out), every_channel)
    weight_part = weight_terms(volume, every_channel)
    input_grad = input_part.astype(jnp.bfloat16)
    summed = lax.psum_scatter(weight_part, "depth", scatter_dimension=2, tiled=True)
    cell_count = grad_out.shape[1] * lax.axis_size("depth") * grad_out.shape[2] * grad_out.shape[3]
    return (input_grad, summed * (1.0 / math.sqrt(cell_count)))


def call(kernel, out_shape, *args, specs=None, scratch=(), cost=None):
    flops, moved = cost
    return pl.pallas_call(
        kernel,
        out_shape=out_shape,
        in_specs=specs or [VMEM] * len(args),
        out_specs=jax.tree.map(lambda _: VMEM, out_shape),
        scratch_shapes=scratch,
        compiler_params=pltpu.CompilerParams(vmem_limit_bytes=LIMIT),
        cost_estimate=pl.CostEstimate(flops=flops, bytes_accessed=moved, transcendentals=0),
    )(*args)


def shards(grad_out, volume, weight):
    count = lax.axis_size("chan")
    depth = lax.axis_size("depth")
    own_outs, _, rows, cols = grad_out.shape
    chans = volume.shape[0]
    channels = weight.shape[2]
    cells = rows * cols
    order = ring_order(count)
    ahead = [(order[i], order[(i + 1) % count]) for i in range(count)]
    back = [(b, a) for a, b in ahead]
    farther = [(i, (i + 1) % depth) for i in range(depth)]
    nearer = [(b, a) for a, b in farther]
    own_weight = lax.dynamic_slice_in_dim(weight, lax.axis_index("chan") * local_in, local_in, 1)
    input_part = phase_grads(own_weight.reshape(27 * local_in, channels_out), every_channel)
    weight_part = weight_terms(volume, every_channel)
    input_grad = input_part.astype(jnp.bfloat16)
    summed = lax.psum_scatter(weight_part, "depth", scatter_dimension=2, tiled=True)
    cell_count = grad_out.shape[1] * lax.axis_size("depth") * grad_out.shape[2] * grad_out.shape[3]
    return (input_grad, summed * (1.0 / math.sqrt(cell_count)))


def call(kernel, out_shape, *args, specs=None, scratch=(), cost=None):
    flops, moved = cost
    return pl.pallas_call(
        kernel,
        out_shape=out_shape,
        in_specs=specs or [VMEM] * len(args),
        out_specs=jax.tree.map(lambda _: VMEM, out_shape),
        scratch_shapes=scratch,
        compiler_params=pltpu.CompilerParams(vmem_limit_bytes=LIMIT),
        cost_estimate=pl.CostEstimate(flops=flops, bytes_accessed=moved, transcendentals=0),
    )(*args)


def shards(grad_out, volume, weight):
    count = lax.axis_size("chan")
    depth = lax.axis_size("depth")
    own_outs, _, rows, cols = grad_out.shape
    chans = volume.shape[0]
    channels = weight.shape[2]
    cells = rows * cols
    order = ring_order(count)
    ahead = [(order[i], order[(i + 1) % count]) for i in range(count)]
    back = [(b, a) for a, b in ahead]
    farther = [(i, (i + 1) % depth) for i in range(depth)]
    nearer = [(b, a) for a, b in farther]
    own_weight = lax.dynamic_slice_in_dim(weight, lax.axis_index("chan") * local_in, local_in, 1)
    input_part = phase_grads(own_weight.reshape(27 * local_in, channels_out), every_channel)
    weight_part = weight_terms(volume, every_channel)
    input_grad = input_part.astype(jnp.bfloat16)
    summed = lax.psum_scatter(weight_part, "depth", scatter_dimension=2, tiled=True)
    cell_count = grad_out.shape[1] * lax.axis_size("depth") * grad_out.shape[2] * grad_out.shape[3]
    return (input_grad, summed * (1.0 / math.sqrt(cell_count)))


def call(kernel, out_shape, *args, specs=None, scratch=(), cost=None):
    flops, moved = cost
    return pl.pallas_call(
        kernel,
        out_shape=out_shape,
        in_specs=specs or [VMEM] * len(args),
        out_specs=jax.tree.map(lambda _: VMEM, out_shape),
        scratch_shapes=scratch,
        compiler_params=pltpu.CompilerParams(vmem_limit_bytes=LIMIT),
        cost_estimate=pl.CostEstimate(flops=flops, bytes_accessed=moved, transcendentals=0),
    )(*args)


def shards(grad_out, volume, weight):
    count = lax.axis_size("chan")
    depth = lax.axis_size("depth")
    own_outs, _, rows, cols = grad_out.shape
    chans = volume.shape[0]
    channels = weight.shape[2]
    cells = rows * cols
    order = ring_order(count)
    ahead = [(order[i], order[(i + 1) % count]) for i in range(count)]
    back = [(b, a) for a, b in ahead]
    farther = [(i, (i + 1) % depth) for i in range(depth)]
    nearer = [(b, a) for a, b in farther]
    own_weight = lax.dynamic_slice_in_dim(weight, lax.axis_index("chan") * local_in, local_in, 1)
    input_part = phase_grads(own_weight.reshape(27 * local_in, channels_out), every_channel)
    weight_part = weight_terms(volume, every_channel)
    input_grad = input_part.astype(jnp.bfloat16)
    summed = lax.psum_scatter(weight_part, "depth", scatter_dimension=2, tiled=True)
    cell_count = grad_out.shape[1] * lax.axis_size("depth") * grad_out.shape[2] * grad_out.shape[3]
    return (input_grad, summed * (1.0 / math.sqrt(cell_count)))


def call(kernel, out_shape, *args, specs=None, scratch=(), cost=None):
    flops, moved = cost
    return pl.pallas_call(
        kernel,
        out_shape=out_shape,
        in_specs=specs or [VMEM] * len(args),
        out_specs=jax.tree.map(lambda _: VMEM, out_shape),
        scratch_shapes=scratch,
        compiler_params=pltpu.CompilerParams(vmem_limit_bytes=LIMIT),
        cost_estimate=pl.CostEstimate(flops=flops, bytes_accessed=moved, transcendentals=0),
    )(*args)


def shards(grad_out, volume, weight):
    count = lax.axis_size("chan")
    depth = lax.axis_size("depth")
    own_outs, _, rows, cols = grad_out.shape
    chans = volume.shape[0]
    channels = weight.shape[2]
    cells = rows * cols
    order = ring_order(count)
    ahead = [(order[i], order[(i + 1) % count]) for i in range(count)]
    back = [(b, a) for a, b in ahead]
    farther = [(i, (i + 1) % depth) for i in range(depth)]
    nearer = [(b, a) for a, b in farther]
    shifts = [0]

    near = []
    up = down = grad_out
    for step in range(1, (count - 1) // 2 + 1):
        up = lax.ppermute(up, "chan", ahead)
        down = lax.ppermute(down, "chan", back)
        near += [up, down]
        shifts += [-step, step]
    last = lax.ppermute(up, "chan", ahead)
    shifts += [count // 2]
    seats = [[order[(order.index(chip) + s) % count] for s in shifts] for chip in range(count)]

    shifts = [0, -1]
    for step in range(1, count // 2):
        shifts += [step, -step - 1]
    seats = [[order[(order.index(chip) + s) % count] for s in shifts] for chip in range(count)]

    own_weight = lax.dynamic_slice_in_dim(weight, lax.axis_index("chan") * chans, chans, 1)
    views, taps, odd = call(
        lambda *refs: own_views_kernel(seats, depth, *refs),
        (
            jax.ShapeDtypeStruct((12 * chans, cells), BF16),
            jax.ShapeDtypeStruct((18 * chans, 2 * channels), BF16),
            jax.ShapeDtypeStruct((chans, 1, 2 * rows, 2 * cols), BF16),
        ),
        volume,
        own_weight,
        cost=(2 * 2 * 2 * cells * chans * 8 * cols, 4 << 20),
    )
    first = lax.ppermute(grad_out, "chan", ahead)
    first, views = lax.optimization_barrier((first, views))
    up, down, far = first, grad_out, []
    for step in range(1, count // 2):
        down = lax.ppermute(down, "chan", back)
        up = lax.ppermute(up, "chan", ahead)
        far += [down, up]
    lines = lambda *parts: call(
        lines_kernel,
        jax.ShapeDtypeStruct((len(parts) * own_outs, cells), BF16),
        *parts,
        scratch=(pltpu.VMEM((own_outs * rows, cols), F32),),
        cost=(1 << 20, 2 << 20),
    )
    near_lines = lines(grad_out, first)
    next_near_lines = lax.ppermute(near_lines, "depth", nearer)
    behind = lax.ppermute(odd, "depth", farther)
    behind_views = call(
        behind_views_kernel,
        jax.ShapeDtypeStruct((6 * chans, cells), BF16),
        behind,
        cost=(2 * 2 * cells * chans * 8 * cols, 2 << 20),
    )
    far_lines = lines(*far)
    next_far_lines = lax.ppermute(far_lines, "depth", nearer)
    outs = channels // depth
    half_terms = jax.ShapeDtypeStruct((channels // 2, 32 * chans), F32)
    keep, send = call(
        lambda *refs: weight_kernel(seats, outs, *refs),
        (half_terms, half_terms),
        views,
        behind_views,
        near_lines,
        far_lines,
        scratch=(
            pltpu.VMEM((channels, cells + cols), BF16),
            pltpu.VMEM((32 * chans, channels), F32),
            pltpu.VMEM((32 * chans, channels), F32),
        ),
        cost=(2 * 27 * chans * channels * cells, 8 << 20),
    )
    chips = depth // 2
    other = lax.ppermute(send, "depth", [(i, i ^ 1) for i in range(depth)])
    own_terms, *terms = call(
        pair_kernel,
        [jax.ShapeDtypeStruct((outs, 32 * chans), F32)] * chips,
        keep,
        other,
        cost=(1 << 16, 1 << 19),
    )
    terms = [lax.ppermute(term, "depth", [(i, i ^ (2 * k + 2)) for i in range(depth)]) for k, term in enumerate(terms)]
    input_grad = call(
        input_kernel,
        jax.ShapeDtypeStruct(volume.shape, BF16),
        taps,
        next_near_lines,
        next_far_lines,
        near_lines,
        far_lines,
        scratch=(
            pltpu.VMEM((18 * chans, cells + cols), F32),
            pltpu.VMEM((2, 256, cols), F32),
        ),
        cost=(2 * 18 * chans * 2 * channels * cells, 8 << 20),
    )
    own_terms, input_grad = lax.optimization_barrier((own_terms, input_grad))
    scale = 1.0 / math.sqrt(depth * cells)
    weight_grad = call(
        lambda *refs: total_kernel(scale, *refs),
        jax.ShapeDtypeStruct((chans, outs, 27), F32),
        own_terms,
        *terms,
        cost=(1 << 16, 1 << 19),
    )
    return input_grad, jnp.transpose(weight_grad, (2, 0, 1))


def solution(mesh):
    in_specs = (P("chan", "depth", None, None), P("chan", "depth", None, None), P())
    out_specs = (P("chan", "depth", None, None), P(None, "chan", "depth"))
    ring, depth = mesh.shape["chan"], mesh.shape["depth"]

    def either(grad_out, volume, weight):
        fits = (
            grad_out.shape[0] % 16 == 0
            and volume.shape[0] == 16
            and grad_out.shape[1] == 1
            and ring % 2 == 0
            and ring >= 4
            and depth & (depth - 1) == 0
            and depth % (2 * ring) == 0
        )
        return (shards if fits else plain_shards)(grad_out, volume, weight)

    return jax.shard_map(either, mesh=mesh, in_specs=in_specs, out_specs=out_specs, check_vma=False)
```

```python
import math

import jax
import jax.numpy as jnp
from jax import lax
from jax.experimental import pallas as pl
from jax.experimental.pallas import tpu as pltpu
from jax.sharding import PartitionSpec as P

F32 = jnp.float32
BF16 = jnp.bfloat16
VMEM = pl.BlockSpec(memory_space=pltpu.VMEM)
SMEM = pl.BlockSpec(memory_space=pltpu.SMEM)
LIMIT = 48 * 1024 * 1024


def ring_order(count):
    return [0] + list(range(1, count, 2)) + list(range(2, count, 2))[::-1]


def matmul(left, right):
    return jnp.dot(left, right, preferred_element_type=F32)


def one_hot(rows, cols, source):
    row = lax.broadcasted_iota(jnp.int32, (rows, cols), 0)
    col = lax.broadcasted_iota(jnp.int32, (rows, cols), 1)
    return jnp.where(source(row, col), 1.0, 0.0).astype(BF16)


def swap_rows(major, minor):
    bits = minor.bit_length() - 1
    return one_hot(
        major * minor,
        major * minor,
        lambda row, col: col == (row & (minor - 1)) * major + (row >> bits),
    )


def place_views(plane, views_ref, base):
    chans, rows, cols = plane.shape
    half = cols // 2
    group = 256 // chans
    swap = swap_rows(group, chans)
    split = one_hot(cols, cols, lambda row, col: row == 2 * (col & (half - 1)) + col // half)
    inner = lax.broadcasted_iota(jnp.int32, (group * chans, half), 1) > 0
    for start in range(0, rows, group):
        block = plane[:, start : start + group, :].reshape(chans * group, cols)
        parted = matmul(matmul(swap, block).astype(BF16), split)
        odd = parted[:, half:]
        before = jnp.where(inner, pltpu.roll(odd, 1, 1), 0.0)
        views = [view.astype(BF16) for view in (before, parted[:, :half], odd)]
        for at in range(group):
            row = start + at
            lanes = slice(row // 2 * half, (row // 2 + 1) * half)
            for e in range(3):
                lo = base + (3 * (row % 2) + e) * chans
                views_ref[lo : lo + chans, lanes] = views[e][at * chans : (at + 1) * chans]


def owner_of(seats, slot):
    here = lax.axis_index("chan")
    owner = jnp.int32(seats[0][slot])
    for chip in range(1, len(seats)):
        owner = jnp.where(here == chip, seats[chip][slot], owner)
    return owner


def own_views_kernel(seats, depth, volume_ref, weight_ref, views_ref, taps_ref, odd_ref):
    chans = volume_ref.shape[0]
    channels = weight_ref.shape[2]
    odd_ref[...] = volume_ref[:, 1:]
    place_views(volume_ref.at[:, 0], views_ref, 0)
    place_views(volume_ref.at[:, 1], views_ref, 6 * chans)
    part = channels // len(seats)
    row = lax.broadcasted_iota(jnp.int32, (channels, channels), 0)
    col = lax.broadcasted_iota(jnp.int32, (channels, channels), 1)
    order = jnp.zeros((channels, channels), F32)
    for slot in range(len(seats)):
        moved = (owner_of(seats, slot) - slot) * part
        inside = (col >= slot * part) & (col < (slot + 1) * part)
        order = jnp.where(inside & (row == col + moved), 1.0, order)
    ordered = matmul(weight_ref[...].reshape(27 * chans, channels), order.astype(BF16)).astype(BF16)
    beyond = jnp.where(lax.axis_index("depth") == depth - 1, 0.0, 1.0).astype(BF16)
    zero = jnp.zeros((chans, channels), BF16)
    for k, e in enumerate((1, 2, 0)):
        for b in range(3):
            pick = lambda a: ordered[(9 * a + 3 * b + e) * chans : (9 * a + 3 * b + e + 1) * chans]
            for plane, line in enumerate(((zero, pick(1)), (pick(0) * beyond, pick(2)))):
                lo = ((3 * plane + k) * 3 + b) * chans
                taps_ref[lo : lo + chans, :] = jnp.concatenate(line, axis=1)


def behind_views_kernel(behind_ref, views_ref):
    first = lax.axis_index("depth") == 0

    @pl.when(jnp.logical_not(first))
    def _():
        place_views(behind_ref.at[:, 0], views_ref, 0)

    @pl.when(first)
    def _():
        views_ref[...] = jnp.zeros(views_ref.shape, BF16)


def place_lines(part, out_ref, at, wide_ref):
    outs, _, rows, cols = part.shape
    wide_ref[...] = part[...].reshape(outs * rows, cols).astype(F32)
    for row in range(rows):
        line = wide_ref[pl.ds(row, outs, stride=rows), :].astype(BF16)
        out_ref[at : at + outs, row * cols : (row + 1) * cols] = line


def lines_kernel(*refs):
    *parts, out_ref, wide_ref = refs
    at = 0
    for part in parts:
        place_lines(part, out_ref, at, wide_ref)
        at += part.shape[0]


def weight_kernel(
    seats, outs, own_ref, behind_ref, near_ref, far_ref, keep_ref, send_ref, grads_ref, terms_ref, placed_ref
):
    channels = grads_ref.shape[0]
    chans = behind_ref.shape[0] // 6
    cells = own_ref.shape[1]
    cols = grads_ref.shape[1] - cells
    known = near_ref.shape[0]
    grads_ref[:known, :cells] = near_ref[...]
    grads_ref[known:, :cells] = far_ref[...]
    grads_ref[:, cells:] = jnp.zeros((channels, cols), BF16)
    both = jnp.concatenate([grads_ref[:, :cells], grads_ref[:, cols:]], axis=0)
    contract = (((1,), (1,)), ((), ()))
    for a, (ref, at) in enumerate(((behind_ref, 0), (own_ref, 0), (own_ref, 6 * chans))):
        terms = lax.dot_general(ref[at : at + 6 * chans], both, contract, preferred_element_type=F32)
        even, odd = terms[: 3 * chans, :channels], terms[3 * chans :]
        for b, block in enumerate((odd[:, channels:], even, odd[:, :channels])):
            lo = (9 * a + 3 * b) * chans
            terms_ref[lo : lo + 3 * chans, :] = block
    terms_ref[27 * chans :, :] = jnp.zeros((5 * chans, channels), F32)
    for c in range(chans):
        placed_ref[32 * c : 32 * c + 32, :] = terms_ref[pl.ds(c, 32, stride=chans), :]
    turned = placed_ref[...].T
    part = channels // len(seats)
    odd_core = lax.axis_index("depth") % 2 == 1
    for slot in range(len(seats)):
        start = owner_of(seats, slot) * (part // 2)
        for at in range(0, part // 2, outs):
            lo = slot * part + 2 * at
            even, odd = turned[lo : lo + outs], turned[lo + outs : lo + 2 * outs]
            place = pl.ds(pl.multiple_of(start + at, outs), outs)
            keep_ref[place, :] = jnp.where(odd_core, odd, even)
            send_ref[place, :] = jnp.where(odd_core, even, odd)


def pair_kernel(keep_ref, other_ref, *out_refs):
    chip = lax.axis_index("depth") // 2
    outs = out_refs[0].shape[0]
    for k, out_ref in enumerate(out_refs):
        place = pl.ds(pl.multiple_of((chip ^ k) * outs, outs), outs)
        out_ref[...] = keep_ref[place, :] + other_ref[place, :]


def input_kernel(taps_ref, next_near_ref, next_far_ref, near_ref, far_ref, out_ref, cells_ref, lines_ref):
    chans, _, rows, cols = out_ref.shape
    half = cols // 2
    grid_cells = half * rows // 2
    grads = [ref[...] for ref in (next_near_ref, next_far_ref, near_ref, far_ref)]
    cells_ref[:, :grid_cells] = matmul(taps_ref[...], jnp.concatenate(grads, axis=0))
    cells_ref[:, grid_cells:] = jnp.zeros((cells_ref.shape[0], half), F32)
    group = 256 // chans
    weave = one_hot(cols, cols, lambda row, col: col == 2 * (row & (half - 1)) + row // half)
    inner = lax.broadcasted_iota(jnp.int32, (chans, half), 1) < half - 1

    def cells(plane, kind, b, r):
        lo = ((3 * plane + kind) * 3 + b) * chans
        return cells_ref[lo : lo + chans, r * half : (r + 1) * half]

    for plane in range(2):
        for start in range(0, rows, group):
            pieces = []
            for row in range(start, start + group):
                r = row // 2
                if row % 2 == 0:
                    even, odd, next_odd = [cells(plane, kind, 1, r) for kind in range(3)]
                else:
                    even, odd, next_odd = [
                        cells(plane, kind, 0, r + 1) + cells(plane, kind, 2, r) for kind in range(3)
                    ]
                odd = odd + jnp.where(inner, pltpu.roll(next_odd, half - 1, 1), 0.0)
                pieces.append(jnp.concatenate([even, odd], axis=1).astype(BF16))
            woven = matmul(jnp.concatenate(pieces, axis=0), weave)
            for side in range(2):
                lanes = slice(side * half, (side + 1) * half)
                lines_ref[side] = woven[:, lanes]
                for c in range(chans):
                    line = lines_ref[side, pl.ds(c, group, stride=chans), :].astype(BF16)
                    out_ref[c, plane, start : start + group, lanes] = line


def total_kernel(scale, *refs):
    *term_refs, out_ref = refs
    chans, outs, taps = out_ref.shape
    total = term_refs[0][...]
    for ref in term_refs[1:]:
        total = total + ref[...]
    total = total * scale
    for c in range(chans):
        out_ref[c] = total[:, 32 * c : 32 * c + taps]


def from_behind(shard, axis, by):
    count = lax.axis_size(axis)
    pairs = [(i, i + by) for i in range(count) if 0 <= i + by < count]
    return lax.ppermute(shard, axis, pairs)


def upsample(stacked, axis, extended):
    tap_zero, tap_one, tap_two = (stacked[0], stacked[1], stacked[2])
    coord_axis = axis - 1
    length = tap_zero.shape[coord_axis]
    if extended:
        outer = length - 1
        even_cells = lax.slice_in_dim(tap_one, 0, outer, axis=coord_axis)
        odd_cells = lax.slice_in_dim(tap_zero, 1, length, axis=coord_axis) + lax.slice_in_dim(
            tap_two, 0, outer, axis=coord_axis
        )
    else:
        outer = length
        shifted = lax.slice_in_dim(tap_zero, 1, length, axis=coord_axis)
        shifted = jnp.concatenate(
            [shifted, jnp.zeros_like(lax.slice_in_dim(tap_zero, 0, 1, axis=coord_axis))],
            axis=coord_axis,
        )
        even_cells = tap_one
        odd_cells = shifted + tap_two
    paired = jnp.stack([even_cells, odd_cells], axis=coord_axis + 1)
    new_shape = list(even_cells.shape)
    new_shape[coord_axis] = 2 * outer
    return paired.reshape(new_shape)


def phase_grads(weight_rows, grads_ext):
    local_in = weight_rows.shape[0] // 27
    channels_out, planes, rows, cols = grads_ext.shape
    taps_out = jnp.dot(
        weight_rows, grads_ext.reshape(channels_out, -1), preferred_element_type=jnp.float32
    )
    taps_out = taps_out.reshape(3, 3, 3, local_in, planes, rows, cols)
    along_w = upsample(jnp.moveaxis(taps_out, 2, 0), 6, False)
    along_h = upsample(jnp.moveaxis(along_w, 1, 0), 4, False)
    return upsample(along_h, 2, True)


def weight_terms(inputs, grads_ext):
    row_extra = 0
    weight_cube = lax.conv_general_dilated(
        inputs[None],
        grads_ext[:, None],
        (1, 1, 1),
        ((1, 2), (1, row_extra), (1, 0)),
        rhs_dilation=(2, 2, 2),
        dimension_numbers=("CNDHW", "OIDHW", "NCDHW"),
        preferred_element_type=jnp.float32,
    )
    return jnp.transpose(weight_cube, (2, 3, 4, 0, 1)).reshape(
        27, weight_cube.shape[0], weight_cube.shape[1]
    )


def plain_shards(grad_out, volume, weight):
    plane_next = from_behind(grad_out, "depth", -1)
    grads_ext = jnp.concatenate([grad_out, plane_next], axis=1)
    channels_out = weight.shape[2]
    local_in = volume.shape[0]
    every_channel = lax.all_gather(grads_ext, "chan", axis=0, tiled=True)
    own_weight = lax.dynamic_slice_in_dim(weight, lax.axis_index("chan") * local_in, local_in, 1)
    input_part = phase_grads(own_weight.reshape(27 * local_in, channels_out), every_channel)
    weight_part = weight_terms(volume, every_channel)
    input_grad = input_part.astype(jnp.bfloat16)
    summed = lax.psum_scatter(weight_part, "depth", scatter_dimension=2, tiled=True)
    cell_count = grad_out.shape[1] * lax.axis_size("depth") * grad_out.shape[2] * grad_out.shape[3]
    return (input_grad, summed * (1.0 / math.sqrt(cell_count)))


def call(kernel, out_shape, *args, specs=None, scratch=(), cost=None):
    flops, moved = cost
    return pl.pallas_call(
        kernel,
        out_shape=out_shape,
        in_specs=specs or [VMEM] * len(args),
        out_specs=jax.tree.map(lambda _: VMEM, out_shape),
        scratch_shapes=scratch,
        compiler_params=pltpu.CompilerParams(vmem_limit_bytes=LIMIT),
        cost_estimate=pl.CostEstimate(flops=flops, bytes_accessed=moved, transcendentals=0),
    )(*args)


def shards(grad_out, volume, weight):
    count = lax.axis_size("chan")
    depth = lax.axis_size("depth")
    own_outs, _, rows, cols = grad_out.shape
    chans = volume.shape[0]
    channels = weight.shape[2]
    cells = rows * cols
    order = ring_order(count)
    ahead = [(order[i], order[(i + 1) % count]) for i in range(count)]
    back = [(b, a) for a, b in ahead]
    farther = [(i, (i + 1) % depth) for i in range(depth)]
    nearer = [(b, a) for a, b in farther]
    own_weight = lax.dynamic_slice_in_dim(weight, lax.axis_index("chan") * local_in, local_in, 1)
    input_part = phase_grads(own_weight.reshape(27 * local_in, channels_out), every_channel)
    weight_part = weight_terms(volume, every_channel)
    input_grad = input_part.astype(jnp.bfloat16)
    summed = lax.psum_scatter(weight_part, "depth", scatter_dimension=2, tiled=True)
    cell_count = grad_out.shape[1] * lax.axis_size("depth") * grad_out.shape[2] * grad_out.shape[3]
    return (input_grad, summed * (1.0 / math.sqrt(cell_count)))


def call(kernel, out_shape, *args, specs=None, scratch=(), cost=None):
    flops, moved = cost
    return pl.pallas_call(
        kernel,
        out_shape=out_shape,
        in_specs=specs or [VMEM] * len(args),
        out_specs=jax.tree.map(lambda _: VMEM, out_shape),
        scratch_shapes=scratch,
        compiler_params=pltpu.CompilerParams(vmem_limit_bytes=LIMIT),
        cost_estimate=pl.CostEstimate(flops=flops, bytes_accessed=moved, transcendentals=0),
    )(*args)


def shards(grad_out, volume, weight):
    count = lax.axis_size("chan")
    depth = lax.axis_size("depth")
    own_outs, _, rows, cols = grad_out.shape
    chans = volume.shape[0]
    channels = weight.shape[2]
    cells = rows * cols
    order = ring_order(count)
    ahead = [(order[i], order[(i + 1) % count]) for i in range(count)]
    back = [(b, a) for a, b in ahead]
    farther = [(i, (i + 1) % depth) for i in range(depth)]
    nearer = [(b, a) for a, b in farther]
    own_weight = lax.dynamic_slice_in_dim(weight, lax.axis_index("chan") * local_in, local_in, 1)
    input_part = phase_grads(own_weight.reshape(27 * local_in, channels_out), every_channel)
    weight_part = weight_terms(volume, every_channel)
    input_grad = input_part.astype(jnp.bfloat16)
    summed = lax.psum_scatter(weight_part, "depth", scatter_dimension=2, tiled=True)
    cell_count = grad_out.shape[1] * lax.axis_size("depth") * grad_out.shape[2] * grad_out.shape[3]
    return (input_grad, summed * (1.0 / math.sqrt(cell_count)))


def call(kernel, out_shape, *args, specs=None, scratch=(), cost=None):
    flops, moved = cost
    return pl.pallas_call(
        kernel,
        out_shape=out_shape,
        in_specs=specs or [VMEM] * len(args),
        out_specs=jax.tree.map(lambda _: VMEM, out_shape),
        scratch_shapes=scratch,
        compiler_params=pltpu.CompilerParams(vmem_limit_bytes=LIMIT),
        cost_estimate=pl.CostEstimate(flops=flops, bytes_accessed=moved, transcendentals=0),
    )(*args)


def shards(grad_out, volume, weight):
    count = lax.axis_size("chan")
    depth = lax.axis_size("depth")
    own_outs, _, rows, cols = grad_out.shape
    chans = volume.shape[0]
    channels = weight.shape[2]
    cells = rows * cols
    order = ring_order(count)
    ahead = [(order[i], order[(i + 1) % count]) for i in range(count)]
    back = [(b, a) for a, b in ahead]
    farther = [(i, (i + 1) % depth) for i in range(depth)]
    nearer = [(b, a) for a, b in farther]
    own_weight = lax.dynamic_slice_in_dim(weight, lax.axis_index("chan") * local_in, local_in, 1)
    input_part = phase_grads(own_weight.reshape(27 * local_in, channels_out), every_channel)
    weight_part = weight_terms(volume, every_channel)
    input_grad = input_part.astype(jnp.bfloat16)
    summed = lax.psum_scatter(weight_part, "depth", scatter_dimension=2, tiled=True)
    cell_count = grad_out.shape[1] * lax.axis_size("depth") * grad_out.shape[2] * grad_out.shape[3]
    return (input_grad, summed * (1.0 / math.sqrt(cell_count)))


def call(kernel, out_shape, *args, specs=None, scratch=(), cost=None):
    flops, moved = cost
    return pl.pallas_call(
        kernel,
        out_shape=out_shape,
        in_specs=specs or [VMEM] * len(args),
        out_specs=jax.tree.map(lambda _: VMEM, out_shape),
        scratch_shapes=scratch,
        compiler_params=pltpu.CompilerParams(vmem_limit_bytes=LIMIT),
        cost_estimate=pl.CostEstimate(flops=flops, bytes_accessed=moved, transcendentals=0),
    )(*args)


def shards(grad_out, volume, weight):
    count = lax.axis_size("chan")
    depth = lax.axis_size("depth")
    own_outs, _, rows, cols = grad_out.shape
    chans = volume.shape[0]
    channels = weight.shape[2]
    cells = rows * cols
    order = ring_order(count)
    ahead = [(order[i], order[(i + 1) % count]) for i in range(count)]
    back = [(b, a) for a, b in ahead]
    farther = [(i, (i + 1) % depth) for i in range(depth)]
    nearer = [(b, a) for a, b in farther]
    shifts = [0]

    near = []
    up = down = grad_out
    for step in range(1, (count - 1) // 2 + 1):
        up = lax.ppermute(up, "chan", ahead)
        down = lax.ppermute(down, "chan", back)
        near += [up, down]
        shifts += [-step, step]
    last = lax.ppermute(up, "chan", ahead)
    shifts += [count // 2]
    seats = [[order[(order.index(chip) + s) % count] for s in shifts] for chip in range(count)]

    shifts = [0, -1]
    for step in range(1, count // 2):
        shifts += [step, -step - 1]
    seats = [[order[(order.index(chip) + s) % count] for s in shifts] for chip in range(count)]

    own_weight = lax.dynamic_slice_in_dim(weight, lax.axis_index("chan") * chans, chans, 1)
    views, taps, odd = call(
        lambda *refs: own_views_kernel(seats, depth, *refs),
        (
            jax.ShapeDtypeStruct((12 * chans, cells), BF16),
            jax.ShapeDtypeStruct((18 * chans, 2 * channels), BF16),
            jax.ShapeDtypeStruct((chans, 1, 2 * rows, 2 * cols), BF16),
        ),
        volume,
        own_weight,
        cost=(2 * 2 * 2 * cells * chans * 8 * cols, 4 << 20),
    )
    first = lax.ppermute(grad_out, "chan", ahead)
    down, views = lax.optimization_barrier((grad_out, views))
    up, far = first, []
    for step in range(1, count // 2):
        down = lax.ppermute(down, "chan", back)
        up = lax.ppermute(up, "chan", ahead)
        far += [down, up]
    lines = lambda *parts: call(
        lines_kernel,
        jax.ShapeDtypeStruct((len(parts) * own_outs, cells), BF16),
        *parts,
        scratch=(pltpu.VMEM((own_outs * rows, cols), F32),),
        cost=(1 << 20, 2 << 20),
    )
    near_lines = lines(grad_out, first)
    next_near_lines = lax.ppermute(near_lines, "depth", nearer)
    behind = lax.ppermute(odd, "depth", farther)
    behind_views = call(
        behind_views_kernel,
        jax.ShapeDtypeStruct((6 * chans, cells), BF16),
        behind,
        cost=(2 * 2 * cells * chans * 8 * cols, 2 << 20),
    )
    far_lines = lines(*far)
    next_far_lines = lax.ppermute(far_lines, "depth", nearer)
    outs = channels // depth
    half_terms = jax.ShapeDtypeStruct((channels // 2, 32 * chans), F32)
    keep, send = call(
        lambda *refs: weight_kernel(seats, outs, *refs),
        (half_terms, half_terms),
        views,
        behind_views,
        near_lines,
        far_lines,
        scratch=(
            pltpu.VMEM((channels, cells + cols), BF16),
            pltpu.VMEM((32 * chans, channels), F32),
            pltpu.VMEM((32 * chans, channels), F32),
        ),
        cost=(2 * 27 * chans * channels * cells, 8 << 20),
    )
    chips = depth // 2
    other = lax.ppermute(send, "depth", [(i, i ^ 1) for i in range(depth)])
    own_terms, *terms = call(
        pair_kernel,
        [jax.ShapeDtypeStruct((outs, 32 * chans), F32)] * chips,
        keep,
        other,
        cost=(1 << 16, 1 << 19),
    )
    terms = [lax.ppermute(term, "depth", [(i, i ^ (2 * k + 2)) for i in range(depth)]) for k, term in enumerate(terms)]
    input_grad = call(
        input_kernel,
        jax.ShapeDtypeStruct(volume.shape, BF16),
        taps,
        next_near_lines,
        next_far_lines,
        near_lines,
        far_lines,
        scratch=(
            pltpu.VMEM((18 * chans, cells + cols), F32),
            pltpu.VMEM((2, 256, cols), F32),
        ),
        cost=(2 * 18 * chans * 2 * channels * cells, 8 << 20),
    )
    own_terms, input_grad = lax.optimization_barrier((own_terms, input_grad))
    scale = 1.0 / math.sqrt(depth * cells)
    weight_grad = call(
        lambda *refs: total_kernel(scale, *refs),
        jax.ShapeDtypeStruct((chans, outs, 27), F32),
        own_terms,
        *terms,
        cost=(1 << 16, 1 << 19),
    )
    return input_grad, jnp.transpose(weight_grad, (2, 0, 1))


def solution(mesh):
    in_specs = (P("chan", "depth", None, None), P("chan", "depth", None, None), P())
    out_specs = (P("chan", "depth", None, None), P(None, "chan", "depth"))
    ring, depth = mesh.shape["chan"], mesh.shape["depth"]

    def either(grad_out, volume, weight):
        fits = (
            grad_out.shape[0] % 16 == 0
            and volume.shape[0] == 16
            and grad_out.shape[1] == 1
            and ring % 2 == 0
            and ring >= 4
            and depth & (depth - 1) == 0
            and depth % (2 * ring) == 0
        )
        return (shards if fits else plain_shards)(grad_out, volume, weight)

    return jax.shard_map(either, mesh=mesh, in_specs=in_specs, out_specs=out_specs, check_vma=False)
```

```python
import math

import jax
import jax.numpy as jnp
from jax import lax
from jax.experimental import pallas as pl
from jax.experimental.pallas import tpu as pltpu
from jax.sharding import PartitionSpec as P

F32 = jnp.float32
BF16 = jnp.bfloat16
VMEM = pl.BlockSpec(memory_space=pltpu.VMEM)
HBM = pl.BlockSpec(memory_space=pltpu.HBM)
LIMIT = 48 * 1024 * 1024


def ring_order(count):
    return [0] + list(range(1, count, 2)) + list(range(2, count, 2))[::-1]


def matmul(left, right):
    return jnp.dot(left, right, preferred_element_type=F32)


def one_hot(rows, cols, source):
    row = lax.broadcasted_iota(jnp.int32, (rows, cols), 0)
    col = lax.broadcasted_iota(jnp.int32, (rows, cols), 1)
    return jnp.where(source(row, col), 1.0, 0.0).astype(BF16)


def swap_rows(major, minor):
    bits = minor.bit_length() - 1
    return one_hot(
        major * minor,
        major * minor,
        lambda row, col: col == (row & (minor - 1)) * major + (row >> bits),
    )


def place_views(plane, views_ref, base):
    chans, rows, cols = plane.shape
    half = cols // 2
    group = 256 // chans
    swap = swap_rows(group, chans)
    split = one_hot(cols, cols, lambda row, col: row == 2 * (col & (half - 1)) + col // half)
    inner = lax.broadcasted_iota(jnp.int32, (group * chans, half), 1) > 0
    for start in range(0, rows, group):
        block = plane[:, start : start + group, :].reshape(chans * group, cols)
        parted = matmul(matmul(swap, block).astype(BF16), split)
        odd = parted[:, half:]
        before = jnp.where(inner, pltpu.roll(odd, 1, 1), 0.0)
        views = [view.astype(BF16) for view in (before, parted[:, :half], odd)]
        for at in range(group):
            row = start + at
            lanes = slice(row // 2 * half, (row // 2 + 1) * half)
            for e in range(3):
                lo = base + (3 * (row % 2) + e) * chans
                views_ref[lo : lo + chans, lanes] = views[e][at * chans : (at + 1) * chans]


def owner_of(seats, slot):
    here = lax.axis_index("chan")
    owner = jnp.int32(seats[0][slot])
    for chip in range(1, len(seats)):
        owner = jnp.where(here == chip, seats[chip][slot], owner)
    return owner


def odd_plane_kernel(volume_ref, odd_ref, sem):
    copy = pltpu.make_async_copy(volume_ref.at[:, 1:], odd_ref, sem)
    copy.start()
    copy.wait()


def own_views_kernel(seats, depth, volume_ref, weight_ref, views_ref, taps_ref):
    chans = volume_ref.shape[0]
    channels = weight_ref.shape[2]
    place_views(volume_ref.at[:, 0], views_ref, 0)
    place_views(volume_ref.at[:, 1], views_ref, 6 * chans)
    part = channels // len(seats)
    row = lax.broadcasted_iota(jnp.int32, (channels, channels), 0)
    col = lax.broadcasted_iota(jnp.int32, (channels, channels), 1)
    order = jnp.zeros((channels, channels), F32)
    for slot in range(len(seats)):
        moved = (owner_of(seats, slot) - slot) * part
        inside = (col >= slot * part) & (col < (slot + 1) * part)
        order = jnp.where(inside & (row == col + moved), 1.0, order)
    ordered = matmul(weight_ref[...].reshape(27 * chans, channels), order.astype(BF16)).astype(BF16)
    beyond = jnp.where(lax.axis_index("depth") == depth - 1, 0.0, 1.0).astype(BF16)
    zero = jnp.zeros((chans, channels), BF16)
    for k, e in enumerate((1, 2, 0)):
        for b in range(3):
            pick = lambda a: ordered[(9 * a + 3 * b + e) * chans : (9 * a + 3 * b + e + 1) * chans]
            for plane, line in enumerate(((zero, pick(1)), (pick(0) * beyond, pick(2)))):
                lo = ((3 * plane + k) * 3 + b) * chans
                taps_ref[lo : lo + chans, :] = jnp.concatenate(line, axis=1)


def behind_views_kernel(behind_ref, views_ref):
    first = lax.axis_index("depth") == 0

    @pl.when(jnp.logical_not(first))
    def _():
        place_views(behind_ref.at[:, 0], views_ref, 0)

    @pl.when(first)
    def _():
        views_ref[...] = jnp.zeros(views_ref.shape, BF16)


def place_lines(part, out_ref, at, wide_ref):
    outs, _, rows, cols = part.shape
    wide_ref[: outs * rows, :] = part[...].reshape(outs * rows, cols).astype(F32)
    for row in range(rows):
        line = wide_ref[pl.ds(row, outs, stride=rows), :].astype(BF16)
        out_ref[at : at + outs, row * cols : (row + 1) * cols] = line


def lines_kernel(*refs):
    *parts, out_ref, wide_ref = refs
    at = 0
    for part in parts:
        place_lines(part, out_ref, at, wide_ref)
        at += part.shape[0]


def weight_kernel(
    seats, outs, own_ref, behind_ref, *refs
):
    *line_refs, keep_ref, send_ref, grads_ref, terms_ref, placed_ref = refs
    channels = grads_ref.shape[0]
    chans = behind_ref.shape[0] // 6
    cells = own_ref.shape[1]
    cols = grads_ref.shape[1] - cells
    at = 0
    for ref in line_refs:
        grads_ref[at : at + ref.shape[0], :cells] = ref[...]
        at += ref.shape[0]
    grads_ref[:, cells:] = jnp.zeros((channels, cols), BF16)
    both = jnp.concatenate([grads_ref[:, :cells], grads_ref[:, cols:]], axis=0)
    contract = (((1,), (1,)), ((), ()))
    for a, (ref, at) in enumerate(((behind_ref, 0), (own_ref, 0), (own_ref, 6 * chans))):
        terms = lax.dot_general(ref[at : at + 6 * chans], both, contract, preferred_element_type=F32)
        even, odd = terms[: 3 * chans, :channels], terms[3 * chans :]
        for b, block in enumerate((odd[:, channels:], even, odd[:, :channels])):
            lo = (9 * a + 3 * b) * chans
            terms_ref[lo : lo + 3 * chans, :] = block
    terms_ref[27 * chans :, :] = jnp.zeros((5 * chans, channels), F32)
    for c in range(chans):
        placed_ref[32 * c : 32 * c + 32, :] = terms_ref[pl.ds(c, 32, stride=chans), :]
    turned = placed_ref[...].T
    part = channels // len(seats)
    odd_core = lax.axis_index("depth") % 2 == 1
    for slot in range(len(seats)):
        start = owner_of(seats, slot) * (part // 2)
        for at in range(0, part // 2, outs):
            lo = slot * part + 2 * at
            even, odd = turned[lo : lo + outs], turned[lo + outs : lo + 2 * outs]
            place = pl.ds(pl.multiple_of(start + at, outs), outs)
            keep_ref[place, :] = jnp.where(odd_core, odd, even)
            send_ref[place, :] = jnp.where(odd_core, even, odd)


def pair_kernel(keep_ref, other_ref, *out_refs):
    chip = lax.axis_index("depth") // 2
    outs = out_refs[0].shape[0]
    for k, out_ref in enumerate(out_refs):
        place = pl.ds(pl.multiple_of((chip ^ k) * outs, outs), outs)
        out_ref[...] = keep_ref[place, :] + other_ref[place, :]


def input_kernel(taps_ref, *refs):
    *line_refs, out_ref, cells_ref, lines_ref = refs
    chans, _, rows, cols = out_ref.shape
    half = cols // 2
    grid_cells = half * rows // 2
    grads = [ref[...] for ref in line_refs]
    cells_ref[:, :grid_cells] = matmul(taps_ref[...], jnp.concatenate(grads, axis=0))
    cells_ref[:, grid_cells:] = jnp.zeros((cells_ref.shape[0], half), F32)
    group = 256 // chans
    weave = one_hot(cols, cols, lambda row, col: col == 2 * (row & (half - 1)) + row // half)
    inner = lax.broadcasted_iota(jnp.int32, (chans, half), 1) < half - 1

    def cells(plane, kind, b, r):
        lo = ((3 * plane + kind) * 3 + b) * chans
        return cells_ref[lo : lo + chans, r * half : (r + 1) * half]

    for plane in range(2):
        for start in range(0, rows, group):
            pieces = []
            for row in range(start, start + group):
                r = row // 2
                if row % 2 == 0:
                    even, odd, next_odd = [cells(plane, kind, 1, r) for kind in range(3)]
                else:
                    even, odd, next_odd = [
                        cells(plane, kind, 0, r + 1) + cells(plane, kind, 2, r) for kind in range(3)
                    ]
                odd = odd + jnp.where(inner, pltpu.roll(next_odd, half - 1, 1), 0.0)
                pieces.append(jnp.concatenate([even, odd], axis=1).astype(BF16))
            woven = matmul(jnp.concatenate(pieces, axis=0), weave)
            for side in range(2):
                lanes = slice(side * half, (side + 1) * half)
                lines_ref[side] = woven[:, lanes]
                for c in range(chans):
                    line = lines_ref[side, pl.ds(c, group, stride=chans), :].astype(BF16)
                    out_ref[c, plane, start : start + group, lanes] = line


def total_kernel(scale, *refs):
    *term_refs, out_ref = refs
    chans, outs, taps = out_ref.shape
    total = term_refs[0][...]
    for ref in term_refs[1:]:
        total = total + ref[...]
    total = total * scale
    for c in range(chans):
        out_ref[c] = total[:, 32 * c : 32 * c + taps]


def from_behind(shard, axis, by):
    count = lax.axis_size(axis)
    pairs = [(i, i + by) for i in range(count) if 0 <= i + by < count]
    return lax.ppermute(shard, axis, pairs)


def upsample(stacked, axis, extended):
    tap_zero, tap_one, tap_two = (stacked[0], stacked[1], stacked[2])
    coord_axis = axis - 1
    length = tap_zero.shape[coord_axis]
    if extended:
        outer = length - 1
        even_cells = lax.slice_in_dim(tap_one, 0, outer, axis=coord_axis)
        odd_cells = lax.slice_in_dim(tap_zero, 1, length, axis=coord_axis) + lax.slice_in_dim(
            tap_two, 0, outer, axis=coord_axis
        )
    else:
        outer = length
        shifted = lax.slice_in_dim(tap_zero, 1, length, axis=coord_axis)
        shifted = jnp.concatenate(
            [shifted, jnp.zeros_like(lax.slice_in_dim(tap_zero, 0, 1, axis=coord_axis))],
            axis=coord_axis,
        )
        even_cells = tap_one
        odd_cells = shifted + tap_two
    paired = jnp.stack([even_cells, odd_cells], axis=coord_axis + 1)
    new_shape = list(even_cells.shape)
    new_shape[coord_axis] = 2 * outer
    return paired.reshape(new_shape)


def phase_grads(weight_rows, grads_ext):
    local_in = weight_rows.shape[0] // 27
    channels_out, planes, rows, cols = grads_ext.shape
    taps_out = jnp.dot(
        weight_rows, grads_ext.reshape(channels_out, -1), preferred_element_type=jnp.float32
    )
    taps_out = taps_out.reshape(3, 3, 3, local_in, planes, rows, cols)
    along_w = upsample(jnp.moveaxis(taps_out, 2, 0), 6, False)
    along_h = upsample(jnp.moveaxis(along_w, 1, 0), 4, False)
    return upsample(along_h, 2, True)


def weight_terms(inputs, grads_ext):
    row_extra = 0
    weight_cube = lax.conv_general_dilated(
        inputs[None],
        grads_ext[:, None],
        (1, 1, 1),
        ((1, 2), (1, row_extra), (1, 0)),
        rhs_dilation=(2, 2, 2),
        dimension_numbers=("CNDHW", "OIDHW", "NCDHW"),
        preferred_element_type=jnp.float32,
    )
    return jnp.transpose(weight_cube, (2, 3, 4, 0, 1)).reshape(
        27, weight_cube.shape[0], weight_cube.shape[1]
    )


def plain_shards(grad_out, volume, weight):
    plane_next = from_behind(grad_out, "depth", -1)
    grads_ext = jnp.concatenate([grad_out, plane_next], axis=1)
    channels_out = weight.shape[2]
    local_in = volume.shape[0]
    every_channel = lax.all_gather(grads_ext, "chan", axis=0, tiled=True)
    own_weight = lax.dynamic_slice_in_dim(weight, lax.axis_index("chan") * local_in, local_in, 1)
    input_part = phase_grads(own_weight.reshape(27 * local_in, channels_out), every_channel)
    weight_part = weight_terms(volume, every_channel)
    input_grad = input_part.astype(jnp.bfloat16)
    summed = lax.psum_scatter(weight_part, "depth", scatter_dimension=2, tiled=True)
    cell_count = grad_out.shape[1] * lax.axis_size("depth") * grad_out.shape[2] * grad_out.shape[3]
    return (input_grad, summed * (1.0 / math.sqrt(cell_count)))


def call(kernel, out_shape, *args, scratch=(), cost=None):
    flops, moved = cost
    return pl.pallas_call(
        kernel,
        out_shape=out_shape,
        in_specs=[VMEM] * len(args),
        out_specs=jax.tree.map(lambda _: VMEM, out_shape),
        scratch_shapes=scratch,
        compiler_params=pltpu.CompilerParams(vmem_limit_bytes=LIMIT),
        cost_estimate=pl.CostEstimate(flops=flops, bytes_accessed=moved, transcendentals=0),
    )(*args)


def shards(grad_out, volume, weight):
    count = lax.axis_size("chan")
    depth = lax.axis_size("depth")
    own_outs, _, rows, cols = grad_out.shape
    chans = volume.shape[0]
    channels = weight.shape[2]
    cells = rows * cols
    order = ring_order(count)
    ahead = [(order[i], order[(i + 1) % count]) for i in range(count)]
    farther = [(i, (i + 1) % depth) for i in range(depth)]
    nearer = [(b, a) for a, b in farther]
    seats = [[order[(order.index(chip) - step) % count] for step in range(count)] for chip in range(count)]

    own_weight = lax.dynamic_slice_in_dim(weight, lax.axis_index("chan") * chans, chans, 1)
    odd = pl.pallas_call(
        odd_plane_kernel,
        out_shape=jax.ShapeDtypeStruct((chans, 1, 2 * rows, 2 * cols), BF16),
        in_specs=[HBM],
        out_specs=HBM,
        scratch_shapes=[pltpu.SemaphoreType.DMA],
        compiler_params=pltpu.CompilerParams(vmem_limit_bytes=63 * 1024 * 1024),
        cost_estimate=pl.CostEstimate(flops=0, bytes_accessed=1 << 20, transcendentals=0),
    )(volume)
    views, taps = call(
        lambda *refs: own_views_kernel(seats, depth, *refs),
        (
            jax.ShapeDtypeStruct((12 * chans, cells), BF16),
            jax.ShapeDtypeStruct((18 * chans, 2 * channels), BF16),
        ),
        volume,
        own_weight,
        cost=(2 * 2 * 2 * cells * chans * 8 * cols, 4 << 20),
    )
    halves = [grad_out[: own_outs // 2], grad_out[own_outs // 2 :]]
    steps = []
    for step in range(1, count):
        halves = [lax.ppermute(half, "chan", ahead) for half in halves]
        steps.append(halves)
    lines = lambda *parts: call(
        lines_kernel,
        jax.ShapeDtypeStruct((sum(part.shape[0] for part in parts), cells), BF16),
        *parts,
        scratch=(pltpu.VMEM((own_outs * rows, cols), F32),),
        cost=(1 << 20, 2 << 20),
    )
    behind = lax.ppermute(odd, "depth", farther)
    behind_views = call(
        behind_views_kernel,
        jax.ShapeDtypeStruct((6 * chans, cells), BF16),
        behind,
        cost=(2 * 2 * cells * chans * 8 * cols, 2 << 20),
    )
    *steps[0], views = lax.optimization_barrier((*steps[0], views))
    own_lines = [lines(grad_out, *steps[0])] + [lines(*step) for step in steps[1:]]
    next_lines = [lax.ppermute(part, "depth", nearer) for part in own_lines]
    outs = channels // depth
    half_terms = jax.ShapeDtypeStruct((channels // 2, 32 * chans), F32)
    keep, send = call(
        lambda *refs: weight_kernel(seats, outs, *refs),
        (half_terms, half_terms),
        views,
        behind_views,
        *own_lines,
        scratch=(
            pltpu.VMEM((channels, cells + cols), BF16),
            pltpu.VMEM((32 * chans, channels), F32),
            pltpu.VMEM((32 * chans, channels), F32),
        ),
        cost=(2 * 27 * chans * channels * cells, 8 << 20),
    )
    chips = depth // 2
    other = lax.ppermute(send, "depth", [(i, i ^ 1) for i in range(depth)])
    own_terms, *terms = call(
        pair_kernel,
        [jax.ShapeDtypeStruct((outs, 32 * chans), F32)] * chips,
        keep,
        other,
        cost=(1 << 16, 1 << 19),
    )
    terms = [lax.ppermute(term, "depth", [(i, i ^ (2 * k + 2)) for i in range(depth)]) for k, term in enumerate(terms)]
    input_grad = call(
        input_kernel,
        jax.ShapeDtypeStruct(volume.shape, BF16),
        taps,
        *next_lines,
        *own_lines,
        scratch=(
            pltpu.VMEM((18 * chans, cells + cols), F32),
            pltpu.VMEM((2, 256, cols), F32),
        ),
        cost=(2 * 18 * chans * 2 * channels * cells, 8 << 20),
    )
    own_terms, input_grad = lax.optimization_barrier((own_terms, input_grad))
    scale = 1.0 / math.sqrt(depth * cells)
    weight_grad = call(
        lambda *refs: total_kernel(scale, *refs),
        jax.ShapeDtypeStruct((chans, outs, 27), F32),
        own_terms,
        *terms,
        cost=(1 << 16, 1 << 19),
    )
    return input_grad, jnp.transpose(weight_grad, (2, 0, 1))


def solution(mesh):
    in_specs = (P("chan", "depth", None, None), P("chan", "depth", None, None), P())
    out_specs = (P("chan", "depth", None, None), P(None, "chan", "depth"))
    ring, depth = mesh.shape["chan"], mesh.shape["depth"]

    def either(grad_out, volume, weight):
        fits = (
            grad_out.shape[0] % 32 == 0
            and volume.shape[0] == 16
            and grad_out.shape[1] == 1
            and ring >= 2
            and depth & (depth - 1) == 0
            and depth % (2 * ring) == 0
        )
        return (shards if fits else plain_shards)(grad_out, volume, weight)

    return jax.shard_map(either, mesh=mesh, in_specs=in_specs, out_specs=out_specs, check_vma=False)
```

```python
import math

import jax
import jax.numpy as jnp
from jax import lax
from jax.experimental import pallas as pl
from jax.experimental.pallas import tpu as pltpu
from jax.sharding import PartitionSpec as P

F32 = jnp.float32
BF16 = jnp.bfloat16
VMEM = pl.BlockSpec(memory_space=pltpu.VMEM)
LIMIT = 48 * 1024 * 1024


def matmul(left, right):
    return jnp.dot(left, right, preferred_element_type=F32)


def one_hot(rows, cols, source):
    row = lax.broadcasted_iota(jnp.int32, (rows, cols), 0)
    col = lax.broadcasted_iota(jnp.int32, (rows, cols), 1)
    return jnp.where(source(row, col), 1.0, 0.0).astype(BF16)


def swap_rows(major, minor):
    bits = minor.bit_length() - 1
    return one_hot(
        major * minor,
        major * minor,
        lambda row, col: col == (row & (minor - 1)) * major + (row >> bits),
    )


def place_views(plane, views_ref, base):
    chans, rows, cols = plane.shape
    half = cols // 2
    group = 256 // chans
    swap = swap_rows(group, chans)
    split = one_hot(cols, cols, lambda row, col: row == 2 * (col & (half - 1)) + col // half)
    inner = lax.broadcasted_iota(jnp.int32, (group * chans, half), 1) > 0
    for start in range(0, rows, group):
        block = plane[:, start : start + group, :].reshape(chans * group, cols)
        parted = matmul(matmul(swap, block).astype(BF16), split)
        odd = parted[:, half:]
        before = jnp.where(inner, pltpu.roll(odd, 1, 1), 0.0)
        views = [view.astype(BF16) for view in (before, parted[:, :half], odd)]
        for at in range(group):
            row = start + at
            lanes = slice(row // 2 * half, (row // 2 + 1) * half)
            for e in range(3):
                lo = base + (3 * (row % 2) + e) * chans
                views_ref[lo : lo + chans, lanes] = views[e][at * chans : (at + 1) * chans]


def own_views_kernel(depth, volume_ref, weight_ref, views_ref, taps_ref, odd_ref):
    chans = volume_ref.shape[0]
    channels = weight_ref.shape[2]
    odd_ref[...] = volume_ref[:, 1:]
    place_views(volume_ref.at[:, 0], views_ref, 0)
    place_views(volume_ref.at[:, 1], views_ref, 6 * chans)
    count = lax.axis_size("chan")
    part = channels // count
    here = lax.axis_index("chan")
    row = lax.broadcasted_iota(jnp.int32, (channels, channels), 0)
    col = lax.broadcasted_iota(jnp.int32, (channels, channels), 1)
    order = jnp.zeros((channels, channels), F32)
    for slot in range(count):
        moved = ((here ^ slot) - slot) * part
        inside = (col >= slot * part) & (col < (slot + 1) * part)
        order = jnp.where(inside & (row == col + moved), 1.0, order)
    ordered = matmul(weight_ref[...].reshape(27 * chans, channels), order.astype(BF16)).astype(BF16)
    beyond = jnp.where(lax.axis_index("depth") == depth - 1, 0.0, 1.0).astype(BF16)
    zero = jnp.zeros((chans, channels), BF16)
    for k, e in enumerate((1, 2, 0)):
        for b in range(3):
            pick = lambda a: ordered[(9 * a + 3 * b + e) * chans : (9 * a + 3 * b + e + 1) * chans]
            for plane, line in enumerate(((zero, pick(1)), (pick(0) * beyond, pick(2)))):
                lo = ((3 * plane + k) * 3 + b) * chans
                taps_ref[lo : lo + chans, :] = jnp.concatenate(line, axis=1)


def behind_views_kernel(behind_ref, views_ref):
    first = lax.axis_index("depth") == 0

    @pl.when(jnp.logical_not(first))
    def _():
        place_views(behind_ref.at[:, 0], views_ref, 0)

    @pl.when(first)
    def _():
        views_ref[...] = jnp.zeros(views_ref.shape, BF16)


def place_lines(part, out_ref, at, wide_ref):
    outs, _, rows, cols = part.shape
    wide_ref[: outs * rows, :] = part[...].reshape(outs * rows, cols).astype(F32)
    for row in range(rows):
        line = wide_ref[pl.ds(row, outs, stride=rows), :].astype(BF16)
        out_ref[at : at + outs, row * cols : (row + 1) * cols] = line


def lines_kernel(*refs):
    *parts, out_ref, wide_ref = refs
    at = 0
    for part in parts:
        place_lines(part, out_ref, at, wide_ref)
        at += part.shape[0]


def weight_kernel(
    outs, own_ref, behind_ref, *refs
):
    *line_refs, keep_ref, send_ref, grads_ref, terms_ref, placed_ref = refs
    channels = grads_ref.shape[0]
    chans = behind_ref.shape[0] // 6
    cells = own_ref.shape[1]
    cols = grads_ref.shape[1] - cells
    at = 0
    for ref in line_refs:
        grads_ref[at : at + ref.shape[0], :cells] = ref[...]
        at += ref.shape[0]
    grads_ref[:, cells:] = jnp.zeros((channels, cols), BF16)
    both = jnp.concatenate([grads_ref[:, :cells], grads_ref[:, cols:]], axis=0)
    contract = (((1,), (1,)), ((), ()))
    for a, (ref, at) in enumerate(((behind_ref, 0), (own_ref, 0), (own_ref, 6 * chans))):
        terms = lax.dot_general(ref[at : at + 6 * chans], both, contract, preferred_element_type=F32)
        even, odd = terms[: 3 * chans, :channels], terms[3 * chans :]
        for b, block in enumerate((odd[:, channels:], even, odd[:, :channels])):
            lo = (9 * a + 3 * b) * chans
            terms_ref[lo : lo + 3 * chans, :] = block
    terms_ref[27 * chans :, :] = jnp.zeros((5 * chans, channels), F32)
    for c in range(chans):
        placed_ref[32 * c : 32 * c + 32, :] = terms_ref[pl.ds(c, 32, stride=chans), :]
    turned = placed_ref[...].T
    count = lax.axis_size("chan")
    part = channels // count
    odd_core = lax.axis_index("depth") % 2 == 1
    for slot in range(count):
        start = (lax.axis_index("chan") ^ slot) * (part // 2)
        for at in range(0, part // 2, outs):
            lo = slot * part + 2 * at
            even, odd = turned[lo : lo + outs], turned[lo + outs : lo + 2 * outs]
            place = pl.ds(pl.multiple_of(start + at, outs), outs)
            keep_ref[place, :] = jnp.where(odd_core, odd, even)
            send_ref[place, :] = jnp.where(odd_core, even, odd)


def pair_kernel(keep_ref, other_ref, *out_refs):
    chip = lax.axis_index("depth") // 2
    outs = out_refs[0].shape[0]
    for k, out_ref in enumerate(out_refs):
        place = pl.ds(pl.multiple_of((chip ^ k) * outs, outs), outs)
        out_ref[...] = keep_ref[place, :] + other_ref[place, :]


def input_kernel(taps_ref, *refs):
    *line_refs, out_ref, cells_ref, lines_ref = refs
    chans, _, rows, cols = out_ref.shape
    half = cols // 2
    grid_cells = half * rows // 2
    grads = [ref[...] for ref in line_refs]
    cells_ref[:, :grid_cells] = matmul(taps_ref[...], jnp.concatenate(grads, axis=0))
    cells_ref[:, grid_cells:] = jnp.zeros((cells_ref.shape[0], half), F32)
    group = 256 // chans
    weave = one_hot(cols, cols, lambda row, col: col == 2 * (row & (half - 1)) + row // half)
    inner = lax.broadcasted_iota(jnp.int32, (chans, half), 1) < half - 1

    def cells(plane, kind, b, r):
        lo = ((3 * plane + kind) * 3 + b) * chans
        return cells_ref[lo : lo + chans, r * half : (r + 1) * half]

    for plane in range(2):
        for start in range(0, rows, group):
            pieces = []
            for row in range(start, start + group):
                r = row // 2
                if row % 2 == 0:
                    even, odd, next_odd = [cells(plane, kind, 1, r) for kind in range(3)]
                else:
                    even, odd, next_odd = [
                        cells(plane, kind, 0, r + 1) + cells(plane, kind, 2, r) for kind in range(3)
                    ]
                odd = odd + jnp.where(inner, pltpu.roll(next_odd, half - 1, 1), 0.0)
                pieces.append(jnp.concatenate([even, odd], axis=1).astype(BF16))
            woven = matmul(jnp.concatenate(pieces, axis=0), weave)
            for side in range(2):
                lanes = slice(side * half, (side + 1) * half)
                lines_ref[side] = woven[:, lanes]
                for c in range(chans):
                    line = lines_ref[side, pl.ds(c, group, stride=chans), :].astype(BF16)
                    out_ref[c, plane, start : start + group, lanes] = line


def total_kernel(scale, *refs):
    *term_refs, out_ref = refs
    chans, outs, taps = out_ref.shape
    total = term_refs[0][...]
    for ref in term_refs[1:]:
        total = total + ref[...]
    total = total * scale
    for c in range(chans):
        out_ref[c] = total[:, 32 * c : 32 * c + taps]


def from_behind(shard, axis, by):
    count = lax.axis_size(axis)
    pairs = [(i, i + by) for i in range(count) if 0 <= i + by < count]
    return lax.ppermute(shard, axis, pairs)


def upsample(stacked, axis, extended):
    tap_zero, tap_one, tap_two = (stacked[0], stacked[1], stacked[2])
    coord_axis = axis - 1
    length = tap_zero.shape[coord_axis]
    if extended:
        outer = length - 1
        even_cells = lax.slice_in_dim(tap_one, 0, outer, axis=coord_axis)
        odd_cells = lax.slice_in_dim(tap_zero, 1, length, axis=coord_axis) + lax.slice_in_dim(
            tap_two, 0, outer, axis=coord_axis
        )
    else:
        outer = length
        shifted = lax.slice_in_dim(tap_zero, 1, length, axis=coord_axis)
        shifted = jnp.concatenate(
            [shifted, jnp.zeros_like(lax.slice_in_dim(tap_zero, 0, 1, axis=coord_axis))],
            axis=coord_axis,
        )
        even_cells = tap_one
        odd_cells = shifted + tap_two
    paired = jnp.stack([even_cells, odd_cells], axis=coord_axis + 1)
    new_shape = list(even_cells.shape)
    new_shape[coord_axis] = 2 * outer
    return paired.reshape(new_shape)


def phase_grads(weight_rows, grads_ext):
    local_in = weight_rows.shape[0] // 27
    channels_out, planes, rows, cols = grads_ext.shape
    taps_out = jnp.dot(
        weight_rows, grads_ext.reshape(channels_out, -1), preferred_element_type=jnp.float32
    )
    taps_out = taps_out.reshape(3, 3, 3, local_in, planes, rows, cols)
    along_w = upsample(jnp.moveaxis(taps_out, 2, 0), 6, False)
    along_h = upsample(jnp.moveaxis(along_w, 1, 0), 4, False)
    return upsample(along_h, 2, True)


def weight_terms(inputs, grads_ext):
    row_extra = 0
    weight_cube = lax.conv_general_dilated(
        inputs[None],
        grads_ext[:, None],
        (1, 1, 1),
        ((1, 2), (1, row_extra), (1, 0)),
        rhs_dilation=(2, 2, 2),
        dimension_numbers=("CNDHW", "OIDHW", "NCDHW"),
        preferred_element_type=jnp.float32,
    )
    return jnp.transpose(weight_cube, (2, 3, 4, 0, 1)).reshape(
        27, weight_cube.shape[0], weight_cube.shape[1]
    )


def plain_shards(grad_out, volume, weight):
    plane_next = from_behind(grad_out, "depth", -1)
    grads_ext = jnp.concatenate([grad_out, plane_next], axis=1)
    channels_out = weight.shape[2]
    local_in = volume.shape[0]
    every_channel = lax.all_gather(grads_ext, "chan", axis=0, tiled=True)
    own_weight = lax.dynamic_slice_in_dim(weight, lax.axis_index("chan") * local_in, local_in, 1)
    input_part = phase_grads(own_weight.reshape(27 * local_in, channels_out), every_channel)
    weight_part = weight_terms(volume, every_channel)
    input_grad = input_part.astype(jnp.bfloat16)
    summed = lax.psum_scatter(weight_part, "depth", scatter_dimension=2, tiled=True)
    cell_count = grad_out.shape[1] * lax.axis_size("depth") * grad_out.shape[2] * grad_out.shape[3]
    return (input_grad, summed * (1.0 / math.sqrt(cell_count)))


def call(kernel, out_shape, *args, scratch=(), cost=None):
    flops, moved = cost
    return pl.pallas_call(
        kernel,
        out_shape=out_shape,
        in_specs=[VMEM] * len(args),
        out_specs=jax.tree.map(lambda _: VMEM, out_shape),
        scratch_shapes=scratch,
        compiler_params=pltpu.CompilerParams(vmem_limit_bytes=LIMIT),
        cost_estimate=pl.CostEstimate(flops=flops, bytes_accessed=moved, transcendentals=0),
    )(*args)


def shards(grad_out, volume, weight):
    count = lax.axis_size("chan")
    depth = lax.axis_size("depth")
    own_outs, _, rows, cols = grad_out.shape
    chans = volume.shape[0]
    channels = weight.shape[2]
    cells = rows * cols
    farther = [(i, (i + 1) % depth) for i in range(depth)]
    nearer = [(b, a) for a, b in farther]

    own_weight = lax.dynamic_slice_in_dim(weight, lax.axis_index("chan") * chans, chans, 1)
    views, taps, odd = call(
        lambda *refs: own_views_kernel(depth, *refs),
        (
            jax.ShapeDtypeStruct((12 * chans, cells), BF16),
            jax.ShapeDtypeStruct((18 * chans, 2 * channels), BF16),
            jax.ShapeDtypeStruct((chans, 1, 2 * rows, 2 * cols), BF16),
        ),
        volume,
        own_weight,
        cost=(2 * 2 * 2 * cells * chans * 8 * cols, 4 << 20),
    )
    got = {0: grad_out}
    for mask in sorted(range(1, count), key=lambda mask: (mask & (mask - 1) > 0, -mask)):
        low = mask & -mask
        got[mask] = lax.ppermute(got[mask - low], "chan", [(i, i ^ low) for i in range(count)])
    got[1], odd = lax.optimization_barrier((got[1], odd))
    lines = lambda *parts: call(
        lines_kernel,
        jax.ShapeDtypeStruct((sum(part.shape[0] for part in parts), cells), BF16),
        *parts,
        scratch=(pltpu.VMEM((own_outs * rows, cols), F32),),
        cost=(1 << 20, 2 << 20),
    )
    behind = lax.ppermute(odd, "depth", farther)
    behind_views = call(
        behind_views_kernel,
        jax.ShapeDtypeStruct((6 * chans, cells), BF16),
        behind,
        cost=(2 * 2 * cells * chans * 8 * cols, 2 << 20),
    )
    own_lines = [lines(got[0], got[1])] + [lines(got[mask]) for mask in range(2, count)]
    next_lines = [lax.ppermute(part, "depth", nearer) for part in own_lines]
    outs = channels // depth
    half_terms = jax.ShapeDtypeStruct((channels // 2, 32 * chans), F32)
    keep, send = call(
        lambda *refs: weight_kernel(outs, *refs),
        (half_terms, half_terms),
        views,
        behind_views,
        *own_lines,
        scratch=(
            pltpu.VMEM((channels, cells + cols), BF16),
            pltpu.VMEM((32 * chans, channels), F32),
            pltpu.VMEM((32 * chans, channels), F32),
        ),
        cost=(2 * 27 * chans * channels * cells, 8 << 20),
    )
    chips = depth // 2
    other = lax.ppermute(send, "depth", [(i, i ^ 1) for i in range(depth)])
    own_terms, *terms = call(
        pair_kernel,
        [jax.ShapeDtypeStruct((outs, 32 * chans), F32)] * chips,
        keep,
        other,
        cost=(1 << 16, 1 << 19),
    )
    terms = [lax.ppermute(term, "depth", [(i, i ^ (2 * k + 2)) for i in range(depth)]) for k, term in enumerate(terms)]
    input_grad = call(
        input_kernel,
        jax.ShapeDtypeStruct(volume.shape, BF16),
        taps,
        *next_lines,
        *own_lines,
        scratch=(
            pltpu.VMEM((18 * chans, cells + cols), F32),
            pltpu.VMEM((2, 256, cols), F32),
        ),
        cost=(2 * 18 * chans * 2 * channels * cells, 8 << 20),
    )
    own_terms, input_grad = lax.optimization_barrier((own_terms, input_grad))
    scale = 1.0 / math.sqrt(depth * cells)
    weight_grad = call(
        lambda *refs: total_kernel(scale, *refs),
        jax.ShapeDtypeStruct((chans, outs, 27), F32),
        own_terms,
        *terms,
        cost=(1 << 16, 1 << 19),
    )
    return input_grad, jnp.transpose(weight_grad, (2, 0, 1))


def solution(mesh):
    in_specs = (P("chan", "depth", None, None), P("chan", "depth", None, None), P())
    out_specs = (P("chan", "depth", None, None), P(None, "chan", "depth"))
    ring, depth = mesh.shape["chan"], mesh.shape["depth"]

    def either(grad_out, volume, weight):
        fits = (
            grad_out.shape[0] % 32 == 0
            and volume.shape[0] == 16
            and grad_out.shape[1] == 1
            and ring >= 2
            and ring & (ring - 1) == 0
            and depth & (depth - 1) == 0
            and depth % (2 * ring) == 0
        )
        return (shards if fits else plain_shards)(grad_out, volume, weight)

    return jax.shard_map(either, mesh=mesh, in_specs=in_specs, out_specs=out_specs, check_vma=False)
```

```python
import functools
import math

import jax
import jax.numpy as jnp
from jax import lax
from jax.experimental import pallas as pl
from jax.experimental.pallas import tpu as pltpu
from jax.sharding import PartitionSpec as P

F32 = jnp.float32
BF16 = jnp.bfloat16
VMEM = pl.BlockSpec(memory_space=pltpu.VMEM)
HBM = pl.BlockSpec(memory_space=pltpu.HBM)
LIMIT = 48 * 1024 * 1024


def matmul(left, right):
    return jnp.dot(left, right, preferred_element_type=F32)


def one_hot(rows, cols, source):
    row = lax.broadcasted_iota(jnp.int32, (rows, cols), 0)
    col = lax.broadcasted_iota(jnp.int32, (rows, cols), 1)
    return jnp.where(source(row, col), 1.0, 0.0).astype(BF16)


def swap_rows(major, minor):
    bits = minor.bit_length() - 1
    return one_hot(
        major * minor,
        major * minor,
        lambda row, col: col == (row & (minor - 1)) * major + (row >> bits),
    )


def place_views(plane, views_ref, base):
    chans, rows, cols = plane.shape
    half = cols // 2
    group = 256 // chans
    swap = swap_rows(group, chans)
    split = one_hot(cols, cols, lambda row, col: row == 2 * (col & (half - 1)) + col // half)
    inner = lax.broadcasted_iota(jnp.int32, (group * chans, half), 1) > 0
    for start in range(0, rows, group):
        block = plane[:, start : start + group, :].reshape(chans * group, cols)
        parted = matmul(matmul(swap, block).astype(BF16), split)
        odd = parted[:, half:]
        before = jnp.where(inner, pltpu.roll(odd, 1, 1), 0.0)
        views = [view.astype(BF16) for view in (before, parted[:, :half], odd)]
        for at in range(group):
            row = start + at
            lanes = slice(row // 2 * half, (row // 2 + 1) * half)
            for e in range(3):
                lo = base + (3 * (row % 2) + e) * chans
                views_ref[lo : lo + chans, lanes] = views[e][at * chans : (at + 1) * chans]


def own_views_kernel(depth, volume_ref, weight_ref, views_ref, even_ref, odd_ref):
    chans = volume_ref.shape[0]
    channels = weight_ref.shape[2]
    place_views(volume_ref.at[:, 0], views_ref, 0)
    place_views(volume_ref.at[:, 1], views_ref, 6 * chans)
    count = lax.axis_size("chan")
    part = channels // count
    here = lax.axis_index("chan")
    row = lax.broadcasted_iota(jnp.int32, (channels, channels), 0)
    col = lax.broadcasted_iota(jnp.int32, (channels, channels), 1)
    order = jnp.zeros((channels, channels), F32)
    for slot in range(count):
        moved = ((here ^ slot) - slot) * part
        inside = (col >= slot * part) & (col < (slot + 1) * part)
        order = jnp.where(inside & (row == col + moved), 1.0, order)
    ordered = matmul(weight_ref[...].reshape(27 * chans, channels), order.astype(BF16)).astype(BF16)
    beyond = jnp.where(lax.axis_index("depth") == depth - 1, 0.0, 1.0).astype(BF16)
    for k, e in enumerate((1, 2, 0)):
        for b in range(3):
            pick = lambda a: ordered[(9 * a + 3 * b + e) * chans : (9 * a + 3 * b + e + 1) * chans]
            lo = (3 * k + b) * chans
            even_ref[lo : lo + chans, :] = pick(1)
            odd_ref[lo : lo + chans, :] = jnp.concatenate([pick(0) * beyond, pick(2)], axis=1)


def behind_views_kernel(behind_ref, views_ref):
    first = lax.axis_index("depth") == 0

    @pl.when(jnp.logical_not(first))
    def _():
        place_views(behind_ref.at[:, 1], views_ref, 0)

    @pl.when(first)
    def _():
        views_ref[...] = jnp.zeros(views_ref.shape, BF16)


def place_lines(part, out_ref, at, wide_ref):
    outs, _, rows, cols = part.shape
    wide_ref[: outs * rows, :] = part[...].reshape(outs * rows, cols).astype(F32)
    for row in range(rows):
        line = wide_ref[pl.ds(row, outs, stride=rows), :].astype(BF16)
        out_ref[at : at + outs, row * cols : (row + 1) * cols] = line


def lines_kernel(*refs):
    *parts, out_ref, wide_ref = refs
    at = 0
    for part in parts:
        place_lines(part, out_ref, at, wide_ref)
        at += part.shape[0]


def weight_kernel(
    outs, cols, chunk, own_ref, behind_ref, *refs
):
    *line_refs, keep_ref, send_ref, terms_ref, placed_ref = refs
    channels = terms_ref.shape[1]
    chans = behind_ref.shape[0] // 6
    cells = own_ref.shape[1]
    contract = (((1,), (1,)), ((), ()))

    def grads(lo, hi):
        return jnp.concatenate([ref[:, lo:hi] for ref in line_refs], axis=0)

    sums = None
    for lo in range(0, cells, chunk):
        hi = lo + chunk
        below = grads(lo + cols, min(hi + cols, cells))
        if hi == cells:
            below = jnp.concatenate([below, jnp.zeros((channels, cols), BF16)], axis=1)
        both = jnp.concatenate([grads(lo, hi), below], axis=0)
        views = jnp.concatenate([behind_ref[:, lo:hi], own_ref[:, lo:hi]], axis=0)
        part = lax.dot_general(views, both, contract, preferred_element_type=F32)
        sums = part if sums is None else sums + part
    for a in range(3):
        terms = sums[6 * a * chans : 6 * (a + 1) * chans]
        even, odd = terms[: 3 * chans, :channels], terms[3 * chans :]
        for b, block in enumerate((odd[:, channels:], even, odd[:, :channels])):
            lo = (9 * a + 3 * b) * chans
            terms_ref[lo : lo + 3 * chans, :] = block
    terms_ref[27 * chans :, :] = jnp.zeros((5 * chans, channels), F32)
    for c in range(chans):
        placed_ref[32 * c : 32 * c + 32, :] = terms_ref[pl.ds(c, 32, stride=chans), :]
    turned = placed_ref[...].T
    count = lax.axis_size("chan")
    part = channels // count
    odd_core = lax.axis_index("depth") % 2 == 1
    for slot in range(count):
        start = (lax.axis_index("chan") ^ slot) * (part // 2)
        for at in range(0, part // 2, outs):
            lo = slot * part + 2 * at
            even, odd = turned[lo : lo + outs], turned[lo + outs : lo + 2 * outs]
            place = pl.ds(pl.multiple_of(start + at, outs), outs)
            keep_ref[place, :] = jnp.where(odd_core, odd, even)
            send_ref[place, :] = jnp.where(odd_core, even, odd)


def pair_kernel(keep_ref, other_ref, *out_refs):
    chip = lax.axis_index("depth") // 2
    outs = out_refs[0].shape[0]
    for k, out_ref in enumerate(out_refs):
        place = pl.ds(pl.multiple_of((chip ^ k) * outs, outs), outs)
        out_ref[...] = keep_ref[place, :] + other_ref[place, :]


def input_kernel(plane, *refs):
    taps_ref, *line_refs, out_ref, cells_ref, lines_ref, rows_ref, sems = refs
    chans, rows, cols = rows_ref.shape
    half = cols // 2
    grid_cells = half * rows // 2
    grads = jnp.concatenate([ref[...] for ref in line_refs], axis=0)
    cells_ref[:, :grid_cells] = matmul(taps_ref[...], grads)
    cells_ref[:, grid_cells:] = jnp.zeros((cells_ref.shape[0], half), F32)
    group = 256 // chans
    weave = one_hot(cols, cols, lambda row, col: col == 2 * (row & (half - 1)) + row // half)
    inner = lax.broadcasted_iota(jnp.int32, (chans, half), 1) < half - 1

    def cells(kind, b, r):
        lo = (3 * kind + b) * chans
        return cells_ref[lo : lo + chans, r * half : (r + 1) * half]

    copies = []
    for start in range(0, rows, group):
        pieces = []
        for row in range(start, start + group):
            r = row // 2
            if row % 2 == 0:
                even, odd, next_odd = [cells(kind, 1, r) for kind in range(3)]
            else:
                even, odd, next_odd = [cells(kind, 0, r + 1) + cells(kind, 2, r) for kind in range(3)]
            odd = odd + jnp.where(inner, pltpu.roll(next_odd, half - 1, 1), 0.0)
            pieces.append(jnp.concatenate([even, odd], axis=1).astype(BF16))
        woven = matmul(jnp.concatenate(pieces, axis=0), weave)
        for side in range(2):
            lanes = slice(side * half, (side + 1) * half)
            lines_ref[side] = woven[:, lanes]
            for c in range(chans):
                line = lines_ref[side, pl.ds(c, group, stride=chans), :].astype(BF16)
                rows_ref[c, start : start + group, lanes] = line
        place = pl.ds(start, group)
        copies.append(
            pltpu.make_async_copy(
                rows_ref.at[:, place], out_ref.at[:, plane, place], sems.at[start // group]
            )
        )
        copies[-1].start()
    for copy in copies:
        copy.wait()


def total_kernel(scale, *refs):
    *term_refs, out_ref = refs
    chans, outs, taps = out_ref.shape
    total = term_refs[0][...]
    for ref in term_refs[1:]:
        total = total + ref[...]
    total = total * scale
    for c in range(chans):
        out_ref[c] = total[:, 32 * c : 32 * c + taps]


def from_behind(shard, axis, by):
    count = lax.axis_size(axis)
    pairs = [(i, i + by) for i in range(count) if 0 <= i + by < count]
    return lax.ppermute(shard, axis, pairs)


def upsample(stacked, axis, extended):
    tap_zero, tap_one, tap_two = (stacked[0], stacked[1], stacked[2])
    coord_axis = axis - 1
    length = tap_zero.shape[coord_axis]
    if extended:
        outer = length - 1
        even_cells = lax.slice_in_dim(tap_one, 0, outer, axis=coord_axis)
        odd_cells = lax.slice_in_dim(tap_zero, 1, length, axis=coord_axis) + lax.slice_in_dim(
            tap_two, 0, outer, axis=coord_axis
        )
    else:
        outer = length
        shifted = lax.slice_in_dim(tap_zero, 1, length, axis=coord_axis)
        shifted = jnp.concatenate(
            [shifted, jnp.zeros_like(lax.slice_in_dim(tap_zero, 0, 1, axis=coord_axis))],
            axis=coord_axis,
        )
        even_cells = tap_one
        odd_cells = shifted + tap_two
    paired = jnp.stack([even_cells, odd_cells], axis=coord_axis + 1)
    new_shape = list(even_cells.shape)
    new_shape[coord_axis] = 2 * outer
    return paired.reshape(new_shape)


def phase_grads(weight_rows, grads_ext):
    local_in = weight_rows.shape[0] // 27
    channels_out, planes, rows, cols = grads_ext.shape
    taps_out = jnp.dot(
        weight_rows, grads_ext.reshape(channels_out, -1), preferred_element_type=jnp.float32
    )
    taps_out = taps_out.reshape(3, 3, 3, local_in, planes, rows, cols)
    along_w = upsample(jnp.moveaxis(taps_out, 2, 0), 6, False)
    along_h = upsample(jnp.moveaxis(along_w, 1, 0), 4, False)
    return upsample(along_h, 2, True)


def weight_terms(inputs, grads_ext):
    row_extra = 0
    weight_cube = lax.conv_general_dilated(
        inputs[None],
        grads_ext[:, None],
        (1, 1, 1),
        ((1, 2), (1, row_extra), (1, 0)),
        rhs_dilation=(2, 2, 2),
        dimension_numbers=("CNDHW", "OIDHW", "NCDHW"),
        preferred_element_type=jnp.float32,
    )
    return jnp.transpose(weight_cube, (2, 3, 4, 0, 1)).reshape(
        27, weight_cube.shape[0], weight_cube.shape[1]
    )


def plain_shards(grad_out, volume, weight):
    plane_next = from_behind(grad_out, "depth", -1)
    grads_ext = jnp.concatenate([grad_out, plane_next], axis=1)
    channels_out = weight.shape[2]
    local_in = volume.shape[0]
    every_channel = lax.all_gather(grads_ext, "chan", axis=0, tiled=True)
    own_weight = lax.dynamic_slice_in_dim(weight, lax.axis_index("chan") * local_in, local_in, 1)
    input_part = phase_grads(own_weight.reshape(27 * local_in, channels_out), every_channel)
    weight_part = weight_terms(volume, every_channel)
    input_grad = input_part.astype(jnp.bfloat16)
    summed = lax.psum_scatter(weight_part, "depth", scatter_dimension=2, tiled=True)
    cell_count = grad_out.shape[1] * lax.axis_size("depth") * grad_out.shape[2] * grad_out.shape[3]
    return (input_grad, summed * (1.0 / math.sqrt(cell_count)))


def call(kernel, out_shape, *args, scratch=(), cost=None):
    flops, moved = cost
    return pl.pallas_call(
        kernel,
        out_shape=out_shape,
        in_specs=[VMEM] * len(args),
        out_specs=jax.tree.map(lambda _: VMEM, out_shape),
        scratch_shapes=scratch,
        compiler_params=pltpu.CompilerParams(vmem_limit_bytes=LIMIT),
        cost_estimate=pl.CostEstimate(flops=flops, bytes_accessed=moved, transcendentals=0),
    )(*args)


def shards(grad_out, volume, weight):
    count = lax.axis_size("chan")
    depth = lax.axis_size("depth")
    own_outs, _, rows, cols = grad_out.shape
    chans = volume.shape[0]
    channels = weight.shape[2]
    cells = rows * cols
    farther = [(i, (i + 1) % depth) for i in range(depth)]
    nearer = [(b, a) for a, b in farther]

    own_weight = lax.dynamic_slice_in_dim(weight, lax.axis_index("chan") * chans, chans, 1)
    views, even_taps, odd_taps = call(
        lambda *refs: own_views_kernel(depth, *refs),
        (
            jax.ShapeDtypeStruct((12 * chans, cells), BF16),
            jax.ShapeDtypeStruct((9 * chans, channels), BF16),
            jax.ShapeDtypeStruct((9 * chans, 2 * channels), BF16),
        ),
        volume,
        own_weight,
        cost=(2 * 2 * 2 * cells * chans * 8 * cols, 4 << 20),
    )
    got = {0: grad_out}
    for mask in sorted(range(1, count), key=lambda mask: (mask & (mask - 1) > 0, -mask)):
        low = mask & -mask
        got[mask] = lax.ppermute(got[mask - low], "chan", [(i, i ^ low) for i in range(count)])
    lines = lambda *parts: call(
        lines_kernel,
        jax.ShapeDtypeStruct((sum(part.shape[0] for part in parts), cells), BF16),
        *parts,
        scratch=(pltpu.VMEM((own_outs * rows, cols), F32),),
        cost=(1 << 20, 2 << 20),
    )
    behind = lax.ppermute(volume, "depth", farther)
    behind_views = call(
        behind_views_kernel,
        jax.ShapeDtypeStruct((6 * chans, cells), BF16),
        behind,
        cost=(2 * 2 * cells * chans * 8 * cols, 2 << 20),
    )
    got[1], views, behind_views = lax.optimization_barrier((got[1], views, behind_views))
    own_lines = [lines(got[0], got[1])] + [lines(got[mask]) for mask in range(2, count)]
    next_lines = [lax.ppermute(part, "depth", nearer) for part in own_lines]
    outs = channels // depth
    half_terms = jax.ShapeDtypeStruct((channels // 2, 32 * chans), F32)
    keep, send = call(
        lambda *refs: weight_kernel(outs, cols, 4 * cols, *refs),
        (half_terms, half_terms),
        views,
        behind_views,
        *own_lines,
        scratch=(
            pltpu.VMEM((32 * chans, channels), F32),
            pltpu.VMEM((32 * chans, channels), F32),
        ),
        cost=(2 * 27 * chans * channels * cells, 8 << 20),
    )
    chips = depth // 2
    other = lax.ppermute(send, "depth", [(i, i ^ 1) for i in range(depth)])
    def input_plane(plane, taps, lines, before):
        kernel = functools.partial(input_kernel, plane)
        earlier = [] if before is None else [before]
        return pl.pallas_call(
            kernel if before is None else lambda before, *refs: kernel(*refs),
            out_shape=jax.ShapeDtypeStruct(volume.shape, BF16),
            in_specs=[HBM] * len(earlier) + [VMEM] * (1 + len(lines)),
            out_specs=HBM,
            input_output_aliases={} if before is None else {0: 0},
            scratch_shapes=(
                pltpu.VMEM((9 * chans, cells + cols), F32),
                pltpu.VMEM((2, 256, cols), F32),
                pltpu.VMEM((chans, 2 * rows, 2 * cols), BF16),
                pltpu.SemaphoreType.DMA((2 * rows * chans // 256,)),
            ),
            compiler_params=pltpu.CompilerParams(vmem_limit_bytes=LIMIT),
            cost_estimate=pl.CostEstimate(
                flops=2 * 9 * chans * taps.shape[1] * cells, bytes_accessed=4 << 20, transcendentals=0
            ),
        )(*earlier, taps, *lines)

    half_grad = input_plane(0, even_taps, own_lines, None)
    other, half_grad = lax.optimization_barrier((other, half_grad))
    own_terms, *terms = call(
        pair_kernel,
        [jax.ShapeDtypeStruct((outs, 32 * chans), F32)] * chips,
        keep,
        other,
        cost=(1 << 16, 1 << 19),
    )
    terms = [lax.ppermute(term, "depth", [(i, i ^ (2 * k + 2)) for i in range(depth)]) for k, term in enumerate(terms)]
    input_grad = input_plane(1, odd_taps, next_lines + own_lines, half_grad)
    own_terms, input_grad = lax.optimization_barrier((own_terms, input_grad))
    scale = 1.0 / math.sqrt(depth * cells)
    weight_grad = call(
        lambda *refs: total_kernel(scale, *refs),
        jax.ShapeDtypeStruct((chans, outs, 27), F32),
        own_terms,
        *terms,
        cost=(1 << 16, 1 << 19),
    )
    return input_grad, jnp.transpose(weight_grad, (2, 0, 1))


def solution(mesh):
    in_specs = (P("chan", "depth", None, None), P("chan", "depth", None, None), P())
    out_specs = (P("chan", "depth", None, None), P(None, "chan", "depth"))
    ring, depth = mesh.shape["chan"], mesh.shape["depth"]

    def either(grad_out, volume, weight):
        fits = (
            grad_out.shape[0] % 32 == 0
            and volume.shape[0] == 16
            and grad_out.shape[1] == 1
            and ring >= 2
            and ring & (ring - 1) == 0
            and depth & (depth - 1) == 0
            and depth % (2 * ring) == 0
        )
        return (shards if fits else plain_shards)(grad_out, volume, weight)

    return jax.shard_map(either, mesh=mesh, in_specs=in_specs, out_specs=out_specs, check_vma=False)
```

```python
import functools
import math

import jax
import jax.numpy as jnp
from jax import lax
from jax.experimental import pallas as pl
from jax.experimental.pallas import tpu as pltpu
from jax.sharding import PartitionSpec as P

F32 = jnp.float32
BF16 = jnp.bfloat16
VMEM = pl.BlockSpec(memory_space=pltpu.VMEM)
HBM = pl.BlockSpec(memory_space=pltpu.HBM)
LIMIT = 48 * 1024 * 1024


def matmul(left, right):
    return jnp.dot(left, right, preferred_element_type=F32)


def one_hot(rows, cols, source):
    row = lax.broadcasted_iota(jnp.int32, (rows, cols), 0)
    col = lax.broadcasted_iota(jnp.int32, (rows, cols), 1)
    return jnp.where(source(row, col), 1.0, 0.0).astype(BF16)


def swap_rows(major, minor):
    bits = minor.bit_length() - 1
    return one_hot(
        major * minor,
        major * minor,
        lambda row, col: col == (row & (minor - 1)) * major + (row >> bits),
    )


def place_views(plane, views_ref, base):
    chans, rows, cols = plane.shape
    half = cols // 2
    group = 256 // chans
    swap = swap_rows(group, chans)
    split = one_hot(cols, cols, lambda row, col: row == 2 * (col & (half - 1)) + col // half)
    inner = lax.broadcasted_iota(jnp.int32, (group * chans, half), 1) > 0
    for start in range(0, rows, group):
        block = plane[:, start : start + group, :].reshape(chans * group, cols)
        parted = matmul(matmul(swap, block).astype(BF16), split)
        odd = parted[:, half:]
        before = jnp.where(inner, pltpu.roll(odd, 1, 1), 0.0)
        views = [view.astype(BF16) for view in (before, parted[:, :half], odd)]
        for at in range(group):
            row = start + at
            lanes = slice(row // 2 * half, (row // 2 + 1) * half)
            for e in range(3):
                lo = base + (3 * (row % 2) + e) * chans
                views_ref[lo : lo + chans, lanes] = views[e][at * chans : (at + 1) * chans]


def own_views_kernel(depth, volume_ref, weight_ref, views_ref, even_ref, odd_ref):
    chans = volume_ref.shape[0]
    channels = weight_ref.shape[2]
    place_views(volume_ref.at[:, 0], views_ref, 0)
    place_views(volume_ref.at[:, 1], views_ref, 6 * chans)
    count = lax.axis_size("chan")
    part = channels // count
    here = lax.axis_index("chan")
    row = lax.broadcasted_iota(jnp.int32, (channels, channels), 0)
    col = lax.broadcasted_iota(jnp.int32, (channels, channels), 1)
    order = jnp.zeros((channels, channels), F32)
    for slot in range(count):
        moved = ((here ^ slot) - slot) * part
        inside = (col >= slot * part) & (col < (slot + 1) * part)
        order = jnp.where(inside & (row == col + moved), 1.0, order)
    ordered = matmul(weight_ref[...].reshape(27 * chans, channels), order.astype(BF16)).astype(BF16)
    beyond = jnp.where(lax.axis_index("depth") == depth - 1, 0.0, 1.0).astype(BF16)
    for k, e in enumerate((1, 2, 0)):
        for b in range(3):
            pick = lambda a: ordered[(9 * a + 3 * b + e) * chans : (9 * a + 3 * b + e + 1) * chans]
            lo = (3 * k + b) * chans
            even_ref[lo : lo + chans, :] = pick(1)
            odd_ref[lo : lo + chans, :] = jnp.concatenate([pick(0) * beyond, pick(2)], axis=1)


def behind_views_kernel(behind_ref, views_ref):
    first = lax.axis_index("depth") == 0

    @pl.when(jnp.logical_not(first))
    def _():
        place_views(behind_ref.at[:, 1], views_ref, 0)

    @pl.when(first)
    def _():
        views_ref[...] = jnp.zeros(views_ref.shape, BF16)


def place_lines(part, out_ref, at, wide_ref):
    outs, _, rows, cols = part.shape
    wide_ref[: outs * rows, :] = part[...].reshape(outs * rows, cols).astype(F32)
    for row in range(rows):
        line = wide_ref[pl.ds(row, outs, stride=rows), :].astype(BF16)
        out_ref[at : at + outs, row * cols : (row + 1) * cols] = line


def lines_kernel(*refs):
    *parts, out_ref, wide_ref = refs
    at = 0
    for part in parts:
        place_lines(part, out_ref, at, wide_ref)
        at += part.shape[0]


def weight_kernel(
    outs, cols, chunk, own_ref, behind_ref, *refs
):
    *line_refs, keep_ref, send_ref, terms_ref, placed_ref = refs
    channels = terms_ref.shape[1]
    chans = behind_ref.shape[0] // 6
    cells = own_ref.shape[1]
    contract = (((1,), (1,)), ((), ()))

    def grads(lo, hi):
        return jnp.concatenate([ref[:, lo:hi] for ref in line_refs], axis=0)

    sums = None
    for lo in range(0, cells, chunk):
        hi = lo + chunk
        below = grads(lo + cols, min(hi + cols, cells))
        if hi == cells:
            below = jnp.concatenate([below, jnp.zeros((channels, cols), BF16)], axis=1)
        both = jnp.concatenate([grads(lo, hi), below], axis=0)
        views = jnp.concatenate([behind_ref[:, lo:hi], own_ref[:, lo:hi]], axis=0)
        part = lax.dot_general(views, both, contract, preferred_element_type=F32)
        sums = part if sums is None else sums + part
    for a in range(3):
        terms = sums[6 * a * chans : 6 * (a + 1) * chans]
        even, odd = terms[: 3 * chans, :channels], terms[3 * chans :]
        for b, block in enumerate((odd[:, channels:], even, odd[:, :channels])):
            lo = (9 * a + 3 * b) * chans
            terms_ref[lo : lo + 3 * chans, :] = block
    terms_ref[27 * chans :, :] = jnp.zeros((5 * chans, channels), F32)
    for c in range(chans):
        placed_ref[32 * c : 32 * c + 32, :] = terms_ref[pl.ds(c, 32, stride=chans), :]
    turned = placed_ref[...].T
    count = lax.axis_size("chan")
    part = channels // count
    odd_core = lax.axis_index("depth") % 2 == 1
    for slot in range(count):
        start = (lax.axis_index("chan") ^ slot) * (part // 2)
        for at in range(0, part // 2, outs):
            lo = slot * part + 2 * at
            even, odd = turned[lo : lo + outs], turned[lo + outs : lo + 2 * outs]
            place = pl.ds(pl.multiple_of(start + at, outs), outs)
            keep_ref[place, :] = jnp.where(odd_core, odd, even)
            send_ref[place, :] = jnp.where(odd_core, even, odd)


def halve_kernel(bit, block, keep_ref, other_ref, next_keep_ref, next_send_ref):
    side = (lax.axis_index("depth") >> bit) & 1
    for at in range(0, next_keep_ref.shape[0], block):
        for out_ref, which in ((next_keep_ref, side), (next_send_ref, 1 - side)):
            place = pl.ds(pl.multiple_of(2 * at + which * block, block), block)
            out_ref[at : at + block, :] = keep_ref[place, :] + other_ref[place, :]


def input_kernel(plane, *refs):
    taps_ref, *line_refs, out_ref, cells_ref, lines_ref, rows_ref, sems = refs
    chans, rows, cols = rows_ref.shape
    half = cols // 2
    grid_cells = half * rows // 2
    grads = jnp.concatenate([ref[...] for ref in line_refs], axis=0)
    cells_ref[:, :grid_cells] = matmul(taps_ref[...], grads)
    cells_ref[:, grid_cells:] = jnp.zeros((cells_ref.shape[0], half), F32)
    group = 256 // chans
    weave = one_hot(cols, cols, lambda row, col: col == 2 * (row & (half - 1)) + row // half)
    inner = lax.broadcasted_iota(jnp.int32, (chans, half), 1) < half - 1

    def cells(kind, b, r):
        lo = (3 * kind + b) * chans
        return cells_ref[lo : lo + chans, r * half : (r + 1) * half]

    copies = []
    for start in range(0, rows, group):
        pieces = []
        for row in range(start, start + group):
            r = row // 2
            if row % 2 == 0:
                even, odd, next_odd = [cells(kind, 1, r) for kind in range(3)]
            else:
                even, odd, next_odd = [cells(kind, 0, r + 1) + cells(kind, 2, r) for kind in range(3)]
            odd = odd + jnp.where(inner, pltpu.roll(next_odd, half - 1, 1), 0.0)
            pieces.append(jnp.concatenate([even, odd], axis=1).astype(BF16))
        woven = matmul(jnp.concatenate(pieces, axis=0), weave)
        for side in range(2):
            lanes = slice(side * half, (side + 1) * half)
            lines_ref[side] = woven[:, lanes]
            for c in range(chans):
                line = lines_ref[side, pl.ds(c, group, stride=chans), :].astype(BF16)
                rows_ref[c, start : start + group, lanes] = line
        place = pl.ds(start, group)
        copies.append(
            pltpu.make_async_copy(
                rows_ref.at[:, place], out_ref.at[:, plane, place], sems.at[start // group]
            )
        )
        copies[-1].start()
    for copy in copies:
        copy.wait()


def total_kernel(scale, *refs):
    *term_refs, out_ref = refs
    chans, outs, taps = out_ref.shape
    total = term_refs[0][...]
    for ref in term_refs[1:]:
        total = total + ref[...]
    total = total * scale
    for c in range(chans):
        out_ref[c] = total[:, 32 * c : 32 * c + taps]


def from_behind(shard, axis, by):
    count = lax.axis_size(axis)
    pairs = [(i, i + by) for i in range(count) if 0 <= i + by < count]
    return lax.ppermute(shard, axis, pairs)


def upsample(stacked, axis, extended):
    tap_zero, tap_one, tap_two = (stacked[0], stacked[1], stacked[2])
    coord_axis = axis - 1
    length = tap_zero.shape[coord_axis]
    if extended:
        outer = length - 1
        even_cells = lax.slice_in_dim(tap_one, 0, outer, axis=coord_axis)
        odd_cells = lax.slice_in_dim(tap_zero, 1, length, axis=coord_axis) + lax.slice_in_dim(
            tap_two, 0, outer, axis=coord_axis
        )
    else:
        outer = length
        shifted = lax.slice_in_dim(tap_zero, 1, length, axis=coord_axis)
        shifted = jnp.concatenate(
            [shifted, jnp.zeros_like(lax.slice_in_dim(tap_zero, 0, 1, axis=coord_axis))],
            axis=coord_axis,
        )
        even_cells = tap_one
        odd_cells = shifted + tap_two
    paired = jnp.stack([even_cells, odd_cells], axis=coord_axis + 1)
    new_shape = list(even_cells.shape)
    new_shape[coord_axis] = 2 * outer
    return paired.reshape(new_shape)


def phase_grads(weight_rows, grads_ext):
    local_in = weight_rows.shape[0] // 27
    channels_out, planes, rows, cols = grads_ext.shape
    taps_out = jnp.dot(
        weight_rows, grads_ext.reshape(channels_out, -1), preferred_element_type=jnp.float32
    )
    taps_out = taps_out.reshape(3, 3, 3, local_in, planes, rows, cols)
    along_w = upsample(jnp.moveaxis(taps_out, 2, 0), 6, False)
    along_h = upsample(jnp.moveaxis(along_w, 1, 0), 4, False)
    return upsample(along_h, 2, True)


def weight_terms(inputs, grads_ext):
    row_extra = 0
    weight_cube = lax.conv_general_dilated(
        inputs[None],
        grads_ext[:, None],
        (1, 1, 1),
        ((1, 2), (1, row_extra), (1, 0)),
        rhs_dilation=(2, 2, 2),
        dimension_numbers=("CNDHW", "OIDHW", "NCDHW"),
        preferred_element_type=jnp.float32,
    )
    return jnp.transpose(weight_cube, (2, 3, 4, 0, 1)).reshape(
        27, weight_cube.shape[0], weight_cube.shape[1]
    )


def plain_shards(grad_out, volume, weight):
    plane_next = from_behind(grad_out, "depth", -1)
    grads_ext = jnp.concatenate([grad_out, plane_next], axis=1)
    channels_out = weight.shape[2]
    local_in = volume.shape[0]
    every_channel = lax.all_gather(grads_ext, "chan", axis=0, tiled=True)
    own_weight = lax.dynamic_slice_in_dim(weight, lax.axis_index("chan") * local_in, local_in, 1)
    input_part = phase_grads(own_weight.reshape(27 * local_in, channels_out), every_channel)
    weight_part = weight_terms(volume, every_channel)
    input_grad = input_part.astype(jnp.bfloat16)
    summed = lax.psum_scatter(weight_part, "depth", scatter_dimension=2, tiled=True)
    cell_count = grad_out.shape[1] * lax.axis_size("depth") * grad_out.shape[2] * grad_out.shape[3]
    return (input_grad, summed * (1.0 / math.sqrt(cell_count)))


def call(kernel, out_shape, *args, scratch=(), cost=None):
    flops, moved = cost
    return pl.pallas_call(
        kernel,
        out_shape=out_shape,
        in_specs=[VMEM] * len(args),
        out_specs=jax.tree.map(lambda _: VMEM, out_shape),
        scratch_shapes=scratch,
        compiler_params=pltpu.CompilerParams(vmem_limit_bytes=LIMIT),
        cost_estimate=pl.CostEstimate(flops=flops, bytes_accessed=moved, transcendentals=0),
    )(*args)


def shards(grad_out, volume, weight):
    count = lax.axis_size("chan")
    depth = lax.axis_size("depth")
    own_outs, _, rows, cols = grad_out.shape
    chans = volume.shape[0]
    channels = weight.shape[2]
    cells = rows * cols
    farther = [(i, (i + 1) % depth) for i in range(depth)]
    nearer = [(b, a) for a, b in farther]

    own_weight = lax.dynamic_slice_in_dim(weight, lax.axis_index("chan") * chans, chans, 1)
    views, even_taps, odd_taps = call(
        lambda *refs: own_views_kernel(depth, *refs),
        (
            jax.ShapeDtypeStruct((12 * chans, cells), BF16),
            jax.ShapeDtypeStruct((9 * chans, channels), BF16),
            jax.ShapeDtypeStruct((9 * chans, 2 * channels), BF16),
        ),
        volume,
        own_weight,
        cost=(2 * 2 * 2 * cells * chans * 8 * cols, 4 << 20),
    )
    got = {0: grad_out}
    for mask in sorted(range(1, count), key=lambda mask: (mask & (mask - 1) > 0, -mask)):
        low = mask & -mask
        got[mask] = lax.ppermute(got[mask - low], "chan", [(i, i ^ low) for i in range(count)])
    lines = lambda *parts: call(
        lines_kernel,
        jax.ShapeDtypeStruct((sum(part.shape[0] for part in parts), cells), BF16),
        *parts,
        scratch=(pltpu.VMEM((own_outs * rows, cols), F32),),
        cost=(1 << 20, 2 << 20),
    )
    behind = lax.ppermute(volume, "depth", farther)
    behind_views = call(
        behind_views_kernel,
        jax.ShapeDtypeStruct((6 * chans, cells), BF16),
        behind,
        cost=(2 * 2 * cells * chans * 8 * cols, 2 << 20),
    )
    got[1], views, behind_views = lax.optimization_barrier((got[1], views, behind_views))
    own_lines = [lines(got[0], got[1])] + [lines(got[mask]) for mask in range(2, count)]
    next_lines = [lax.ppermute(part, "depth", nearer) for part in own_lines[:-1]]
    outs = channels // depth
    half_terms = jax.ShapeDtypeStruct((channels // 2, 32 * chans), F32)
    keep, send = call(
        lambda *refs: weight_kernel(outs, cols, 4 * cols, *refs),
        (half_terms, half_terms),
        views,
        behind_views,
        *own_lines,
        scratch=(
            pltpu.VMEM((32 * chans, channels), F32),
            pltpu.VMEM((32 * chans, channels), F32),
        ),
        cost=(2 * 27 * chans * channels * cells, 8 << 20),
    )
    last_lines, send = lax.optimization_barrier((own_lines[-1], send))
    next_lines.append(lax.ppermute(last_lines, "depth", nearer))

    def input_plane(plane, taps, lines, before):
        kernel = functools.partial(input_kernel, plane)
        earlier = [] if before is None else [before]
        return pl.pallas_call(
            kernel if before is None else lambda before, *refs: kernel(*refs),
            out_shape=jax.ShapeDtypeStruct(volume.shape, BF16),
            in_specs=[HBM] * len(earlier) + [VMEM] * (1 + len(lines)),
            out_specs=HBM,
            input_output_aliases={} if before is None else {0: 0},
            scratch_shapes=(
                pltpu.VMEM((9 * chans, cells + cols), F32),
                pltpu.VMEM((2, 256, cols), F32),
                pltpu.VMEM((chans, 2 * rows, 2 * cols), BF16),
                pltpu.SemaphoreType.DMA((2 * rows * chans // 256,)),
            ),
            compiler_params=pltpu.CompilerParams(vmem_limit_bytes=LIMIT),
            cost_estimate=pl.CostEstimate(
                flops=2 * 9 * chans * taps.shape[1] * cells, bytes_accessed=4 << 20, transcendentals=0
            ),
        )(*earlier, taps, *lines)

    def exchange(part, bit):
        return lax.ppermute(part, "depth", [(i, i ^ (1 << bit)) for i in range(depth)])

    other = exchange(send, 0)
    half_grad = input_plane(0, even_taps, own_lines, None)
    input_grad = input_plane(1, odd_taps, next_lines + own_lines, half_grad)
    for bit in range(1, depth.bit_length() - 1):
        if bit == 2:
            other, half_grad = lax.optimization_barrier((other, half_grad))
        halved = jax.ShapeDtypeStruct((keep.shape[0] // 2, keep.shape[1]), F32)
        keep, send = call(
            functools.partial(halve_kernel, bit, outs), (halved, halved), keep, other, cost=(1 << 16, 1 << 19)
        )
        other = exchange(send, bit)
    other, input_grad = lax.optimization_barrier((other, input_grad))
    scale = 1.0 / math.sqrt(depth * cells)
    weight_grad = call(
        functools.partial(total_kernel, scale),
        jax.ShapeDtypeStruct((chans, outs, 27), F32),
        keep,
        other,
        cost=(1 << 16, 1 << 19),
    )
    return input_grad, jnp.transpose(weight_grad, (2, 0, 1))


def solution(mesh):
    in_specs = (P("chan", "depth", None, None), P("chan", "depth", None, None), P())
    out_specs = (P("chan", "depth", None, None), P(None, "chan", "depth"))
    ring, depth = mesh.shape["chan"], mesh.shape["depth"]

    def either(grad_out, volume, weight):
        fits = (
            grad_out.shape[0] % 32 == 0
            and volume.shape[0] == 16
            and grad_out.shape[1] == 1
            and ring >= 2
            and ring & (ring - 1) == 0
            and depth & (depth - 1) == 0
            and depth % (2 * ring) == 0
        )
        return (shards if fits else plain_shards)(grad_out, volume, weight)

    return jax.shard_map(either, mesh=mesh, in_specs=in_specs, out_specs=out_specs, check_vma=False)
```

```python
import functools
import math

import jax
import jax.numpy as jnp
from jax import lax
from jax.experimental import pallas as pl
from jax.experimental.pallas import tpu as pltpu
from jax.sharding import PartitionSpec as P

F32 = jnp.float32
BF16 = jnp.bfloat16
VMEM = pl.BlockSpec(memory_space=pltpu.VMEM)
HBM = pl.BlockSpec(memory_space=pltpu.HBM)
LIMIT = 48 * 1024 * 1024


def matmul(left, right):
    return jnp.dot(left, right, preferred_element_type=F32)


def one_hot(rows, cols, source):
    row = lax.broadcasted_iota(jnp.int32, (rows, cols), 0)
    col = lax.broadcasted_iota(jnp.int32, (rows, cols), 1)
    return jnp.where(source(row, col), 1.0, 0.0).astype(BF16)


def swap_rows(major, minor):
    bits = minor.bit_length() - 1
    return one_hot(
        major * minor,
        major * minor,
        lambda row, col: col == (row & (minor - 1)) * major + (row >> bits),
    )


def place_views(plane, views_ref, base):
    chans, rows, cols = plane.shape
    half = cols // 2
    group = 256 // chans
    swap = swap_rows(group, chans)
    split = one_hot(cols, cols, lambda row, col: row == 2 * (col & (half - 1)) + col // half)
    inner = lax.broadcasted_iota(jnp.int32, (group * chans, half), 1) > 0
    for start in range(0, rows, group):
        block = plane[:, start : start + group, :].reshape(chans * group, cols)
        parted = matmul(matmul(swap, block).astype(BF16), split)
        odd = parted[:, half:]
        before = jnp.where(inner, pltpu.roll(odd, 1, 1), 0.0)
        views = [view.astype(BF16) for view in (before, parted[:, :half], odd)]
        for at in range(group):
            row = start + at
            lanes = slice(row // 2 * half, (row // 2 + 1) * half)
            for e in range(3):
                lo = base + (3 * (row % 2) + e) * chans
                views_ref[lo : lo + chans, lanes] = views[e][at * chans : (at + 1) * chans]


def own_views_kernel(depth, volume_ref, weight_ref, views_ref, even_ref, odd_ref):
    chans = volume_ref.shape[0]
    channels = weight_ref.shape[2]
    place_views(volume_ref.at[:, 0], views_ref, 0)
    place_views(volume_ref.at[:, 1], views_ref, 6 * chans)
    count = lax.axis_size("chan")
    part = channels // count
    here = lax.axis_index("chan")
    row = lax.broadcasted_iota(jnp.int32, (channels, channels), 0)
    col = lax.broadcasted_iota(jnp.int32, (channels, channels), 1)
    order = jnp.zeros((channels, channels), F32)
    for slot in range(count):
        moved = ((here ^ slot) - slot) * part
        inside = (col >= slot * part) & (col < (slot + 1) * part)
        order = jnp.where(inside & (row == col + moved), 1.0, order)
    ordered = matmul(weight_ref[...].reshape(27 * chans, channels), order.astype(BF16)).astype(BF16)
    beyond = jnp.where(lax.axis_index("depth") == depth - 1, 0.0, 1.0).astype(BF16)
    for k, e in enumerate((1, 2, 0)):
        for b in range(3):
            pick = lambda a: ordered[(9 * a + 3 * b + e) * chans : (9 * a + 3 * b + e + 1) * chans]
            lo = (3 * k + b) * chans
            even_ref[lo : lo + chans, :] = pick(1)
            odd_ref[lo : lo + chans, :] = jnp.concatenate([pick(0) * beyond, pick(2)], axis=1)


def behind_views_kernel(behind_ref, views_ref):
    first = lax.axis_index("depth") == 0

    @pl.when(jnp.logical_not(first))
    def _():
        place_views(behind_ref.at[:, 1], views_ref, 0)

    @pl.when(first)
    def _():
        views_ref[...] = jnp.zeros(views_ref.shape, BF16)


def place_lines(part, out_ref, at, wide_ref):
    outs, _, rows, cols = part.shape
    wide_ref[: outs * rows, :] = part[...].reshape(outs * rows, cols).astype(F32)
    for row in range(rows):
        line = wide_ref[pl.ds(row, outs, stride=rows), :].astype(BF16)
        out_ref[at : at + outs, row * cols : (row + 1) * cols] = line


def lines_kernel(*refs):
    *parts, out_ref, wide_ref = refs
    at = 0
    for part in parts:
        place_lines(part, out_ref, at, wide_ref)
        at += part.shape[0]


def weight_kernel(
    outs, cols, chunk, own_ref, behind_ref, *refs
):
    *line_refs, keep_ref, send_ref, terms_ref, placed_ref = refs
    channels = terms_ref.shape[1]
    chans = behind_ref.shape[0] // 6
    cells = own_ref.shape[1]
    contract = (((1,), (1,)), ((), ()))

    def grads(lo, hi):
        return jnp.concatenate([ref[:, lo:hi] for ref in line_refs], axis=0)

    sums = None
    for lo in range(0, cells, chunk):
        hi = lo + chunk
        below = grads(lo + cols, min(hi + cols, cells))
        if hi == cells:
            below = jnp.concatenate([below, jnp.zeros((channels, cols), BF16)], axis=1)
        both = jnp.concatenate([grads(lo, hi), below], axis=0)
        views = jnp.concatenate([behind_ref[:, lo:hi], own_ref[:, lo:hi]], axis=0)
        part = lax.dot_general(views, both, contract, preferred_element_type=F32)
        sums = part if sums is None else sums + part
    for a in range(3):
        terms = sums[6 * a * chans : 6 * (a + 1) * chans]
        even, odd = terms[: 3 * chans, :channels], terms[3 * chans :]
        for b, block in enumerate((odd[:, channels:], even, odd[:, :channels])):
            lo = (9 * a + 3 * b) * chans
            terms_ref[lo : lo + 3 * chans, :] = block
    terms_ref[27 * chans :, :] = jnp.zeros((5 * chans, channels), F32)
    for c in range(chans):
        placed_ref[32 * c : 32 * c + 32, :] = terms_ref[pl.ds(c, 32, stride=chans), :]
    turned = placed_ref[...].T
    count = lax.axis_size("chan")
    part = channels // count
    odd_core = lax.axis_index("depth") % 2 == 1
    for slot in range(count):
        start = (lax.axis_index("chan") ^ slot) * (part // 2)
        for at in range(0, part // 2, outs):
            lo = slot * part + 2 * at
            even, odd = turned[lo : lo + outs], turned[lo + outs : lo + 2 * outs]
            place = pl.ds(pl.multiple_of(start + at, outs), outs)
            keep_ref[place, :] = jnp.where(odd_core, odd, even)
            send_ref[place, :] = jnp.where(odd_core, even, odd)


def halve_kernel(bit, block, keep_ref, other_ref, next_keep_ref, next_send_ref):
    side = (lax.axis_index("depth") >> bit) & 1
    for at in range(0, next_keep_ref.shape[0], block):
        for out_ref, which in ((next_keep_ref, side), (next_send_ref, 1 - side)):
            place = pl.ds(pl.multiple_of(2 * at + which * block, block), block)
            out_ref[at : at + block, :] = keep_ref[place, :] + other_ref[place, :]


def input_kernel(plane, *refs):
    taps_ref, *line_refs, out_ref, cells_ref, lines_ref, rows_ref, sems = refs
    chans, rows, cols = rows_ref.shape
    half = cols // 2
    grid_cells = half * rows // 2
    grads = jnp.concatenate([ref[...] for ref in line_refs], axis=0)
    cells_ref[:, :grid_cells] = matmul(taps_ref[...], grads)
    cells_ref[:, grid_cells:] = jnp.zeros((cells_ref.shape[0], half), F32)
    group = 256 // chans
    weave = one_hot(cols, cols, lambda row, col: col == 2 * (row & (half - 1)) + row // half)
    inner = lax.broadcasted_iota(jnp.int32, (chans, half), 1) < half - 1

    def cells(kind, b, r):
        lo = (3 * kind + b) * chans
        return cells_ref[lo : lo + chans, r * half : (r + 1) * half]

    copies = []
    for start in range(0, rows, group):
        pieces = []
        for row in range(start, start + group):
            r = row // 2
            if row % 2 == 0:
                even, odd, next_odd = [cells(kind, 1, r) for kind in range(3)]
            else:
                even, odd, next_odd = [cells(kind, 0, r + 1) + cells(kind, 2, r) for kind in range(3)]
            odd = odd + jnp.where(inner, pltpu.roll(next_odd, half - 1, 1), 0.0)
            pieces.append(jnp.concatenate([even, odd], axis=1).astype(BF16))
        woven = matmul(jnp.concatenate(pieces, axis=0), weave)
        for side in range(2):
            lanes = slice(side * half, (side + 1) * half)
            lines_ref[side] = woven[:, lanes]
            for c in range(chans):
                line = lines_ref[side, pl.ds(c, group, stride=chans), :].astype(BF16)
                rows_ref[c, start : start + group, lanes] = line
        place = pl.ds(start, group)
        copies.append(
            pltpu.make_async_copy(
                rows_ref.at[:, place], out_ref.at[:, plane, place], sems.at[start // group]
            )
        )
        copies[-1].start()
    for copy in copies:
        copy.wait()


def total_kernel(scale, *refs):
    *term_refs, out_ref = refs
    chans, outs, taps = out_ref.shape
    total = term_refs[0][...]
    for ref in term_refs[1:]:
        total = total + ref[...]
    total = total * scale
    for c in range(chans):
        out_ref[c] = total[:, 32 * c : 32 * c + taps]


def from_behind(shard, axis, by):
    count = lax.axis_size(axis)
    pairs = [(i, i + by) for i in range(count) if 0 <= i + by < count]
    return lax.ppermute(shard, axis, pairs)


def upsample(stacked, axis, extended):
    tap_zero, tap_one, tap_two = (stacked[0], stacked[1], stacked[2])
    coord_axis = axis - 1
    length = tap_zero.shape[coord_axis]
    if extended:
        outer = length - 1
        even_cells = lax.slice_in_dim(tap_one, 0, outer, axis=coord_axis)
        odd_cells = lax.slice_in_dim(tap_zero, 1, length, axis=coord_axis) + lax.slice_in_dim(
            tap_two, 0, outer, axis=coord_axis
        )
    else:
        outer = length
        shifted = lax.slice_in_dim(tap_zero, 1, length, axis=coord_axis)
        shifted = jnp.concatenate(
            [shifted, jnp.zeros_like(lax.slice_in_dim(tap_zero, 0, 1, axis=coord_axis))],
            axis=coord_axis,
        )
        even_cells = tap_one
        odd_cells = shifted + tap_two
    paired = jnp.stack([even_cells, odd_cells], axis=coord_axis + 1)
    new_shape = list(even_cells.shape)
    new_shape[coord_axis] = 2 * outer
    return paired.reshape(new_shape)


def phase_grads(weight_rows, grads_ext):
    local_in = weight_rows.shape[0] // 27
    channels_out, planes, rows, cols = grads_ext.shape
    taps_out = jnp.dot(
        weight_rows, grads_ext.reshape(channels_out, -1), preferred_element_type=jnp.float32
    )
    taps_out = taps_out.reshape(3, 3, 3, local_in, planes, rows, cols)
    along_w = upsample(jnp.moveaxis(taps_out, 2, 0), 6, False)
    along_h = upsample(jnp.moveaxis(along_w, 1, 0), 4, False)
    return upsample(along_h, 2, True)


def weight_terms(inputs, grads_ext):
    row_extra = 0
    weight_cube = lax.conv_general_dilated(
        inputs[None],
        grads_ext[:, None],
        (1, 1, 1),
        ((1, 2), (1, row_extra), (1, 0)),
        rhs_dilation=(2, 2, 2),
        dimension_numbers=("CNDHW", "OIDHW", "NCDHW"),
        preferred_element_type=jnp.float32,
    )
    return jnp.transpose(weight_cube, (2, 3, 4, 0, 1)).reshape(
        27, weight_cube.shape[0], weight_cube.shape[1]
    )


def plain_shards(grad_out, volume, weight):
    plane_next = from_behind(grad_out, "depth", -1)
    grads_ext = jnp.concatenate([grad_out, plane_next], axis=1)
    channels_out = weight.shape[2]
    local_in = volume.shape[0]
    every_channel = lax.all_gather(grads_ext, "chan", axis=0, tiled=True)
    own_weight = lax.dynamic_slice_in_dim(weight, lax.axis_index("chan") * local_in, local_in, 1)
    input_part = phase_grads(own_weight.reshape(27 * local_in, channels_out), every_channel)
    weight_part = weight_terms(volume, every_channel)
    input_grad = input_part.astype(jnp.bfloat16)
    summed = lax.psum_scatter(weight_part, "depth", scatter_dimension=2, tiled=True)
    cell_count = grad_out.shape[1] * lax.axis_size("depth") * grad_out.shape[2] * grad_out.shape[3]
    return (input_grad, summed * (1.0 / math.sqrt(cell_count)))


def call(kernel, out_shape, *args, scratch=(), cost=None):
    flops, moved = cost
    return pl.pallas_call(
        kernel,
        out_shape=out_shape,
        in_specs=[VMEM] * len(args),
        out_specs=jax.tree.map(lambda _: VMEM, out_shape),
        scratch_shapes=scratch,
        compiler_params=pltpu.CompilerParams(vmem_limit_bytes=LIMIT),
        cost_estimate=pl.CostEstimate(flops=flops, bytes_accessed=moved, transcendentals=0),
    )(*args)


def shards(grad_out, volume, weight):
    count = lax.axis_size("chan")
    depth = lax.axis_size("depth")
    own_outs, _, rows, cols = grad_out.shape
    chans = volume.shape[0]
    channels = weight.shape[2]
    cells = rows * cols
    farther = [(i, (i + 1) % depth) for i in range(depth)]
    nearer = [(b, a) for a, b in farther]

    own_weight = lax.dynamic_slice_in_dim(weight, lax.axis_index("chan") * chans, chans, 1)
    views, even_taps, odd_taps = call(
        lambda *refs: own_views_kernel(depth, *refs),
        (
            jax.ShapeDtypeStruct((12 * chans, cells), BF16),
            jax.ShapeDtypeStruct((9 * chans, channels), BF16),
            jax.ShapeDtypeStruct((9 * chans, 2 * channels), BF16),
        ),
        volume,
        own_weight,
        cost=(2 * 2 * 2 * cells * chans * 8 * cols, 4 << 20),
    )
    got = {0: grad_out}
    for mask in sorted(range(1, count), key=lambda mask: (mask & (mask - 1) > 0, -mask)):
        low = mask & -mask
        if mask == 3:
            got[2], views = lax.optimization_barrier((got[2], views))
        got[mask] = lax.ppermute(got[mask - low], "chan", [(i, i ^ low) for i in range(count)])
    lines = lambda *parts: call(
        lines_kernel,
        jax.ShapeDtypeStruct((sum(part.shape[0] for part in parts), cells), BF16),
        *parts,
        scratch=(pltpu.VMEM((own_outs * rows, cols), F32),),
        cost=(1 << 20, 2 << 20),
    )
    behind = lax.ppermute(volume, "depth", farther)
    behind_views = call(
        behind_views_kernel,
        jax.ShapeDtypeStruct((6 * chans, cells), BF16),
        behind,
        cost=(2 * 2 * cells * chans * 8 * cols, 2 << 20),
    )
    got[1], views, behind_views = lax.optimization_barrier((got[1], views, behind_views))
    own_lines = [lines(got[0], got[1])] + [lines(got[mask]) for mask in range(2, count)]
    next_lines = [lax.ppermute(part, "depth", nearer) for part in own_lines]
    outs = channels // depth
    half_terms = jax.ShapeDtypeStruct((channels // 2, 32 * chans), F32)
    keep, send = call(
        lambda *refs: weight_kernel(outs, cols, 4 * cols, *refs),
        (half_terms, half_terms),
        views,
        behind_views,
        *own_lines,
        scratch=(
            pltpu.VMEM((32 * chans, channels), F32),
            pltpu.VMEM((32 * chans, channels), F32),
        ),
        cost=(2 * 27 * chans * channels * cells, 8 << 20),
    )
    def input_plane(plane, taps, lines, before):
        kernel = functools.partial(input_kernel, plane)
        earlier = [] if before is None else [before]
        return pl.pallas_call(
            kernel if before is None else lambda before, *refs: kernel(*refs),
            out_shape=jax.ShapeDtypeStruct(volume.shape, BF16),
            in_specs=[HBM] * len(earlier) + [VMEM] * (1 + len(lines)),
            out_specs=HBM,
            input_output_aliases={} if before is None else {0: 0},
            scratch_shapes=(
                pltpu.VMEM((9 * chans, cells + cols), F32),
                pltpu.VMEM((2, 256, cols), F32),
                pltpu.VMEM((chans, 2 * rows, 2 * cols), BF16),
                pltpu.SemaphoreType.DMA((2 * rows * chans // 256,)),
            ),
            compiler_params=pltpu.CompilerParams(vmem_limit_bytes=LIMIT),
            cost_estimate=pl.CostEstimate(
                flops=2 * 9 * chans * taps.shape[1] * cells, bytes_accessed=4 << 20, transcendentals=0
            ),
        )(*earlier, taps, *lines)

    def exchange(part, bit):
        return lax.ppermute(part, "depth", [(i, i ^ (1 << bit)) for i in range(depth)])

    other = exchange(send, 0)
    half_grad = input_plane(0, even_taps, own_lines, None)
    input_grad = input_plane(1, odd_taps, next_lines + own_lines, half_grad)
    for bit in range(1, depth.bit_length() - 1):
        if bit == 2:
            other, half_grad = lax.optimization_barrier((other, half_grad))
        halved = jax.ShapeDtypeStruct((keep.shape[0] // 2, keep.shape[1]), F32)
        keep, send = call(
            functools.partial(halve_kernel, bit, outs), (halved, halved), keep, other, cost=(1 << 16, 1 << 19)
        )
        other = exchange(send, bit)
    other, input_grad = lax.optimization_barrier((other, input_grad))
    scale = 1.0 / math.sqrt(depth * cells)
    weight_grad = call(
        functools.partial(total_kernel, scale),
        jax.ShapeDtypeStruct((chans, outs, 27), F32),
        keep,
        other,
        cost=(1 << 16, 1 << 19),
    )
    return input_grad, jnp.transpose(weight_grad, (2, 0, 1))


def solution(mesh):
    in_specs = (P("chan", "depth", None, None), P("chan", "depth", None, None), P())
    out_specs = (P("chan", "depth", None, None), P(None, "chan", "depth"))
    ring, depth = mesh.shape["chan"], mesh.shape["depth"]

    def either(grad_out, volume, weight):
        fits = (
            grad_out.shape[0] % 32 == 0
            and volume.shape[0] == 16
            and grad_out.shape[1] == 1
            and ring >= 2
            and ring & (ring - 1) == 0
            and depth & (depth - 1) == 0
            and depth % (2 * ring) == 0
        )
        return (shards if fits else plain_shards)(grad_out, volume, weight)

    return jax.shard_map(either, mesh=mesh, in_specs=in_specs, out_specs=out_specs, check_vma=False)
```

```python
import functools
import math

import jax
import jax.numpy as jnp
from jax import lax
from jax.experimental import pallas as pl
from jax.experimental.pallas import tpu as pltpu
from jax.sharding import PartitionSpec as P

F32 = jnp.float32
BF16 = jnp.bfloat16
VMEM = pl.BlockSpec(memory_space=pltpu.VMEM)
HBM = pl.BlockSpec(memory_space=pltpu.HBM)
LIMIT = 48 * 1024 * 1024


def matmul(left, right):
    return jnp.dot(left, right, preferred_element_type=F32)


def one_hot(rows, cols, source):
    row = lax.broadcasted_iota(jnp.int32, (rows, cols), 0)
    col = lax.broadcasted_iota(jnp.int32, (rows, cols), 1)
    return jnp.where(source(row, col), 1.0, 0.0).astype(BF16)


def swap_rows(major, minor):
    bits = minor.bit_length() - 1
    return one_hot(
        major * minor,
        major * minor,
        lambda row, col: col == (row & (minor - 1)) * major + (row >> bits),
    )


def place_views(plane, views_ref, base):
    chans, rows, cols = plane.shape
    half = cols // 2
    group = 256 // chans
    swap = swap_rows(group, chans)
    split = one_hot(cols, cols, lambda row, col: row == 2 * (col & (half - 1)) + col // half)
    inner = lax.broadcasted_iota(jnp.int32, (group * chans, half), 1) > 0
    for start in range(0, rows, group):
        block = plane[:, start : start + group, :].reshape(chans * group, cols)
        parted = matmul(matmul(swap, block).astype(BF16), split)
        odd = parted[:, half:]
        before = jnp.where(inner, pltpu.roll(odd, 1, 1), 0.0)
        views = [view.astype(BF16) for view in (before, parted[:, :half], odd)]
        for at in range(group):
            row = start + at
            lanes = slice(row // 2 * half, (row // 2 + 1) * half)
            for e in range(3):
                lo = base + (3 * (row % 2) + e) * chans
                views_ref[lo : lo + chans, lanes] = views[e][at * chans : (at + 1) * chans]


def own_views_kernel(depth, volume_ref, weight_ref, views_ref, even_ref, odd_ref):
    chans = volume_ref.shape[0]
    channels = weight_ref.shape[2]
    place_views(volume_ref.at[:, 0], views_ref, 0)
    place_views(volume_ref.at[:, 1], views_ref, 6 * chans)
    count = lax.axis_size("chan")
    part = channels // count
    here = lax.axis_index("chan")
    row = lax.broadcasted_iota(jnp.int32, (channels, channels), 0)
    col = lax.broadcasted_iota(jnp.int32, (channels, channels), 1)
    order = jnp.zeros((channels, channels), F32)
    for slot in range(count):
        moved = ((here ^ slot) - slot) * part
        inside = (col >= slot * part) & (col < (slot + 1) * part)
        order = jnp.where(inside & (row == col + moved), 1.0, order)
    ordered = matmul(weight_ref[...].reshape(27 * chans, channels), order.astype(BF16)).astype(BF16)
    beyond = jnp.where(lax.axis_index("depth") == depth - 1, 0.0, 1.0).astype(BF16)
    for k, e in enumerate((1, 2, 0)):
        for b in range(3):
            pick = lambda a: ordered[(9 * a + 3 * b + e) * chans : (9 * a + 3 * b + e + 1) * chans]
            lo = (3 * k + b) * chans
            even_ref[lo : lo + chans, :] = pick(1)
            odd_ref[lo : lo + chans, :] = jnp.concatenate([pick(0) * beyond, pick(2)], axis=1)


def behind_views_kernel(behind_ref, views_ref):
    first = lax.axis_index("depth") == 0

    @pl.when(jnp.logical_not(first))
    def _():
        place_views(behind_ref.at[:, 1], views_ref, 0)

    @pl.when(first)
    def _():
        views_ref[...] = jnp.zeros(views_ref.shape, BF16)


def place_lines(part, out_ref, at, wide_ref):
    outs, _, rows, cols = part.shape
    wide_ref[: outs * rows, :] = part[...].reshape(outs * rows, cols).astype(F32)
    for row in range(rows):
        line = wide_ref[pl.ds(row, outs, stride=rows), :].astype(BF16)
        out_ref[at : at + outs, row * cols : (row + 1) * cols] = line


def lines_kernel(*refs):
    *parts, out_ref, wide_ref = refs
    at = 0
    for part in parts:
        place_lines(part, out_ref, at, wide_ref)
        at += part.shape[0]


def weight_kernel(
    outs, cols, chunk, own_ref, behind_ref, *refs
):
    *line_refs, keep_ref, send_ref, terms_ref, placed_ref = refs
    channels = terms_ref.shape[1]
    chans = behind_ref.shape[0] // 6
    cells = own_ref.shape[1]
    contract = (((1,), (1,)), ((), ()))

    def grads(lo, hi):
        return jnp.concatenate([ref[:, lo:hi] for ref in line_refs], axis=0)

    sums = None
    for lo in range(0, cells, chunk):
        hi = lo + chunk
        below = grads(lo + cols, min(hi + cols, cells))
        if hi == cells:
            below = jnp.concatenate([below, jnp.zeros((channels, cols), BF16)], axis=1)
        both = jnp.concatenate([grads(lo, hi), below], axis=0)
        views = jnp.concatenate([behind_ref[:, lo:hi], own_ref[:, lo:hi]], axis=0)
        part = lax.dot_general(views, both, contract, preferred_element_type=F32)
        sums = part if sums is None else sums + part
    for a in range(3):
        terms = sums[6 * a * chans : 6 * (a + 1) * chans]
        even, odd = terms[: 3 * chans, :channels], terms[3 * chans :]
        for b, block in enumerate((odd[:, channels:], even, odd[:, :channels])):
            lo = (9 * a + 3 * b) * chans
            terms_ref[lo : lo + 3 * chans, :] = block
    terms_ref[27 * chans :, :] = jnp.zeros((5 * chans, channels), F32)
    for c in range(chans):
        placed_ref[32 * c : 32 * c + 32, :] = terms_ref[pl.ds(c, 32, stride=chans), :]
    turned = placed_ref[...].T
    count = lax.axis_size("chan")
    part = channels // count
    odd_core = lax.axis_index("depth") % 2 == 1
    for slot in range(count):
        start = (lax.axis_index("chan") ^ slot) * (part // 2)
        for at in range(0, part // 2, outs):
            lo = slot * part + 2 * at
            even, odd = turned[lo : lo + outs], turned[lo + outs : lo + 2 * outs]
            place = pl.ds(pl.multiple_of(start + at, outs), outs)
            keep_ref[place, :] = jnp.where(odd_core, odd, even)
            send_ref[place, :] = jnp.where(odd_core, even, odd)


def halve_kernel(bit, keep_ref, other_ref, next_keep_ref, next_send_ref):
    side = (lax.axis_index("depth") >> bit) & 1
    rows = next_keep_ref.shape[0]
    for out_ref, which in ((next_keep_ref, side), (next_send_ref, 1 - side)):
        place = pl.ds(pl.multiple_of(which * rows, rows), rows)
        out_ref[...] = keep_ref[place, :] + other_ref[place, :]


def input_kernel(plane, *refs):
    taps_ref, *line_refs, out_ref, cells_ref, lines_ref, rows_ref, sems = refs
    chans, rows, cols = rows_ref.shape
    half = cols // 2
    grid_cells = half * rows // 2
    grads = jnp.concatenate([ref[...] for ref in line_refs], axis=0)
    cells_ref[:, :grid_cells] = matmul(taps_ref[...], grads)
    cells_ref[:, grid_cells:] = jnp.zeros((cells_ref.shape[0], half), F32)
    group = 256 // chans
    weave = one_hot(cols, cols, lambda row, col: col == 2 * (row & (half - 1)) + row // half)
    inner = lax.broadcasted_iota(jnp.int32, (chans, half), 1) < half - 1

    def cells(kind, b, r):
        lo = (3 * kind + b) * chans
        return cells_ref[lo : lo + chans, r * half : (r + 1) * half]

    copies = []
    for start in range(0, rows, group):
        pieces = []
        for row in range(start, start + group):
            r = row // 2
            if row % 2 == 0:
                even, odd, next_odd = [cells(kind, 1, r) for kind in range(3)]
            else:
                even, odd, next_odd = [cells(kind, 0, r + 1) + cells(kind, 2, r) for kind in range(3)]
            odd = odd + jnp.where(inner, pltpu.roll(next_odd, half - 1, 1), 0.0)
            pieces.append(jnp.concatenate([even, odd], axis=1).astype(BF16))
        woven = matmul(jnp.concatenate(pieces, axis=0), weave)
        for side in range(2):
            lanes = slice(side * half, (side + 1) * half)
            lines_ref[side] = woven[:, lanes]
            for c in range(chans):
                line = lines_ref[side, pl.ds(c, group, stride=chans), :].astype(BF16)
                rows_ref[c, start : start + group, lanes] = line
        place = pl.ds(start, group)
        copies.append(
            pltpu.make_async_copy(
                rows_ref.at[:, place], out_ref.at[:, plane, place], sems.at[start // group]
            )
        )
        copies[-1].start()
    for copy in copies:
        copy.wait()


def total_kernel(scale, *refs):
    *term_refs, out_ref = refs
    chans, outs, taps = out_ref.shape
    total = term_refs[0][...]
    for ref in term_refs[1:]:
        total = total + ref[...]
    total = total * scale
    for c in range(chans):
        out_ref[c] = total[:, 32 * c : 32 * c + taps]


def from_behind(shard, axis, by):
    count = lax.axis_size(axis)
    pairs = [(i, i + by) for i in range(count) if 0 <= i + by < count]
    return lax.ppermute(shard, axis, pairs)


def upsample(stacked, axis, extended):
    tap_zero, tap_one, tap_two = (stacked[0], stacked[1], stacked[2])
    coord_axis = axis - 1
    length = tap_zero.shape[coord_axis]
    if extended:
        outer = length - 1
        even_cells = lax.slice_in_dim(tap_one, 0, outer, axis=coord_axis)
        odd_cells = lax.slice_in_dim(tap_zero, 1, length, axis=coord_axis) + lax.slice_in_dim(
            tap_two, 0, outer, axis=coord_axis
        )
    else:
        outer = length
        shifted = lax.slice_in_dim(tap_zero, 1, length, axis=coord_axis)
        shifted = jnp.concatenate(
            [shifted, jnp.zeros_like(lax.slice_in_dim(tap_zero, 0, 1, axis=coord_axis))],
            axis=coord_axis,
        )
        even_cells = tap_one
        odd_cells = shifted + tap_two
    paired = jnp.stack([even_cells, odd_cells], axis=coord_axis + 1)
    new_shape = list(even_cells.shape)
    new_shape[coord_axis] = 2 * outer
    return paired.reshape(new_shape)


def phase_grads(weight_rows, grads_ext):
    local_in = weight_rows.shape[0] // 27
    channels_out, planes, rows, cols = grads_ext.shape
    taps_out = jnp.dot(
        weight_rows, grads_ext.reshape(channels_out, -1), preferred_element_type=jnp.float32
    )
    taps_out = taps_out.reshape(3, 3, 3, local_in, planes, rows, cols)
    along_w = upsample(jnp.moveaxis(taps_out, 2, 0), 6, False)
    along_h = upsample(jnp.moveaxis(along_w, 1, 0), 4, False)
    return upsample(along_h, 2, True)


def weight_terms(inputs, grads_ext):
    row_extra = 0
    weight_cube = lax.conv_general_dilated(
        inputs[None],
        grads_ext[:, None],
        (1, 1, 1),
        ((1, 2), (1, row_extra), (1, 0)),
        rhs_dilation=(2, 2, 2),
        dimension_numbers=("CNDHW", "OIDHW", "NCDHW"),
        preferred_element_type=jnp.float32,
    )
    return jnp.transpose(weight_cube, (2, 3, 4, 0, 1)).reshape(
        27, weight_cube.shape[0], weight_cube.shape[1]
    )


def plain_shards(grad_out, volume, weight):
    plane_next = from_behind(grad_out, "depth", -1)
    grads_ext = jnp.concatenate([grad_out, plane_next], axis=1)
    channels_out = weight.shape[2]
    local_in = volume.shape[0]
    every_channel = lax.all_gather(grads_ext, "chan", axis=0, tiled=True)
    own_weight = lax.dynamic_slice_in_dim(weight, lax.axis_index("chan") * local_in, local_in, 1)
    input_part = phase_grads(own_weight.reshape(27 * local_in, channels_out), every_channel)
    weight_part = weight_terms(volume, every_channel)
    input_grad = input_part.astype(jnp.bfloat16)
    summed = lax.psum_scatter(weight_part, "depth", scatter_dimension=2, tiled=True)
    cell_count = grad_out.shape[1] * lax.axis_size("depth") * grad_out.shape[2] * grad_out.shape[3]
    return (input_grad, summed * (1.0 / math.sqrt(cell_count)))


def call(kernel, out_shape, *args, scratch=(), cost=None):
    flops, moved = cost
    return pl.pallas_call(
        kernel,
        out_shape=out_shape,
        in_specs=[VMEM] * len(args),
        out_specs=jax.tree.map(lambda _: VMEM, out_shape),
        scratch_shapes=scratch,
        compiler_params=pltpu.CompilerParams(vmem_limit_bytes=LIMIT),
        cost_estimate=pl.CostEstimate(flops=flops, bytes_accessed=moved, transcendentals=0),
    )(*args)


def shards(grad_out, volume, weight):
    count = lax.axis_size("chan")
    depth = lax.axis_size("depth")
    own_outs, _, rows, cols = grad_out.shape
    chans = volume.shape[0]
    channels = weight.shape[2]
    cells = rows * cols
    farther = [(i, (i + 1) % depth) for i in range(depth)]
    nearer = [(b, a) for a, b in farther]

    own_weight = lax.dynamic_slice_in_dim(weight, lax.axis_index("chan") * chans, chans, 1)
    views, even_taps, odd_taps = call(
        lambda *refs: own_views_kernel(depth, *refs),
        (
            jax.ShapeDtypeStruct((12 * chans, cells), BF16),
            jax.ShapeDtypeStruct((9 * chans, channels), BF16),
            jax.ShapeDtypeStruct((9 * chans, 2 * channels), BF16),
        ),
        volume,
        own_weight,
        cost=(2 * 2 * 2 * cells * chans * 8 * cols, 4 << 20),
    )
    got = {0: grad_out}
    for mask in sorted(range(1, count), key=lambda mask: (mask & (mask - 1) > 0, -mask)):
        low = mask & -mask
        if mask == 3:
            got[2], views = lax.optimization_barrier((got[2], views))
        got[mask] = lax.ppermute(got[mask - low], "chan", [(i, i ^ low) for i in range(count)])
    lines = lambda *parts: call(
        lines_kernel,
        jax.ShapeDtypeStruct((sum(part.shape[0] for part in parts), cells), BF16),
        *parts,
        scratch=(pltpu.VMEM((own_outs * rows, cols), F32),),
        cost=(1 << 20, 2 << 20),
    )
    behind = lax.ppermute(volume, "depth", farther)
    next_own = lax.ppermute(grad_out, "depth", nearer)
    behind_views = call(
        behind_views_kernel,
        jax.ShapeDtypeStruct((6 * chans, cells), BF16),
        behind,
        cost=(2 * 2 * cells * chans * 8 * cols, 2 << 20),
    )
    first_lines, next_first_lines = lines(grad_out), lines(next_own)
    got[1], views, behind_views, first_lines, next_first_lines = lax.optimization_barrier(
        (got[1], views, behind_views, first_lines, next_first_lines)
    )
    later_lines = [lines(*[got[mask] for mask in range(1, count - 1)]), lines(got[count - 1])]
    own_lines = [first_lines] + later_lines
    next_lines = [next_first_lines] + [lax.ppermute(part, "depth", nearer) for part in later_lines]
    outs = channels // depth
    half_terms = jax.ShapeDtypeStruct((channels // 2, 32 * chans), F32)
    keep, send = call(
        lambda *refs: weight_kernel(outs, cols, 4 * cols, *refs),
        (half_terms, half_terms),
        views,
        behind_views,
        *own_lines,
        scratch=(
            pltpu.VMEM((32 * chans, channels), F32),
            pltpu.VMEM((32 * chans, channels), F32),
        ),
        cost=(2 * 27 * chans * channels * cells, 8 << 20),
    )
    def input_plane(plane, taps, lines, before):
        kernel = functools.partial(input_kernel, plane)
        earlier = [] if before is None else [before]
        return pl.pallas_call(
            kernel if before is None else lambda before, *refs: kernel(*refs),
            out_shape=jax.ShapeDtypeStruct(volume.shape, BF16),
            in_specs=[HBM] * len(earlier) + [VMEM] * (1 + len(lines)),
            out_specs=HBM,
            input_output_aliases={} if before is None else {0: 0},
            scratch_shapes=(
                pltpu.VMEM((9 * chans, cells + cols), F32),
                pltpu.VMEM((2, 256, cols), F32),
                pltpu.VMEM((chans, 2 * rows, 2 * cols), BF16),
                pltpu.SemaphoreType.DMA((2 * rows * chans // 256,)),
            ),
            compiler_params=pltpu.CompilerParams(vmem_limit_bytes=LIMIT),
            cost_estimate=pl.CostEstimate(
                flops=2 * 9 * chans * taps.shape[1] * cells, bytes_accessed=4 << 20, transcendentals=0
            ),
        )(*earlier, taps, *lines)

    def exchange(part, bit):
        return lax.ppermute(part, "depth", [(i, i ^ (1 << bit)) for i in range(depth)])

    other = exchange(send, 0)
    half_grad = input_plane(0, even_taps, own_lines, None)
    input_grad = input_plane(1, odd_taps, next_lines + own_lines, half_grad)
    bits = list(range(1, depth.bit_length() - 1))[::-1]
    for bit in bits:
        if bit == bits[-1]:
            other, half_grad = lax.optimization_barrier((other, half_grad))
        halved = jax.ShapeDtypeStruct((keep.shape[0] // 2, keep.shape[1]), F32)
        keep, send = call(
            functools.partial(halve_kernel, bit), (halved, halved), keep, other, cost=(1 << 16, 1 << 19)
        )
        other = exchange(send, bit)
    other, input_grad = lax.optimization_barrier((other, input_grad))
    scale = 1.0 / math.sqrt(depth * cells)
    weight_grad = call(
        functools.partial(total_kernel, scale),
        jax.ShapeDtypeStruct((chans, outs, 27), F32),
        keep,
        other,
        cost=(1 << 16, 1 << 19),
    )
    return input_grad, jnp.transpose(weight_grad, (2, 0, 1))


def solution(mesh):
    in_specs = (P("chan", "depth", None, None), P("chan", "depth", None, None), P())
    out_specs = (P("chan", "depth", None, None), P(None, "chan", "depth"))
    ring, depth = mesh.shape["chan"], mesh.shape["depth"]

    def either(grad_out, volume, weight):
        fits = (
            grad_out.shape[0] % 32 == 0
            and volume.shape[0] == 16
            and grad_out.shape[1] == 1
            and ring >= 4
            and ring & (ring - 1) == 0
            and depth & (depth - 1) == 0
            and depth % (2 * ring) == 0
        )
        return (shards if fits else plain_shards)(grad_out, volume, weight)

    return jax.shard_map(either, mesh=mesh, in_specs=in_specs, out_specs=out_specs, check_vma=False)
```

```python
import functools
import math

import jax
import jax.numpy as jnp
from jax import lax
from jax.experimental import pallas as pl
from jax.experimental.pallas import tpu as pltpu
from jax.sharding import PartitionSpec as P

F32 = jnp.float32
BF16 = jnp.bfloat16
VMEM = pl.BlockSpec(memory_space=pltpu.VMEM)
HBM = pl.BlockSpec(memory_space=pltpu.HBM)
LIMIT = 48 * 1024 * 1024


def matmul(left, right):
    return jnp.dot(left, right, preferred_element_type=F32)


def one_hot(rows, cols, source):
    row = lax.broadcasted_iota(jnp.int32, (rows, cols), 0)
    col = lax.broadcasted_iota(jnp.int32, (rows, cols), 1)
    return jnp.where(source(row, col), 1.0, 0.0).astype(BF16)


def swap_rows(major, minor):
    bits = minor.bit_length() - 1
    return one_hot(
        major * minor,
        major * minor,
        lambda row, col: col == (row & (minor - 1)) * major + (row >> bits),
    )


def place_views(plane, views_ref, base):
    chans, rows, cols = plane.shape
    half = cols // 2
    group = 256 // chans
    swap = swap_rows(group, chans)
    split = one_hot(cols, cols, lambda row, col: row == 2 * (col & (half - 1)) + col // half)
    inner = lax.broadcasted_iota(jnp.int32, (group * chans, half), 1) > 0
    for start in range(0, rows, group):
        block = plane[:, start : start + group, :].reshape(chans * group, cols)
        parted = matmul(matmul(swap, block).astype(BF16), split)
        odd = parted[:, half:]
        before = jnp.where(inner, pltpu.roll(odd, 1, 1), 0.0)
        views = [view.astype(BF16) for view in (before, parted[:, :half], odd)]
        for at in range(group):
            row = start + at
            lanes = slice(row // 2 * half, (row // 2 + 1) * half)
            for e in range(3):
                lo = base + (3 * (row % 2) + e) * chans
                views_ref[lo : lo + chans, lanes] = views[e][at * chans : (at + 1) * chans]


def own_views_kernel(depth, volume_ref, weight_ref, views_ref, even_ref, odd_ref):
    chans = volume_ref.shape[0]
    channels = weight_ref.shape[2]
    place_views(volume_ref.at[:, 0], views_ref, 0)
    place_views(volume_ref.at[:, 1], views_ref, 6 * chans)
    count = lax.axis_size("chan")
    part = channels // count
    here = lax.axis_index("chan")
    row = lax.broadcasted_iota(jnp.int32, (channels, channels), 0)
    col = lax.broadcasted_iota(jnp.int32, (channels, channels), 1)
    order = jnp.zeros((channels, channels), F32)
    for slot in range(count):
        moved = ((here ^ slot) - slot) * part
        inside = (col >= slot * part) & (col < (slot + 1) * part)
        order = jnp.where(inside & (row == col + moved), 1.0, order)
    ordered = matmul(weight_ref[...].reshape(27 * chans, channels), order.astype(BF16)).astype(BF16)
    beyond = jnp.where(lax.axis_index("depth") == depth - 1, 0.0, 1.0).astype(BF16)
    for k, e in enumerate((1, 2, 0)):
        for b in range(3):
            pick = lambda a: ordered[(9 * a + 3 * b + e) * chans : (9 * a + 3 * b + e + 1) * chans]
            lo = (3 * k + b) * chans
            even_ref[lo : lo + chans, :] = pick(1)
            odd_ref[lo : lo + chans, :] = jnp.concatenate([pick(0) * beyond, pick(2)], axis=1)


def behind_views_kernel(behind_ref, views_ref):
    first = lax.axis_index("depth") == 0

    @pl.when(jnp.logical_not(first))
    def _():
        place_views(behind_ref.at[:, 1], views_ref, 0)

    @pl.when(first)
    def _():
        views_ref[...] = jnp.zeros(views_ref.shape, BF16)


def place_lines(part, out_ref, at, wide_ref):
    outs, _, rows, cols = part.shape
    pitch = rows + 8
    for o in range(outs):
        wide_ref[o * pitch : o * pitch + rows, :] = part[o, 0].astype(F32)
    for row in range(rows):
        line = wide_ref[pl.ds(row, outs, stride=pitch), :].astype(BF16)
        out_ref[at : at + outs, row * cols : (row + 1) * cols] = line


def lines_kernel(*refs):
    *parts, out_ref, wide_ref = refs
    at = 0
    for part in parts:
        place_lines(part, out_ref, at, wide_ref)
        at += part.shape[0]


def weight_kernel(
    outs, cols, chunk, own_ref, behind_ref, *refs
):
    *line_refs, keep_ref, send_ref, terms_ref, placed_ref = refs
    channels = terms_ref.shape[1]
    chans = behind_ref.shape[0] // 6
    cells = own_ref.shape[1]
    contract = (((1,), (1,)), ((), ()))

    def grads(lo, hi):
        return jnp.concatenate([ref[:, lo:hi] for ref in line_refs], axis=0)

    pitch = chans + 8
    sums = None
    for lo in range(0, cells, chunk):
        hi = lo + chunk
        below = grads(lo + cols, min(hi + cols, cells))
        if hi == cells:
            below = jnp.concatenate([below, jnp.zeros((channels, cols), BF16)], axis=1)
        both = jnp.concatenate([grads(lo, hi), below], axis=0)
        views = jnp.concatenate([behind_ref[:, lo:hi], own_ref[:, lo:hi]], axis=0)
        part = lax.dot_general(views, both, contract, preferred_element_type=F32)
        sums = part if sums is None else sums + part
    for a in range(3):
        terms = sums[6 * a * chans : 6 * (a + 1) * chans]
        even, odd = terms[: 3 * chans, :channels], terms[3 * chans :]
        for b, block in enumerate((odd[:, channels:], even, odd[:, :channels])):
            for e in range(3):
                lo = (9 * a + 3 * b + e) * pitch
                terms_ref[lo : lo + chans, :] = block[e * chans : (e + 1) * chans]
    terms_ref[27 * pitch :, :] = jnp.zeros((5 * pitch, channels), F32)
    for c in range(chans):
        placed_ref[32 * c : 32 * c + 32, :] = terms_ref[pl.ds(c, 32, stride=pitch), :]
    turned = placed_ref[...].T
    count = lax.axis_size("chan")
    part = channels // count
    odd_core = lax.axis_index("depth") % 2 == 1
    for slot in range(count):
        start = (lax.axis_index("chan") ^ slot) * (part // 2)
        for at in range(0, part // 2, outs):
            lo = slot * part + 2 * at
            even, odd = turned[lo : lo + outs], turned[lo + outs : lo + 2 * outs]
            place = pl.ds(pl.multiple_of(start + at, outs), outs)
            keep_ref[place, :] = jnp.where(odd_core, odd, even)
            send_ref[place, :] = jnp.where(odd_core, even, odd)


def pair_kernel(keep_ref, other_ref, *out_refs):
    chip = lax.axis_index("depth") // 2
    outs = out_refs[0].shape[0]
    for k, out_ref in enumerate(out_refs):
        place = pl.ds(pl.multiple_of((chip ^ k) * outs, outs), outs)
        out_ref[...] = keep_ref[place, :] + other_ref[place, :]


def input_kernel(plane, *refs):
    taps_ref, *line_refs, out_ref, cells_ref, lines_ref, rows_ref, sems = refs
    chans, rows, cols = rows_ref.shape
    half = cols // 2
    grid_cells = half * rows // 2
    grads = jnp.concatenate([ref[...] for ref in line_refs], axis=0)
    cells_ref[:, :grid_cells] = matmul(taps_ref[...], grads)
    cells_ref[:, grid_cells:] = jnp.zeros((cells_ref.shape[0], half), F32)
    group = 256 // chans
    pitch = chans + 8
    weave = one_hot(cols, cols, lambda row, col: col == 2 * (row & (half - 1)) + row // half)
    inner = lax.broadcasted_iota(jnp.int32, (chans, half), 1) < half - 1

    def cells(kind, b, r):
        lo = (3 * kind + b) * chans
        return cells_ref[lo : lo + chans, r * half : (r + 1) * half]

    copies = []
    for start in range(0, rows, group):
        pieces = []
        for row in range(start, start + group):
            r = row // 2
            if row % 2 == 0:
                even, odd, next_odd = [cells(kind, 1, r) for kind in range(3)]
            else:
                even, odd, next_odd = [cells(kind, 0, r + 1) + cells(kind, 2, r) for kind in range(3)]
            odd = odd + jnp.where(inner, pltpu.roll(next_odd, half - 1, 1), 0.0)
            pieces.append(jnp.concatenate([even, odd], axis=1).astype(BF16))
        woven = matmul(jnp.concatenate(pieces, axis=0), weave)
        for side in range(2):
            lanes = slice(side * half, (side + 1) * half)
            for at in range(group):
                lines_ref[side, at * pitch : at * pitch + chans] = woven[at * chans : (at + 1) * chans, lanes]
            for c in range(chans):
                line = lines_ref[side, pl.ds(c, group, stride=pitch), :].astype(BF16)
                rows_ref[c, start : start + group, lanes] = line
        place = pl.ds(start, group)
        copies.append(
            pltpu.make_async_copy(
                rows_ref.at[:, place], out_ref.at[:, plane, place], sems.at[start // group]
            )
        )
        copies[-1].start()
    for copy in copies:
        copy.wait()


def total_kernel(scale, *refs):
    *term_refs, out_ref = refs
    chans, outs, taps = out_ref.shape
    total = term_refs[0][...]
    for ref in term_refs[1:]:
        total = total + ref[...]
    total = total * scale
    for c in range(chans):
        out_ref[c] = total[:, 32 * c : 32 * c + taps]


def from_behind(shard, axis, by):
    count = lax.axis_size(axis)
    pairs = [(i, i + by) for i in range(count) if 0 <= i + by < count]
    return lax.ppermute(shard, axis, pairs)


def upsample(stacked, axis, extended):
    tap_zero, tap_one, tap_two = (stacked[0], stacked[1], stacked[2])
    coord_axis = axis - 1
    length = tap_zero.shape[coord_axis]
    if extended:
        outer = length - 1
        even_cells = lax.slice_in_dim(tap_one, 0, outer, axis=coord_axis)
        odd_cells = lax.slice_in_dim(tap_zero, 1, length, axis=coord_axis) + lax.slice_in_dim(
            tap_two, 0, outer, axis=coord_axis
        )
    else:
        outer = length
        shifted = lax.slice_in_dim(tap_zero, 1, length, axis=coord_axis)
        shifted = jnp.concatenate(
            [shifted, jnp.zeros_like(lax.slice_in_dim(tap_zero, 0, 1, axis=coord_axis))],
            axis=coord_axis,
        )
        even_cells = tap_one
        odd_cells = shifted + tap_two
    paired = jnp.stack([even_cells, odd_cells], axis=coord_axis + 1)
    new_shape = list(even_cells.shape)
    new_shape[coord_axis] = 2 * outer
    return paired.reshape(new_shape)


def phase_grads(weight_rows, grads_ext):
    local_in = weight_rows.shape[0] // 27
    channels_out, planes, rows, cols = grads_ext.shape
    taps_out = jnp.dot(
        weight_rows, grads_ext.reshape(channels_out, -1), preferred_element_type=jnp.float32
    )
    taps_out = taps_out.reshape(3, 3, 3, local_in, planes, rows, cols)
    along_w = upsample(jnp.moveaxis(taps_out, 2, 0), 6, False)
    along_h = upsample(jnp.moveaxis(along_w, 1, 0), 4, False)
    return upsample(along_h, 2, True)


def weight_terms(inputs, grads_ext):
    row_extra = 0
    weight_cube = lax.conv_general_dilated(
        inputs[None],
        grads_ext[:, None],
        (1, 1, 1),
        ((1, 2), (1, row_extra), (1, 0)),
        rhs_dilation=(2, 2, 2),
        dimension_numbers=("CNDHW", "OIDHW", "NCDHW"),
        preferred_element_type=jnp.float32,
    )
    return jnp.transpose(weight_cube, (2, 3, 4, 0, 1)).reshape(
        27, weight_cube.shape[0], weight_cube.shape[1]
    )


def plain_shards(grad_out, volume, weight):
    plane_next = from_behind(grad_out, "depth", -1)
    grads_ext = jnp.concatenate([grad_out, plane_next], axis=1)
    channels_out = weight.shape[2]
    local_in = volume.shape[0]
    every_channel = lax.all_gather(grads_ext, "chan", axis=0, tiled=True)
    own_weight = lax.dynamic_slice_in_dim(weight, lax.axis_index("chan") * local_in, local_in, 1)
    input_part = phase_grads(own_weight.reshape(27 * local_in, channels_out), every_channel)
    weight_part = weight_terms(volume, every_channel)
    input_grad = input_part.astype(jnp.bfloat16)
    summed = lax.psum_scatter(weight_part, "depth", scatter_dimension=2, tiled=True)
    cell_count = grad_out.shape[1] * lax.axis_size("depth") * grad_out.shape[2] * grad_out.shape[3]
    return (input_grad, summed * (1.0 / math.sqrt(cell_count)))


def call(kernel, out_shape, *args, scratch=(), cost=None):
    flops, moved = cost
    return pl.pallas_call(
        kernel,
        out_shape=out_shape,
        in_specs=[VMEM] * len(args),
        out_specs=jax.tree.map(lambda _: VMEM, out_shape),
        scratch_shapes=scratch,
        compiler_params=pltpu.CompilerParams(vmem_limit_bytes=LIMIT),
        cost_estimate=pl.CostEstimate(flops=flops, bytes_accessed=moved, transcendentals=0),
    )(*args)


def shards(grad_out, volume, weight):
    count = lax.axis_size("chan")
    depth = lax.axis_size("depth")
    own_outs, _, rows, cols = grad_out.shape
    chans = volume.shape[0]
    channels = weight.shape[2]
    cells = rows * cols
    farther = [(i, (i + 1) % depth) for i in range(depth)]
    nearer = [(b, a) for a, b in farther]

    own_weight = lax.dynamic_slice_in_dim(weight, lax.axis_index("chan") * chans, chans, 1)
    views, even_taps, odd_taps = call(
        lambda *refs: own_views_kernel(depth, *refs),
        (
            jax.ShapeDtypeStruct((12 * chans, cells), BF16),
            jax.ShapeDtypeStruct((9 * chans, channels), BF16),
            jax.ShapeDtypeStruct((9 * chans, 2 * channels), BF16),
        ),
        volume,
        own_weight,
        cost=(2 * 2 * 2 * cells * chans * 8 * cols, 4 << 20),
    )
    got = {0: grad_out}
    for mask in sorted(range(1, count), key=lambda mask: (mask & (mask - 1) > 0, -mask)):
        low = mask & -mask
        if mask == 3:
            got[2], views = lax.optimization_barrier((got[2], views))
        got[mask] = lax.ppermute(got[mask - low], "chan", [(i, i ^ low) for i in range(count)])
    lines = lambda *parts: call(
        lines_kernel,
        jax.ShapeDtypeStruct((sum(part.shape[0] for part in parts), cells), BF16),
        *parts,
        scratch=(pltpu.VMEM((own_outs * (rows + 8), cols), F32),),
        cost=(1 << 20, 2 << 20),
    )
    behind = lax.ppermute(volume, "depth", farther)
    next_own = lax.ppermute(grad_out, "depth", nearer)
    behind_views = call(
        behind_views_kernel,
        jax.ShapeDtypeStruct((6 * chans, cells), BF16),
        behind,
        cost=(2 * 2 * cells * chans * 8 * cols, 2 << 20),
    )
    first_lines, next_first_lines = lines(grad_out), lines(next_own)
    got[1], views, behind_views, first_lines, next_first_lines = lax.optimization_barrier(
        (got[1], views, behind_views, first_lines, next_first_lines)
    )
    later_lines = [lines(*[got[mask] for mask in range(1, count - 1)]), lines(got[count - 1])]
    own_lines = [first_lines] + later_lines
    next_lines = [next_first_lines] + [lax.ppermute(part, "depth", nearer) for part in later_lines]
    outs = channels // depth
    half_terms = jax.ShapeDtypeStruct((channels // 2, 32 * chans), F32)
    keep, send = call(
        lambda *refs: weight_kernel(outs, cols, 4 * cols, *refs),
        (half_terms, half_terms),
        views,
        behind_views,
        *own_lines,
        scratch=(
            pltpu.VMEM((32 * (chans + 8), channels), F32),
            pltpu.VMEM((32 * chans, channels), F32),
        ),
        cost=(2 * 27 * chans * channels * cells, 8 << 20),
    )
    def input_plane(plane, taps, lines, before):
        kernel = functools.partial(input_kernel, plane)
        earlier = [] if before is None else [before]
        return pl.pallas_call(
            kernel if before is None else lambda before, *refs: kernel(*refs),
            out_shape=jax.ShapeDtypeStruct(volume.shape, BF16),
            in_specs=[HBM] * len(earlier) + [VMEM] * (1 + len(lines)),
            out_specs=HBM,
            input_output_aliases={} if before is None else {0: 0},
            scratch_shapes=(
                pltpu.VMEM((9 * chans, cells + cols), F32),
                pltpu.VMEM((2, 256 // chans * (chans + 8), cols), F32),
                pltpu.VMEM((chans, 2 * rows, 2 * cols), BF16),
                pltpu.SemaphoreType.DMA((2 * rows * chans // 256,)),
            ),
            compiler_params=pltpu.CompilerParams(vmem_limit_bytes=LIMIT),
            cost_estimate=pl.CostEstimate(
                flops=2 * 9 * chans * taps.shape[1] * cells, bytes_accessed=4 << 20, transcendentals=0
            ),
        )(*earlier, taps, *lines)

    other = lax.ppermute(send, "depth", [(i, i ^ 1) for i in range(depth)])
    half_grad = input_plane(0, even_taps, own_lines, None)
    other, half_grad = lax.optimization_barrier((other, half_grad))
    own_terms, *terms = call(
        pair_kernel,
        [jax.ShapeDtypeStruct((outs, 32 * chans), F32)] * (depth // 2),
        keep,
        other,
        cost=(1 << 16, 1 << 19),
    )
    terms = [lax.ppermute(term, "depth", [(i, i ^ (2 * k + 2)) for i in range(depth)]) for k, term in enumerate(terms)]
    input_grad = input_plane(1, odd_taps, next_lines + own_lines, half_grad)
    own_terms, input_grad = lax.optimization_barrier((own_terms, input_grad))
    scale = 1.0 / math.sqrt(depth * cells)
    weight_grad = call(
        functools.partial(total_kernel, scale),
        jax.ShapeDtypeStruct((chans, outs, 27), F32),
        own_terms,
        *terms,
        cost=(1 << 16, 1 << 19),
    )
    return input_grad, jnp.transpose(weight_grad, (2, 0, 1))


def solution(mesh):
    in_specs = (P("chan", "depth", None, None), P("chan", "depth", None, None), P())
    out_specs = (P("chan", "depth", None, None), P(None, "chan", "depth"))
    ring, depth = mesh.shape["chan"], mesh.shape["depth"]

    def either(grad_out, volume, weight):
        fits = (
            grad_out.shape[0] % 32 == 0
            and volume.shape[0] == 16
            and grad_out.shape[1] == 1
            and ring >= 4
            and ring & (ring - 1) == 0
            and depth & (depth - 1) == 0
            and depth % (2 * ring) == 0
        )
        return (shards if fits else plain_shards)(grad_out, volume, weight)

    return jax.shard_map(either, mesh=mesh, in_specs=in_specs, out_specs=out_specs, check_vma=False)
```

```python
import functools
import math

import jax
import jax.numpy as jnp
from jax import lax
from jax.experimental import pallas as pl
from jax.experimental.pallas import tpu as pltpu
from jax.sharding import PartitionSpec as P

F32 = jnp.float32
BF16 = jnp.bfloat16
VMEM = pl.BlockSpec(memory_space=pltpu.VMEM)
HBM = pl.BlockSpec(memory_space=pltpu.HBM)
LIMIT = 48 * 1024 * 1024


def ring_order(count):
    return [0] + list(range(1, count, 2)) + list(range(2, count, 2))[::-1]


def holder(order, step):
    here = lax.axis_index("chan")
    count = len(order)
    owner = jnp.int32(order[-step % count])
    for seat in range(1, count):
        owner = jnp.where(here == order[seat], order[(seat - step) % count], owner)
    return owner


def matmul(left, right):
    return jnp.dot(left, right, preferred_element_type=F32)


def one_hot(rows, cols, source):
    row = lax.broadcasted_iota(jnp.int32, (rows, cols), 0)
    col = lax.broadcasted_iota(jnp.int32, (rows, cols), 1)
    return jnp.where(source(row, col), 1.0, 0.0).astype(BF16)


def swap_rows(major, minor):
    bits = minor.bit_length() - 1
    return one_hot(
        major * minor,
        major * minor,
        lambda row, col: col == (row & (minor - 1)) * major + (row >> bits),
    )


def place_views(plane, views_ref, base):
    chans, rows, cols = plane.shape
    half = cols // 2
    group = 256 // chans
    swap = swap_rows(group, chans)
    split = one_hot(cols, cols, lambda row, col: row == 2 * (col & (half - 1)) + col // half)
    inner = lax.broadcasted_iota(jnp.int32, (group * chans, half), 1) > 0
    for start in range(0, rows, group):
        block = plane[:, start : start + group, :].reshape(chans * group, cols)
        parted = matmul(matmul(swap, block).astype(BF16), split)
        odd = parted[:, half:]
        before = jnp.where(inner, pltpu.roll(odd, 1, 1), 0.0)
        views = [view.astype(BF16) for view in (before, parted[:, :half], odd)]
        for at in range(group):
            row = start + at
            lanes = slice(row // 2 * half, (row // 2 + 1) * half)
            for e in range(3):
                lo = base + (3 * (row % 2) + e) * chans
                views_ref[lo : lo + chans, lanes] = views[e][at * chans : (at + 1) * chans]


def own_views_kernel(ring, depth, volume_ref, weight_ref, views_ref, even_ref, odd_ref):
    chans = volume_ref.shape[0]
    channels = weight_ref.shape[2]
    place_views(volume_ref.at[:, 0], views_ref, 0)
    place_views(volume_ref.at[:, 1], views_ref, 6 * chans)
    count = len(ring)
    part = channels // count
    row = lax.broadcasted_iota(jnp.int32, (channels, channels), 0)
    col = lax.broadcasted_iota(jnp.int32, (channels, channels), 1)
    order = jnp.zeros((channels, channels), F32)
    for slot in range(count):
        moved = (holder(ring, slot) - slot) * part
        inside = (col >= slot * part) & (col < (slot + 1) * part)
        order = jnp.where(inside & (row == col + moved), 1.0, order)
    ordered = matmul(weight_ref[...].reshape(27 * chans, channels), order.astype(BF16)).astype(BF16)
    beyond = jnp.where(lax.axis_index("depth") == depth - 1, 0.0, 1.0).astype(BF16)
    for k, e in enumerate((1, 2, 0)):
        for b in range(3):
            pick = lambda a: ordered[(9 * a + 3 * b + e) * chans : (9 * a + 3 * b + e + 1) * chans]
            lo = (3 * k + b) * chans
            even_ref[lo : lo + chans, :] = pick(1)
            odd_ref[lo : lo + chans, :] = jnp.concatenate([pick(0) * beyond, pick(2)], axis=1)


def behind_views_kernel(behind_ref, views_ref):
    first = lax.axis_index("depth") == 0

    @pl.when(jnp.logical_not(first))
    def _():
        place_views(behind_ref.at[:, 1], views_ref, 0)

    @pl.when(first)
    def _():
        views_ref[...] = jnp.zeros(views_ref.shape, BF16)


def place_lines(part, out_ref, at, wide_ref):
    outs, _, rows, cols = part.shape
    pitch = rows + 8
    for o in range(outs):
        wide_ref[o * pitch : o * pitch + rows, :] = part[o, 0].astype(F32)
    for row in range(rows):
        line = wide_ref[pl.ds(row, outs, stride=pitch), :].astype(BF16)
        out_ref[at : at + outs, row * cols : (row + 1) * cols] = line


def lines_kernel(*refs):
    *parts, out_ref, wide_ref = refs
    at = 0
    for part in parts:
        place_lines(part, out_ref, at, wide_ref)
        at += part.shape[0]


def weight_kernel(
    ring, outs, cols, chunk, own_ref, behind_ref, *refs
):
    *line_refs, keep_ref, send_ref, terms_ref, placed_ref = refs
    channels = terms_ref.shape[1]
    chans = behind_ref.shape[0] // 6
    cells = own_ref.shape[1]
    contract = (((1,), (1,)), ((), ()))

    def grads(lo, hi):
        return jnp.concatenate([ref[:, lo:hi] for ref in line_refs], axis=0)

    pitch = chans + 8
    sums = None
    for lo in range(0, cells, chunk):
        hi = lo + chunk
        below = grads(lo + cols, min(hi + cols, cells))
        if hi == cells:
            below = jnp.concatenate([below, jnp.zeros((channels, cols), BF16)], axis=1)
        both = jnp.concatenate([grads(lo, hi), below], axis=0)
        views = jnp.concatenate([behind_ref[:, lo:hi], own_ref[:, lo:hi]], axis=0)
        part = lax.dot_general(views, both, contract, preferred_element_type=F32)
        sums = part if sums is None else sums + part
    for a in range(3):
        terms = sums[6 * a * chans : 6 * (a + 1) * chans]
        even, odd = terms[: 3 * chans, :channels], terms[3 * chans :]
        for b, block in enumerate((odd[:, channels:], even, odd[:, :channels])):
            for e in range(3):
                lo = (9 * a + 3 * b + e) * pitch
                terms_ref[lo : lo + chans, :] = block[e * chans : (e + 1) * chans]
    terms_ref[27 * pitch :, :] = jnp.zeros((5 * pitch, channels), F32)
    for c in range(chans):
        placed_ref[32 * c : 32 * c + 32, :] = terms_ref[pl.ds(c, 32, stride=pitch), :]
    turned = placed_ref[...].T
    count = len(ring)
    part = channels // count
    odd_core = lax.axis_index("depth") % 2 == 1
    for slot in range(count):
        start = holder(ring, slot) * (part // 2)
        for at in range(0, part // 2, outs):
            lo = slot * part + 2 * at
            even, odd = turned[lo : lo + outs], turned[lo + outs : lo + 2 * outs]
            place = pl.ds(pl.multiple_of(start + at, outs), outs)
            keep_ref[place, :] = jnp.where(odd_core, odd, even)
            send_ref[place, :] = jnp.where(odd_core, even, odd)


def pair_kernel(keep_ref, other_ref, *out_refs):
    chip = lax.axis_index("depth") // 2
    outs = out_refs[0].shape[0]
    for k, out_ref in enumerate(out_refs):
        place = pl.ds(pl.multiple_of((chip ^ k) * outs, outs), outs)
        out_ref[...] = keep_ref[place, :] + other_ref[place, :]


def input_kernel(plane, *refs):
    taps_ref, *line_refs, out_ref, cells_ref, lines_ref, rows_ref, sems = refs
    chans, rows, cols = rows_ref.shape
    half = cols // 2
    grid_cells = half * rows // 2
    grads = jnp.concatenate([ref[...] for ref in line_refs], axis=0)
    cells_ref[:, :grid_cells] = matmul(taps_ref[...], grads)
    cells_ref[:, grid_cells:] = jnp.zeros((cells_ref.shape[0], half), F32)
    group = 256 // chans
    pitch = chans + 8
    weave = one_hot(cols, cols, lambda row, col: col == 2 * (row & (half - 1)) + row // half)
    inner = lax.broadcasted_iota(jnp.int32, (chans, half), 1) < half - 1

    def cells(kind, b, r):
        lo = (3 * kind + b) * chans
        return cells_ref[lo : lo + chans, r * half : (r + 1) * half]

    copies = []
    for start in range(0, rows, group):
        pieces = []
        for row in range(start, start + group):
            r = row // 2
            if row % 2 == 0:
                even, odd, next_odd = [cells(kind, 1, r) for kind in range(3)]
            else:
                even, odd, next_odd = [cells(kind, 0, r + 1) + cells(kind, 2, r) for kind in range(3)]
            odd = odd + jnp.where(inner, pltpu.roll(next_odd, half - 1, 1), 0.0)
            pieces.append(jnp.concatenate([even, odd], axis=1).astype(BF16))
        woven = matmul(jnp.concatenate(pieces, axis=0), weave)
        for side in range(2):
            lanes = slice(side * half, (side + 1) * half)
            for at in range(group):
                lines_ref[side, at * pitch : at * pitch + chans] = woven[at * chans : (at + 1) * chans, lanes]
            for c in range(chans):
                line = lines_ref[side, pl.ds(c, group, stride=pitch), :].astype(BF16)
                rows_ref[c, start : start + group, lanes] = line
        place = pl.ds(start, group)
        copies.append(
            pltpu.make_async_copy(
                rows_ref.at[:, place], out_ref.at[:, plane, place], sems.at[start // group]
            )
        )
        copies[-1].start()
    for copy in copies:
        copy.wait()


def total_kernel(scale, *refs):
    *term_refs, out_ref = refs
    chans, outs, taps = out_ref.shape
    total = term_refs[0][...]
    for ref in term_refs[1:]:
        total = total + ref[...]
    total = total * scale
    for c in range(chans):
        out_ref[c] = total[:, 32 * c : 32 * c + taps]


def from_behind(shard, axis, by):
    count = lax.axis_size(axis)
    pairs = [(i, i + by) for i in range(count) if 0 <= i + by < count]
    return lax.ppermute(shard, axis, pairs)


def upsample(stacked, axis, extended):
    tap_zero, tap_one, tap_two = (stacked[0], stacked[1], stacked[2])
    coord_axis = axis - 1
    length = tap_zero.shape[coord_axis]
    if extended:
        outer = length - 1
        even_cells = lax.slice_in_dim(tap_one, 0, outer, axis=coord_axis)
        odd_cells = lax.slice_in_dim(tap_zero, 1, length, axis=coord_axis) + lax.slice_in_dim(
            tap_two, 0, outer, axis=coord_axis
        )
    else:
        outer = length
        shifted = lax.slice_in_dim(tap_zero, 1, length, axis=coord_axis)
        shifted = jnp.concatenate(
            [shifted, jnp.zeros_like(lax.slice_in_dim(tap_zero, 0, 1, axis=coord_axis))],
            axis=coord_axis,
        )
        even_cells = tap_one
        odd_cells = shifted + tap_two
    paired = jnp.stack([even_cells, odd_cells], axis=coord_axis + 1)
    new_shape = list(even_cells.shape)
    new_shape[coord_axis] = 2 * outer
    return paired.reshape(new_shape)


def phase_grads(weight_rows, grads_ext):
    local_in = weight_rows.shape[0] // 27
    channels_out, planes, rows, cols = grads_ext.shape
    taps_out = jnp.dot(
        weight_rows, grads_ext.reshape(channels_out, -1), preferred_element_type=jnp.float32
    )
    taps_out = taps_out.reshape(3, 3, 3, local_in, planes, rows, cols)
    along_w = upsample(jnp.moveaxis(taps_out, 2, 0), 6, False)
    along_h = upsample(jnp.moveaxis(along_w, 1, 0), 4, False)
    return upsample(along_h, 2, True)


def weight_terms(inputs, grads_ext):
    row_extra = 0
    weight_cube = lax.conv_general_dilated(
        inputs[None],
        grads_ext[:, None],
        (1, 1, 1),
        ((1, 2), (1, row_extra), (1, 0)),
        rhs_dilation=(2, 2, 2),
        dimension_numbers=("CNDHW", "OIDHW", "NCDHW"),
        preferred_element_type=jnp.float32,
    )
    return jnp.transpose(weight_cube, (2, 3, 4, 0, 1)).reshape(
        27, weight_cube.shape[0], weight_cube.shape[1]
    )


def plain_shards(grad_out, volume, weight):
    plane_next = from_behind(grad_out, "depth", -1)
    grads_ext = jnp.concatenate([grad_out, plane_next], axis=1)
    channels_out = weight.shape[2]
    local_in = volume.shape[0]
    every_channel = lax.all_gather(grads_ext, "chan", axis=0, tiled=True)
    own_weight = lax.dynamic_slice_in_dim(weight, lax.axis_index("chan") * local_in, local_in, 1)
    input_part = phase_grads(own_weight.reshape(27 * local_in, channels_out), every_channel)
    weight_part = weight_terms(volume, every_channel)
    input_grad = input_part.astype(jnp.bfloat16)
    summed = lax.psum_scatter(weight_part, "depth", scatter_dimension=2, tiled=True)
    cell_count = grad_out.shape[1] * lax.axis_size("depth") * grad_out.shape[2] * grad_out.shape[3]
    return (input_grad, summed * (1.0 / math.sqrt(cell_count)))


def call(kernel, out_shape, *args, scratch=(), cost=None):
    flops, moved = cost
    return pl.pallas_call(
        kernel,
        out_shape=out_shape,
        in_specs=[VMEM] * len(args),
        out_specs=jax.tree.map(lambda _: VMEM, out_shape),
        scratch_shapes=scratch,
        compiler_params=pltpu.CompilerParams(vmem_limit_bytes=LIMIT),
        cost_estimate=pl.CostEstimate(flops=flops, bytes_accessed=moved, transcendentals=0),
    )(*args)


def shards(grad_out, volume, weight):
    count = lax.axis_size("chan")
    depth = lax.axis_size("depth")
    own_outs, _, rows, cols = grad_out.shape
    chans = volume.shape[0]
    channels = weight.shape[2]
    cells = rows * cols
    ring = ring_order(count)
    ahead = [(ring[i], ring[(i + 1) % count]) for i in range(count)]
    farther = [(i, (i + 1) % depth) for i in range(depth)]
    nearer = [(b, a) for a, b in farther]

    own_weight = lax.dynamic_slice_in_dim(weight, lax.axis_index("chan") * chans, chans, 1)
    views, even_taps, odd_taps = call(
        lambda *refs: own_views_kernel(ring, depth, *refs),
        (
            jax.ShapeDtypeStruct((12 * chans, cells), BF16),
            jax.ShapeDtypeStruct((9 * chans, channels), BF16),
            jax.ShapeDtypeStruct((9 * chans, 2 * channels), BF16),
        ),
        volume,
        own_weight,
        cost=(2 * 2 * 2 * cells * chans * 8 * cols, 4 << 20),
    )
    got = [grad_out]
    for step in range(1, count):
        got.append(lax.ppermute(got[-1], "chan", ahead))
        if step == 1:
            got[1], views = lax.optimization_barrier((got[1], views))
    lines = lambda *parts: call(
        lines_kernel,
        jax.ShapeDtypeStruct((sum(part.shape[0] for part in parts), cells), BF16),
        *parts,
        scratch=(pltpu.VMEM((own_outs * (rows + 8), cols), F32),),
        cost=(1 << 20, 2 << 20),
    )
    behind = lax.ppermute(volume, "depth", farther)
    next_own = lax.ppermute(grad_out, "depth", nearer)
    behind_views = call(
        behind_views_kernel,
        jax.ShapeDtypeStruct((6 * chans, cells), BF16),
        behind,
        cost=(2 * 2 * cells * chans * 8 * cols, 2 << 20),
    )
    first_lines, next_first_lines = lines(grad_out), lines(next_own)
    got[2], views, behind_views, first_lines, next_first_lines = lax.optimization_barrier(
        (got[2], views, behind_views, first_lines, next_first_lines)
    )
    later_lines = [lines(*got[1:-1]), lines(got[-1])]
    own_lines = [first_lines] + later_lines
    next_lines = [next_first_lines] + [lax.ppermute(part, "depth", nearer) for part in later_lines]
    outs = channels // depth
    half_terms = jax.ShapeDtypeStruct((channels // 2, 32 * chans), F32)
    keep, send = call(
        lambda *refs: weight_kernel(ring, outs, cols, 4 * cols, *refs),
        (half_terms, half_terms),
        views,
        behind_views,
        *own_lines,
        scratch=(
            pltpu.VMEM((32 * (chans + 8), channels), F32),
            pltpu.VMEM((32 * chans, channels), F32),
        ),
        cost=(2 * 27 * chans * channels * cells, 8 << 20),
    )
    def input_plane(plane, taps, lines, before):
        kernel = functools.partial(input_kernel, plane)
        earlier = [] if before is None else [before]
        return pl.pallas_call(
            kernel if before is None else lambda before, *refs: kernel(*refs),
            out_shape=jax.ShapeDtypeStruct(volume.shape, BF16),
            in_specs=[HBM] * len(earlier) + [VMEM] * (1 + len(lines)),
            out_specs=HBM,
            input_output_aliases={} if before is None else {0: 0},
            scratch_shapes=(
                pltpu.VMEM((9 * chans, cells + cols), F32),
                pltpu.VMEM((2, 256 // chans * (chans + 8), cols), F32),
                pltpu.VMEM((chans, 2 * rows, 2 * cols), BF16),
                pltpu.SemaphoreType.DMA((2 * rows * chans // 256,)),
            ),
            compiler_params=pltpu.CompilerParams(vmem_limit_bytes=LIMIT),
            cost_estimate=pl.CostEstimate(
                flops=2 * 9 * chans * taps.shape[1] * cells, bytes_accessed=4 << 20, transcendentals=0
            ),
        )(*earlier, taps, *lines)

    other = lax.ppermute(send, "depth", [(i, i ^ 1) for i in range(depth)])
    half_grad = input_plane(0, even_taps, own_lines, None)
    other, half_grad = lax.optimization_barrier((other, half_grad))
    own_terms, *terms = call(
        pair_kernel,
        [jax.ShapeDtypeStruct((outs, 32 * chans), F32)] * (depth // 2),
        keep,
        other,
        cost=(1 << 16, 1 << 19),
    )
    terms = [lax.ppermute(term, "depth", [(i, i ^ (2 * k + 2)) for i in range(depth)]) for k, term in enumerate(terms)]
    input_grad = input_plane(1, odd_taps, next_lines + own_lines, half_grad)
    own_terms, input_grad = lax.optimization_barrier((own_terms, input_grad))
    scale = 1.0 / math.sqrt(depth * cells)
    weight_grad = call(
        functools.partial(total_kernel, scale),
        jax.ShapeDtypeStruct((chans, outs, 27), F32),
        own_terms,
        *terms,
        cost=(1 << 16, 1 << 19),
    )
    return input_grad, jnp.transpose(weight_grad, (2, 0, 1))


def solution(mesh):
    in_specs = (P("chan", "depth", None, None), P("chan", "depth", None, None), P())
    out_specs = (P("chan", "depth", None, None), P(None, "chan", "depth"))
    ring, depth = mesh.shape["chan"], mesh.shape["depth"]

    def either(grad_out, volume, weight):
        fits = (
            grad_out.shape[0] % 32 == 0
            and volume.shape[0] == 16
            and grad_out.shape[1] == 1
            and ring >= 4
            and depth & (depth - 1) == 0
            and depth % (2 * ring) == 0
        )
        return (shards if fits else plain_shards)(grad_out, volume, weight)

    return jax.shard_map(either, mesh=mesh, in_specs=in_specs, out_specs=out_specs, check_vma=False)
```

```python
import functools
import math

import jax
import jax.numpy as jnp
from jax import lax
from jax.experimental import pallas as pl
from jax.experimental.pallas import tpu as pltpu
from jax.sharding import PartitionSpec as P

F32 = jnp.float32
BF16 = jnp.bfloat16
VMEM = pl.BlockSpec(memory_space=pltpu.VMEM)
HBM = pl.BlockSpec(memory_space=pltpu.HBM)
LIMIT = 48 * 1024 * 1024


def matmul(left, right):
    return jnp.dot(left, right, preferred_element_type=F32)


def one_hot(rows, cols, source):
    row = lax.broadcasted_iota(jnp.int32, (rows, cols), 0)
    col = lax.broadcasted_iota(jnp.int32, (rows, cols), 1)
    return jnp.where(source(row, col), 1.0, 0.0).astype(BF16)


def swap_rows(major, minor):
    bits = minor.bit_length() - 1
    return one_hot(
        major * minor,
        major * minor,
        lambda row, col: col == (row & (minor - 1)) * major + (row >> bits),
    )


def place_views(plane, views_ref, base):
    chans, rows, cols = plane.shape
    half = cols // 2
    group = 256 // chans
    swap = swap_rows(group, chans)
    split = one_hot(cols, cols, lambda row, col: row == 2 * (col & (half - 1)) + col // half)
    inner = lax.broadcasted_iota(jnp.int32, (group * chans, half), 1) > 0
    for start in range(0, rows, group):
        block = plane[:, start : start + group, :].reshape(chans * group, cols)
        parted = matmul(matmul(swap, block).astype(BF16), split)
        odd = parted[:, half:]
        before = jnp.where(inner, pltpu.roll(odd, 1, 1), 0.0)
        views = [view.astype(BF16) for view in (before, parted[:, :half], odd)]
        for at in range(group):
            row = start + at
            lanes = slice(row // 2 * half, (row // 2 + 1) * half)
            for e in range(3):
                lo = base + (3 * (row % 2) + e) * chans
                views_ref[lo : lo + chans, lanes] = views[e][at * chans : (at + 1) * chans]


def own_views_kernel(depth, volume_ref, weight_ref, views_ref, even_ref, odd_ref):
    chans = volume_ref.shape[0]
    channels = weight_ref.shape[2]
    place_views(volume_ref.at[:, 0], views_ref, 0)
    place_views(volume_ref.at[:, 1], views_ref, 6 * chans)
    count = lax.axis_size("chan")
    part = channels // count
    here = lax.axis_index("chan")
    row = lax.broadcasted_iota(jnp.int32, (channels, channels), 0)
    col = lax.broadcasted_iota(jnp.int32, (channels, channels), 1)
    order = jnp.zeros((channels, channels), F32)
    for slot in range(count):
        moved = ((here ^ slot) - slot) * part
        inside = (col >= slot * part) & (col < (slot + 1) * part)
        order = jnp.where(inside & (row == col + moved), 1.0, order)
    ordered = matmul(weight_ref[...].reshape(27 * chans, channels), order.astype(BF16)).astype(BF16)
    beyond = jnp.where(lax.axis_index("depth") == depth - 1, 0.0, 1.0).astype(BF16)
    for k, e in enumerate((1, 2, 0)):
        for b in range(3):
            pick = lambda a: ordered[(9 * a + 3 * b + e) * chans : (9 * a + 3 * b + e + 1) * chans]
            lo = (3 * k + b) * chans
            even_ref[lo : lo + chans, :] = pick(1)
            odd_ref[lo : lo + chans, :] = jnp.concatenate([pick(0) * beyond, pick(2)], axis=1)


def behind_views_kernel(behind_ref, views_ref):
    first = lax.axis_index("depth") == 0

    @pl.when(jnp.logical_not(first))
    def _():
        place_views(behind_ref.at[:, 0], views_ref, 0)

    @pl.when(first)
    def _():
        views_ref[...] = jnp.zeros(views_ref.shape, BF16)


def place_lines(part, out_ref, at, wide_ref):
    outs, _, rows, cols = part.shape
    pitch = rows + 8
    for o in range(outs):
        wide_ref[o * pitch : o * pitch + rows, :] = part[o, 0].astype(F32)
    for row in range(rows):
        line = wide_ref[pl.ds(row, outs, stride=pitch), :].astype(BF16)
        out_ref[at : at + outs, row * cols : (row + 1) * cols] = line


def lines_kernel(*refs):
    *parts, out_ref, wide_ref = refs
    at = 0
    for part in parts:
        place_lines(part, out_ref, at, wide_ref)
        at += part.shape[0]


def weight_kernel(
    outs, cols, chunk, own_ref, behind_ref, *refs
):
    *line_refs, keep_ref, send_ref, terms_ref, placed_ref = refs
    channels = terms_ref.shape[1]
    chans = behind_ref.shape[0] // 6
    cells = own_ref.shape[1]
    contract = (((1,), (1,)), ((), ()))

    def grads(lo, hi):
        return jnp.concatenate([ref[:, lo:hi] for ref in line_refs], axis=0)

    pitch = chans + 8
    sums = None
    for lo in range(0, cells, chunk):
        hi = lo + chunk
        below = grads(lo + cols, min(hi + cols, cells))
        if hi == cells:
            below = jnp.concatenate([below, jnp.zeros((channels, cols), BF16)], axis=1)
        both = jnp.concatenate([grads(lo, hi), below], axis=0)
        views = jnp.concatenate([behind_ref[:, lo:hi], own_ref[:, lo:hi]], axis=0)
        part = lax.dot_general(views, both, contract, preferred_element_type=F32)
        sums = part if sums is None else sums + part
    for a in range(3):
        terms = sums[6 * a * chans : 6 * (a + 1) * chans]
        even, odd = terms[: 3 * chans, :channels], terms[3 * chans :]
        for b, block in enumerate((odd[:, channels:], even, odd[:, :channels])):
            for e in range(3):
                lo = (9 * a + 3 * b + e) * pitch
                terms_ref[lo : lo + chans, :] = block[e * chans : (e + 1) * chans]
    terms_ref[27 * pitch :, :] = jnp.zeros((5 * pitch, channels), F32)
    for c in range(chans):
        placed_ref[32 * c : 32 * c + 32, :] = terms_ref[pl.ds(c, 32, stride=pitch), :]
    turned = placed_ref[...].T
    count = lax.axis_size("chan")
    part = channels // count
    odd_core = lax.axis_index("depth") % 2 == 1
    for slot in range(count):
        start = (lax.axis_index("chan") ^ slot) * (part // 2)
        for at in range(0, part // 2, outs):
            lo = slot * part + 2 * at
            even, odd = turned[lo : lo + outs], turned[lo + outs : lo + 2 * outs]
            place = pl.ds(pl.multiple_of(start + at, outs), outs)
            keep_ref[place, :] = jnp.where(odd_core, odd, even)
            send_ref[place, :] = jnp.where(odd_core, even, odd)


def pair_kernel(keep_ref, other_ref, *out_refs):
    chip = lax.axis_index("depth") // 2
    outs = out_refs[0].shape[0]
    for k, out_ref in enumerate(out_refs):
        place = pl.ds(pl.multiple_of((chip ^ k) * outs, outs), outs)
        out_ref[...] = keep_ref[place, :] + other_ref[place, :]


def input_kernel(plane, *refs):
    taps_ref, *line_refs, out_ref, cells_ref, lines_ref, rows_ref, sems = refs
    chans, rows, cols = rows_ref.shape
    half = cols // 2
    grid_cells = half * rows // 2
    grads = jnp.concatenate([ref[...] for ref in line_refs], axis=0)
    cells_ref[:, :grid_cells] = matmul(taps_ref[...], grads)
    cells_ref[:, grid_cells:] = jnp.zeros((cells_ref.shape[0], half), F32)
    group = 256 // chans
    pitch = chans + 8
    weave = one_hot(cols, cols, lambda row, col: col == 2 * (row & (half - 1)) + row // half)
    inner = lax.broadcasted_iota(jnp.int32, (chans, half), 1) < half - 1

    def cells(kind, b, r):
        lo = (3 * kind + b) * chans
        return cells_ref[lo : lo + chans, r * half : (r + 1) * half]

    copies = []
    for start in range(0, rows, group):
        pieces = []
        for row in range(start, start + group):
            r = row // 2
            if row % 2 == 0:
                even, odd, next_odd = [cells(kind, 1, r) for kind in range(3)]
            else:
                even, odd, next_odd = [cells(kind, 0, r + 1) + cells(kind, 2, r) for kind in range(3)]
            odd = odd + jnp.where(inner, pltpu.roll(next_odd, half - 1, 1), 0.0)
            pieces.append(jnp.concatenate([even, odd], axis=1).astype(BF16))
        woven = matmul(jnp.concatenate(pieces, axis=0), weave)
        for side in range(2):
            lanes = slice(side * half, (side + 1) * half)
            for at in range(group):
                lines_ref[side, at * pitch : at * pitch + chans] = woven[at * chans : (at + 1) * chans, lanes]
            for c in range(chans):
                line = lines_ref[side, pl.ds(c, group, stride=pitch), :].astype(BF16)
                rows_ref[c, start : start + group, lanes] = line
        place = pl.ds(start, group)
        copies.append(
            pltpu.make_async_copy(
                rows_ref.at[:, place], out_ref.at[:, plane, place], sems.at[start // group]
            )
        )
        copies[-1].start()
    for copy in copies:
        copy.wait()


def total_kernel(scale, *refs):
    *term_refs, out_ref = refs
    chans, outs, taps = out_ref.shape
    total = term_refs[0][...]
    for ref in term_refs[1:]:
        total = total + ref[...]
    total = total * scale
    for c in range(chans):
        out_ref[c] = total[:, 32 * c : 32 * c + taps]


def from_behind(shard, axis, by):
    count = lax.axis_size(axis)
    pairs = [(i, i + by) for i in range(count) if 0 <= i + by < count]
    return lax.ppermute(shard, axis, pairs)


def upsample(stacked, axis, extended):
    tap_zero, tap_one, tap_two = (stacked[0], stacked[1], stacked[2])
    coord_axis = axis - 1
    length = tap_zero.shape[coord_axis]
    if extended:
        outer = length - 1
        even_cells = lax.slice_in_dim(tap_one, 0, outer, axis=coord_axis)
        odd_cells = lax.slice_in_dim(tap_zero, 1, length, axis=coord_axis) + lax.slice_in_dim(
            tap_two, 0, outer, axis=coord_axis
        )
    else:
        outer = length
        shifted = lax.slice_in_dim(tap_zero, 1, length, axis=coord_axis)
        shifted = jnp.concatenate(
            [shifted, jnp.zeros_like(lax.slice_in_dim(tap_zero, 0, 1, axis=coord_axis))],
            axis=coord_axis,
        )
        even_cells = tap_one
        odd_cells = shifted + tap_two
    paired = jnp.stack([even_cells, odd_cells], axis=coord_axis + 1)
    new_shape = list(even_cells.shape)
    new_shape[coord_axis] = 2 * outer
    return paired.reshape(new_shape)


def phase_grads(weight_rows, grads_ext):
    local_in = weight_rows.shape[0] // 27
    channels_out, planes, rows, cols = grads_ext.shape
    taps_out = jnp.dot(
        weight_rows, grads_ext.reshape(channels_out, -1), preferred_element_type=jnp.float32
    )
    taps_out = taps_out.reshape(3, 3, 3, local_in, planes, rows, cols)
    along_w = upsample(jnp.moveaxis(taps_out, 2, 0), 6, False)
    along_h = upsample(jnp.moveaxis(along_w, 1, 0), 4, False)
    return upsample(along_h, 2, True)


def weight_terms(inputs, grads_ext):
    row_extra = 0
    weight_cube = lax.conv_general_dilated(
        inputs[None],
        grads_ext[:, None],
        (1, 1, 1),
        ((1, 2), (1, row_extra), (1, 0)),
        rhs_dilation=(2, 2, 2),
        dimension_numbers=("CNDHW", "OIDHW", "NCDHW"),
        preferred_element_type=jnp.float32,
    )
    return jnp.transpose(weight_cube, (2, 3, 4, 0, 1)).reshape(
        27, weight_cube.shape[0], weight_cube.shape[1]
    )


def plain_shards(grad_out, volume, weight):
    plane_next = from_behind(grad_out, "depth", -1)
    grads_ext = jnp.concatenate([grad_out, plane_next], axis=1)
    channels_out = weight.shape[2]
    local_in = volume.shape[0]
    every_channel = lax.all_gather(grads_ext, "chan", axis=0, tiled=True)
    own_weight = lax.dynamic_slice_in_dim(weight, lax.axis_index("chan") * local_in, local_in, 1)
    input_part = phase_grads(own_weight.reshape(27 * local_in, channels_out), every_channel)
    weight_part = weight_terms(volume, every_channel)
    input_grad = input_part.astype(jnp.bfloat16)
    summed = lax.psum_scatter(weight_part, "depth", scatter_dimension=2, tiled=True)
    cell_count = grad_out.shape[1] * lax.axis_size("depth") * grad_out.shape[2] * grad_out.shape[3]
    return (input_grad, summed * (1.0 / math.sqrt(cell_count)))


def call(kernel, out_shape, *args, scratch=(), cost=None):
    flops, moved = cost
    return pl.pallas_call(
        kernel,
        out_shape=out_shape,
        in_specs=[VMEM] * len(args),
        out_specs=jax.tree.map(lambda _: VMEM, out_shape),
        scratch_shapes=scratch,
        compiler_params=pltpu.CompilerParams(vmem_limit_bytes=LIMIT),
        cost_estimate=pl.CostEstimate(flops=flops, bytes_accessed=moved, transcendentals=0),
    )(*args)


def shards(grad_out, volume, weight):
    count = lax.axis_size("chan")
    depth = lax.axis_size("depth")
    own_outs, _, rows, cols = grad_out.shape
    chans = volume.shape[0]
    channels = weight.shape[2]
    cells = rows * cols
    farther = [(i, (i + 1) % depth) for i in range(depth)]
    nearer = [(b, a) for a, b in farther]

    own_weight = lax.dynamic_slice_in_dim(weight, lax.axis_index("chan") * chans, chans, 1)
    views, even_taps, odd_taps = call(
        lambda *refs: own_views_kernel(depth, *refs),
        (
            jax.ShapeDtypeStruct((12 * chans, cells), BF16),
            jax.ShapeDtypeStruct((9 * chans, channels), BF16),
            jax.ShapeDtypeStruct((9 * chans, 2 * channels), BF16),
        ),
        volume,
        own_weight,
        cost=(2 * 2 * 2 * cells * chans * 8 * cols, 4 << 20),
    )
    got = {0: grad_out}
    for mask in sorted(range(1, count), key=lambda mask: (mask & (mask - 1) > 0, -mask)):
        low = mask & -mask
        if mask == 3:
            got[2], views = lax.optimization_barrier((got[2], views))
        got[mask] = lax.ppermute(got[mask - low], "chan", [(i, i ^ low) for i in range(count)])
    lines = lambda *parts: call(
        lines_kernel,
        jax.ShapeDtypeStruct((sum(part.shape[0] for part in parts), cells), BF16),
        *parts,
        scratch=(pltpu.VMEM((own_outs * (rows + 8), cols), F32),),
        cost=(1 << 20, 2 << 20),
    )
    behind = lax.ppermute(volume[:, 1:], "depth", farther)
    next_own = lax.ppermute(grad_out, "depth", nearer)
    behind_views = call(
        behind_views_kernel,
        jax.ShapeDtypeStruct((6 * chans, cells), BF16),
        behind,
        cost=(2 * 2 * cells * chans * 8 * cols, 2 << 20),
    )
    first_lines, next_first_lines = lines(grad_out), lines(next_own)
    got[1], views, behind_views, first_lines, next_first_lines = lax.optimization_barrier(
        (got[1], views, behind_views, first_lines, next_first_lines)
    )
    later_lines = [lines(*[got[mask] for mask in range(1, count - 1)]), lines(got[count - 1])]
    own_lines = [first_lines] + later_lines
    next_lines = [next_first_lines] + [lax.ppermute(part, "depth", nearer) for part in later_lines]
    outs = channels // depth
    half_terms = jax.ShapeDtypeStruct((channels // 2, 32 * chans), F32)
    keep, send = call(
        lambda *refs: weight_kernel(outs, cols, 4 * cols, *refs),
        (half_terms, half_terms),
        views,
        behind_views,
        *own_lines,
        scratch=(
            pltpu.VMEM((32 * (chans + 8), channels), F32),
            pltpu.VMEM((32 * chans, channels), F32),
        ),
        cost=(2 * 27 * chans * channels * cells, 8 << 20),
    )
    def input_plane(plane, taps, lines, before):
        kernel = functools.partial(input_kernel, plane)
        earlier = [] if before is None else [before]
        return pl.pallas_call(
            kernel if before is None else lambda before, *refs: kernel(*refs),
            out_shape=jax.ShapeDtypeStruct(volume.shape, BF16),
            in_specs=[HBM] * len(earlier) + [VMEM] * (1 + len(lines)),
            out_specs=HBM,
            input_output_aliases={} if before is None else {0: 0},
            scratch_shapes=(
                pltpu.VMEM((9 * chans, cells + cols), F32),
                pltpu.VMEM((2, 256 // chans * (chans + 8), cols), F32),
                pltpu.VMEM((chans, 2 * rows, 2 * cols), BF16),
                pltpu.SemaphoreType.DMA((2 * rows * chans // 256,)),
            ),
            compiler_params=pltpu.CompilerParams(vmem_limit_bytes=LIMIT),
            cost_estimate=pl.CostEstimate(
                flops=2 * 9 * chans * taps.shape[1] * cells, bytes_accessed=4 << 20, transcendentals=0
            ),
        )(*earlier, taps, *lines)

    other = lax.ppermute(send, "depth", [(i, i ^ 1) for i in range(depth)])
    half_grad = input_plane(0, even_taps, own_lines, None)
    other, half_grad = lax.optimization_barrier((other, half_grad))
    own_terms, *terms = call(
        pair_kernel,
        [jax.ShapeDtypeStruct((outs, 32 * chans), F32)] * (depth // 2),
        keep,
        other,
        cost=(1 << 16, 1 << 19),
    )
    terms = [lax.ppermute(term, "depth", [(i, i ^ (2 * k + 2)) for i in range(depth)]) for k, term in enumerate(terms)]
    input_grad = input_plane(1, odd_taps, next_lines + own_lines, half_grad)
    own_terms, input_grad = lax.optimization_barrier((own_terms, input_grad))
    scale = 1.0 / math.sqrt(depth * cells)
    weight_grad = call(
        functools.partial(total_kernel, scale),
        jax.ShapeDtypeStruct((chans, outs, 27), F32),
        own_terms,
        *terms,
        cost=(1 << 16, 1 << 19),
    )
    return input_grad, jnp.transpose(weight_grad, (2, 0, 1))


def solution(mesh):
    in_specs = (P("chan", "depth", None, None), P("chan", "depth", None, None), P())
    out_specs = (P("chan", "depth", None, None), P(None, "chan", "depth"))
    ring, depth = mesh.shape["chan"], mesh.shape["depth"]

    def either(grad_out, volume, weight):
        fits = (
            grad_out.shape[0] % 32 == 0
            and volume.shape[0] == 16
            and grad_out.shape[1] == 1
            and ring >= 4
            and ring & (ring - 1) == 0
            and depth & (depth - 1) == 0
            and depth % (2 * ring) == 0
        )
        return (shards if fits else plain_shards)(grad_out, volume, weight)

    return jax.shard_map(either, mesh=mesh, in_specs=in_specs, out_specs=out_specs, check_vma=False)
```

```python
import functools
import math

import jax
import jax.numpy as jnp
from jax import lax
from jax.experimental import pallas as pl
from jax.experimental.pallas import tpu as pltpu
from jax.sharding import PartitionSpec as P

F32 = jnp.float32
BF16 = jnp.bfloat16
VMEM = pl.BlockSpec(memory_space=pltpu.VMEM)
HBM = pl.BlockSpec(memory_space=pltpu.HBM)
LIMIT = 48 * 1024 * 1024


def matmul(left, right):
    return jnp.dot(left, right, preferred_element_type=F32)


def one_hot(rows, cols, source):
    row = lax.broadcasted_iota(jnp.int32, (rows, cols), 0)
    col = lax.broadcasted_iota(jnp.int32, (rows, cols), 1)
    return jnp.where(source(row, col), 1.0, 0.0).astype(BF16)


def swap_rows(major, minor):
    bits = minor.bit_length() - 1
    return one_hot(
        major * minor,
        major * minor,
        lambda row, col: col == (row & (minor - 1)) * major + (row >> bits),
    )


def place_views(plane, views_ref, base):
    chans, rows, cols = plane.shape
    half = cols // 2
    group = 256 // chans
    swap = swap_rows(group, chans)
    split = one_hot(cols, cols, lambda row, col: row == 2 * (col & (half - 1)) + col // half)
    inner = lax.broadcasted_iota(jnp.int32, (group * chans, half), 1) > 0
    for start in range(0, rows, group):
        block = plane[:, start : start + group, :].reshape(chans * group, cols)
        parted = matmul(matmul(swap, block).astype(BF16), split)
        odd = parted[:, half:]
        before = jnp.where(inner, pltpu.roll(odd, 1, 1), 0.0)
        views = [view.astype(BF16) for view in (before, parted[:, :half], odd)]
        for at in range(group):
            row = start + at
            lanes = slice(row // 2 * half, (row // 2 + 1) * half)
            for e in range(3):
                lo = base + (3 * (row % 2) + e) * chans
                views_ref[lo : lo + chans, lanes] = views[e][at * chans : (at + 1) * chans]


def own_views_kernel(depth, volume_ref, weight_ref, views_ref, even_ref, odd_ref):
    chans = volume_ref.shape[0]
    channels = weight_ref.shape[2]
    place_views(volume_ref.at[:, 0], views_ref, 0)
    place_views(volume_ref.at[:, 1], views_ref, 6 * chans)
    count = lax.axis_size("chan")
    part = channels // count
    here = lax.axis_index("chan")
    row = lax.broadcasted_iota(jnp.int32, (channels, channels), 0)
    col = lax.broadcasted_iota(jnp.int32, (channels, channels), 1)
    order = jnp.zeros((channels, channels), F32)
    for slot in range(count):
        moved = ((here ^ slot) - slot) * part
        inside = (col >= slot * part) & (col < (slot + 1) * part)
        order = jnp.where(inside & (row == col + moved), 1.0, order)
    ordered = matmul(weight_ref[...].reshape(27 * chans, channels), order.astype(BF16)).astype(BF16)
    beyond = jnp.where(lax.axis_index("depth") == depth - 1, 0.0, 1.0).astype(BF16)
    for k, e in enumerate((1, 2, 0)):
        for b in range(3):
            pick = lambda a: ordered[(9 * a + 3 * b + e) * chans : (9 * a + 3 * b + e + 1) * chans]
            lo = (3 * k + b) * chans
            even_ref[lo : lo + chans, :] = pick(1)
            odd_ref[lo : lo + chans, :] = jnp.concatenate([pick(0) * beyond, pick(2)], axis=1)


def behind_views_kernel(behind_ref, views_ref):
    first = lax.axis_index("depth") == 0

    @pl.when(jnp.logical_not(first))
    def _():
        place_views(behind_ref.at[:, 1], views_ref, 0)

    @pl.when(first)
    def _():
        views_ref[...] = jnp.zeros(views_ref.shape, BF16)


def place_lines(part, out_ref, at, wide_ref):
    outs, _, rows, cols = part.shape
    pitch = rows + 8
    for o in range(outs):
        wide_ref[o * pitch : o * pitch + rows, :] = part[o, 0].astype(F32)
    for row in range(rows):
        line = wide_ref[pl.ds(row, outs, stride=pitch), :].astype(BF16)
        out_ref[at : at + outs, row * cols : (row + 1) * cols] = line


def lines_kernel(*refs):
    *parts, out_ref, wide_ref = refs
    at = 0
    for part in parts:
        place_lines(part, out_ref, at, wide_ref)
        at += part.shape[0]


def weight_kernel(
    outs, cols, chunk, own_ref, behind_ref, *refs
):
    *line_refs, keep_ref, send_ref, terms_ref, placed_ref = refs
    channels = terms_ref.shape[1]
    chans = behind_ref.shape[0] // 6
    cells = own_ref.shape[1]
    contract = (((1,), (1,)), ((), ()))

    def grads(lo, hi):
        return jnp.concatenate([ref[:, lo:hi] for ref in line_refs], axis=0)

    pitch = chans + 8
    sums = None
    for lo in range(0, cells, chunk):
        hi = lo + chunk
        below = grads(lo + cols, min(hi + cols, cells))
        if hi == cells:
            below = jnp.concatenate([below, jnp.zeros((channels, cols), BF16)], axis=1)
        both = jnp.concatenate([grads(lo, hi), below], axis=0)
        views = jnp.concatenate([behind_ref[:, lo:hi], own_ref[:, lo:hi]], axis=0)
        part = lax.dot_general(views, both, contract, preferred_element_type=F32)
        sums = part if sums is None else sums + part
    for a in range(3):
        terms = sums[6 * a * chans : 6 * (a + 1) * chans]
        even, odd = terms[: 3 * chans, :channels], terms[3 * chans :]
        for b, block in enumerate((odd[:, channels:], even, odd[:, :channels])):
            for e in range(3):
                lo = (9 * a + 3 * b + e) * pitch
                terms_ref[lo : lo + chans, :] = block[e * chans : (e + 1) * chans]
    terms_ref[27 * pitch :, :] = jnp.zeros((5 * pitch, channels), F32)
    for c in range(chans):
        placed_ref[32 * c : 32 * c + 32, :] = terms_ref[pl.ds(c, 32, stride=pitch), :]
    turned = placed_ref[...].T
    count = lax.axis_size("chan")
    part = channels // count
    odd_core = lax.axis_index("depth") % 2 == 1
    for slot in range(count):
        start = (lax.axis_index("chan") ^ slot) * (part // 2)
        for at in range(0, part // 2, outs):
            lo = slot * part + 2 * at
            even, odd = turned[lo : lo + outs], turned[lo + outs : lo + 2 * outs]
            place = pl.ds(pl.multiple_of(start + at, outs), outs)
            keep_ref[place, :] = jnp.where(odd_core, odd, even)
            send_ref[place, :] = jnp.where(odd_core, even, odd)


def pair_kernel(keep_ref, other_ref, *out_refs):
    chip = lax.axis_index("depth") // 2
    outs = out_refs[0].shape[0]
    for k, out_ref in enumerate(out_refs):
        place = pl.ds(pl.multiple_of((chip ^ k) * outs, outs), outs)
        out_ref[...] = keep_ref[place, :] + other_ref[place, :]


def input_kernel(plane, *refs):
    taps_ref, *line_refs, out_ref, cells_ref, lines_ref, rows_ref, sems = refs
    chans, rows, cols = rows_ref.shape
    half = cols // 2
    grid_cells = half * rows // 2
    grads = jnp.concatenate([ref[...] for ref in line_refs], axis=0)
    cells_ref[:, :grid_cells] = matmul(taps_ref[...], grads)
    cells_ref[:, grid_cells:] = jnp.zeros((cells_ref.shape[0], half), F32)
    group = 256 // chans
    pitch = chans + 8
    weave = one_hot(cols, cols, lambda row, col: col == 2 * (row & (half - 1)) + row // half)
    inner = lax.broadcasted_iota(jnp.int32, (chans, half), 1) < half - 1

    def cells(kind, b, r):
        lo = (3 * kind + b) * chans
        return cells_ref[lo : lo + chans, r * half : (r + 1) * half]

    copies = []
    for start in range(0, rows, group):
        pieces = []
        for row in range(start, start + group):
            r = row // 2
            if row % 2 == 0:
                even, odd, next_odd = [cells(kind, 1, r) for kind in range(3)]
            else:
                even, odd, next_odd = [cells(kind, 0, r + 1) + cells(kind, 2, r) for kind in range(3)]
            odd = odd + jnp.where(inner, pltpu.roll(next_odd, half - 1, 1), 0.0)
            pieces.append(jnp.concatenate([even, odd], axis=1).astype(BF16))
        woven = matmul(jnp.concatenate(pieces, axis=0), weave)
        for side in range(2):
            lanes = slice(side * half, (side + 1) * half)
            for at in range(group):
                lines_ref[side, at * pitch : at * pitch + chans] = woven[at * chans : (at + 1) * chans, lanes]
            for c in range(chans):
                line = lines_ref[side, pl.ds(c, group, stride=pitch), :].astype(BF16)
                rows_ref[c, start : start + group, lanes] = line
        place = pl.ds(start, group)
        copies.append(
            pltpu.make_async_copy(
                rows_ref.at[:, place], out_ref.at[:, plane, place], sems.at[start // group]
            )
        )
        copies[-1].start()
    for copy in copies:
        copy.wait()


def total_kernel(scale, *refs):
    *term_refs, out_ref = refs
    chans, outs, taps = out_ref.shape
    total = term_refs[0][...]
    for ref in term_refs[1:]:
        total = total + ref[...]
    total = total * scale
    for c in range(chans):
        out_ref[c] = total[:, 32 * c : 32 * c + taps]


def from_behind(shard, axis, by):
    count = lax.axis_size(axis)
    pairs = [(i, i + by) for i in range(count) if 0 <= i + by < count]
    return lax.ppermute(shard, axis, pairs)


def upsample(stacked, axis, extended):
    tap_zero, tap_one, tap_two = (stacked[0], stacked[1], stacked[2])
    coord_axis = axis - 1
    length = tap_zero.shape[coord_axis]
    if extended:
        outer = length - 1
        even_cells = lax.slice_in_dim(tap_one, 0, outer, axis=coord_axis)
        odd_cells = lax.slice_in_dim(tap_zero, 1, length, axis=coord_axis) + lax.slice_in_dim(
            tap_two, 0, outer, axis=coord_axis
        )
    else:
        outer = length
        shifted = lax.slice_in_dim(tap_zero, 1, length, axis=coord_axis)
        shifted = jnp.concatenate(
            [shifted, jnp.zeros_like(lax.slice_in_dim(tap_zero, 0, 1, axis=coord_axis))],
            axis=coord_axis,
        )
        even_cells = tap_one
        odd_cells = shifted + tap_two
    paired = jnp.stack([even_cells, odd_cells], axis=coord_axis + 1)
    new_shape = list(even_cells.shape)
    new_shape[coord_axis] = 2 * outer
    return paired.reshape(new_shape)


def phase_grads(weight_rows, grads_ext):
    local_in = weight_rows.shape[0] // 27
    channels_out, planes, rows, cols = grads_ext.shape
    taps_out = jnp.dot(
        weight_rows, grads_ext.reshape(channels_out, -1), preferred_element_type=jnp.float32
    )
    taps_out = taps_out.reshape(3, 3, 3, local_in, planes, rows, cols)
    along_w = upsample(jnp.moveaxis(taps_out, 2, 0), 6, False)
    along_h = upsample(jnp.moveaxis(along_w, 1, 0), 4, False)
    return upsample(along_h, 2, True)


def weight_terms(inputs, grads_ext):
    row_extra = 0
    weight_cube = lax.conv_general_dilated(
        inputs[None],
        grads_ext[:, None],
        (1, 1, 1),
        ((1, 2), (1, row_extra), (1, 0)),
        rhs_dilation=(2, 2, 2),
        dimension_numbers=("CNDHW", "OIDHW", "NCDHW"),
        preferred_element_type=jnp.float32,
    )
    return jnp.transpose(weight_cube, (2, 3, 4, 0, 1)).reshape(
        27, weight_cube.shape[0], weight_cube.shape[1]
    )


def plain_shards(grad_out, volume, weight):
    plane_next = from_behind(grad_out, "depth", -1)
    grads_ext = jnp.concatenate([grad_out, plane_next], axis=1)
    channels_out = weight.shape[2]
    local_in = volume.shape[0]
    every_channel = lax.all_gather(grads_ext, "chan", axis=0, tiled=True)
    own_weight = lax.dynamic_slice_in_dim(weight, lax.axis_index("chan") * local_in, local_in, 1)
    input_part = phase_grads(own_weight.reshape(27 * local_in, channels_out), every_channel)
    weight_part = weight_terms(volume, every_channel)
    input_grad = input_part.astype(jnp.bfloat16)
    summed = lax.psum_scatter(weight_part, "depth", scatter_dimension=2, tiled=True)
    cell_count = grad_out.shape[1] * lax.axis_size("depth") * grad_out.shape[2] * grad_out.shape[3]
    return (input_grad, summed * (1.0 / math.sqrt(cell_count)))


def call(kernel, out_shape, *args, scratch=(), cost=None):
    flops, moved = cost
    return pl.pallas_call(
        kernel,
        out_shape=out_shape,
        in_specs=[VMEM] * len(args),
        out_specs=jax.tree.map(lambda _: VMEM, out_shape),
        scratch_shapes=scratch,
        compiler_params=pltpu.CompilerParams(vmem_limit_bytes=LIMIT),
        cost_estimate=pl.CostEstimate(flops=flops, bytes_accessed=moved, transcendentals=0),
    )(*args)


def shards(grad_out, volume, weight):
    count = lax.axis_size("chan")
    depth = lax.axis_size("depth")
    own_outs, _, rows, cols = grad_out.shape
    chans = volume.shape[0]
    channels = weight.shape[2]
    cells = rows * cols
    farther = [(i, (i + 1) % depth) for i in range(depth)]
    nearer = [(b, a) for a, b in farther]

    own_weight = lax.dynamic_slice_in_dim(weight, lax.axis_index("chan") * chans, chans, 1)
    views, even_taps, odd_taps = call(
        lambda *refs: own_views_kernel(depth, *refs),
        (
            jax.ShapeDtypeStruct((12 * chans, cells), BF16),
            jax.ShapeDtypeStruct((9 * chans, channels), BF16),
            jax.ShapeDtypeStruct((9 * chans, 2 * channels), BF16),
        ),
        volume,
        own_weight,
        cost=(2 * 2 * 2 * cells * chans * 8 * cols, 4 << 20),
    )
    got = {0: grad_out}
    for mask in sorted(range(1, count), key=lambda mask: (mask & (mask - 1) > 0, -mask)):
        low = mask & -mask
        if mask == 1:
            got[0], views = lax.optimization_barrier((got[0], views))
        got[mask] = lax.ppermute(got[mask - low], "chan", [(i, i ^ low) for i in range(count)])
    lines = lambda *parts: call(
        lines_kernel,
        jax.ShapeDtypeStruct((sum(part.shape[0] for part in parts), cells), BF16),
        *parts,
        scratch=(pltpu.VMEM((own_outs * (rows + 8), cols), F32),),
        cost=(1 << 20, 2 << 20),
    )
    behind = lax.ppermute(volume, "depth", farther)
    next_own = lax.ppermute(got[0], "depth", nearer)
    behind_views = call(
        behind_views_kernel,
        jax.ShapeDtypeStruct((6 * chans, cells), BF16),
        behind,
        cost=(2 * 2 * cells * chans * 8 * cols, 2 << 20),
    )
    first_lines, next_first_lines = lines(grad_out), lines(next_own)
    got[1], views, behind_views, first_lines, next_first_lines = lax.optimization_barrier(
        (got[1], views, behind_views, first_lines, next_first_lines)
    )
    later_lines = [lines(*[got[mask] for mask in range(1, count - 1)]), lines(got[count - 1])]
    own_lines = [first_lines] + later_lines
    next_lines = [next_first_lines] + [lax.ppermute(part, "depth", nearer) for part in later_lines]
    outs = channels // depth
    half_terms = jax.ShapeDtypeStruct((channels // 2, 32 * chans), F32)
    keep, send = call(
        lambda *refs: weight_kernel(outs, cols, 4 * cols, *refs),
        (half_terms, half_terms),
        views,
        behind_views,
        *own_lines,
        scratch=(
            pltpu.VMEM((32 * (chans + 8), channels), F32),
            pltpu.VMEM((32 * chans, channels), F32),
        ),
        cost=(2 * 27 * chans * channels * cells, 8 << 20),
    )
    def input_plane(plane, taps, lines, before):
        kernel = functools.partial(input_kernel, plane)
        earlier = [] if before is None else [before]
        return pl.pallas_call(
            kernel if before is None else lambda before, *refs: kernel(*refs),
            out_shape=jax.ShapeDtypeStruct(volume.shape, BF16),
            in_specs=[HBM] * len(earlier) + [VMEM] * (1 + len(lines)),
            out_specs=HBM,
            input_output_aliases={} if before is None else {0: 0},
            scratch_shapes=(
                pltpu.VMEM((9 * chans, cells + cols), F32),
                pltpu.VMEM((2, 256 // chans * (chans + 8), cols), F32),
                pltpu.VMEM((chans, 2 * rows, 2 * cols), BF16),
                pltpu.SemaphoreType.DMA((2 * rows * chans // 256,)),
            ),
            compiler_params=pltpu.CompilerParams(vmem_limit_bytes=LIMIT),
            cost_estimate=pl.CostEstimate(
                flops=2 * 9 * chans * taps.shape[1] * cells, bytes_accessed=4 << 20, transcendentals=0
            ),
        )(*earlier, taps, *lines)

    other = lax.ppermute(send, "depth", [(i, i ^ 1) for i in range(depth)])
    half_grad = input_plane(0, even_taps, own_lines, None)
    other, half_grad = lax.optimization_barrier((other, half_grad))
    own_terms, *terms = call(
        pair_kernel,
        [jax.ShapeDtypeStruct((outs, 32 * chans), F32)] * (depth // 2),
        keep,
        other,
        cost=(1 << 16, 1 << 19),
    )
    terms = [lax.ppermute(term, "depth", [(i, i ^ (2 * k + 2)) for i in range(depth)]) for k, term in enumerate(terms)]
    input_grad = input_plane(1, odd_taps, next_lines + own_lines, half_grad)
    own_terms, input_grad = lax.optimization_barrier((own_terms, input_grad))
    scale = 1.0 / math.sqrt(depth * cells)
    weight_grad = call(
        functools.partial(total_kernel, scale),
        jax.ShapeDtypeStruct((chans, outs, 27), F32),
        own_terms,
        *terms,
        cost=(1 << 16, 1 << 19),
    )
    return input_grad, jnp.transpose(weight_grad, (2, 0, 1))


def solution(mesh):
    in_specs = (P("chan", "depth", None, None), P("chan", "depth", None, None), P())
    out_specs = (P("chan", "depth", None, None), P(None, "chan", "depth"))
    ring, depth = mesh.shape["chan"], mesh.shape["depth"]

    def either(grad_out, volume, weight):
        fits = (
            grad_out.shape[0] % 32 == 0
            and volume.shape[0] == 16
            and grad_out.shape[1] == 1
            and ring >= 4
            and ring & (ring - 1) == 0
            and depth & (depth - 1) == 0
            and depth % (2 * ring) == 0
        )
        return (shards if fits else plain_shards)(grad_out, volume, weight)

    return jax.shard_map(either, mesh=mesh, in_specs=in_specs, out_specs=out_specs, check_vma=False)
```

```python
import functools
import math

import jax
import jax.numpy as jnp
from jax import lax
from jax.experimental import pallas as pl
from jax.experimental.pallas import tpu as pltpu
from jax.sharding import PartitionSpec as P

F32 = jnp.float32
BF16 = jnp.bfloat16
VMEM = pl.BlockSpec(memory_space=pltpu.VMEM)
HBM = pl.BlockSpec(memory_space=pltpu.HBM)
LIMIT = 48 * 1024 * 1024


def matmul(left, right):
    return jnp.dot(left, right, preferred_element_type=F32)


def one_hot(rows, cols, source):
    row = lax.broadcasted_iota(jnp.int32, (rows, cols), 0)
    col = lax.broadcasted_iota(jnp.int32, (rows, cols), 1)
    return jnp.where(source(row, col), 1.0, 0.0).astype(BF16)


def swap_rows(major, minor):
    bits = minor.bit_length() - 1
    return one_hot(
        major * minor,
        major * minor,
        lambda row, col: col == (row & (minor - 1)) * major + (row >> bits),
    )


def place_views(plane, views_ref, base):
    chans, rows, cols = plane.shape
    half = cols // 2
    group = 256 // chans
    swap = swap_rows(group, chans)
    split = one_hot(cols, cols, lambda row, col: row == 2 * (col & (half - 1)) + col // half)
    inner = lax.broadcasted_iota(jnp.int32, (group * chans, half), 1) > 0
    for start in range(0, rows, group):
        block = plane[:, start : start + group, :].reshape(chans * group, cols)
        parted = matmul(matmul(swap, block).astype(BF16), split)
        odd = parted[:, half:]
        before = jnp.where(inner, pltpu.roll(odd, 1, 1), 0.0)
        views = [view.astype(BF16) for view in (before, parted[:, :half], odd)]
        for at in range(group):
            row = start + at
            lanes = slice(row // 2 * half, (row // 2 + 1) * half)
            for e in range(3):
                lo = base + (3 * (row % 2) + e) * chans
                views_ref[lo : lo + chans, lanes] = views[e][at * chans : (at + 1) * chans]


def own_views_kernel(depth, volume_ref, weight_ref, views_ref, even_ref, odd_ref):
    chans = volume_ref.shape[0]
    channels = weight_ref.shape[2]
    place_views(volume_ref.at[:, 0], views_ref, 0)
    place_views(volume_ref.at[:, 1], views_ref, 6 * chans)
    count = lax.axis_size("chan")
    part = channels // count
    here = lax.axis_index("chan")
    row = lax.broadcasted_iota(jnp.int32, (channels, channels), 0)
    col = lax.broadcasted_iota(jnp.int32, (channels, channels), 1)
    order = jnp.zeros((channels, channels), F32)
    for slot in range(count):
        moved = ((here ^ slot) - slot) * part
        inside = (col >= slot * part) & (col < (slot + 1) * part)
        order = jnp.where(inside & (row == col + moved), 1.0, order)
    ordered = matmul(weight_ref[...].reshape(27 * chans, channels), order.astype(BF16)).astype(BF16)
    beyond = jnp.where(lax.axis_index("depth") == depth - 1, 0.0, 1.0).astype(BF16)
    for k, e in enumerate((1, 2, 0)):
        for b in range(3):
            pick = lambda a: ordered[(9 * a + 3 * b + e) * chans : (9 * a + 3 * b + e + 1) * chans]
            lo = (3 * k + b) * chans
            even_ref[lo : lo + chans, :] = pick(1)
            odd_ref[lo : lo + chans, :] = jnp.concatenate([pick(0) * beyond, pick(2)], axis=1)


def behind_views_kernel(behind_ref, views_ref):
    first = lax.axis_index("depth") == 0

    @pl.when(jnp.logical_not(first))
    def _():
        place_views(behind_ref.at[:, 1], views_ref, 0)

    @pl.when(first)
    def _():
        views_ref[...] = jnp.zeros(views_ref.shape, BF16)


def place_lines(part, out_ref, at, wide_ref):
    outs, _, rows, cols = part.shape
    pitch = rows + 8
    for o in range(outs):
        wide_ref[o * pitch : o * pitch + rows, :] = part[o, 0].astype(F32)
    for row in range(rows):
        line = wide_ref[pl.ds(row, outs, stride=pitch), :].astype(BF16)
        out_ref[at : at + outs, row * cols : (row + 1) * cols] = line


def lines_kernel(*refs):
    *parts, out_ref, wide_ref = refs
    at = 0
    for part in parts:
        place_lines(part, out_ref, at, wide_ref)
        at += part.shape[0]


def weight_kernel(
    outs, cols, chunk, own_ref, behind_ref, *refs
):
    *line_refs, keep_ref, send_ref, terms_ref, placed_ref = refs
    channels = terms_ref.shape[1]
    chans = behind_ref.shape[0] // 6
    cells = own_ref.shape[1]
    contract = (((1,), (1,)), ((), ()))

    def grads(lo, hi):
        return jnp.concatenate([ref[:, lo:hi] for ref in line_refs], axis=0)

    pitch = chans + 8
    sums = None
    for lo in range(0, cells, chunk):
        hi = lo + chunk
        below = grads(lo + cols, min(hi + cols, cells))
        if hi == cells:
            below = jnp.concatenate([below, jnp.zeros((channels, cols), BF16)], axis=1)
        both = jnp.concatenate([grads(lo, hi), below], axis=0)
        views = jnp.concatenate([behind_ref[:, lo:hi], own_ref[:, lo:hi]], axis=0)
        part = lax.dot_general(views, both, contract, preferred_element_type=F32)
        sums = part if sums is None else sums + part
    for a in range(3):
        terms = sums[6 * a * chans : 6 * (a + 1) * chans]
        even, odd = terms[: 3 * chans, :channels], terms[3 * chans :]
        for b, block in enumerate((odd[:, channels:], even, odd[:, :channels])):
            for e in range(3):
                lo = (9 * a + 3 * b + e) * pitch
                terms_ref[lo : lo + chans, :] = block[e * chans : (e + 1) * chans]
    terms_ref[27 * pitch :, :] = jnp.zeros((5 * pitch, channels), F32)
    for c in range(chans):
        placed_ref[32 * c : 32 * c + 32, :] = terms_ref[pl.ds(c, 32, stride=pitch), :]
    turned = placed_ref[...].T
    count = lax.axis_size("chan")
    part = channels // count
    odd_core = lax.axis_index("depth") % 2 == 1
    for slot in range(count):
        start = (lax.axis_index("chan") ^ slot) * (part // 2)
        for at in range(0, part // 2, outs):
            lo = slot * part + 2 * at
            even, odd = turned[lo : lo + outs], turned[lo + outs : lo + 2 * outs]
            place = pl.ds(pl.multiple_of(start + at, outs), outs)
            keep_ref[place, :] = jnp.where(odd_core, odd, even)
            send_ref[place, :] = jnp.where(odd_core, even, odd)


def pair_kernel(keep_ref, other_ref, *out_refs):
    chip = lax.axis_index("depth") // 2
    outs = out_refs[0].shape[0]
    for k, out_ref in enumerate(out_refs):
        place = pl.ds(pl.multiple_of((chip ^ k) * outs, outs), outs)
        out_ref[...] = keep_ref[place, :] + other_ref[place, :]


def input_kernel(plane, *refs):
    taps_ref, *line_refs, out_ref, cells_ref, lines_ref, rows_ref, sems = refs
    chans, rows, cols = rows_ref.shape
    half = cols // 2
    grid_cells = half * rows // 2
    grads = jnp.concatenate([ref[...] for ref in line_refs], axis=0)
    cells_ref[:, :grid_cells] = matmul(taps_ref[...], grads)
    cells_ref[:, grid_cells:] = jnp.zeros((cells_ref.shape[0], half), F32)
    group = 256 // chans
    pitch = chans + 8
    weave = one_hot(cols, cols, lambda row, col: col == 2 * (row & (half - 1)) + row // half)
    inner = lax.broadcasted_iota(jnp.int32, (chans, half), 1) < half - 1

    def cells(kind, b, r):
        lo = (3 * kind + b) * chans
        return cells_ref[lo : lo + chans, r * half : (r + 1) * half]

    copies = []
    for start in range(0, rows, group):
        pieces = []
        for row in range(start, start + group):
            r = row // 2
            if row % 2 == 0:
                even, odd, next_odd = [cells(kind, 1, r) for kind in range(3)]
            else:
                even, odd, next_odd = [cells(kind, 0, r + 1) + cells(kind, 2, r) for kind in range(3)]
            odd = odd + jnp.where(inner, pltpu.roll(next_odd, half - 1, 1), 0.0)
            pieces.append(jnp.concatenate([even, odd], axis=1).astype(BF16))
        woven = matmul(jnp.concatenate(pieces, axis=0), weave)
        for side in range(2):
            lanes = slice(side * half, (side + 1) * half)
            for at in range(group):
                lines_ref[side, at * pitch : at * pitch + chans] = woven[at * chans : (at + 1) * chans, lanes]
            for c in range(chans):
                line = lines_ref[side, pl.ds(c, group, stride=pitch), :].astype(BF16)
                rows_ref[c, start : start + group, lanes] = line
        place = pl.ds(start, group)
        copies.append(
            pltpu.make_async_copy(
                rows_ref.at[:, place], out_ref.at[:, plane, place], sems.at[start // group]
            )
        )
        copies[-1].start()
    for copy in copies:
        copy.wait()


def total_kernel(scale, *refs):
    *term_refs, out_ref = refs
    chans, outs, taps = out_ref.shape
    total = term_refs[0][...]
    for ref in term_refs[1:]:
        total = total + ref[...]
    total = total * scale
    for c in range(chans):
        out_ref[c] = total[:, 32 * c : 32 * c + taps]


def from_behind(shard, axis, by):
    count = lax.axis_size(axis)
    pairs = [(i, i + by) for i in range(count) if 0 <= i + by < count]
    return lax.ppermute(shard, axis, pairs)


def upsample(stacked, axis, extended):
    tap_zero, tap_one, tap_two = (stacked[0], stacked[1], stacked[2])
    coord_axis = axis - 1
    length = tap_zero.shape[coord_axis]
    if extended:
        outer = length - 1
        even_cells = lax.slice_in_dim(tap_one, 0, outer, axis=coord_axis)
        odd_cells = lax.slice_in_dim(tap_zero, 1, length, axis=coord_axis) + lax.slice_in_dim(
            tap_two, 0, outer, axis=coord_axis
        )
    else:
        outer = length
        shifted = lax.slice_in_dim(tap_zero, 1, length, axis=coord_axis)
        shifted = jnp.concatenate(
            [shifted, jnp.zeros_like(lax.slice_in_dim(tap_zero, 0, 1, axis=coord_axis))],
            axis=coord_axis,
        )
        even_cells = tap_one
        odd_cells = shifted + tap_two
    paired = jnp.stack([even_cells, odd_cells], axis=coord_axis + 1)
    new_shape = list(even_cells.shape)
    new_shape[coord_axis] = 2 * outer
    return paired.reshape(new_shape)


def phase_grads(weight_rows, grads_ext):
    local_in = weight_rows.shape[0] // 27
    channels_out, planes, rows, cols = grads_ext.shape
    taps_out = jnp.dot(
        weight_rows, grads_ext.reshape(channels_out, -1), preferred_element_type=jnp.float32
    )
    taps_out = taps_out.reshape(3, 3, 3, local_in, planes, rows, cols)
    along_w = upsample(jnp.moveaxis(taps_out, 2, 0), 6, False)
    along_h = upsample(jnp.moveaxis(along_w, 1, 0), 4, False)
    return upsample(along_h, 2, True)


def weight_terms(inputs, grads_ext):
    row_extra = 0
    weight_cube = lax.conv_general_dilated(
        inputs[None],
        grads_ext[:, None],
        (1, 1, 1),
        ((1, 2), (1, row_extra), (1, 0)),
        rhs_dilation=(2, 2, 2),
        dimension_numbers=("CNDHW", "OIDHW", "NCDHW"),
        preferred_element_type=jnp.float32,
    )
    return jnp.transpose(weight_cube, (2, 3, 4, 0, 1)).reshape(
        27, weight_cube.shape[0], weight_cube.shape[1]
    )


def plain_shards(grad_out, volume, weight):
    plane_next = from_behind(grad_out, "depth", -1)
    grads_ext = jnp.concatenate([grad_out, plane_next], axis=1)
    channels_out = weight.shape[2]
    local_in = volume.shape[0]
    every_channel = lax.all_gather(grads_ext, "chan", axis=0, tiled=True)
    own_weight = lax.dynamic_slice_in_dim(weight, lax.axis_index("chan") * local_in, local_in, 1)
    input_part = phase_grads(own_weight.reshape(27 * local_in, channels_out), every_channel)
    weight_part = weight_terms(volume, every_channel)
    input_grad = input_part.astype(jnp.bfloat16)
    summed = lax.psum_scatter(weight_part, "depth", scatter_dimension=2, tiled=True)
    cell_count = grad_out.shape[1] * lax.axis_size("depth") * grad_out.shape[2] * grad_out.shape[3]
    return (input_grad, summed * (1.0 / math.sqrt(cell_count)))


def call(kernel, out_shape, *args, scratch=(), cost=None):
    flops, moved = cost
    return pl.pallas_call(
        kernel,
        out_shape=out_shape,
        in_specs=[VMEM] * len(args),
        out_specs=jax.tree.map(lambda _: VMEM, out_shape),
        scratch_shapes=scratch,
        compiler_params=pltpu.CompilerParams(vmem_limit_bytes=LIMIT),
        cost_estimate=pl.CostEstimate(flops=flops, bytes_accessed=moved, transcendentals=0),
    )(*args)


def shards(grad_out, volume, weight):
    count = lax.axis_size("chan")
    depth = lax.axis_size("depth")
    own_outs, _, rows, cols = grad_out.shape
    chans = volume.shape[0]
    channels = weight.shape[2]
    cells = rows * cols
    farther = [(i, (i + 1) % depth) for i in range(depth)]
    nearer = [(b, a) for a, b in farther]

    own_weight = lax.dynamic_slice_in_dim(weight, lax.axis_index("chan") * chans, chans, 1)
    views, even_taps, odd_taps = call(
        lambda *refs: own_views_kernel(depth, *refs),
        (
            jax.ShapeDtypeStruct((12 * chans, cells), BF16),
            jax.ShapeDtypeStruct((9 * chans, channels), BF16),
            jax.ShapeDtypeStruct((9 * chans, 2 * channels), BF16),
        ),
        volume,
        own_weight,
        cost=(2 * 2 * 2 * cells * chans * 8 * cols, 4 << 20),
    )
    pairs = lambda mask: [(i, i ^ mask) for i in range(count)]
    middle = own_outs // 2
    by_two = lax.ppermute(grad_out[:middle], "chan", pairs(2))
    by_one = lax.ppermute(grad_out, "chan", pairs(1))
    own, by_two, views = lax.optimization_barrier((grad_out, by_two, views))
    by_two_later = lax.ppermute(own[middle:], "chan", pairs(2))
    by_three = lax.ppermute(by_two, "chan", pairs(1))
    by_three_later = lax.ppermute(by_two_later, "chan", pairs(1))
    lines = lambda *parts: call(
        lines_kernel,
        jax.ShapeDtypeStruct((sum(part.shape[0] for part in parts), cells), BF16),
        *parts,
        scratch=(pltpu.VMEM((own_outs * (rows + 8), cols), F32),),
        cost=(1 << 20, 2 << 20),
    )
    behind = lax.ppermute(volume, "depth", farther)
    next_own = lax.ppermute(own, "depth", nearer)
    behind_views = call(
        behind_views_kernel,
        jax.ShapeDtypeStruct((6 * chans, cells), BF16),
        behind,
        cost=(2 * 2 * cells * chans * 8 * cols, 2 << 20),
    )
    first_lines, next_first_lines = lines(grad_out), lines(next_own)
    second_lines = lines(by_one, by_two)
    by_three, behind_views, first_lines, next_first_lines = lax.optimization_barrier(
        (by_three, behind_views, first_lines, next_first_lines)
    )
    later_lines = [second_lines, lines(by_two_later, by_three), lines(by_three_later)]
    own_lines = [first_lines] + later_lines
    next_lines = [next_first_lines] + [lax.ppermute(part, "depth", nearer) for part in later_lines]
    outs = channels // depth
    half_terms = jax.ShapeDtypeStruct((channels // 2, 32 * chans), F32)
    keep, send = call(
        lambda *refs: weight_kernel(outs, cols, 4 * cols, *refs),
        (half_terms, half_terms),
        views,
        behind_views,
        *own_lines,
        scratch=(
            pltpu.VMEM((32 * (chans + 8), channels), F32),
            pltpu.VMEM((32 * chans, channels), F32),
        ),
        cost=(2 * 27 * chans * channels * cells, 8 << 20),
    )
    def input_plane(plane, taps, lines, before):
        kernel = functools.partial(input_kernel, plane)
        earlier = [] if before is None else [before]
        return pl.pallas_call(
            kernel if before is None else lambda before, *refs: kernel(*refs),
            out_shape=jax.ShapeDtypeStruct(volume.shape, BF16),
            in_specs=[HBM] * len(earlier) + [VMEM] * (1 + len(lines)),
            out_specs=HBM,
            input_output_aliases={} if before is None else {0: 0},
            scratch_shapes=(
                pltpu.VMEM((9 * chans, cells + cols), F32),
                pltpu.VMEM((2, 256 // chans * (chans + 8), cols), F32),
                pltpu.VMEM((chans, 2 * rows, 2 * cols), BF16),
                pltpu.SemaphoreType.DMA((2 * rows * chans // 256,)),
            ),
            compiler_params=pltpu.CompilerParams(vmem_limit_bytes=LIMIT),
            cost_estimate=pl.CostEstimate(
                flops=2 * 9 * chans * taps.shape[1] * cells, bytes_accessed=4 << 20, transcendentals=0
            ),
        )(*earlier, taps, *lines)

    other = lax.ppermute(send, "depth", [(i, i ^ 1) for i in range(depth)])
    half_grad = input_plane(0, even_taps, own_lines, None)
    other, half_grad = lax.optimization_barrier((other, half_grad))
    own_terms, *terms = call(
        pair_kernel,
        [jax.ShapeDtypeStruct((outs, 32 * chans), F32)] * (depth // 2),
        keep,
        other,
        cost=(1 << 16, 1 << 19),
    )
    terms = [lax.ppermute(term, "depth", [(i, i ^ (2 * k + 2)) for i in range(depth)]) for k, term in enumerate(terms)]
    input_grad = input_plane(1, odd_taps, next_lines + own_lines, half_grad)
    own_terms, input_grad = lax.optimization_barrier((own_terms, input_grad))
    scale = 1.0 / math.sqrt(depth * cells)
    weight_grad = call(
        functools.partial(total_kernel, scale),
        jax.ShapeDtypeStruct((chans, outs, 27), F32),
        own_terms,
        *terms,
        cost=(1 << 16, 1 << 19),
    )
    return input_grad, jnp.transpose(weight_grad, (2, 0, 1))


def solution(mesh):
    in_specs = (P("chan", "depth", None, None), P("chan", "depth", None, None), P())
    out_specs = (P("chan", "depth", None, None), P(None, "chan", "depth"))
    ring, depth = mesh.shape["chan"], mesh.shape["depth"]

    def either(grad_out, volume, weight):
        fits = (
            grad_out.shape[0] % 32 == 0
            and volume.shape[0] == 16
            and grad_out.shape[1] == 1
            and ring == 4
            and ring & (ring - 1) == 0
            and depth & (depth - 1) == 0
            and depth % (2 * ring) == 0
        )
        return (shards if fits else plain_shards)(grad_out, volume, weight)

    return jax.shard_map(either, mesh=mesh, in_specs=in_specs, out_specs=out_specs, check_vma=False)
```

```python
import functools
import math

import jax
import jax.numpy as jnp
from jax import lax
from jax.experimental import pallas as pl
from jax.experimental.pallas import tpu as pltpu
from jax.sharding import PartitionSpec as P

F32 = jnp.float32
BF16 = jnp.bfloat16
VMEM = pl.BlockSpec(memory_space=pltpu.VMEM)
HBM = pl.BlockSpec(memory_space=pltpu.HBM)
LIMIT = 48 * 1024 * 1024


def matmul(left, right):
    return jnp.dot(left, right, preferred_element_type=F32)


def one_hot(rows, cols, source):
    row = lax.broadcasted_iota(jnp.int32, (rows, cols), 0)
    col = lax.broadcasted_iota(jnp.int32, (rows, cols), 1)
    return jnp.where(source(row, col), 1.0, 0.0).astype(BF16)


def swap_rows(major, minor):
    bits = minor.bit_length() - 1
    return one_hot(
        major * minor,
        major * minor,
        lambda row, col: col == (row & (minor - 1)) * major + (row >> bits),
    )


def place_views(plane, views_ref, base):
    chans, rows, cols = plane.shape
    half = cols // 2
    group = 256 // chans
    swap = swap_rows(group, chans)
    split = one_hot(cols, cols, lambda row, col: row == 2 * (col & (half - 1)) + col // half)
    inner = lax.broadcasted_iota(jnp.int32, (group * chans, half), 1) > 0
    for start in range(0, rows, group):
        block = plane[:, start : start + group, :].reshape(chans * group, cols)
        parted = matmul(matmul(swap, block).astype(BF16), split)
        odd = parted[:, half:]
        before = jnp.where(inner, pltpu.roll(odd, 1, 1), 0.0)
        views = [view.astype(BF16) for view in (before, parted[:, :half], odd)]
        for at in range(group):
            row = start + at
            lanes = slice(row // 2 * half, (row // 2 + 1) * half)
            for e in range(3):
                lo = base + (3 * (row % 2) + e) * chans
                views_ref[lo : lo + chans, lanes] = views[e][at * chans : (at + 1) * chans]


def own_views_kernel(depth, volume_ref, weight_ref, views_ref, even_ref, odd_ref):
    chans = volume_ref.shape[0]
    channels = weight_ref.shape[2]
    place_views(volume_ref.at[:, 0], views_ref, 0)
    place_views(volume_ref.at[:, 1], views_ref, 6 * chans)
    count = lax.axis_size("chan")
    part = channels // count
    here = lax.axis_index("chan")
    row = lax.broadcasted_iota(jnp.int32, (channels, channels), 0)
    col = lax.broadcasted_iota(jnp.int32, (channels, channels), 1)
    order = jnp.zeros((channels, channels), F32)
    for slot in range(count):
        moved = ((here ^ slot) - slot) * part
        inside = (col >= slot * part) & (col < (slot + 1) * part)
        order = jnp.where(inside & (row == col + moved), 1.0, order)
    ordered = matmul(weight_ref[...].reshape(27 * chans, channels), order.astype(BF16)).astype(BF16)
    beyond = jnp.where(lax.axis_index("depth") == depth - 1, 0.0, 1.0).astype(BF16)
    for k, e in enumerate((1, 2, 0)):
        for b in range(3):
            pick = lambda a: ordered[(9 * a + 3 * b + e) * chans : (9 * a + 3 * b + e + 1) * chans]
            lo = (3 * k + b) * chans
            even_ref[lo : lo + chans, :] = pick(1)
            odd_ref[lo : lo + chans, :] = jnp.concatenate([pick(0) * beyond, pick(2)], axis=1)


def behind_views_kernel(behind_ref, views_ref):
    first = lax.axis_index("depth") == 0

    @pl.when(jnp.logical_not(first))
    def _():
        place_views(behind_ref.at[:, 1], views_ref, 0)

    @pl.when(first)
    def _():
        views_ref[...] = jnp.zeros(views_ref.shape, BF16)


def place_lines(part, out_ref, at, wide_ref):
    outs, _, rows, cols = part.shape
    pitch = rows + 8
    for o in range(outs):
        wide_ref[o * pitch : o * pitch + rows, :] = part[o, 0].astype(F32)
    for row in range(rows):
        line = wide_ref[pl.ds(row, outs, stride=pitch), :].astype(BF16)
        out_ref[at : at + outs, row * cols : (row + 1) * cols] = line


def lines_kernel(*refs):
    *parts, out_ref, wide_ref = refs
    at = 0
    for part in parts:
        place_lines(part, out_ref, at, wide_ref)
        at += part.shape[0]


def weight_kernel(
    outs, cols, chunk, own_ref, behind_ref, *refs
):
    *line_refs, keep_ref, send_ref, terms_ref, placed_ref = refs
    channels = terms_ref.shape[1]
    chans = behind_ref.shape[0] // 6
    cells = own_ref.shape[1]
    contract = (((1,), (1,)), ((), ()))

    def grads(lo, hi):
        return jnp.concatenate([ref[:, lo:hi] for ref in line_refs], axis=0)

    pitch = chans + 8
    sums = None
    for lo in range(0, cells, chunk):
        hi = lo + chunk
        below = grads(lo + cols, min(hi + cols, cells))
        if hi == cells:
            below = jnp.concatenate([below, jnp.zeros((channels, cols), BF16)], axis=1)
        both = jnp.concatenate([grads(lo, hi), below], axis=0)
        views = jnp.concatenate([behind_ref[:, lo:hi], own_ref[:, lo:hi]], axis=0)
        part = lax.dot_general(views, both, contract, preferred_element_type=F32)
        sums = part if sums is None else sums + part
    for a in range(3):
        terms = sums[6 * a * chans : 6 * (a + 1) * chans]
        even, odd = terms[: 3 * chans, :channels], terms[3 * chans :]
        for b, block in enumerate((odd[:, channels:], even, odd[:, :channels])):
            for e in range(3):
                lo = (9 * a + 3 * b + e) * pitch
                terms_ref[lo : lo + chans, :] = block[e * chans : (e + 1) * chans]
    terms_ref[27 * pitch :, :] = jnp.zeros((5 * pitch, channels), F32)
    for c in range(chans):
        placed_ref[32 * c : 32 * c + 32, :] = terms_ref[pl.ds(c, 32, stride=pitch), :]
    turned = placed_ref[...].T
    count = lax.axis_size("chan")
    part = channels // count
    odd_core = lax.axis_index("depth") % 2 == 1
    for slot in range(count):
        start = (lax.axis_index("chan") ^ slot) * (part // 2)
        for at in range(0, part // 2, outs):
            lo = slot * part + 2 * at
            even, odd = turned[lo : lo + outs], turned[lo + outs : lo + 2 * outs]
            place = pl.ds(pl.multiple_of(start + at, outs), outs)
            keep_ref[place, :] = jnp.where(odd_core, odd, even)
            send_ref[place, :] = jnp.where(odd_core, even, odd)


def pair_kernel(keep_ref, other_ref, *out_refs):
    chip = lax.axis_index("depth") // 2
    outs = out_refs[0].shape[0]
    for k, out_ref in enumerate(out_refs):
        place = pl.ds(pl.multiple_of((chip ^ k) * outs, outs), outs)
        out_ref[...] = keep_ref[place, :] + other_ref[place, :]


def input_kernel(plane, *refs):
    taps_ref, *line_refs, out_ref, cells_ref, lines_ref, rows_ref, sems = refs
    chans, rows, cols = rows_ref.shape
    half = cols // 2
    grid_cells = half * rows // 2
    cells_ref[:, grid_cells:] = jnp.zeros((cells_ref.shape[0], half), F32)
    group = 256 // chans

    def compute(start):
        lanes = slice(start // 2 * half, (start + group) // 2 * half)
        grads = jnp.concatenate([ref[:, lanes] for ref in line_refs], axis=0)
        cells_ref[:, lanes] = matmul(taps_ref[...], grads)

    compute(0)
    pitch = chans + 8
    weave = one_hot(cols, cols, lambda row, col: col == 2 * (row & (half - 1)) + row // half)
    inner = lax.broadcasted_iota(jnp.int32, (chans, half), 1) < half - 1

    def cells(kind, b, r):
        lo = (3 * kind + b) * chans
        return cells_ref[lo : lo + chans, r * half : (r + 1) * half]

    copies = []
    for start in range(0, rows, group):
        if start + group < rows:
            compute(start + group)
        pieces = []
        for row in range(start, start + group):
            r = row // 2
            if row % 2 == 0:
                even, odd, next_odd = [cells(kind, 1, r) for kind in range(3)]
            else:
                even, odd, next_odd = [cells(kind, 0, r + 1) + cells(kind, 2, r) for kind in range(3)]
            odd = odd + jnp.where(inner, pltpu.roll(next_odd, half - 1, 1), 0.0)
            pieces.append(jnp.concatenate([even, odd], axis=1).astype(BF16))
        woven = matmul(jnp.concatenate(pieces, axis=0), weave)
        for side in range(2):
            lanes = slice(side * half, (side + 1) * half)
            for at in range(group):
                lines_ref[side, at * pitch : at * pitch + chans] = woven[at * chans : (at + 1) * chans, lanes]
            for c in range(chans):
                line = lines_ref[side, pl.ds(c, group, stride=pitch), :].astype(BF16)
                rows_ref[c, start : start + group, lanes] = line
        place = pl.ds(start, group)
        copies.append(
            pltpu.make_async_copy(
                rows_ref.at[:, place], out_ref.at[:, plane, place], sems.at[start // group]
            )
        )
        copies[-1].start()
    for copy in copies:
        copy.wait()


def total_kernel(scale, *refs):
    *term_refs, out_ref = refs
    chans, outs, taps = out_ref.shape
    total = term_refs[0][...]
    for ref in term_refs[1:]:
        total = total + ref[...]
    total = total * scale
    for c in range(chans):
        out_ref[c] = total[:, 32 * c : 32 * c + taps]


def from_behind(shard, axis, by):
    count = lax.axis_size(axis)
    pairs = [(i, i + by) for i in range(count) if 0 <= i + by < count]
    return lax.ppermute(shard, axis, pairs)


def upsample(stacked, axis, extended):
    tap_zero, tap_one, tap_two = (stacked[0], stacked[1], stacked[2])
    coord_axis = axis - 1
    length = tap_zero.shape[coord_axis]
    if extended:
        outer = length - 1
        even_cells = lax.slice_in_dim(tap_one, 0, outer, axis=coord_axis)
        odd_cells = lax.slice_in_dim(tap_zero, 1, length, axis=coord_axis) + lax.slice_in_dim(
            tap_two, 0, outer, axis=coord_axis
        )
    else:
        outer = length
        shifted = lax.slice_in_dim(tap_zero, 1, length, axis=coord_axis)
        shifted = jnp.concatenate(
            [shifted, jnp.zeros_like(lax.slice_in_dim(tap_zero, 0, 1, axis=coord_axis))],
            axis=coord_axis,
        )
        even_cells = tap_one
        odd_cells = shifted + tap_two
    paired = jnp.stack([even_cells, odd_cells], axis=coord_axis + 1)
    new_shape = list(even_cells.shape)
    new_shape[coord_axis] = 2 * outer
    return paired.reshape(new_shape)


def phase_grads(weight_rows, grads_ext):
    local_in = weight_rows.shape[0] // 27
    channels_out, planes, rows, cols = grads_ext.shape
    taps_out = jnp.dot(
        weight_rows, grads_ext.reshape(channels_out, -1), preferred_element_type=jnp.float32
    )
    taps_out = taps_out.reshape(3, 3, 3, local_in, planes, rows, cols)
    along_w = upsample(jnp.moveaxis(taps_out, 2, 0), 6, False)
    along_h = upsample(jnp.moveaxis(along_w, 1, 0), 4, False)
    return upsample(along_h, 2, True)


def weight_terms(inputs, grads_ext):
    row_extra = 0
    weight_cube = lax.conv_general_dilated(
        inputs[None],
        grads_ext[:, None],
        (1, 1, 1),
        ((1, 2), (1, row_extra), (1, 0)),
        rhs_dilation=(2, 2, 2),
        dimension_numbers=("CNDHW", "OIDHW", "NCDHW"),
        preferred_element_type=jnp.float32,
    )
    return jnp.transpose(weight_cube, (2, 3, 4, 0, 1)).reshape(
        27, weight_cube.shape[0], weight_cube.shape[1]
    )


def plain_shards(grad_out, volume, weight):
    plane_next = from_behind(grad_out, "depth", -1)
    grads_ext = jnp.concatenate([grad_out, plane_next], axis=1)
    channels_out = weight.shape[2]
    local_in = volume.shape[0]
    every_channel = lax.all_gather(grads_ext, "chan", axis=0, tiled=True)
    own_weight = lax.dynamic_slice_in_dim(weight, lax.axis_index("chan") * local_in, local_in, 1)
    input_part = phase_grads(own_weight.reshape(27 * local_in, channels_out), every_channel)
    weight_part = weight_terms(volume, every_channel)
    input_grad = input_part.astype(jnp.bfloat16)
    summed = lax.psum_scatter(weight_part, "depth", scatter_dimension=2, tiled=True)
    cell_count = grad_out.shape[1] * lax.axis_size("depth") * grad_out.shape[2] * grad_out.shape[3]
    return (input_grad, summed * (1.0 / math.sqrt(cell_count)))


def call(kernel, out_shape, *args, scratch=(), cost=None):
    flops, moved = cost
    return pl.pallas_call(
        kernel,
        out_shape=out_shape,
        in_specs=[VMEM] * len(args),
        out_specs=jax.tree.map(lambda _: VMEM, out_shape),
        scratch_shapes=scratch,
        compiler_params=pltpu.CompilerParams(vmem_limit_bytes=LIMIT),
        cost_estimate=pl.CostEstimate(flops=flops, bytes_accessed=moved, transcendentals=0),
    )(*args)


def shards(grad_out, volume, weight):
    count = lax.axis_size("chan")
    depth = lax.axis_size("depth")
    own_outs, _, rows, cols = grad_out.shape
    chans = volume.shape[0]
    channels = weight.shape[2]
    cells = rows * cols
    farther = [(i, (i + 1) % depth) for i in range(depth)]
    nearer = [(b, a) for a, b in farther]

    own_weight = lax.dynamic_slice_in_dim(weight, lax.axis_index("chan") * chans, chans, 1)
    views, even_taps, odd_taps = call(
        lambda *refs: own_views_kernel(depth, *refs),
        (
            jax.ShapeDtypeStruct((12 * chans, cells), BF16),
            jax.ShapeDtypeStruct((9 * chans, channels), BF16),
            jax.ShapeDtypeStruct((9 * chans, 2 * channels), BF16),
        ),
        volume,
        own_weight,
        cost=(2 * 2 * 2 * cells * chans * 8 * cols, 4 << 20),
    )
    got = {0: grad_out}
    for mask in sorted(range(1, count), key=lambda mask: (mask & (mask - 1) > 0, -mask)):
        low = mask & -mask
        if mask == 3:
            got[2], views = lax.optimization_barrier((got[2], views))
        got[mask] = lax.ppermute(got[mask - low], "chan", [(i, i ^ low) for i in range(count)])
    lines = lambda *parts: call(
        lines_kernel,
        jax.ShapeDtypeStruct((sum(part.shape[0] for part in parts), cells), BF16),
        *parts,
        scratch=(pltpu.VMEM((own_outs * (rows + 8), cols), F32),),
        cost=(1 << 20, 2 << 20),
    )
    behind = lax.ppermute(volume, "depth", farther)
    next_own = lax.ppermute(grad_out, "depth", nearer)
    behind_views = call(
        behind_views_kernel,
        jax.ShapeDtypeStruct((6 * chans, cells), BF16),
        behind,
        cost=(2 * 2 * cells * chans * 8 * cols, 2 << 20),
    )
    first_lines, next_first_lines = lines(grad_out), lines(next_own)
    got[1], views, behind_views, first_lines, next_first_lines = lax.optimization_barrier(
        (got[1], views, behind_views, first_lines, next_first_lines)
    )
    later_lines = [lines(*[got[mask] for mask in range(1, count - 1)]), lines(got[count - 1])]
    own_lines = [first_lines] + later_lines
    next_lines = [next_first_lines] + [lax.ppermute(part, "depth", nearer) for part in later_lines]
    outs = channels // depth
    half_terms = jax.ShapeDtypeStruct((channels // 2, 32 * chans), F32)
    keep, send = call(
        lambda *refs: weight_kernel(outs, cols, 4 * cols, *refs),
        (half_terms, half_terms),
        views,
        behind_views,
        *own_lines,
        scratch=(
            pltpu.VMEM((32 * (chans + 8), channels), F32),
            pltpu.VMEM((32 * chans, channels), F32),
        ),
        cost=(2 * 27 * chans * channels * cells, 8 << 20),
    )
    def input_plane(plane, taps, lines, before):
        kernel = functools.partial(input_kernel, plane)
        earlier = [] if before is None else [before]
        return pl.pallas_call(
            kernel if before is None else lambda before, *refs: kernel(*refs),
            out_shape=jax.ShapeDtypeStruct(volume.shape, BF16),
            in_specs=[HBM] * len(earlier) + [VMEM] * (1 + len(lines)),
            out_specs=HBM,
            input_output_aliases={} if before is None else {0: 0},
            scratch_shapes=(
                pltpu.VMEM((9 * chans, cells + cols), F32),
                pltpu.VMEM((2, 256 // chans * (chans + 8), cols), F32),
                pltpu.VMEM((chans, 2 * rows, 2 * cols), BF16),
                pltpu.SemaphoreType.DMA((2 * rows * chans // 256,)),
            ),
            compiler_params=pltpu.CompilerParams(vmem_limit_bytes=LIMIT),
            cost_estimate=pl.CostEstimate(
                flops=2 * 9 * chans * taps.shape[1] * cells, bytes_accessed=4 << 20, transcendentals=0
            ),
        )(*earlier, taps, *lines)

    other = lax.ppermute(send, "depth", [(i, i ^ 1) for i in range(depth)])
    half_grad = input_plane(0, even_taps, own_lines, None)
    other, half_grad = lax.optimization_barrier((other, half_grad))
    own_terms, *terms = call(
        pair_kernel,
        [jax.ShapeDtypeStruct((outs, 32 * chans), F32)] * (depth // 2),
        keep,
        other,
        cost=(1 << 16, 1 << 19),
    )
    terms = [
        lax.ppermute(terms[k - 1], "depth", [(i, i ^ (2 * k)) for i in range(depth)])
        for k in range(depth // 2 - 1, 0, -1)
    ]
    input_grad = input_plane(1, odd_taps, next_lines + own_lines, half_grad)
    own_terms, input_grad = lax.optimization_barrier((own_terms, input_grad))
    scale = 1.0 / math.sqrt(depth * cells)
    weight_grad = call(
        functools.partial(total_kernel, scale),
        jax.ShapeDtypeStruct((chans, outs, 27), F32),
        own_terms,
        *terms,
        cost=(1 << 16, 1 << 19),
    )
    return input_grad, jnp.transpose(weight_grad, (2, 0, 1))


def solution(mesh):
    in_specs = (P("chan", "depth", None, None), P("chan", "depth", None, None), P())
    out_specs = (P("chan", "depth", None, None), P(None, "chan", "depth"))
    ring, depth = mesh.shape["chan"], mesh.shape["depth"]

    def either(grad_out, volume, weight):
        fits = (
            grad_out.shape[0] % 32 == 0
            and volume.shape[0] == 16
            and grad_out.shape[1] == 1
            and ring >= 4
            and ring & (ring - 1) == 0
            and depth & (depth - 1) == 0
            and depth % (2 * ring) == 0
        )
        return (shards if fits else plain_shards)(grad_out, volume, weight)

    return jax.shard_map(either, mesh=mesh, in_specs=in_specs, out_specs=out_specs, check_vma=False)
```

```python
import functools
import math

import jax
import jax.numpy as jnp
from jax import lax
from jax.experimental import pallas as pl
from jax.experimental.pallas import tpu as pltpu
from jax.sharding import PartitionSpec as P

F32 = jnp.float32
BF16 = jnp.bfloat16
VMEM = pl.BlockSpec(memory_space=pltpu.VMEM)
HBM = pl.BlockSpec(memory_space=pltpu.HBM)
LIMIT = 48 * 1024 * 1024


def matmul(left, right):
    return jnp.dot(left, right, preferred_element_type=F32)


def one_hot(rows, cols, source):
    row = lax.broadcasted_iota(jnp.int32, (rows, cols), 0)
    col = lax.broadcasted_iota(jnp.int32, (rows, cols), 1)
    return jnp.where(source(row, col), 1.0, 0.0).astype(BF16)


def swap_rows(major, minor):
    bits = minor.bit_length() - 1
    return one_hot(
        major * minor,
        major * minor,
        lambda row, col: col == (row & (minor - 1)) * major + (row >> bits),
    )


def place_views(plane, views_ref, base):
    chans, rows, cols = plane.shape
    half = cols // 2
    group = 256 // chans
    swap = swap_rows(group, chans)
    split = one_hot(cols, cols, lambda row, col: row == 2 * (col & (half - 1)) + col // half)
    inner = lax.broadcasted_iota(jnp.int32, (group * chans, half), 1) > 0
    for start in range(0, rows, group):
        block = plane[:, start : start + group, :].reshape(chans * group, cols)
        parted = matmul(matmul(swap, block).astype(BF16), split)
        odd = parted[:, half:]
        before = jnp.where(inner, pltpu.roll(odd, 1, 1), 0.0)
        views = [view.astype(BF16) for view in (before, parted[:, :half], odd)]
        for at in range(group):
            row = start + at
            lanes = slice(row // 2 * half, (row // 2 + 1) * half)
            for e in range(3):
                lo = base + (3 * (row % 2) + e) * chans
                views_ref[lo : lo + chans, lanes] = views[e][at * chans : (at + 1) * chans]


def own_views_kernel(depth, volume_ref, weight_ref, views_ref, even_ref, odd_ref):
    chans = volume_ref.shape[0]
    channels = weight_ref.shape[2]
    place_views(volume_ref.at[:, 0], views_ref, 0)
    place_views(volume_ref.at[:, 1], views_ref, 6 * chans)
    count = lax.axis_size("chan")
    part = channels // count
    here = lax.axis_index("chan")
    row = lax.broadcasted_iota(jnp.int32, (channels, channels), 0)
    col = lax.broadcasted_iota(jnp.int32, (channels, channels), 1)
    order = jnp.zeros((channels, channels), F32)
    for slot in range(count):
        moved = ((here ^ slot) - slot) * part
        inside = (col >= slot * part) & (col < (slot + 1) * part)
        order = jnp.where(inside & (row == col + moved), 1.0, order)
    ordered = matmul(weight_ref[...].reshape(27 * chans, channels), order.astype(BF16)).astype(BF16)
    beyond = jnp.where(lax.axis_index("depth") == depth - 1, 0.0, 1.0).astype(BF16)
    for k, e in enumerate((1, 2, 0)):
        for b in range(3):
            pick = lambda a: ordered[(9 * a + 3 * b + e) * chans : (9 * a + 3 * b + e + 1) * chans]
            lo = (3 * k + b) * chans
            even_ref[lo : lo + chans, :] = pick(1)
            odd_ref[lo : lo + chans, :] = jnp.concatenate([pick(0) * beyond, pick(2)], axis=1)


def behind_views_kernel(behind_ref, views_ref):
    first = lax.axis_index("depth") == 0

    @pl.when(jnp.logical_not(first))
    def _():
        place_views(behind_ref.at[:, 1], views_ref, 0)

    @pl.when(first)
    def _():
        views_ref[...] = jnp.zeros(views_ref.shape, BF16)


def place_lines(part, out_ref, at, wide_ref):
    outs, _, rows, cols = part.shape
    pitch = rows + 8
    for o in range(outs):
        wide_ref[o * pitch : o * pitch + rows, :] = part[o, 0].astype(F32)
    for row in range(rows):
        line = wide_ref[pl.ds(row, outs, stride=pitch), :].astype(BF16)
        out_ref[at : at + outs, row * cols : (row + 1) * cols] = line


def lines_kernel(*refs):
    *parts, out_ref, wide_ref = refs
    at = 0
    for part in parts:
        place_lines(part, out_ref, at, wide_ref)
        at += part.shape[0]


def weight_kernel(
    outs, cols, chunk, own_ref, behind_ref, *refs
):
    *line_refs, keep_ref, send_ref, terms_ref, placed_ref = refs
    channels = terms_ref.shape[1]
    chans = behind_ref.shape[0] // 6
    cells = own_ref.shape[1]
    contract = (((1,), (1,)), ((), ()))

    def grads(lo, hi):
        return jnp.concatenate([ref[:, lo:hi] for ref in line_refs], axis=0)

    pitch = chans + 8
    sums = None
    for lo in range(0, cells, chunk):
        hi = lo + chunk
        below = grads(lo + cols, min(hi + cols, cells))
        if hi == cells:
            below = jnp.concatenate([below, jnp.zeros((channels, cols), BF16)], axis=1)
        both = jnp.concatenate([grads(lo, hi), below], axis=0)
        views = jnp.concatenate([behind_ref[:, lo:hi], own_ref[:, lo:hi]], axis=0)
        part = lax.dot_general(views, both, contract, preferred_element_type=F32)
        sums = part if sums is None else sums + part
    for a in range(3):
        terms = sums[6 * a * chans : 6 * (a + 1) * chans]
        even, odd = terms[: 3 * chans, :channels], terms[3 * chans :]
        for b, block in enumerate((odd[:, channels:], even, odd[:, :channels])):
            for e in range(3):
                lo = (9 * a + 3 * b + e) * pitch
                terms_ref[lo : lo + chans, :] = block[e * chans : (e + 1) * chans]
    terms_ref[27 * pitch :, :] = jnp.zeros((5 * pitch, channels), F32)
    for c in range(chans):
        placed_ref[32 * c : 32 * c + 32, :] = terms_ref[pl.ds(c, 32, stride=pitch), :]
    turned = placed_ref[...].T
    count = lax.axis_size("chan")
    part = channels // count
    odd_core = lax.axis_index("depth") % 2 == 1
    for slot in range(count):
        start = (lax.axis_index("chan") ^ slot) * (part // 2)
        for at in range(0, part // 2, outs):
            lo = slot * part + 2 * at
            even, odd = turned[lo : lo + outs], turned[lo + outs : lo + 2 * outs]
            place = pl.ds(pl.multiple_of(start + at, outs), outs)
            keep_ref[place, :] = jnp.where(odd_core, odd, even)
            send_ref[place, :] = jnp.where(odd_core, even, odd)


def pair_kernel(keep_ref, other_ref, *out_refs):
    chip = lax.axis_index("depth") // 2
    outs = out_refs[0].shape[0]
    for k, out_ref in enumerate(out_refs):
        place = pl.ds(pl.multiple_of((chip ^ k) * outs, outs), outs)
        out_ref[...] = keep_ref[place, :] + other_ref[place, :]


def input_rows(taps_ref, line_refs, rows_ref, cells_ref, lines_ref, finished):
    chans, rows, cols = rows_ref.shape
    half = cols // 2
    grid_cells = half * rows // 2
    cells_ref[:, grid_cells:] = jnp.zeros((cells_ref.shape[0], half), F32)
    group = 256 // chans

    def compute(start):
        lanes = slice(start // 2 * half, (start + group) // 2 * half)
        grads = jnp.concatenate([ref[:, lanes] for ref in line_refs], axis=0)
        cells_ref[:, lanes] = matmul(taps_ref[...], grads)

    compute(0)
    pitch = chans + 8
    weave = one_hot(cols, cols, lambda row, col: col == 2 * (row & (half - 1)) + row // half)
    inner = lax.broadcasted_iota(jnp.int32, (chans, half), 1) < half - 1

    def cells(kind, b, r):
        lo = (3 * kind + b) * chans
        return cells_ref[lo : lo + chans, r * half : (r + 1) * half]

    for start in range(0, rows, group):
        if start + group < rows:
            compute(start + group)
        pieces = []
        for row in range(start, start + group):
            r = row // 2
            if row % 2 == 0:
                even, odd, next_odd = [cells(kind, 1, r) for kind in range(3)]
            else:
                even, odd, next_odd = [cells(kind, 0, r + 1) + cells(kind, 2, r) for kind in range(3)]
            odd = odd + jnp.where(inner, pltpu.roll(next_odd, half - 1, 1), 0.0)
            pieces.append(jnp.concatenate([even, odd], axis=1).astype(BF16))
        woven = matmul(jnp.concatenate(pieces, axis=0), weave)
        for side in range(2):
            lanes = slice(side * half, (side + 1) * half)
            for at in range(group):
                lines_ref[side, at * pitch : at * pitch + chans] = woven[at * chans : (at + 1) * chans, lanes]
            for c in range(chans):
                line = lines_ref[side, pl.ds(c, group, stride=pitch), :].astype(BF16)
                rows_ref[c, start : start + group, lanes] = line
        finished(start, group)


def even_kernel(taps_ref, *refs):
    *line_refs, rows_ref, cells_ref, lines_ref = refs
    input_rows(taps_ref, line_refs, rows_ref, cells_ref, lines_ref, lambda start, size: None)


def odd_kernel(even_ref, taps_ref, *refs):
    *line_refs, out_ref, cells_ref, lines_ref, rows_ref, even_sem, sems = refs
    copies = [pltpu.make_async_copy(even_ref, out_ref.at[:, 0], even_sem)]
    copies[0].start()

    def finished(start, size):
        place = pl.ds(start, size)
        copy = pltpu.make_async_copy(rows_ref.at[:, place], out_ref.at[:, 1, place], sems.at[start // size])
        copy.start()
        copies.append(copy)

    input_rows(taps_ref, line_refs, rows_ref, cells_ref, lines_ref, finished)
    for copy in copies:
        copy.wait()


def total_kernel(scale, *refs):
    *term_refs, out_ref = refs
    chans, outs, taps = out_ref.shape
    total = term_refs[0][...]
    for ref in term_refs[1:]:
        total = total + ref[...]
    total = total * scale
    for c in range(chans):
        out_ref[c] = total[:, 32 * c : 32 * c + taps]


def from_behind(shard, axis, by):
    count = lax.axis_size(axis)
    pairs = [(i, i + by) for i in range(count) if 0 <= i + by < count]
    return lax.ppermute(shard, axis, pairs)


def upsample(stacked, axis, extended):
    tap_zero, tap_one, tap_two = (stacked[0], stacked[1], stacked[2])
    coord_axis = axis - 1
    length = tap_zero.shape[coord_axis]
    if extended:
        outer = length - 1
        even_cells = lax.slice_in_dim(tap_one, 0, outer, axis=coord_axis)
        odd_cells = lax.slice_in_dim(tap_zero, 1, length, axis=coord_axis) + lax.slice_in_dim(
            tap_two, 0, outer, axis=coord_axis
        )
    else:
        outer = length
        shifted = lax.slice_in_dim(tap_zero, 1, length, axis=coord_axis)
        shifted = jnp.concatenate(
            [shifted, jnp.zeros_like(lax.slice_in_dim(tap_zero, 0, 1, axis=coord_axis))],
            axis=coord_axis,
        )
        even_cells = tap_one
        odd_cells = shifted + tap_two
    paired = jnp.stack([even_cells, odd_cells], axis=coord_axis + 1)
    new_shape = list(even_cells.shape)
    new_shape[coord_axis] = 2 * outer
    return paired.reshape(new_shape)


def phase_grads(weight_rows, grads_ext):
    local_in = weight_rows.shape[0] // 27
    channels_out, planes, rows, cols = grads_ext.shape
    taps_out = jnp.dot(
        weight_rows, grads_ext.reshape(channels_out, -1), preferred_element_type=jnp.float32
    )
    taps_out = taps_out.reshape(3, 3, 3, local_in, planes, rows, cols)
    along_w = upsample(jnp.moveaxis(taps_out, 2, 0), 6, False)
    along_h = upsample(jnp.moveaxis(along_w, 1, 0), 4, False)
    return upsample(along_h, 2, True)


def weight_terms(inputs, grads_ext):
    row_extra = 0
    weight_cube = lax.conv_general_dilated(
        inputs[None],
        grads_ext[:, None],
        (1, 1, 1),
        ((1, 2), (1, row_extra), (1, 0)),
        rhs_dilation=(2, 2, 2),
        dimension_numbers=("CNDHW", "OIDHW", "NCDHW"),
        preferred_element_type=jnp.float32,
    )
    return jnp.transpose(weight_cube, (2, 3, 4, 0, 1)).reshape(
        27, weight_cube.shape[0], weight_cube.shape[1]
    )


def plain_shards(grad_out, volume, weight):
    plane_next = from_behind(grad_out, "depth", -1)
    grads_ext = jnp.concatenate([grad_out, plane_next], axis=1)
    channels_out = weight.shape[2]
    local_in = volume.shape[0]
    every_channel = lax.all_gather(grads_ext, "chan", axis=0, tiled=True)
    own_weight = lax.dynamic_slice_in_dim(weight, lax.axis_index("chan") * local_in, local_in, 1)
    input_part = phase_grads(own_weight.reshape(27 * local_in, channels_out), every_channel)
    weight_part = weight_terms(volume, every_channel)
    input_grad = input_part.astype(jnp.bfloat16)
    summed = lax.psum_scatter(weight_part, "depth", scatter_dimension=2, tiled=True)
    cell_count = grad_out.shape[1] * lax.axis_size("depth") * grad_out.shape[2] * grad_out.shape[3]
    return (input_grad, summed * (1.0 / math.sqrt(cell_count)))


def call(kernel, out_shape, *args, out_spec=VMEM, scratch=(), cost=None):
    flops, moved = cost
    return pl.pallas_call(
        kernel,
        out_shape=out_shape,
        in_specs=[VMEM] * len(args),
        out_specs=jax.tree.map(lambda _: out_spec, out_shape),
        scratch_shapes=scratch,
        compiler_params=pltpu.CompilerParams(vmem_limit_bytes=LIMIT),
        cost_estimate=pl.CostEstimate(flops=flops, bytes_accessed=moved, transcendentals=0),
    )(*args)


def shards(grad_out, volume, weight):
    count = lax.axis_size("chan")
    depth = lax.axis_size("depth")
    own_outs, _, rows, cols = grad_out.shape
    chans = volume.shape[0]
    channels = weight.shape[2]
    cells = rows * cols
    farther = [(i, (i + 1) % depth) for i in range(depth)]
    nearer = [(b, a) for a, b in farther]

    own_weight = lax.dynamic_slice_in_dim(weight, lax.axis_index("chan") * chans, chans, 1)
    views, even_taps, odd_taps = call(
        lambda *refs: own_views_kernel(depth, *refs),
        (
            jax.ShapeDtypeStruct((12 * chans, cells), BF16),
            jax.ShapeDtypeStruct((9 * chans, channels), BF16),
            jax.ShapeDtypeStruct((9 * chans, 2 * channels), BF16),
        ),
        volume,
        own_weight,
        cost=(2 * 2 * 2 * cells * chans * 8 * cols, 4 << 20),
    )
    got = {0: grad_out}
    for mask in sorted(range(1, count), key=lambda mask: (mask & (mask - 1) > 0, -mask)):
        low = mask & -mask
        if mask == 3:
            got[2], views = lax.optimization_barrier((got[2], views))
        got[mask] = lax.ppermute(got[mask - low], "chan", [(i, i ^ low) for i in range(count)])
    lines = lambda *parts: call(
        lines_kernel,
        jax.ShapeDtypeStruct((sum(part.shape[0] for part in parts), cells), BF16),
        *parts,
        scratch=(pltpu.VMEM((own_outs * (rows + 8), cols), F32),),
        cost=(1 << 20, 2 << 20),
    )
    behind = lax.ppermute(volume, "depth", farther)
    next_own = lax.ppermute(grad_out, "depth", nearer)
    behind_views = call(
        behind_views_kernel,
        jax.ShapeDtypeStruct((6 * chans, cells), BF16),
        behind,
        cost=(2 * 2 * cells * chans * 8 * cols, 2 << 20),
    )
    first_lines, next_first_lines = lines(grad_out), lines(next_own)
    got[1], views, behind_views, first_lines, next_first_lines = lax.optimization_barrier(
        (got[1], views, behind_views, first_lines, next_first_lines)
    )
    later_lines = [lines(*[got[mask] for mask in range(1, count - 1)]), lines(got[count - 1])]
    own_lines = [first_lines] + later_lines
    next_lines = [next_first_lines] + [lax.ppermute(part, "depth", nearer) for part in later_lines]
    outs = channels // depth
    half_terms = jax.ShapeDtypeStruct((channels // 2, 32 * chans), F32)
    keep, send = call(
        lambda *refs: weight_kernel(outs, cols, 4 * cols, *refs),
        (half_terms, half_terms),
        views,
        behind_views,
        *own_lines,
        scratch=(
            pltpu.VMEM((32 * (chans + 8), channels), F32),
            pltpu.VMEM((32 * chans, channels), F32),
        ),
        cost=(2 * 27 * chans * channels * cells, 8 << 20),
    )
    cells_scratch = (
        pltpu.VMEM((9 * chans, cells + cols), F32),
        pltpu.VMEM((2, 256 // chans * (chans + 8), cols), F32),
    )
    plane = jax.ShapeDtypeStruct((chans, 2 * rows, 2 * cols), BF16)
    other = lax.ppermute(send, "depth", [(i, i ^ 1) for i in range(depth)])
    even_grad = call(
        even_kernel,
        plane,
        even_taps,
        *own_lines,
        scratch=cells_scratch,
        cost=(2 * 9 * chans * channels * cells, 4 << 20),
    )
    other, even_grad = lax.optimization_barrier((other, even_grad))
    own_terms, *terms = call(
        pair_kernel,
        [jax.ShapeDtypeStruct((outs, 32 * chans), F32)] * (depth // 2),
        keep,
        other,
        cost=(1 << 16, 1 << 19),
    )
    terms = [
        lax.ppermute(terms[k - 1], "depth", [(i, i ^ (2 * k)) for i in range(depth)])
        for k in range(depth // 2 - 1, 0, -1)
    ]
    input_grad = call(
        odd_kernel,
        jax.ShapeDtypeStruct(volume.shape, BF16),
        even_grad,
        odd_taps,
        *next_lines,
        *own_lines,
        out_spec=HBM,
        scratch=cells_scratch
        + (
            pltpu.VMEM(plane.shape, BF16),
            pltpu.SemaphoreType.DMA,
            pltpu.SemaphoreType.DMA((2 * rows * chans // 256,)),
        ),
        cost=(4 * 9 * chans * channels * cells, 4 << 20),
    )
    own_terms, input_grad = lax.optimization_barrier((own_terms, input_grad))
    scale = 1.0 / math.sqrt(depth * cells)
    weight_grad = call(
        functools.partial(total_kernel, scale),
        jax.ShapeDtypeStruct((chans, outs, 27), F32),
        own_terms,
        *terms,
        cost=(1 << 16, 1 << 19),
    )
    return input_grad, jnp.transpose(weight_grad, (2, 0, 1))


def solution(mesh):
    in_specs = (P("chan", "depth", None, None), P("chan", "depth", None, None), P())
    out_specs = (P("chan", "depth", None, None), P(None, "chan", "depth"))
    ring, depth = mesh.shape["chan"], mesh.shape["depth"]

    def either(grad_out, volume, weight):
        fits = (
            grad_out.shape[0] % 32 == 0
            and volume.shape[0] == 16
            and grad_out.shape[1] == 1
            and ring >= 4
            and ring & (ring - 1) == 0
            and depth & (depth - 1) == 0
            and depth % (2 * ring) == 0
        )
        return (shards if fits else plain_shards)(grad_out, volume, weight)

    return jax.shard_map(either, mesh=mesh, in_specs=in_specs, out_specs=out_specs, check_vma=False)
```

```python
import functools
import math

import jax
import jax.numpy as jnp
from jax import lax
from jax.experimental import pallas as pl
from jax.experimental.pallas import tpu as pltpu
from jax.sharding import PartitionSpec as P

F32 = jnp.float32
BF16 = jnp.bfloat16
VMEM = pl.BlockSpec(memory_space=pltpu.VMEM)
HBM = pl.BlockSpec(memory_space=pltpu.HBM)
LIMIT = 48 * 1024 * 1024


def matmul(left, right):
    return jnp.dot(left, right, preferred_element_type=F32)


def one_hot(rows, cols, source):
    row = lax.broadcasted_iota(jnp.int32, (rows, cols), 0)
    col = lax.broadcasted_iota(jnp.int32, (rows, cols), 1)
    return jnp.where(source(row, col), 1.0, 0.0).astype(BF16)


def swap_rows(major, minor):
    bits = minor.bit_length() - 1
    return one_hot(
        major * minor,
        major * minor,
        lambda row, col: col == (row & (minor - 1)) * major + (row >> bits),
    )


def place_views(plane, views_ref, base):
    chans, rows, cols = plane.shape
    half = cols // 2
    group = 256 // chans
    swap = swap_rows(group, chans)
    split = one_hot(cols, cols, lambda row, col: row == 2 * (col & (half - 1)) + col // half)
    inner = lax.broadcasted_iota(jnp.int32, (group * chans, half), 1) > 0
    for start in range(0, rows, group):
        block = plane[:, start : start + group, :].reshape(chans * group, cols)
        parted = matmul(matmul(swap, block).astype(BF16), split)
        odd = parted[:, half:]
        before = jnp.where(inner, pltpu.roll(odd, 1, 1), 0.0)
        views = [view.astype(BF16) for view in (before, parted[:, :half], odd)]
        for at in range(group):
            row = start + at
            lanes = slice(row // 2 * half, (row // 2 + 1) * half)
            for e in range(3):
                lo = base + (3 * (row % 2) + e) * chans
                views_ref[lo : lo + chans, lanes] = views[e][at * chans : (at + 1) * chans]


def own_views_kernel(depth, volume_ref, weight_ref, views_ref, even_ref, odd_ref):
    chans = volume_ref.shape[0]
    channels = weight_ref.shape[2]
    place_views(volume_ref.at[:, 0], views_ref, 0)
    place_views(volume_ref.at[:, 1], views_ref, 6 * chans)
    count = lax.axis_size("chan")
    part = channels // count
    here = lax.axis_index("chan")
    row = lax.broadcasted_iota(jnp.int32, (channels, channels), 0)
    col = lax.broadcasted_iota(jnp.int32, (channels, channels), 1)
    order = jnp.zeros((channels, channels), F32)
    for slot in range(count):
        moved = ((here ^ slot) - slot) * part
        inside = (col >= slot * part) & (col < (slot + 1) * part)
        order = jnp.where(inside & (row == col + moved), 1.0, order)
    ordered = matmul(weight_ref[...].reshape(27 * chans, channels), order.astype(BF16)).astype(BF16)
    beyond = jnp.where(lax.axis_index("depth") == depth - 1, 0.0, 1.0).astype(BF16)
    for k, e in enumerate((1, 2, 0)):
        for b in range(3):
            pick = lambda a: ordered[(9 * a + 3 * b + e) * chans : (9 * a + 3 * b + e + 1) * chans]
            lo = (3 * k + b) * chans
            even_ref[lo : lo + chans, :] = pick(1)
            odd_ref[lo : lo + chans, :] = jnp.concatenate([pick(0) * beyond, pick(2)], axis=1)


def behind_views_kernel(behind_ref, views_ref):
    first = lax.axis_index("depth") == 0

    @pl.when(jnp.logical_not(first))
    def _():
        place_views(behind_ref.at[:, 1], views_ref, 0)

    @pl.when(first)
    def _():
        views_ref[...] = jnp.zeros(views_ref.shape, BF16)


def place_lines(part, out_ref, at, wide_ref):
    outs, _, rows, cols = part.shape
    pitch = rows + 8
    for o in range(outs):
        wide_ref[o * pitch : o * pitch + rows, :] = part[o, 0].astype(F32)
    for row in range(rows):
        line = wide_ref[pl.ds(row, outs, stride=pitch), :].astype(BF16)
        out_ref[at : at + outs, row * cols : (row + 1) * cols] = line


def lines_kernel(*refs):
    *parts, out_ref, wide_ref = refs
    at = 0
    for part in parts:
        place_lines(part, out_ref, at, wide_ref)
        at += part.shape[0]


def weight_kernel(
    outs, cols, chunk, own_ref, behind_ref, *refs
):
    *line_refs, keep_ref, send_ref, terms_ref, placed_ref = refs
    channels = terms_ref.shape[1]
    chans = behind_ref.shape[0] // 6
    cells = own_ref.shape[1]
    contract = (((1,), (1,)), ((), ()))

    def grads(lo, hi):
        return jnp.concatenate([ref[:, lo:hi] for ref in line_refs], axis=0)

    pitch = chans + 8
    sums = None
    for lo in range(0, cells, chunk):
        hi = lo + chunk
        below = grads(lo + cols, min(hi + cols, cells))
        if hi == cells:
            below = jnp.concatenate([below, jnp.zeros((channels, cols), BF16)], axis=1)
        both = jnp.concatenate([grads(lo, hi), below], axis=0)
        views = jnp.concatenate([behind_ref[:, lo:hi], own_ref[:, lo:hi]], axis=0)
        part = lax.dot_general(views, both, contract, preferred_element_type=F32)
        sums = part if sums is None else sums + part
    for a in range(3):
        terms = sums[6 * a * chans : 6 * (a + 1) * chans]
        even, odd = terms[: 3 * chans, :channels], terms[3 * chans :]
        for b, block in enumerate((odd[:, channels:], even, odd[:, :channels])):
            for e in range(3):
                lo = (9 * a + 3 * b + e) * pitch
                terms_ref[lo : lo + chans, :] = block[e * chans : (e + 1) * chans]
    terms_ref[27 * pitch :, :] = jnp.zeros((5 * pitch, channels), F32)
    for c in range(chans):
        placed_ref[32 * c : 32 * c + 32, :] = terms_ref[pl.ds(c, 32, stride=pitch), :]
    turned = placed_ref[...].T
    count = lax.axis_size("chan")
    part = channels // count
    odd_core = lax.axis_index("depth") % 2 == 1
    for slot in range(count):
        start = (lax.axis_index("chan") ^ slot) * (part // 2)
        for at in range(0, part // 2, outs):
            lo = slot * part + 2 * at
            even, odd = turned[lo : lo + outs], turned[lo + outs : lo + 2 * outs]
            place = pl.ds(pl.multiple_of(start + at, outs), outs)
            keep_ref[place, :] = jnp.where(odd_core, odd, even)
            send_ref[place, :] = jnp.where(odd_core, even, odd)


def pair_kernel(keep_ref, other_ref, out_ref):
    out_ref[...] = keep_ref[...] + other_ref[...]


def input_rows(taps_ref, line_refs, rows_ref, cells_ref, lines_ref, finished):
    chans, rows, cols = rows_ref.shape
    half = cols // 2
    grid_cells = half * rows // 2
    cells_ref[:, grid_cells:] = jnp.zeros((cells_ref.shape[0], half), F32)
    group = 256 // chans

    def compute(start):
        lanes = slice(start // 2 * half, (start + group) // 2 * half)
        grads = jnp.concatenate([ref[:, lanes] for ref in line_refs], axis=0)
        cells_ref[:, lanes] = matmul(taps_ref[...], grads)

    compute(0)
    pitch = chans + 8
    weave = one_hot(cols, cols, lambda row, col: col == 2 * (row & (half - 1)) + row // half)
    inner = lax.broadcasted_iota(jnp.int32, (chans, half), 1) < half - 1

    def cells(kind, b, r):
        lo = (3 * kind + b) * chans
        return cells_ref[lo : lo + chans, r * half : (r + 1) * half]

    for start in range(0, rows, group):
        if start + group < rows:
            compute(start + group)
        pieces = []
        for row in range(start, start + group):
            r = row // 2
            if row % 2 == 0:
                even, odd, next_odd = [cells(kind, 1, r) for kind in range(3)]
            else:
                even, odd, next_odd = [cells(kind, 0, r + 1) + cells(kind, 2, r) for kind in range(3)]
            odd = odd + jnp.where(inner, pltpu.roll(next_odd, half - 1, 1), 0.0)
            pieces.append(jnp.concatenate([even, odd], axis=1).astype(BF16))
        woven = matmul(jnp.concatenate(pieces, axis=0), weave)
        for side in range(2):
            lanes = slice(side * half, (side + 1) * half)
            for at in range(group):
                lines_ref[side, at * pitch : at * pitch + chans] = woven[at * chans : (at + 1) * chans, lanes]
            for c in range(chans):
                line = lines_ref[side, pl.ds(c, group, stride=pitch), :].astype(BF16)
                rows_ref[c, start : start + group, lanes] = line
        finished(start, group)


def even_kernel(taps_ref, *refs):
    *line_refs, rows_ref, cells_ref, lines_ref = refs
    input_rows(taps_ref, line_refs, rows_ref, cells_ref, lines_ref, lambda start, size: None)


def odd_kernel(even_ref, taps_ref, *refs):
    *line_refs, out_ref, cells_ref, lines_ref, rows_ref, even_sem, sems = refs
    copies = [pltpu.make_async_copy(even_ref, out_ref.at[:, 0], even_sem)]
    copies[0].start()

    def finished(start, size):
        place = pl.ds(start, size)
        copy = pltpu.make_async_copy(rows_ref.at[:, place], out_ref.at[:, 1, place], sems.at[start // size])
        copy.start()
        copies.append(copy)

    input_rows(taps_ref, line_refs, rows_ref, cells_ref, lines_ref, finished)
    for copy in copies:
        copy.wait()


def total_kernel(scale, terms_ref, out_ref):
    chans, outs, taps = out_ref.shape
    total = terms_ref[0]
    for source in range(1, terms_ref.shape[0]):
        total = total + terms_ref[source]
    total = total * scale
    for c in range(chans):
        out_ref[c] = total[:, 32 * c : 32 * c + taps]


def from_behind(shard, axis, by):
    count = lax.axis_size(axis)
    pairs = [(i, i + by) for i in range(count) if 0 <= i + by < count]
    return lax.ppermute(shard, axis, pairs)


def upsample(stacked, axis, extended):
    tap_zero, tap_one, tap_two = (stacked[0], stacked[1], stacked[2])
    coord_axis = axis - 1
    length = tap_zero.shape[coord_axis]
    if extended:
        outer = length - 1
        even_cells = lax.slice_in_dim(tap_one, 0, outer, axis=coord_axis)
        odd_cells = lax.slice_in_dim(tap_zero, 1, length, axis=coord_axis) + lax.slice_in_dim(
            tap_two, 0, outer, axis=coord_axis
        )
    else:
        outer = length
        shifted = lax.slice_in_dim(tap_zero, 1, length, axis=coord_axis)
        shifted = jnp.concatenate(
            [shifted, jnp.zeros_like(lax.slice_in_dim(tap_zero, 0, 1, axis=coord_axis))],
            axis=coord_axis,
        )
        even_cells = tap_one
        odd_cells = shifted + tap_two
    paired = jnp.stack([even_cells, odd_cells], axis=coord_axis + 1)
    new_shape = list(even_cells.shape)
    new_shape[coord_axis] = 2 * outer
    return paired.reshape(new_shape)


def phase_grads(weight_rows, grads_ext):
    local_in = weight_rows.shape[0] // 27
    channels_out, planes, rows, cols = grads_ext.shape
    taps_out = jnp.dot(
        weight_rows, grads_ext.reshape(channels_out, -1), preferred_element_type=jnp.float32
    )
    taps_out = taps_out.reshape(3, 3, 3, local_in, planes, rows, cols)
    along_w = upsample(jnp.moveaxis(taps_out, 2, 0), 6, False)
    along_h = upsample(jnp.moveaxis(along_w, 1, 0), 4, False)
    return upsample(along_h, 2, True)


def weight_terms(inputs, grads_ext):
    row_extra = 0
    weight_cube = lax.conv_general_dilated(
        inputs[None],
        grads_ext[:, None],
        (1, 1, 1),
        ((1, 2), (1, row_extra), (1, 0)),
        rhs_dilation=(2, 2, 2),
        dimension_numbers=("CNDHW", "OIDHW", "NCDHW"),
        preferred_element_type=jnp.float32,
    )
    return jnp.transpose(weight_cube, (2, 3, 4, 0, 1)).reshape(
        27, weight_cube.shape[0], weight_cube.shape[1]
    )


def plain_shards(grad_out, volume, weight):
    plane_next = from_behind(grad_out, "depth", -1)
    grads_ext = jnp.concatenate([grad_out, plane_next], axis=1)
    channels_out = weight.shape[2]
    local_in = volume.shape[0]
    every_channel = lax.all_gather(grads_ext, "chan", axis=0, tiled=True)
    own_weight = lax.dynamic_slice_in_dim(weight, lax.axis_index("chan") * local_in, local_in, 1)
    input_part = phase_grads(own_weight.reshape(27 * local_in, channels_out), every_channel)
    weight_part = weight_terms(volume, every_channel)
    input_grad = input_part.astype(jnp.bfloat16)
    summed = lax.psum_scatter(weight_part, "depth", scatter_dimension=2, tiled=True)
    cell_count = grad_out.shape[1] * lax.axis_size("depth") * grad_out.shape[2] * grad_out.shape[3]
    return (input_grad, summed * (1.0 / math.sqrt(cell_count)))


def call(kernel, out_shape, *args, out_spec=VMEM, scratch=(), cost=None):
    flops, moved = cost
    return pl.pallas_call(
        kernel,
        out_shape=out_shape,
        in_specs=[VMEM] * len(args),
        out_specs=jax.tree.map(lambda _: out_spec, out_shape),
        scratch_shapes=scratch,
        compiler_params=pltpu.CompilerParams(vmem_limit_bytes=LIMIT),
        cost_estimate=pl.CostEstimate(flops=flops, bytes_accessed=moved, transcendentals=0),
    )(*args)


def shards(grad_out, volume, weight):
    count = lax.axis_size("chan")
    depth = lax.axis_size("depth")
    own_outs, _, rows, cols = grad_out.shape
    chans = volume.shape[0]
    channels = weight.shape[2]
    cells = rows * cols
    farther = [(i, (i + 1) % depth) for i in range(depth)]
    nearer = [(b, a) for a, b in farther]

    own_weight = lax.dynamic_slice_in_dim(weight, lax.axis_index("chan") * chans, chans, 1)
    views, even_taps, odd_taps = call(
        lambda *refs: own_views_kernel(depth, *refs),
        (
            jax.ShapeDtypeStruct((12 * chans, cells), BF16),
            jax.ShapeDtypeStruct((9 * chans, channels), BF16),
            jax.ShapeDtypeStruct((9 * chans, 2 * channels), BF16),
        ),
        volume,
        own_weight,
        cost=(2 * 2 * 2 * cells * chans * 8 * cols, 4 << 20),
    )
    got = {0: grad_out}
    for mask in sorted(range(1, count), key=lambda mask: (mask & (mask - 1) > 0, -mask)):
        low = mask & -mask
        if mask == 3:
            got[2], views = lax.optimization_barrier((got[2], views))
        got[mask] = lax.ppermute(got[mask - low], "chan", [(i, i ^ low) for i in range(count)])
    lines = lambda *parts: call(
        lines_kernel,
        jax.ShapeDtypeStruct((sum(part.shape[0] for part in parts), cells), BF16),
        *parts,
        scratch=(pltpu.VMEM((own_outs * (rows + 8), cols), F32),),
        cost=(1 << 20, 2 << 20),
    )
    behind = lax.ppermute(volume, "depth", farther)
    next_own = lax.ppermute(grad_out, "depth", nearer)
    behind_views = call(
        behind_views_kernel,
        jax.ShapeDtypeStruct((6 * chans, cells), BF16),
        behind,
        cost=(2 * 2 * cells * chans * 8 * cols, 2 << 20),
    )
    first_lines, next_first_lines = lines(grad_out), lines(next_own)
    got[1], views, behind_views, first_lines, next_first_lines = lax.optimization_barrier(
        (got[1], views, behind_views, first_lines, next_first_lines)
    )
    later_lines = [lines(*[got[mask] for mask in range(1, count - 1)]), lines(got[count - 1])]
    own_lines = [first_lines] + later_lines
    next_lines = [next_first_lines] + [lax.ppermute(part, "depth", nearer) for part in later_lines]
    outs = channels // depth
    half_terms = jax.ShapeDtypeStruct((channels // 2, 32 * chans), F32)
    keep, send = call(
        lambda *refs: weight_kernel(outs, cols, 4 * cols, *refs),
        (half_terms, half_terms),
        views,
        behind_views,
        *own_lines,
        scratch=(
            pltpu.VMEM((32 * (chans + 8), channels), F32),
            pltpu.VMEM((32 * chans, channels), F32),
        ),
        cost=(2 * 27 * chans * channels * cells, 8 << 20),
    )
    cells_scratch = (
        pltpu.VMEM((9 * chans, cells + cols), F32),
        pltpu.VMEM((2, 256 // chans * (chans + 8), cols), F32),
    )
    plane = jax.ShapeDtypeStruct((chans, 2 * rows, 2 * cols), BF16)
    other = lax.ppermute(send, "depth", [(i, i ^ 1) for i in range(depth)])
    even_grad = call(
        even_kernel,
        plane,
        even_taps,
        *own_lines,
        scratch=cells_scratch,
        cost=(2 * 9 * chans * channels * cells, 4 << 20),
    )
    other, even_grad = lax.optimization_barrier((other, even_grad))
    pair_terms = call(pair_kernel, half_terms, keep, other, cost=(1 << 16, 1 << 19))
    chips = [[chip * 2 + core for chip in range(depth // 2)] for core in range(2)]
    terms = lax.all_to_all(
        pair_terms, "depth", split_axis=0, concat_axis=0, axis_index_groups=chips, tiled=True
    )
    input_grad = call(
        odd_kernel,
        jax.ShapeDtypeStruct(volume.shape, BF16),
        even_grad,
        odd_taps,
        *next_lines,
        *own_lines,
        out_spec=HBM,
        scratch=cells_scratch
        + (
            pltpu.VMEM(plane.shape, BF16),
            pltpu.SemaphoreType.DMA,
            pltpu.SemaphoreType.DMA((2 * rows * chans // 256,)),
        ),
        cost=(4 * 9 * chans * channels * cells, 4 << 20),
    )
    terms, input_grad = lax.optimization_barrier((terms, input_grad))
    scale = 1.0 / math.sqrt(depth * cells)
    weight_grad = call(
        functools.partial(total_kernel, scale),
        jax.ShapeDtypeStruct((chans, outs, 27), F32),
        terms.reshape(depth // 2, outs, 32 * chans),
        cost=(1 << 16, 1 << 19),
    )
    return input_grad, jnp.transpose(weight_grad, (2, 0, 1))


def solution(mesh):
    in_specs = (P("chan", "depth", None, None), P("chan", "depth", None, None), P())
    out_specs = (P("chan", "depth", None, None), P(None, "chan", "depth"))
    ring, depth = mesh.shape["chan"], mesh.shape["depth"]

    def either(grad_out, volume, weight):
        fits = (
            grad_out.shape[0] % 32 == 0
            and volume.shape[0] == 16
            and grad_out.shape[1] == 1
            and ring >= 4
            and ring & (ring - 1) == 0
            and depth & (depth - 1) == 0
            and depth % (2 * ring) == 0
        )
        return (shards if fits else plain_shards)(grad_out, volume, weight)

    return jax.shard_map(either, mesh=mesh, in_specs=in_specs, out_specs=out_specs, check_vma=False)
```

```python
import functools
import math

import jax
import jax.numpy as jnp
from jax import lax
from jax.experimental import pallas as pl
from jax.experimental.pallas import tpu as pltpu
from jax.sharding import PartitionSpec as P

F32 = jnp.float32
BF16 = jnp.bfloat16
VMEM = pl.BlockSpec(memory_space=pltpu.VMEM)
HBM = pl.BlockSpec(memory_space=pltpu.HBM)
LIMIT = 48 * 1024 * 1024


def matmul(left, right):
    return jnp.dot(left, right, preferred_element_type=F32)


def one_hot(rows, cols, source):
    row = lax.broadcasted_iota(jnp.int32, (rows, cols), 0)
    col = lax.broadcasted_iota(jnp.int32, (rows, cols), 1)
    return jnp.where(source(row, col), 1.0, 0.0).astype(BF16)


def swap_rows(major, minor):
    bits = minor.bit_length() - 1
    return one_hot(
        major * minor,
        major * minor,
        lambda row, col: col == (row & (minor - 1)) * major + (row >> bits),
    )


def place_views(plane, views_ref, base):
    chans, rows, cols = plane.shape
    half = cols // 2
    group = 256 // chans
    swap = swap_rows(group, chans)
    split = one_hot(cols, cols, lambda row, col: row == 2 * (col & (half - 1)) + col // half)
    inner = lax.broadcasted_iota(jnp.int32, (group * chans, half), 1) > 0
    for start in range(0, rows, group):
        block = plane[:, start : start + group, :].reshape(chans * group, cols)
        parted = matmul(matmul(swap, block).astype(BF16), split)
        odd = parted[:, half:]
        before = jnp.where(inner, pltpu.roll(odd, 1, 1), 0.0)
        views = [view.astype(BF16) for view in (before, parted[:, :half], odd)]
        for at in range(group):
            row = start + at
            lanes = slice(row // 2 * half, (row // 2 + 1) * half)
            for e in range(3):
                lo = base + (3 * (row % 2) + e) * chans
                views_ref[lo : lo + chans, lanes] = views[e][at * chans : (at + 1) * chans]


def own_views_kernel(depth, volume_ref, weight_ref, views_ref, even_ref, odd_ref):
    chans = volume_ref.shape[0]
    channels = weight_ref.shape[2]
    place_views(volume_ref.at[:, 0], views_ref, 0)
    place_views(volume_ref.at[:, 1], views_ref, 6 * chans)
    count = lax.axis_size("chan")
    part = channels // count
    here = lax.axis_index("chan")
    row = lax.broadcasted_iota(jnp.int32, (channels, channels), 0)
    col = lax.broadcasted_iota(jnp.int32, (channels, channels), 1)
    order = jnp.zeros((channels, channels), F32)
    for slot in range(count):
        moved = ((here ^ slot) - slot) * part
        inside = (col >= slot * part) & (col < (slot + 1) * part)
        order = jnp.where(inside & (row == col + moved), 1.0, order)
    ordered = matmul(weight_ref[...].reshape(27 * chans, channels), order.astype(BF16)).astype(BF16)
    beyond = jnp.where(lax.axis_index("depth") == depth - 1, 0.0, 1.0).astype(BF16)
    for k, e in enumerate((1, 2, 0)):
        for b in range(3):
            pick = lambda a: ordered[(9 * a + 3 * b + e) * chans : (9 * a + 3 * b + e + 1) * chans]
            lo = (3 * k + b) * chans
            even_ref[lo : lo + chans, :] = pick(1)
            odd_ref[lo : lo + chans, :] = jnp.concatenate([pick(0) * beyond, pick(2)], axis=1)


def behind_views_kernel(behind_ref, views_ref):
    first = lax.axis_index("depth") == 0

    @pl.when(jnp.logical_not(first))
    def _():
        place_views(behind_ref.at[:, 1], views_ref, 0)

    @pl.when(first)
    def _():
        views_ref[...] = jnp.zeros(views_ref.shape, BF16)


def place_lines(part, out_ref, at, wide_ref):
    outs, _, rows, cols = part.shape
    pitch = rows + 8
    for o in range(outs):
        wide_ref[o * pitch : o * pitch + rows, :] = part[o, 0].astype(F32)
    for row in range(rows):
        line = wide_ref[pl.ds(row, outs, stride=pitch), :].astype(BF16)
        out_ref[at : at + outs, row * cols : (row + 1) * cols] = line


def lines_kernel(*refs):
    *parts, out_ref, wide_ref = refs
    at = 0
    for part in parts:
        place_lines(part, out_ref, at, wide_ref)
        at += part.shape[0]


def weight_kernel(
    outs, cols, chunk, own_ref, behind_ref, *refs
):
    *line_refs, keep_ref, send_ref, terms_ref, placed_ref = refs
    channels = terms_ref.shape[1]
    chans = behind_ref.shape[0] // 6
    cells = own_ref.shape[1]
    contract = (((1,), (1,)), ((), ()))

    def grads(lo, hi):
        return jnp.concatenate([ref[:, lo:hi] for ref in line_refs], axis=0)

    pitch = chans + 8
    sums = None
    for lo in range(0, cells, chunk):
        hi = lo + chunk
        below = grads(lo + cols, min(hi + cols, cells))
        if hi == cells:
            below = jnp.concatenate([below, jnp.zeros((channels, cols), BF16)], axis=1)
        both = jnp.concatenate([grads(lo, hi), below], axis=0)
        views = jnp.concatenate([behind_ref[:, lo:hi], own_ref[:, lo:hi]], axis=0)
        part = lax.dot_general(views, both, contract, preferred_element_type=F32)
        sums = part if sums is None else sums + part
    for a in range(3):
        terms = sums[6 * a * chans : 6 * (a + 1) * chans]
        even, odd = terms[: 3 * chans, :channels], terms[3 * chans :]
        for b, block in enumerate((odd[:, channels:], even, odd[:, :channels])):
            for e in range(3):
                lo = (9 * a + 3 * b + e) * pitch
                terms_ref[lo : lo + chans, :] = block[e * chans : (e + 1) * chans]
    terms_ref[27 * pitch :, :] = jnp.zeros((6 * pitch, channels), F32)
    for c in range(chans):
        placed_ref[32 * c : 32 * c + 32, :] = terms_ref[pl.ds(c, 32, stride=pitch), :]
    turned = placed_ref[...].T
    count = lax.axis_size("chan")
    part = channels // count
    odd_core = lax.axis_index("depth") % 2 == 1
    for slot in range(count):
        start = (lax.axis_index("chan") ^ slot) * (part // 2)
        for at in range(0, part // 2, outs):
            lo = slot * part + 2 * at
            even, odd = turned[lo : lo + outs], turned[lo + outs : lo + 2 * outs]
            place = pl.ds(pl.multiple_of(start + at, outs), outs)
            keep_ref[place, :] = jnp.where(odd_core, odd, even)
            send_ref[place, :] = jnp.where(odd_core, even, odd)


def pair_kernel(keep_ref, other_ref, *out_refs):
    chip = lax.axis_index("depth") // 2
    outs = out_refs[0].shape[0]
    for k, out_ref in enumerate(out_refs):
        place = pl.ds(pl.multiple_of((chip ^ k) * outs, outs), outs)
        out_ref[...] = keep_ref[place, :] + other_ref[place, :]


def input_rows(taps_ref, line_refs, rows_ref, cells_ref, lines_ref, finished):
    chans, rows, cols = rows_ref.shape
    half = cols // 2
    grid_cells = half * rows // 2
    cells_ref[:, grid_cells:] = jnp.zeros((cells_ref.shape[0], half), F32)
    group = 256 // chans

    def compute(start):
        lanes = slice(start // 2 * half, (start + group) // 2 * half)
        grads = jnp.concatenate([ref[:, lanes] for ref in line_refs], axis=0)
        cells_ref[:, lanes] = matmul(taps_ref[...], grads)

    compute(0)
    pitch = chans + 8
    weave = one_hot(cols, cols, lambda row, col: col == 2 * (row & (half - 1)) + row // half)
    inner = lax.broadcasted_iota(jnp.int32, (chans, half), 1) < half - 1

    def cells(kind, b, r):
        lo = (3 * kind + b) * chans
        return cells_ref[lo : lo + chans, r * half : (r + 1) * half]

    for start in range(0, rows, group):
        if start + group < rows:
            compute(start + group)
        pieces = []
        for row in range(start, start + group):
            r = row // 2
            if row % 2 == 0:
                even, odd, next_odd = [cells(kind, 1, r) for kind in range(3)]
            else:
                even, odd, next_odd = [cells(kind, 0, r + 1) + cells(kind, 2, r) for kind in range(3)]
            odd = odd + jnp.where(inner, pltpu.roll(next_odd, half - 1, 1), 0.0)
            pieces.append(jnp.concatenate([even, odd], axis=1).astype(BF16))
        woven = matmul(jnp.concatenate(pieces, axis=0), weave)
        for side in range(2):
            lanes = slice(side * half, (side + 1) * half)
            for at in range(group):
                lines_ref[side, at * pitch : at * pitch + chans] = woven[at * chans : (at + 1) * chans, lanes]
            for c in range(chans):
                line = lines_ref[side, pl.ds(c, group, stride=pitch), :].astype(BF16)
                rows_ref[c, start : start + group, lanes] = line
        finished(start, group)


def even_kernel(taps_ref, *refs):
    *line_refs, rows_ref, cells_ref, lines_ref = refs
    input_rows(taps_ref, line_refs, rows_ref, cells_ref, lines_ref, lambda start, size: None)


def odd_kernel(even_ref, taps_ref, *refs):
    *line_refs, out_ref, cells_ref, lines_ref, rows_ref, even_sem, sems = refs
    copies = [pltpu.make_async_copy(even_ref, out_ref.at[:, 0], even_sem)]
    copies[0].start()

    def finished(start, size):
        place = pl.ds(start, size)
        copy = pltpu.make_async_copy(rows_ref.at[:, place], out_ref.at[:, 1, place], sems.at[start // size])
        copy.start()
        copies.append(copy)

    input_rows(taps_ref, line_refs, rows_ref, cells_ref, lines_ref, finished)
    for copy in copies:
        copy.wait()


def total_kernel(scale, *refs):
    *term_refs, out_ref = refs
    chans, outs, taps = out_ref.shape
    total = term_refs[0][...]
    for ref in term_refs[1:]:
        total = total + ref[...]
    total = total * scale
    for c in range(chans):
        out_ref[c] = total[:, 32 * c : 32 * c + taps]


def from_behind(shard, axis, by):
    count = lax.axis_size(axis)
    pairs = [(i, i + by) for i in range(count) if 0 <= i + by < count]
    return lax.ppermute(shard, axis, pairs)


def upsample(stacked, axis, extended):
    tap_zero, tap_one, tap_two = (stacked[0], stacked[1], stacked[2])
    coord_axis = axis - 1
    length = tap_zero.shape[coord_axis]
    if extended:
        outer = length - 1
        even_cells = lax.slice_in_dim(tap_one, 0, outer, axis=coord_axis)
        odd_cells = lax.slice_in_dim(tap_zero, 1, length, axis=coord_axis) + lax.slice_in_dim(
            tap_two, 0, outer, axis=coord_axis
        )
    else:
        outer = length
        shifted = lax.slice_in_dim(tap_zero, 1, length, axis=coord_axis)
        shifted = jnp.concatenate(
            [shifted, jnp.zeros_like(lax.slice_in_dim(tap_zero, 0, 1, axis=coord_axis))],
            axis=coord_axis,
        )
        even_cells = tap_one
        odd_cells = shifted + tap_two
    paired = jnp.stack([even_cells, odd_cells], axis=coord_axis + 1)
    new_shape = list(even_cells.shape)
    new_shape[coord_axis] = 2 * outer
    return paired.reshape(new_shape)


def phase_grads(weight_rows, grads_ext):
    local_in = weight_rows.shape[0] // 27
    channels_out, planes, rows, cols = grads_ext.shape
    taps_out = jnp.dot(
        weight_rows, grads_ext.reshape(channels_out, -1), preferred_element_type=jnp.float32
    )
    taps_out = taps_out.reshape(3, 3, 3, local_in, planes, rows, cols)
    along_w = upsample(jnp.moveaxis(taps_out, 2, 0), 6, False)
    along_h = upsample(jnp.moveaxis(along_w, 1, 0), 4, False)
    return upsample(along_h, 2, True)


def weight_terms(inputs, grads_ext):
    row_extra = 0
    weight_cube = lax.conv_general_dilated(
        inputs[None],
        grads_ext[:, None],
        (1, 1, 1),
        ((1, 2), (1, row_extra), (1, 0)),
        rhs_dilation=(2, 2, 2),
        dimension_numbers=("CNDHW", "OIDHW", "NCDHW"),
        preferred_element_type=jnp.float32,
    )
    return jnp.transpose(weight_cube, (2, 3, 4, 0, 1)).reshape(
        27, weight_cube.shape[0], weight_cube.shape[1]
    )


def plain_shards(grad_out, volume, weight):
    plane_next = from_behind(grad_out, "depth", -1)
    grads_ext = jnp.concatenate([grad_out, plane_next], axis=1)
    channels_out = weight.shape[2]
    local_in = volume.shape[0]
    every_channel = lax.all_gather(grads_ext, "chan", axis=0, tiled=True)
    own_weight = lax.dynamic_slice_in_dim(weight, lax.axis_index("chan") * local_in, local_in, 1)
    input_part = phase_grads(own_weight.reshape(27 * local_in, channels_out), every_channel)
    weight_part = weight_terms(volume, every_channel)
    input_grad = input_part.astype(jnp.bfloat16)
    summed = lax.psum_scatter(weight_part, "depth", scatter_dimension=2, tiled=True)
    cell_count = grad_out.shape[1] * lax.axis_size("depth") * grad_out.shape[2] * grad_out.shape[3]
    return (input_grad, summed * (1.0 / math.sqrt(cell_count)))


def call(kernel, out_shape, *args, out_spec=VMEM, scratch=(), cost=None):
    flops, moved = cost
    return pl.pallas_call(
        kernel,
        out_shape=out_shape,
        in_specs=[VMEM] * len(args),
        out_specs=jax.tree.map(lambda _: out_spec, out_shape),
        scratch_shapes=scratch,
        compiler_params=pltpu.CompilerParams(vmem_limit_bytes=LIMIT),
        cost_estimate=pl.CostEstimate(flops=flops, bytes_accessed=moved, transcendentals=0),
    )(*args)


def shards(grad_out, volume, weight):
    count = lax.axis_size("chan")
    depth = lax.axis_size("depth")
    own_outs, _, rows, cols = grad_out.shape
    chans = volume.shape[0]
    channels = weight.shape[2]
    cells = rows * cols
    farther = [(i, (i + 1) % depth) for i in range(depth)]
    nearer = [(b, a) for a, b in farther]

    own_weight = lax.dynamic_slice_in_dim(weight, lax.axis_index("chan") * chans, chans, 1)
    views, even_taps, odd_taps = call(
        lambda *refs: own_views_kernel(depth, *refs),
        (
            jax.ShapeDtypeStruct((12 * chans, cells), BF16),
            jax.ShapeDtypeStruct((9 * chans, channels), BF16),
            jax.ShapeDtypeStruct((9 * chans, 2 * channels), BF16),
        ),
        volume,
        own_weight,
        cost=(2 * 2 * 2 * cells * chans * 8 * cols, 4 << 20),
    )
    got = {0: grad_out}
    for mask in sorted(range(1, count), key=lambda mask: (mask & (mask - 1) > 0, -mask)):
        low = mask & -mask
        if mask == 3:
            got[2], views = lax.optimization_barrier((got[2], views))
        got[mask] = lax.ppermute(got[mask - low], "chan", [(i, i ^ low) for i in range(count)])
    lines = lambda *parts: call(
        lines_kernel,
        jax.ShapeDtypeStruct((sum(part.shape[0] for part in parts), cells), BF16),
        *parts,
        scratch=(pltpu.VMEM(((own_outs + 1) * (rows + 8), cols), F32),),
        cost=(1 << 20, 2 << 20),
    )
    behind = lax.ppermute(volume, "depth", farther)
    next_own = lax.ppermute(grad_out, "depth", nearer)
    behind_views = call(
        behind_views_kernel,
        jax.ShapeDtypeStruct((6 * chans, cells), BF16),
        behind,
        cost=(2 * 2 * cells * chans * 8 * cols, 2 << 20),
    )
    first_lines, next_first_lines = lines(grad_out), lines(next_own)
    got[1], views, behind_views, first_lines, next_first_lines = lax.optimization_barrier(
        (got[1], views, behind_views, first_lines, next_first_lines)
    )
    later_lines = [lines(*[got[mask] for mask in range(1, count - 1)]), lines(got[count - 1])]
    own_lines = [first_lines] + later_lines
    next_lines = [next_first_lines] + [lax.ppermute(part, "depth", nearer) for part in later_lines[:-1]]
    outs = channels // depth
    half_terms = jax.ShapeDtypeStruct((channels // 2, 32 * chans), F32)
    keep, send = call(
        lambda *refs: weight_kernel(outs, cols, 4 * cols, *refs),
        (half_terms, half_terms),
        views,
        behind_views,
        *own_lines,
        scratch=(
            pltpu.VMEM((33 * (chans + 8), channels), F32),
            pltpu.VMEM((32 * chans, channels), F32),
        ),
        cost=(2 * 27 * chans * channels * cells, 8 << 20),
    )
    cells_scratch = (
        pltpu.VMEM((9 * chans, cells + cols), F32),
        pltpu.VMEM((2, (256 // chans + 1) * (chans + 8), cols), F32),
    )
    plane = jax.ShapeDtypeStruct((chans, 2 * rows, 2 * cols), BF16)
    last_lines, send = lax.optimization_barrier((later_lines[-1], send))
    next_lines.append(lax.ppermute(last_lines, "depth", nearer))
    other = lax.ppermute(send, "depth", [(i, i ^ 1) for i in range(depth)])
    own_terms, *terms = call(
        pair_kernel,
        [jax.ShapeDtypeStruct((outs, 32 * chans), F32)] * (depth // 2),
        keep,
        other,
        cost=(1 << 16, 1 << 19),
    )
    terms = [
        lax.ppermute(terms[k - 1], "depth", [(i, i ^ (2 * k)) for i in range(depth)])
        for k in range(depth // 2 - 1, 0, -1)
    ]
    even_taps, own_terms = lax.optimization_barrier((even_taps, own_terms))
    even_grad = call(
        even_kernel,
        plane,
        even_taps,
        *own_lines,
        scratch=cells_scratch,
        cost=(24 * 9 * chans * channels * cells, 4 << 20),
    )
    input_grad = call(
        odd_kernel,
        jax.ShapeDtypeStruct(volume.shape, BF16),
        even_grad,
        odd_taps,
        *next_lines,
        *own_lines,
        out_spec=HBM,
        scratch=cells_scratch
        + (
            pltpu.VMEM(plane.shape, BF16),
            pltpu.SemaphoreType.DMA,
            pltpu.SemaphoreType.DMA((2 * rows * chans // 256,)),
        ),
        cost=(4 * 9 * chans * channels * cells, 4 << 20),
    )
    own_terms, input_grad = lax.optimization_barrier((own_terms, input_grad))
    scale = 1.0 / math.sqrt(depth * cells)
    weight_grad = call(
        functools.partial(total_kernel, scale),
        jax.ShapeDtypeStruct((chans, outs, 27), F32),
        own_terms,
        *terms,
        cost=(1 << 16, 1 << 19),
    )
    return input_grad, jnp.transpose(weight_grad, (2, 0, 1))


def solution(mesh):
    in_specs = (P("chan", "depth", None, None), P("chan", "depth", None, None), P())
    out_specs = (P("chan", "depth", None, None), P(None, "chan", "depth"))
    ring, depth = mesh.shape["chan"], mesh.shape["depth"]

    def either(grad_out, volume, weight):
        fits = (
            grad_out.shape[0] % 32 == 0
            and volume.shape[0] == 16
            and grad_out.shape[1] == 1
            and ring >= 4
            and ring & (ring - 1) == 0
            and depth & (depth - 1) == 0
            and depth % (2 * ring) == 0
        )
        return (shards if fits else plain_shards)(grad_out, volume, weight)

    return jax.shard_map(either, mesh=mesh, in_specs=in_specs, out_specs=out_specs, check_vma=False)
```

```python
import functools
import math

import jax
import jax.numpy as jnp
from jax import lax
from jax.experimental import pallas as pl
from jax.experimental.pallas import tpu as pltpu
from jax.sharding import PartitionSpec as P

F32 = jnp.float32
BF16 = jnp.bfloat16
VMEM = pl.BlockSpec(memory_space=pltpu.VMEM)
HBM = pl.BlockSpec(memory_space=pltpu.HBM)
LIMIT = 48 * 1024 * 1024


def matmul(left, right):
    return jnp.dot(left, right, preferred_element_type=F32)


def one_hot(rows, cols, source):
    row = lax.broadcasted_iota(jnp.int32, (rows, cols), 0)
    col = lax.broadcasted_iota(jnp.int32, (rows, cols), 1)
    return jnp.where(source(row, col), 1.0, 0.0).astype(BF16)


def swap_rows(major, minor):
    bits = minor.bit_length() - 1
    return one_hot(
        major * minor,
        major * minor,
        lambda row, col: col == (row & (minor - 1)) * major + (row >> bits),
    )


def place_views(plane, views_ref, base):
    chans, rows, cols = plane.shape
    half = cols // 2
    group = 256 // chans
    swap = swap_rows(group, chans)
    split = one_hot(cols, cols, lambda row, col: row == 2 * (col & (half - 1)) + col // half)
    inner = lax.broadcasted_iota(jnp.int32, (group * chans, half), 1) > 0
    for start in range(0, rows, group):
        block = plane[:, start : start + group, :].reshape(chans * group, cols)
        parted = matmul(matmul(swap, block).astype(BF16), split)
        odd = parted[:, half:]
        before = jnp.where(inner, pltpu.roll(odd, 1, 1), 0.0)
        views = [view.astype(BF16) for view in (before, parted[:, :half], odd)]
        for at in range(group):
            row = start + at
            lanes = slice(row // 2 * half, (row // 2 + 1) * half)
            for e in range(3):
                lo = base + (3 * (row % 2) + e) * chans
                views_ref[lo : lo + chans, lanes] = views[e][at * chans : (at + 1) * chans]


def own_views_kernel(depth, volume_ref, weight_ref, views_ref, even_ref, odd_ref):
    chans = volume_ref.shape[0]
    channels = weight_ref.shape[2]
    place_views(volume_ref.at[:, 0], views_ref, 0)
    place_views(volume_ref.at[:, 1], views_ref, 6 * chans)
    count = lax.axis_size("chan")
    part = channels // count
    here = lax.axis_index("chan")
    row = lax.broadcasted_iota(jnp.int32, (channels, channels), 0)
    col = lax.broadcasted_iota(jnp.int32, (channels, channels), 1)
    order = jnp.zeros((channels, channels), F32)
    for slot in range(count):
        moved = ((here ^ slot) - slot) * part
        inside = (col >= slot * part) & (col < (slot + 1) * part)
        order = jnp.where(inside & (row == col + moved), 1.0, order)
    ordered = matmul(weight_ref[...].reshape(27 * chans, channels), order.astype(BF16)).astype(BF16)
    beyond = jnp.where(lax.axis_index("depth") == depth - 1, 0.0, 1.0).astype(BF16)
    for k, e in enumerate((1, 2, 0)):
        for b in range(3):
            pick = lambda a: ordered[(9 * a + 3 * b + e) * chans : (9 * a + 3 * b + e + 1) * chans]
            lo = (3 * k + b) * chans
            even_ref[lo : lo + chans, :] = pick(1)
            odd_ref[lo : lo + chans, :] = jnp.concatenate([pick(0) * beyond, pick(2)], axis=1)


def behind_views_kernel(behind_ref, views_ref):
    first = lax.axis_index("depth") == 0

    @pl.when(jnp.logical_not(first))
    def _():
        place_views(behind_ref.at[:, 1], views_ref, 0)

    @pl.when(first)
    def _():
        views_ref[...] = jnp.zeros(views_ref.shape, BF16)


def place_lines(part, out_ref, at, wide_ref):
    outs, _, rows, cols = part.shape
    pitch = rows + 8
    for o in range(outs):
        wide_ref[o * pitch : o * pitch + rows, :] = part[o, 0].astype(F32)
    for row in range(rows):
        line = wide_ref[pl.ds(row, outs, stride=pitch), :].astype(BF16)
        out_ref[at : at + outs, row * cols : (row + 1) * cols] = line


def lines_kernel(*refs):
    *parts, out_ref, wide_ref = refs
    at = 0
    for part in parts:
        place_lines(part, out_ref, at, wide_ref)
        at += part.shape[0]


def weight_kernel(
    outs, cols, chunk, own_ref, behind_ref, *refs
):
    *line_refs, keep_ref, send_ref, terms_ref, placed_ref = refs
    channels = terms_ref.shape[1]
    chans = behind_ref.shape[0] // 6
    cells = own_ref.shape[1]
    contract = (((1,), (1,)), ((), ()))

    def grads(lo, hi):
        return jnp.concatenate([ref[:, lo:hi] for ref in line_refs], axis=0)

    pitch = chans + 8
    sums = None
    for lo in range(0, cells, chunk):
        hi = lo + chunk
        below = grads(lo + cols, min(hi + cols, cells))
        if hi == cells:
            below = jnp.concatenate([below, jnp.zeros((channels, cols), BF16)], axis=1)
        both = jnp.concatenate([grads(lo, hi), below], axis=0)
        views = jnp.concatenate([behind_ref[:, lo:hi], own_ref[:, lo:hi]], axis=0)
        part = lax.dot_general(views, both, contract, preferred_element_type=F32)
        sums = part if sums is None else sums + part
    for a in range(3):
        terms = sums[6 * a * chans : 6 * (a + 1) * chans]
        even, odd = terms[: 3 * chans, :channels], terms[3 * chans :]
        for b, block in enumerate((odd[:, channels:], even, odd[:, :channels])):
            for e in range(3):
                lo = (9 * a + 3 * b + e) * pitch
                terms_ref[lo : lo + chans, :] = block[e * chans : (e + 1) * chans]
    terms_ref[27 * pitch :, :] = jnp.zeros((6 * pitch, channels), F32)
    for c in range(chans):
        placed_ref[32 * c : 32 * c + 32, :] = terms_ref[pl.ds(c, 32, stride=pitch), :]
    turned = placed_ref[...].T
    count = lax.axis_size("chan")
    part = channels // count
    odd_core = lax.axis_index("depth") % 2 == 1
    for slot in range(count):
        start = (lax.axis_index("chan") ^ slot) * (part // 2)
        for at in range(0, part // 2, outs):
            lo = slot * part + 2 * at
            even, odd = turned[lo : lo + outs], turned[lo + outs : lo + 2 * outs]
            place = pl.ds(pl.multiple_of(start + at, outs), outs)
            keep_ref[place, :] = jnp.where(odd_core, odd, even)
            send_ref[place, :] = jnp.where(odd_core, even, odd)


def pair_kernel(keep_ref, other_ref, *out_refs):
    chip = lax.axis_index("depth") // 2
    outs = out_refs[0].shape[0]
    for k, out_ref in enumerate(out_refs):
        place = pl.ds(pl.multiple_of((chip ^ k) * outs, outs), outs)
        out_ref[...] = keep_ref[place, :] + other_ref[place, :]


def input_rows(taps_ref, line_refs, rows_ref, cells_ref, lines_ref, finished):
    chans, rows, cols = rows_ref.shape
    half = cols // 2
    grid_cells = half * rows // 2
    cells_ref[:, grid_cells:] = jnp.zeros((cells_ref.shape[0], half), F32)
    group = 256 // chans

    def compute(start):
        lanes = slice(start // 2 * half, (start + group) // 2 * half)
        grads = jnp.concatenate([ref[:, lanes] for ref in line_refs], axis=0)
        cells_ref[:, lanes] = matmul(taps_ref[...], grads)

    compute(0)
    pitch = chans + 8
    weave = one_hot(cols, cols, lambda row, col: col == 2 * (row & (half - 1)) + row // half)
    inner = lax.broadcasted_iota(jnp.int32, (chans, half), 1) < half - 1

    def cells(kind, b, r):
        lo = (3 * kind + b) * chans
        return cells_ref[lo : lo + chans, r * half : (r + 1) * half]

    for start in range(0, rows, group):
        if start + group < rows:
            compute(start + group)
        pieces = []
        for row in range(start, start + group):
            r = row // 2
            if row % 2 == 0:
                even, odd, next_odd = [cells(kind, 1, r) for kind in range(3)]
            else:
                even, odd, next_odd = [cells(kind, 0, r + 1) + cells(kind, 2, r) for kind in range(3)]
            odd = odd + jnp.where(inner, pltpu.roll(next_odd, half - 1, 1), 0.0)
            pieces.append(jnp.concatenate([even, odd], axis=1).astype(BF16))
        woven = matmul(jnp.concatenate(pieces, axis=0), weave)
        for side in range(2):
            lanes = slice(side * half, (side + 1) * half)
            for at in range(group):
                lines_ref[side, at * pitch : at * pitch + chans] = woven[at * chans : (at + 1) * chans, lanes]
            for c in range(chans):
                line = lines_ref[side, pl.ds(c, group, stride=pitch), :].astype(BF16)
                rows_ref[c, start : start + group, lanes] = line
        finished(start, group)


def even_kernel(taps_ref, *refs):
    *line_refs, rows_ref, cells_ref, lines_ref = refs
    input_rows(taps_ref, line_refs, rows_ref, cells_ref, lines_ref, lambda start, size: None)


def odd_kernel(even_ref, taps_ref, *refs):
    *line_refs, out_ref, cells_ref, lines_ref, rows_ref, even_sem, sems = refs
    copies = [pltpu.make_async_copy(even_ref, out_ref.at[:, 0], even_sem)]
    copies[0].start()

    def finished(start, size):
        place = pl.ds(start, size)
        copy = pltpu.make_async_copy(rows_ref.at[:, place], out_ref.at[:, 1, place], sems.at[start // size])
        copy.start()
        copies.append(copy)

    input_rows(taps_ref, line_refs, rows_ref, cells_ref, lines_ref, finished)
    for copy in copies:
        copy.wait()


def total_kernel(scale, *refs):
    *term_refs, out_ref = refs
    chans, outs, taps = out_ref.shape
    total = term_refs[0][...]
    for ref in term_refs[1:]:
        total = total + ref[...]
    total = total * scale
    for c in range(chans):
        out_ref[c] = total[:, 32 * c : 32 * c + taps]


def from_behind(shard, axis, by):
    count = lax.axis_size(axis)
    pairs = [(i, i + by) for i in range(count) if 0 <= i + by < count]
    return lax.ppermute(shard, axis, pairs)


def upsample(stacked, axis, extended):
    tap_zero, tap_one, tap_two = (stacked[0], stacked[1], stacked[2])
    coord_axis = axis - 1
    length = tap_zero.shape[coord_axis]
    if extended:
        outer = length - 1
        even_cells = lax.slice_in_dim(tap_one, 0, outer, axis=coord_axis)
        odd_cells = lax.slice_in_dim(tap_zero, 1, length, axis=coord_axis) + lax.slice_in_dim(
            tap_two, 0, outer, axis=coord_axis
        )
    else:
        outer = length
        shifted = lax.slice_in_dim(tap_zero, 1, length, axis=coord_axis)
        shifted = jnp.concatenate(
            [shifted, jnp.zeros_like(lax.slice_in_dim(tap_zero, 0, 1, axis=coord_axis))],
            axis=coord_axis,
        )
        even_cells = tap_one
        odd_cells = shifted + tap_two
    paired = jnp.stack([even_cells, odd_cells], axis=coord_axis + 1)
    new_shape = list(even_cells.shape)
    new_shape[coord_axis] = 2 * outer
    return paired.reshape(new_shape)


def phase_grads(weight_rows, grads_ext):
    local_in = weight_rows.shape[0] // 27
    channels_out, planes, rows, cols = grads_ext.shape
    taps_out = jnp.dot(
        weight_rows, grads_ext.reshape(channels_out, -1), preferred_element_type=jnp.float32
    )
    taps_out = taps_out.reshape(3, 3, 3, local_in, planes, rows, cols)
    along_w = upsample(jnp.moveaxis(taps_out, 2, 0), 6, False)
    along_h = upsample(jnp.moveaxis(along_w, 1, 0), 4, False)
    return upsample(along_h, 2, True)


def weight_terms(inputs, grads_ext):
    row_extra = 0
    weight_cube = lax.conv_general_dilated(
        inputs[None],
        grads_ext[:, None],
        (1, 1, 1),
        ((1, 2), (1, row_extra), (1, 0)),
        rhs_dilation=(2, 2, 2),
        dimension_numbers=("CNDHW", "OIDHW", "NCDHW"),
        preferred_element_type=jnp.float32,
    )
    return jnp.transpose(weight_cube, (2, 3, 4, 0, 1)).reshape(
        27, weight_cube.shape[0], weight_cube.shape[1]
    )


def plain_shards(grad_out, volume, weight):
    plane_next = from_behind(grad_out, "depth", -1)
    grads_ext = jnp.concatenate([grad_out, plane_next], axis=1)
    channels_out = weight.shape[2]
    local_in = volume.shape[0]
    every_channel = lax.all_gather(grads_ext, "chan", axis=0, tiled=True)
    own_weight = lax.dynamic_slice_in_dim(weight, lax.axis_index("chan") * local_in, local_in, 1)
    input_part = phase_grads(own_weight.reshape(27 * local_in, channels_out), every_channel)
    weight_part = weight_terms(volume, every_channel)
    input_grad = input_part.astype(jnp.bfloat16)
    summed = lax.psum_scatter(weight_part, "depth", scatter_dimension=2, tiled=True)
    cell_count = grad_out.shape[1] * lax.axis_size("depth") * grad_out.shape[2] * grad_out.shape[3]
    return (input_grad, summed * (1.0 / math.sqrt(cell_count)))


def call(kernel, out_shape, *args, out_spec=VMEM, scratch=(), cost=None):
    flops, moved = cost
    return pl.pallas_call(
        kernel,
        out_shape=out_shape,
        in_specs=[VMEM] * len(args),
        out_specs=jax.tree.map(lambda _: out_spec, out_shape),
        scratch_shapes=scratch,
        compiler_params=pltpu.CompilerParams(vmem_limit_bytes=LIMIT),
        cost_estimate=pl.CostEstimate(flops=flops, bytes_accessed=moved, transcendentals=0),
    )(*args)


def shards(grad_out, volume, weight):
    count = lax.axis_size("chan")
    depth = lax.axis_size("depth")
    own_outs, _, rows, cols = grad_out.shape
    chans = volume.shape[0]
    channels = weight.shape[2]
    cells = rows * cols
    farther = [(i, (i + 1) % depth) for i in range(depth)]
    nearer = [(b, a) for a, b in farther]

    own_weight = lax.dynamic_slice_in_dim(weight, lax.axis_index("chan") * chans, chans, 1)
    views, even_taps, odd_taps = call(
        lambda *refs: own_views_kernel(depth, *refs),
        (
            jax.ShapeDtypeStruct((12 * chans, cells), BF16),
            jax.ShapeDtypeStruct((9 * chans, channels), BF16),
            jax.ShapeDtypeStruct((9 * chans, 2 * channels), BF16),
        ),
        volume,
        own_weight,
        cost=(2 * 2 * 2 * cells * chans * 8 * cols, 4 << 20),
    )
    got = {0: grad_out}
    for mask in sorted(range(1, count), key=lambda mask: (mask & (mask - 1) > 0, -mask)):
        low = mask & -mask
        if mask == 3:
            got[2], views = lax.optimization_barrier((got[2], views))
        got[mask] = lax.ppermute(got[mask - low], "chan", [(i, i ^ low) for i in range(count)])
    lines = lambda *parts: call(
        lines_kernel,
        jax.ShapeDtypeStruct((sum(part.shape[0] for part in parts), cells), BF16),
        *parts,
        scratch=(pltpu.VMEM(((own_outs + 1) * (rows + 8), cols), F32),),
        cost=(1 << 20, 2 << 20),
    )
    behind = lax.ppermute(volume, "depth", farther)
    next_own = lax.ppermute(grad_out, "depth", nearer)
    behind_views = call(
        behind_views_kernel,
        jax.ShapeDtypeStruct((6 * chans, cells), BF16),
        behind,
        cost=(2 * 2 * cells * chans * 8 * cols, 2 << 20),
    )
    first_lines, next_first_lines = lines(grad_out), lines(next_own)
    got[1], views, behind_views, first_lines, next_first_lines = lax.optimization_barrier(
        (got[1], views, behind_views, first_lines, next_first_lines)
    )
    later_lines = [lines(*[got[mask] for mask in range(1, count - 1)]), lines(got[count - 1])]
    own_lines = [first_lines] + later_lines
    next_lines = [next_first_lines] + [lax.ppermute(part, "depth", nearer) for part in later_lines]
    outs = channels // depth
    half_terms = jax.ShapeDtypeStruct((channels // 2, 32 * chans), F32)
    keep, send = call(
        lambda *refs: weight_kernel(outs, cols, 8 * cols, *refs),
        (half_terms, half_terms),
        views,
        behind_views,
        *own_lines,
        scratch=(
            pltpu.VMEM((33 * (chans + 8), channels), F32),
            pltpu.VMEM((32 * chans, channels), F32),
        ),
        cost=(2 * 27 * chans * channels * cells, 8 << 20),
    )
    cells_scratch = (
        pltpu.VMEM((9 * chans, cells + cols), F32),
        pltpu.VMEM((2, (256 // chans + 1) * (chans + 8), cols), F32),
    )
    plane = jax.ShapeDtypeStruct((chans, 2 * rows, 2 * cols), BF16)
    other = lax.ppermute(send, "depth", [(i, i ^ 1) for i in range(depth)])
    even_grad = call(
        even_kernel,
        plane,
        even_taps,
        *own_lines,
        scratch=cells_scratch,
        cost=(2 * 9 * chans * channels * cells, 4 << 20),
    )
    other, even_grad = lax.optimization_barrier((other, even_grad))
    own_terms, *terms = call(
        pair_kernel,
        [jax.ShapeDtypeStruct((outs, 32 * chans), F32)] * (depth // 2),
        keep,
        other,
        cost=(1 << 16, 1 << 19),
    )
    terms = [
        lax.ppermute(terms[k - 1], "depth", [(i, i ^ (2 * k)) for i in range(depth)])
        for k in range(depth // 2 - 1, 0, -1)
    ]
    input_grad = call(
        odd_kernel,
        jax.ShapeDtypeStruct(volume.shape, BF16),
        even_grad,
        odd_taps,
        *next_lines,
        *own_lines,
        out_spec=HBM,
        scratch=cells_scratch
        + (
            pltpu.VMEM(plane.shape, BF16),
            pltpu.SemaphoreType.DMA,
            pltpu.SemaphoreType.DMA((2 * rows * chans // 256,)),
        ),
        cost=(4 * 9 * chans * channels * cells, 4 << 20),
    )
    own_terms, input_grad = lax.optimization_barrier((own_terms, input_grad))
    scale = 1.0 / math.sqrt(depth * cells)
    weight_grad = call(
        functools.partial(total_kernel, scale),
        jax.ShapeDtypeStruct((chans, outs, 27), F32),
        own_terms,
        *terms,
        cost=(1 << 16, 1 << 19),
    )
    return input_grad, jnp.transpose(weight_grad, (2, 0, 1))


def solution(mesh):
    in_specs = (P("chan", "depth", None, None), P("chan", "depth", None, None), P())
    out_specs = (P("chan", "depth", None, None), P(None, "chan", "depth"))
    ring, depth = mesh.shape["chan"], mesh.shape["depth"]

    def either(grad_out, volume, weight):
        fits = (
            grad_out.shape[0] % 32 == 0
            and volume.shape[0] == 16
            and grad_out.shape[1] == 1
            and ring >= 4
            and ring & (ring - 1) == 0
            and depth & (depth - 1) == 0
            and depth % (2 * ring) == 0
        )
        return (shards if fits else plain_shards)(grad_out, volume, weight)

    return jax.shard_map(either, mesh=mesh, in_specs=in_specs, out_specs=out_specs, check_vma=False)
```

```python
import functools
import math

import jax
import jax.numpy as jnp
from jax import lax
from jax.experimental import pallas as pl
from jax.experimental.pallas import tpu as pltpu
from jax.sharding import PartitionSpec as P

F32 = jnp.float32
BF16 = jnp.bfloat16
VMEM = pl.BlockSpec(memory_space=pltpu.VMEM)
HBM = pl.BlockSpec(memory_space=pltpu.HBM)
LIMIT = 48 * 1024 * 1024


def matmul(left, right):
    return jnp.dot(left, right, preferred_element_type=F32)


def one_hot(rows, cols, source):
    row = lax.broadcasted_iota(jnp.int32, (rows, cols), 0)
    col = lax.broadcasted_iota(jnp.int32, (rows, cols), 1)
    return jnp.where(source(row, col), 1.0, 0.0).astype(BF16)


def swap_rows(major, minor):
    bits = minor.bit_length() - 1
    return one_hot(
        major * minor,
        major * minor,
        lambda row, col: col == (row & (minor - 1)) * major + (row >> bits),
    )


def place_views(plane, views_ref, base):
    chans, rows, cols = plane.shape
    half = cols // 2
    group = 256 // chans
    swap = swap_rows(group, chans)
    split = one_hot(cols, cols, lambda row, col: row == 2 * (col & (half - 1)) + col // half)
    inner = lax.broadcasted_iota(jnp.int32, (group * chans, half), 1) > 0
    for start in range(0, rows, group):
        block = plane[:, start : start + group, :].reshape(chans * group, cols)
        parted = matmul(matmul(swap, block).astype(BF16), split)
        odd = parted[:, half:]
        before = jnp.where(inner, pltpu.roll(odd, 1, 1), 0.0)
        views = [view.astype(BF16) for view in (before, parted[:, :half], odd)]
        for at in range(group):
            row = start + at
            lanes = slice(row // 2 * half, (row // 2 + 1) * half)
            for e in range(3):
                lo = base + (3 * (row % 2) + e) * chans
                views_ref[lo : lo + chans, lanes] = views[e][at * chans : (at + 1) * chans]


def own_views_kernel(depth, volume_ref, weight_ref, views_ref, even_ref, odd_ref):
    chans = volume_ref.shape[0]
    channels = weight_ref.shape[2]
    place_views(volume_ref.at[:, 0], views_ref, 0)
    place_views(volume_ref.at[:, 1], views_ref, 6 * chans)
    count = lax.axis_size("chan")
    part = channels // count
    here = lax.axis_index("chan")
    row = lax.broadcasted_iota(jnp.int32, (channels, channels), 0)
    col = lax.broadcasted_iota(jnp.int32, (channels, channels), 1)
    order = jnp.zeros((channels, channels), F32)
    for slot in range(count):
        moved = ((here ^ slot) - slot) * part
        inside = (col >= slot * part) & (col < (slot + 1) * part)
        order = jnp.where(inside & (row == col + moved), 1.0, order)
    ordered = matmul(weight_ref[...].reshape(27 * chans, channels), order.astype(BF16)).astype(BF16)
    beyond = jnp.where(lax.axis_index("depth") == depth - 1, 0.0, 1.0).astype(BF16)
    for k, e in enumerate((1, 2, 0)):
        for b in range(3):
            pick = lambda a: ordered[(9 * a + 3 * b + e) * chans : (9 * a + 3 * b + e + 1) * chans]
            lo = (3 * k + b) * chans
            even_ref[lo : lo + chans, :] = pick(1)
            odd_ref[lo : lo + chans, :] = jnp.concatenate([pick(0) * beyond, pick(2)], axis=1)


def behind_views_kernel(behind_ref, views_ref):
    first = lax.axis_index("depth") == 0

    @pl.when(jnp.logical_not(first))
    def _():
        place_views(behind_ref.at[:, 1], views_ref, 0)

    @pl.when(first)
    def _():
        views_ref[...] = jnp.zeros(views_ref.shape, BF16)


def place_lines(part, out_ref, at, wide_ref):
    outs, _, rows, cols = part.shape
    pitch = rows + 8
    for o in range(outs):
        wide_ref[o * pitch : o * pitch + rows, :] = part[o, 0].astype(F32)
    for row in range(rows):
        line = wide_ref[pl.ds(row, outs, stride=pitch), :].astype(BF16)
        out_ref[at : at + outs, row * cols : (row + 1) * cols] = line


def lines_kernel(*refs):
    *parts, out_ref, wide_ref = refs
    at = 0
    for part in parts:
        place_lines(part, out_ref, at, wide_ref)
        at += part.shape[0]


def weight_kernel(
    outs, cols, chunk, own_ref, behind_ref, *refs
):
    *line_refs, keep_ref, send_ref, terms_ref, placed_ref = refs
    channels = terms_ref.shape[1]
    chans = behind_ref.shape[0] // 6
    cells = own_ref.shape[1]
    contract = (((1,), (1,)), ((), ()))

    def grads(lo, hi):
        return jnp.concatenate([ref[:, lo:hi] for ref in line_refs], axis=0)

    pitch = chans + 8
    sums = None
    for lo in range(0, cells, chunk):
        hi = lo + chunk
        below = grads(lo + cols, min(hi + cols, cells))
        if hi == cells:
            below = jnp.concatenate([below, jnp.zeros((channels, cols), BF16)], axis=1)
        both = jnp.concatenate([grads(lo, hi), below], axis=0)
        views = jnp.concatenate([behind_ref[:, lo:hi], own_ref[:, lo:hi]], axis=0)
        part = lax.dot_general(views, both, contract, preferred_element_type=F32)
        sums = part if sums is None else sums + part
    for a in range(3):
        terms = sums[6 * a * chans : 6 * (a + 1) * chans]
        even, odd = terms[: 3 * chans, :channels], terms[3 * chans :]
        for b, block in enumerate((odd[:, channels:], even, odd[:, :channels])):
            for e in range(3):
                lo = (9 * a + 3 * b + e) * pitch
                terms_ref[lo : lo + chans, :] = block[e * chans : (e + 1) * chans]
    terms_ref[27 * pitch :, :] = jnp.zeros((6 * pitch, channels), F32)
    for c in range(chans):
        placed_ref[32 * c : 32 * c + 32, :] = terms_ref[pl.ds(c, 32, stride=pitch), :]
    turned = placed_ref[...].T
    count = lax.axis_size("chan")
    part = channels // count
    odd_core = lax.axis_index("depth") % 2 == 1
    for slot in range(count):
        start = (lax.axis_index("chan") ^ slot) * (part // 2)
        for at in range(0, part // 2, outs):
            lo = slot * part + 2 * at
            even, odd = turned[lo : lo + outs], turned[lo + outs : lo + 2 * outs]
            place = pl.ds(pl.multiple_of(start + at, outs), outs)
            keep_ref[place, :] = jnp.where(odd_core, odd, even)
            send_ref[place, :] = jnp.where(odd_core, even, odd)


def pair_kernel(keep_ref, other_ref, *out_refs):
    chip = lax.axis_index("depth") // 2
    outs = out_refs[0].shape[0]
    for k, out_ref in enumerate(out_refs):
        place = pl.ds(pl.multiple_of((chip ^ k) * outs, outs), outs)
        out_ref[...] = keep_ref[place, :] + other_ref[place, :]


def input_rows(taps_ref, line_refs, rows_ref, cells_ref, lines_ref, finished):
    chans, rows, cols = rows_ref.shape
    half = cols // 2
    grid_cells = half * rows // 2
    cells_ref[:, grid_cells:] = jnp.zeros((cells_ref.shape[0], half), F32)
    group = 256 // chans

    def compute(start):
        lanes = slice(start // 2 * half, (start + group) // 2 * half)
        grads = jnp.concatenate([ref[:, lanes] for ref in line_refs], axis=0)
        cells_ref[:, lanes] = matmul(taps_ref[...], grads)

    compute(0)
    pitch = chans + 8
    weave = one_hot(cols, cols, lambda row, col: col == 2 * (row & (half - 1)) + row // half)
    inner = lax.broadcasted_iota(jnp.int32, (chans, half), 1) < half - 1

    def cells(kind, b, r):
        lo = (3 * kind + b) * chans
        return cells_ref[lo : lo + chans, r * half : (r + 1) * half]

    for start in range(0, rows, group):
        if start + group < rows:
            compute(start + group)
        pieces = []
        for row in range(start, start + group):
            r = row // 2
            if row % 2 == 0:
                even, odd, next_odd = [cells(kind, 1, r) for kind in range(3)]
            else:
                even, odd, next_odd = [cells(kind, 0, r + 1) + cells(kind, 2, r) for kind in range(3)]
            odd = odd + jnp.where(inner, pltpu.roll(next_odd, half - 1, 1), 0.0)
            pieces.append(jnp.concatenate([even, odd], axis=1).astype(BF16))
        woven = matmul(jnp.concatenate(pieces, axis=0), weave)
        for side in range(2):
            lanes = slice(side * half, (side + 1) * half)
            for at in range(group):
                lines_ref[side, at * pitch : at * pitch + chans] = woven[at * chans : (at + 1) * chans, lanes]
            for c in range(chans):
                line = lines_ref[side, pl.ds(c, group, stride=pitch), :].astype(BF16)
                rows_ref[c, start : start + group, lanes] = line
        finished(start, group)


def even_kernel(taps_ref, *refs):
    *line_refs, rows_ref, cells_ref, lines_ref = refs
    input_rows(taps_ref, line_refs, rows_ref, cells_ref, lines_ref, lambda start, size: None)


def odd_kernel(even_ref, taps_ref, *refs):
    *line_refs, out_ref, cells_ref, lines_ref, rows_ref, even_sem, sems = refs
    copies = [pltpu.make_async_copy(even_ref, out_ref.at[:, 0], even_sem)]
    copies[0].start()

    def finished(start, size):
        place = pl.ds(start, size)
        copy = pltpu.make_async_copy(rows_ref.at[:, place], out_ref.at[:, 1, place], sems.at[start // size])
        copy.start()
        copies.append(copy)

    input_rows(taps_ref, line_refs, rows_ref, cells_ref, lines_ref, finished)
    for copy in copies:
        copy.wait()


def total_kernel(scale, *refs):
    *term_refs, out_ref = refs
    chans, outs, taps = out_ref.shape
    total = term_refs[0][...]
    for ref in term_refs[1:]:
        total = total + ref[...]
    total = total * scale
    for c in range(chans):
        out_ref[c] = total[:, 32 * c : 32 * c + taps]


def from_behind(shard, axis, by):
    count = lax.axis_size(axis)
    pairs = [(i, i + by) for i in range(count) if 0 <= i + by < count]
    return lax.ppermute(shard, axis, pairs)


def upsample(stacked, axis, extended):
    tap_zero, tap_one, tap_two = (stacked[0], stacked[1], stacked[2])
    coord_axis = axis - 1
    length = tap_zero.shape[coord_axis]
    if extended:
        outer = length - 1
        even_cells = lax.slice_in_dim(tap_one, 0, outer, axis=coord_axis)
        odd_cells = lax.slice_in_dim(tap_zero, 1, length, axis=coord_axis) + lax.slice_in_dim(
            tap_two, 0, outer, axis=coord_axis
        )
    else:
        outer = length
        shifted = lax.slice_in_dim(tap_zero, 1, length, axis=coord_axis)
        shifted = jnp.concatenate(
            [shifted, jnp.zeros_like(lax.slice_in_dim(tap_zero, 0, 1, axis=coord_axis))],
            axis=coord_axis,
        )
        even_cells = tap_one
        odd_cells = shifted + tap_two
    paired = jnp.stack([even_cells, odd_cells], axis=coord_axis + 1)
    new_shape = list(even_cells.shape)
    new_shape[coord_axis] = 2 * outer
    return paired.reshape(new_shape)


def phase_grads(weight_rows, grads_ext):
    local_in = weight_rows.shape[0] // 27
    channels_out, planes, rows, cols = grads_ext.shape
    taps_out = jnp.dot(
        weight_rows, grads_ext.reshape(channels_out, -1), preferred_element_type=jnp.float32
    )
    taps_out = taps_out.reshape(3, 3, 3, local_in, planes, rows, cols)
    along_w = upsample(jnp.moveaxis(taps_out, 2, 0), 6, False)
    along_h = upsample(jnp.moveaxis(along_w, 1, 0), 4, False)
    return upsample(along_h, 2, True)


def weight_terms(inputs, grads_ext):
    row_extra = 0
    weight_cube = lax.conv_general_dilated(
        inputs[None],
        grads_ext[:, None],
        (1, 1, 1),
        ((1, 2), (1, row_extra), (1, 0)),
        rhs_dilation=(2, 2, 2),
        dimension_numbers=("CNDHW", "OIDHW", "NCDHW"),
        preferred_element_type=jnp.float32,
    )
    return jnp.transpose(weight_cube, (2, 3, 4, 0, 1)).reshape(
        27, weight_cube.shape[0], weight_cube.shape[1]
    )


def plain_shards(grad_out, volume, weight):
    plane_next = from_behind(grad_out, "depth", -1)
    grads_ext = jnp.concatenate([grad_out, plane_next], axis=1)
    channels_out = weight.shape[2]
    local_in = volume.shape[0]
    every_channel = lax.all_gather(grads_ext, "chan", axis=0, tiled=True)
    own_weight = lax.dynamic_slice_in_dim(weight, lax.axis_index("chan") * local_in, local_in, 1)
    input_part = phase_grads(own_weight.reshape(27 * local_in, channels_out), every_channel)
    weight_part = weight_terms(volume, every_channel)
    input_grad = input_part.astype(jnp.bfloat16)
    summed = lax.psum_scatter(weight_part, "depth", scatter_dimension=2, tiled=True)
    cell_count = grad_out.shape[1] * lax.axis_size("depth") * grad_out.shape[2] * grad_out.shape[3]
    return (input_grad, summed * (1.0 / math.sqrt(cell_count)))


def call(kernel, out_shape, *args, out_spec=VMEM, scratch=(), cost=None):
    flops, moved = cost
    return pl.pallas_call(
        kernel,
        out_shape=out_shape,
        in_specs=[VMEM] * len(args),
        out_specs=jax.tree.map(lambda _: out_spec, out_shape),
        scratch_shapes=scratch,
        compiler_params=pltpu.CompilerParams(vmem_limit_bytes=LIMIT),
        cost_estimate=pl.CostEstimate(flops=flops, bytes_accessed=moved, transcendentals=0),
    )(*args)


def shards(grad_out, volume, weight):
    count = lax.axis_size("chan")
    depth = lax.axis_size("depth")
    own_outs, _, rows, cols = grad_out.shape
    chans = volume.shape[0]
    channels = weight.shape[2]
    cells = rows * cols
    farther = [(i, (i + 1) % depth) for i in range(depth)]
    nearer = [(b, a) for a, b in farther]

    own_weight = lax.dynamic_slice_in_dim(weight, lax.axis_index("chan") * chans, chans, 1)
    views, even_taps, odd_taps = call(
        lambda *refs: own_views_kernel(depth, *refs),
        (
            jax.ShapeDtypeStruct((12 * chans, cells), BF16),
            jax.ShapeDtypeStruct((9 * chans, channels), BF16),
            jax.ShapeDtypeStruct((9 * chans, 2 * channels), BF16),
        ),
        volume,
        own_weight,
        cost=(2 * 2 * 2 * cells * chans * 8 * cols, 4 << 20),
    )
    got = {0: grad_out}
    for mask in sorted(range(1, count), key=lambda mask: (mask & (mask - 1) > 0, -mask)):
        low = mask & -mask
        if mask == 3:
            got[2], views = lax.optimization_barrier((got[2], views))
        got[mask] = lax.ppermute(got[mask - low], "chan", [(i, i ^ low) for i in range(count)])
    lines = lambda *parts: call(
        lines_kernel,
        jax.ShapeDtypeStruct((sum(part.shape[0] for part in parts), cells), BF16),
        *parts,
        scratch=(pltpu.VMEM(((own_outs + 1) * (rows + 8), cols), F32),),
        cost=(1 << 20, 2 << 20),
    )
    behind = lax.ppermute(volume, "depth", farther)
    own, views = lax.optimization_barrier((grad_out, views))
    next_own = lax.ppermute(own, "depth", nearer)
    behind_views = call(
        behind_views_kernel,
        jax.ShapeDtypeStruct((6 * chans, cells), BF16),
        behind,
        cost=(2 * 2 * cells * chans * 8 * cols, 2 << 20),
    )
    first_lines, next_first_lines = lines(grad_out), lines(next_own)
    got[1], views, behind_views, first_lines, next_first_lines = lax.optimization_barrier(
        (got[1], views, behind_views, first_lines, next_first_lines)
    )
    later_lines = [lines(*[got[mask] for mask in range(1, count - 1)]), lines(got[count - 1])]
    own_lines = [first_lines] + later_lines
    next_lines = [next_first_lines] + [lax.ppermute(part, "depth", nearer) for part in later_lines]
    outs = channels // depth
    half_terms = jax.ShapeDtypeStruct((channels // 2, 32 * chans), F32)
    keep, send = call(
        lambda *refs: weight_kernel(outs, cols, 4 * cols, *refs),
        (half_terms, half_terms),
        views,
        behind_views,
        *own_lines,
        scratch=(
            pltpu.VMEM((33 * (chans + 8), channels), F32),
            pltpu.VMEM((32 * chans, channels), F32),
        ),
        cost=(2 * 27 * chans * channels * cells, 8 << 20),
    )
    cells_scratch = (
        pltpu.VMEM((9 * chans, cells + cols), F32),
        pltpu.VMEM((2, (256 // chans + 1) * (chans + 8), cols), F32),
    )
    plane = jax.ShapeDtypeStruct((chans, 2 * rows, 2 * cols), BF16)
    other = lax.ppermute(send, "depth", [(i, i ^ 1) for i in range(depth)])
    even_grad = call(
        even_kernel,
        plane,
        even_taps,
        *own_lines,
        scratch=cells_scratch,
        cost=(2 * 9 * chans * channels * cells, 4 << 20),
    )
    other, even_grad = lax.optimization_barrier((other, even_grad))
    own_terms, *terms = call(
        pair_kernel,
        [jax.ShapeDtypeStruct((outs, 32 * chans), F32)] * (depth // 2),
        keep,
        other,
        cost=(1 << 16, 1 << 19),
    )
    terms = [
        lax.ppermute(terms[k - 1], "depth", [(i, i ^ (2 * k)) for i in range(depth)])
        for k in range(depth // 2 - 1, 0, -1)
    ]
    input_grad = call(
        odd_kernel,
        jax.ShapeDtypeStruct(volume.shape, BF16),
        even_grad,
        odd_taps,
        *next_lines,
        *own_lines,
        out_spec=HBM,
        scratch=cells_scratch
        + (
            pltpu.VMEM(plane.shape, BF16),
            pltpu.SemaphoreType.DMA,
            pltpu.SemaphoreType.DMA((2 * rows * chans // 256,)),
        ),
        cost=(4 * 9 * chans * channels * cells, 4 << 20),
    )
    own_terms, input_grad = lax.optimization_barrier((own_terms, input_grad))
    scale = 1.0 / math.sqrt(depth * cells)
    weight_grad = call(
        functools.partial(total_kernel, scale),
        jax.ShapeDtypeStruct((chans, outs, 27), F32),
        own_terms,
        *terms,
        cost=(1 << 16, 1 << 19),
    )
    return input_grad, jnp.transpose(weight_grad, (2, 0, 1))


def solution(mesh):
    in_specs = (P("chan", "depth", None, None), P("chan", "depth", None, None), P())
    out_specs = (P("chan", "depth", None, None), P(None, "chan", "depth"))
    ring, depth = mesh.shape["chan"], mesh.shape["depth"]

    def either(grad_out, volume, weight):
        fits = (
            grad_out.shape[0] % 32 == 0
            and volume.shape[0] == 16
            and grad_out.shape[1] == 1
            and ring >= 4
            and ring & (ring - 1) == 0
            and depth & (depth - 1) == 0
            and depth % (2 * ring) == 0
        )
        return (shards if fits else plain_shards)(grad_out, volume, weight)

    return jax.shard_map(either, mesh=mesh, in_specs=in_specs, out_specs=out_specs, check_vma=False)
```

```python
import functools
import math

import jax
import jax.numpy as jnp
from jax import lax
from jax.experimental import pallas as pl
from jax.experimental.pallas import tpu as pltpu
from jax.sharding import PartitionSpec as P

F32 = jnp.float32
BF16 = jnp.bfloat16
VMEM = pl.BlockSpec(memory_space=pltpu.VMEM)
HBM = pl.BlockSpec(memory_space=pltpu.HBM)
LIMIT = 48 * 1024 * 1024


def matmul(left, right):
    return jnp.dot(left, right, preferred_element_type=F32)


def one_hot(rows, cols, source):
    row = lax.broadcasted_iota(jnp.int32, (rows, cols), 0)
    col = lax.broadcasted_iota(jnp.int32, (rows, cols), 1)
    return jnp.where(source(row, col), 1.0, 0.0).astype(BF16)


def swap_rows(major, minor):
    bits = minor.bit_length() - 1
    return one_hot(
        major * minor,
        major * minor,
        lambda row, col: col == (row & (minor - 1)) * major + (row >> bits),
    )


def place_views(plane, views_ref, base):
    chans, rows, cols = plane.shape
    half = cols // 2
    group = 256 // chans
    swap = swap_rows(group, chans)
    split = one_hot(cols, cols, lambda row, col: row == 2 * (col & (half - 1)) + col // half)
    inner = lax.broadcasted_iota(jnp.int32, (group * chans, half), 1) > 0
    for start in range(0, rows, group):
        block = plane[:, start : start + group, :].reshape(chans * group, cols)
        parted = matmul(matmul(swap, block).astype(BF16), split)
        odd = parted[:, half:]
        before = jnp.where(inner, pltpu.roll(odd, 1, 1), 0.0)
        views = [view.astype(BF16) for view in (before, parted[:, :half], odd)]
        for at in range(group):
            row = start + at
            lanes = slice(row // 2 * half, (row // 2 + 1) * half)
            for e in range(3):
                lo = base + (3 * (row % 2) + e) * chans
                views_ref[lo : lo + chans, lanes] = views[e][at * chans : (at + 1) * chans]


def own_views_kernel(depth, volume_ref, weight_ref, views_ref, even_ref, odd_ref):
    chans = volume_ref.shape[0]
    channels = weight_ref.shape[2]
    place_views(volume_ref.at[:, 0], views_ref, 0)
    place_views(volume_ref.at[:, 1], views_ref, 6 * chans)
    count = lax.axis_size("chan")
    part = channels // count
    here = lax.axis_index("chan")
    row = lax.broadcasted_iota(jnp.int32, (channels, channels), 0)
    col = lax.broadcasted_iota(jnp.int32, (channels, channels), 1)
    order = jnp.zeros((channels, channels), F32)
    for slot in range(count):
        moved = ((here ^ slot) - slot) * part
        inside = (col >= slot * part) & (col < (slot + 1) * part)
        order = jnp.where(inside & (row == col + moved), 1.0, order)
    ordered = matmul(weight_ref[...].reshape(27 * chans, channels), order.astype(BF16)).astype(BF16)
    beyond = jnp.where(lax.axis_index("depth") == depth - 1, 0.0, 1.0).astype(BF16)
    for k, e in enumerate((1, 2, 0)):
        for b in range(3):
            pick = lambda a: ordered[(9 * a + 3 * b + e) * chans : (9 * a + 3 * b + e + 1) * chans]
            lo = (3 * k + b) * chans
            even_ref[lo : lo + chans, :] = pick(1)
            odd_ref[lo : lo + chans, :] = jnp.concatenate([pick(0) * beyond, pick(2)], axis=1)


def behind_views_kernel(behind_ref, views_ref):
    first = lax.axis_index("depth") == 0

    @pl.when(jnp.logical_not(first))
    def _():
        place_views(behind_ref.at[:, 1], views_ref, 0)

    @pl.when(first)
    def _():
        views_ref[...] = jnp.zeros(views_ref.shape, BF16)


def place_lines(part, out_ref, at, wide_ref):
    outs, _, rows, cols = part.shape
    pitch = rows + 8
    for o in range(outs):
        wide_ref[o * pitch : o * pitch + rows, :] = part[o, 0].astype(F32)
    for row in range(rows):
        line = wide_ref[pl.ds(row, outs, stride=pitch), :].astype(BF16)
        out_ref[at : at + outs, row * cols : (row + 1) * cols] = line


def lines_kernel(*refs):
    *parts, out_ref, wide_ref = refs
    at = 0
    for part in parts:
        place_lines(part, out_ref, at, wide_ref)
        at += part.shape[0]


def weight_kernel(
    outs, cols, chunk, own_ref, behind_ref, *refs
):
    *line_refs, keep_ref, send_ref, terms_ref, placed_ref = refs
    channels = terms_ref.shape[1]
    chans = behind_ref.shape[0] // 6
    cells = own_ref.shape[1]
    contract = (((1,), (1,)), ((), ()))

    def grads(lo, hi):
        return jnp.concatenate([ref[:, lo:hi] for ref in line_refs], axis=0)

    pitch = chans + 8
    sums = None
    for lo in range(0, cells, chunk):
        hi = lo + chunk
        below = grads(lo + cols, min(hi + cols, cells))
        if hi == cells:
            below = jnp.concatenate([below, jnp.zeros((channels, cols), BF16)], axis=1)
        both = jnp.concatenate([grads(lo, hi), below], axis=0)
        views = jnp.concatenate([behind_ref[:, lo:hi], own_ref[:, lo:hi]], axis=0)
        part = lax.dot_general(views, both, contract, preferred_element_type=F32)
        sums = part if sums is None else sums + part
    for a in range(3):
        terms = sums[6 * a * chans : 6 * (a + 1) * chans]
        even, odd = terms[: 3 * chans, :channels], terms[3 * chans :]
        for b, block in enumerate((odd[:, channels:], even, odd[:, :channels])):
            for e in range(3):
                lo = (9 * a + 3 * b + e) * pitch
                terms_ref[lo : lo + chans, :] = block[e * chans : (e + 1) * chans]
    terms_ref[27 * pitch :, :] = jnp.zeros((6 * pitch, channels), F32)
    for c in range(chans):
        placed_ref[32 * c : 32 * c + 32, :] = terms_ref[pl.ds(c, 32, stride=pitch), :]
    turned = placed_ref[...].T
    count = lax.axis_size("chan")
    part = channels // count
    odd_core = lax.axis_index("depth") % 2 == 1
    for slot in range(count):
        start = (lax.axis_index("chan") ^ slot) * (part // 2)
        for at in range(0, part // 2, outs):
            lo = slot * part + 2 * at
            even, odd = turned[lo : lo + outs], turned[lo + outs : lo + 2 * outs]
            place = pl.ds(pl.multiple_of(start + at, outs), outs)
            keep_ref[place, :] = jnp.where(odd_core, odd, even)
            send_ref[place, :] = jnp.where(odd_core, even, odd)


def pair_kernel(keep_ref, other_ref, *out_refs):
    chip = lax.axis_index("depth") // 2
    outs = out_refs[0].shape[0]
    for k, out_ref in enumerate(out_refs):
        place = pl.ds(pl.multiple_of((chip ^ k) * outs, outs), outs)
        out_ref[...] = keep_ref[place, :] + other_ref[place, :]


def input_rows(taps_ref, line_refs, rows_ref, cells_ref, lines_ref, finished):
    chans, rows, cols = rows_ref.shape
    half = cols // 2
    grid_cells = half * rows // 2
    cells_ref[:, grid_cells:] = jnp.zeros((cells_ref.shape[0], half), F32)
    group = 256 // chans

    def compute(start):
        lanes = slice(start // 2 * half, (start + group) // 2 * half)
        grads = jnp.concatenate([ref[:, lanes] for ref in line_refs], axis=0)
        cells_ref[:, lanes] = matmul(taps_ref[...], grads)

    compute(0)
    pitch = chans + 8
    weave = one_hot(cols, cols, lambda row, col: col == 2 * (row & (half - 1)) + row // half)
    inner = lax.broadcasted_iota(jnp.int32, (chans, half), 1) < half - 1

    def cells(kind, b, r):
        lo = (3 * kind + b) * chans
        return cells_ref[lo : lo + chans, r * half : (r + 1) * half]

    for start in range(0, rows, group):
        if start + group < rows:
            compute(start + group)
        pieces = []
        for row in range(start, start + group):
            r = row // 2
            if row % 2 == 0:
                even, odd, next_odd = [cells(kind, 1, r) for kind in range(3)]
            else:
                even, odd, next_odd = [cells(kind, 0, r + 1) + cells(kind, 2, r) for kind in range(3)]
            odd = odd + jnp.where(inner, pltpu.roll(next_odd, half - 1, 1), 0.0)
            pieces.append(jnp.concatenate([even, odd], axis=1).astype(BF16))
        woven = matmul(jnp.concatenate(pieces, axis=0), weave)
        for side in range(2):
            lanes = slice(side * half, (side + 1) * half)
            for at in range(group):
                lines_ref[side, at * pitch : at * pitch + chans] = woven[at * chans : (at + 1) * chans, lanes]
            for c in range(chans):
                line = lines_ref[side, pl.ds(c, group, stride=pitch), :].astype(BF16)
                rows_ref[c, start : start + group, lanes] = line
        finished(start, group)


def even_kernel(taps_ref, *refs):
    *line_refs, rows_ref, cells_ref, lines_ref = refs
    input_rows(taps_ref, line_refs, rows_ref, cells_ref, lines_ref, lambda start, size: None)


def odd_kernel(even_ref, taps_ref, *refs):
    *line_refs, out_ref, cells_ref, lines_ref, rows_ref, even_sem, sems = refs
    copies = [pltpu.make_async_copy(even_ref, out_ref.at[:, 0], even_sem)]
    copies[0].start()

    def finished(start, size):
        place = pl.ds(start, size)
        copy = pltpu.make_async_copy(rows_ref.at[:, place], out_ref.at[:, 1, place], sems.at[start // size])
        copy.start()
        copies.append(copy)

    input_rows(taps_ref, line_refs, rows_ref, cells_ref, lines_ref, finished)
    for copy in copies:
        copy.wait()


def total_kernel(scale, *refs):
    *term_refs, out_ref = refs
    chans, outs, taps = out_ref.shape
    total = term_refs[0][...]
    for ref in term_refs[1:]:
        total = total + ref[...]
    total = total * scale
    for c in range(chans):
        out_ref[c] = total[:, 32 * c : 32 * c + taps]


def from_behind(shard, axis, by):
    count = lax.axis_size(axis)
    pairs = [(i, i + by) for i in range(count) if 0 <= i + by < count]
    return lax.ppermute(shard, axis, pairs)


def upsample(stacked, axis, extended):
    tap_zero, tap_one, tap_two = (stacked[0], stacked[1], stacked[2])
    coord_axis = axis - 1
    length = tap_zero.shape[coord_axis]
    if extended:
        outer = length - 1
        even_cells = lax.slice_in_dim(tap_one, 0, outer, axis=coord_axis)
        odd_cells = lax.slice_in_dim(tap_zero, 1, length, axis=coord_axis) + lax.slice_in_dim(
            tap_two, 0, outer, axis=coord_axis
        )
    else:
        outer = length
        shifted = lax.slice_in_dim(tap_zero, 1, length, axis=coord_axis)
        shifted = jnp.concatenate(
            [shifted, jnp.zeros_like(lax.slice_in_dim(tap_zero, 0, 1, axis=coord_axis))],
            axis=coord_axis,
        )
        even_cells = tap_one
        odd_cells = shifted + tap_two
    paired = jnp.stack([even_cells, odd_cells], axis=coord_axis + 1)
    new_shape = list(even_cells.shape)
    new_shape[coord_axis] = 2 * outer
    return paired.reshape(new_shape)


def phase_grads(weight_rows, grads_ext):
    local_in = weight_rows.shape[0] // 27
    channels_out, planes, rows, cols = grads_ext.shape
    taps_out = jnp.dot(
        weight_rows, grads_ext.reshape(channels_out, -1), preferred_element_type=jnp.float32
    )
    taps_out = taps_out.reshape(3, 3, 3, local_in, planes, rows, cols)
    along_w = upsample(jnp.moveaxis(taps_out, 2, 0), 6, False)
    along_h = upsample(jnp.moveaxis(along_w, 1, 0), 4, False)
    return upsample(along_h, 2, True)


def weight_terms(inputs, grads_ext):
    row_extra = 0
    weight_cube = lax.conv_general_dilated(
        inputs[None],
        grads_ext[:, None],
        (1, 1, 1),
        ((1, 2), (1, row_extra), (1, 0)),
        rhs_dilation=(2, 2, 2),
        dimension_numbers=("CNDHW", "OIDHW", "NCDHW"),
        preferred_element_type=jnp.float32,
    )
    return jnp.transpose(weight_cube, (2, 3, 4, 0, 1)).reshape(
        27, weight_cube.shape[0], weight_cube.shape[1]
    )


def plain_shards(grad_out, volume, weight):
    plane_next = from_behind(grad_out, "depth", -1)
    grads_ext = jnp.concatenate([grad_out, plane_next], axis=1)
    channels_out = weight.shape[2]
    local_in = volume.shape[0]
    every_channel = lax.all_gather(grads_ext, "chan", axis=0, tiled=True)
    own_weight = lax.dynamic_slice_in_dim(weight, lax.axis_index("chan") * local_in, local_in, 1)
    input_part = phase_grads(own_weight.reshape(27 * local_in, channels_out), every_channel)
    weight_part = weight_terms(volume, every_channel)
    input_grad = input_part.astype(jnp.bfloat16)
    summed = lax.psum_scatter(weight_part, "depth", scatter_dimension=2, tiled=True)
    cell_count = grad_out.shape[1] * lax.axis_size("depth") * grad_out.shape[2] * grad_out.shape[3]
    return (input_grad, summed * (1.0 / math.sqrt(cell_count)))


def call(kernel, out_shape, *args, out_spec=VMEM, scratch=(), cost=None):
    flops, moved = cost
    return pl.pallas_call(
        kernel,
        out_shape=out_shape,
        in_specs=[VMEM] * len(args),
        out_specs=jax.tree.map(lambda _: out_spec, out_shape),
        scratch_shapes=scratch,
        compiler_params=pltpu.CompilerParams(vmem_limit_bytes=LIMIT),
        cost_estimate=pl.CostEstimate(flops=flops, bytes_accessed=moved, transcendentals=0),
    )(*args)


def shards(grad_out, volume, weight):
    count = lax.axis_size("chan")
    depth = lax.axis_size("depth")
    own_outs, _, rows, cols = grad_out.shape
    chans = volume.shape[0]
    channels = weight.shape[2]
    cells = rows * cols
    farther = [(i, (i + 1) % depth) for i in range(depth)]
    nearer = [(b, a) for a, b in farther]

    own_weight = lax.dynamic_slice_in_dim(weight, lax.axis_index("chan") * chans, chans, 1)
    views, even_taps, odd_taps = call(
        lambda *refs: own_views_kernel(depth, *refs),
        (
            jax.ShapeDtypeStruct((12 * chans, cells), BF16),
            jax.ShapeDtypeStruct((9 * chans, channels), BF16),
            jax.ShapeDtypeStruct((9 * chans, 2 * channels), BF16),
        ),
        volume,
        own_weight,
        cost=(2 * 2 * 2 * cells * chans * 8 * cols, 4 << 20),
    )
    pairs = lambda mask: [(i, i ^ mask) for i in range(count)]
    middle = own_outs // 2
    by_two = lax.ppermute(grad_out[:middle], "chan", pairs(2))
    own, views = lax.optimization_barrier((grad_out, views))
    by_one = lax.ppermute(own, "chan", pairs(1))
    by_two, rest = lax.optimization_barrier((by_two, own[middle:]))
    by_two_later = lax.ppermute(rest, "chan", pairs(2))
    by_three = lax.ppermute(by_two, "chan", pairs(1))
    by_three_later = lax.ppermute(by_two_later, "chan", pairs(1))
    lines = lambda *parts: call(
        lines_kernel,
        jax.ShapeDtypeStruct((sum(part.shape[0] for part in parts), cells), BF16),
        *parts,
        scratch=(pltpu.VMEM(((own_outs + 1) * (rows + 8), cols), F32),),
        cost=(1 << 20, 2 << 20),
    )
    behind = lax.ppermute(volume, "depth", farther)
    next_own = lax.ppermute(own, "depth", nearer)
    behind_views = call(
        behind_views_kernel,
        jax.ShapeDtypeStruct((6 * chans, cells), BF16),
        behind,
        cost=(2 * 2 * cells * chans * 8 * cols, 2 << 20),
    )
    first_lines, next_first_lines = lines(grad_out), lines(next_own)
    second_lines = lines(by_one, by_two)
    by_three, behind_views, first_lines, next_first_lines = lax.optimization_barrier(
        (by_three, behind_views, first_lines, next_first_lines)
    )
    later_lines = [second_lines, lines(by_two_later, by_three), lines(by_three_later)]
    own_lines = [first_lines] + later_lines
    next_lines = [next_first_lines] + [lax.ppermute(part, "depth", nearer) for part in later_lines]
    outs = channels // depth
    half_terms = jax.ShapeDtypeStruct((channels // 2, 32 * chans), F32)
    keep, send = call(
        lambda *refs: weight_kernel(outs, cols, 4 * cols, *refs),
        (half_terms, half_terms),
        views,
        behind_views,
        *own_lines,
        scratch=(
            pltpu.VMEM((33 * (chans + 8), channels), F32),
            pltpu.VMEM((32 * chans, channels), F32),
        ),
        cost=(2 * 27 * chans * channels * cells, 8 << 20),
    )
    cells_scratch = (
        pltpu.VMEM((9 * chans, cells + cols), F32),
        pltpu.VMEM((2, (256 // chans + 1) * (chans + 8), cols), F32),
    )
    plane = jax.ShapeDtypeStruct((chans, 2 * rows, 2 * cols), BF16)
    other = lax.ppermute(send, "depth", [(i, i ^ 1) for i in range(depth)])
    even_grad = call(
        even_kernel,
        plane,
        even_taps,
        *own_lines,
        scratch=cells_scratch,
        cost=(2 * 9 * chans * channels * cells, 4 << 20),
    )
    other, even_grad = lax.optimization_barrier((other, even_grad))
    own_terms, *terms = call(
        pair_kernel,
        [jax.ShapeDtypeStruct((outs, 32 * chans), F32)] * (depth // 2),
        keep,
        other,
        cost=(1 << 16, 1 << 19),
    )
    terms = [
        lax.ppermute(terms[k - 1], "depth", [(i, i ^ (2 * k)) for i in range(depth)])
        for k in range(depth // 2 - 1, 0, -1)
    ]
    input_grad = call(
        odd_kernel,
        jax.ShapeDtypeStruct(volume.shape, BF16),
        even_grad,
        odd_taps,
        *next_lines,
        *own_lines,
        out_spec=HBM,
        scratch=cells_scratch
        + (
            pltpu.VMEM(plane.shape, BF16),
            pltpu.SemaphoreType.DMA,
            pltpu.SemaphoreType.DMA((2 * rows * chans // 256,)),
        ),
        cost=(4 * 9 * chans * channels * cells, 4 << 20),
    )
    own_terms, input_grad = lax.optimization_barrier((own_terms, input_grad))
    scale = 1.0 / math.sqrt(depth * cells)
    weight_grad = call(
        functools.partial(total_kernel, scale),
        jax.ShapeDtypeStruct((chans, outs, 27), F32),
        own_terms,
        *terms,
        cost=(1 << 16, 1 << 19),
    )
    return input_grad, jnp.transpose(weight_grad, (2, 0, 1))


def solution(mesh):
    in_specs = (P("chan", "depth", None, None), P("chan", "depth", None, None), P())
    out_specs = (P("chan", "depth", None, None), P(None, "chan", "depth"))
    ring, depth = mesh.shape["chan"], mesh.shape["depth"]

    def either(grad_out, volume, weight):
        fits = (
            grad_out.shape[0] % 32 == 0
            and volume.shape[0] == 16
            and grad_out.shape[1] == 1
            and ring == 4
            and ring & (ring - 1) == 0
            and depth & (depth - 1) == 0
            and depth % (2 * ring) == 0
        )
        return (shards if fits else plain_shards)(grad_out, volume, weight)

    return jax.shard_map(either, mesh=mesh, in_specs=in_specs, out_specs=out_specs, check_vma=False)
```

```python
import functools
import math

import jax
import jax.numpy as jnp
from jax import lax
from jax.experimental import pallas as pl
from jax.experimental.pallas import tpu as pltpu
from jax.sharding import PartitionSpec as P

F32 = jnp.float32
BF16 = jnp.bfloat16
VMEM = pl.BlockSpec(memory_space=pltpu.VMEM)
HBM = pl.BlockSpec(memory_space=pltpu.HBM)
LIMIT = 48 * 1024 * 1024


def matmul(left, right):
    return jnp.dot(left, right, preferred_element_type=F32)


def one_hot(rows, cols, source):
    row = lax.broadcasted_iota(jnp.int32, (rows, cols), 0)
    col = lax.broadcasted_iota(jnp.int32, (rows, cols), 1)
    return jnp.where(source(row, col), 1.0, 0.0).astype(BF16)


def swap_rows(major, minor):
    bits = minor.bit_length() - 1
    return one_hot(
        major * minor,
        major * minor,
        lambda row, col: col == (row & (minor - 1)) * major + (row >> bits),
    )


def place_views(plane, views_ref, base):
    chans, rows, cols = plane.shape
    half = cols // 2
    group = 256 // chans
    swap = swap_rows(group, chans)
    split = one_hot(cols, cols, lambda row, col: row == 2 * (col & (half - 1)) + col // half)
    inner = lax.broadcasted_iota(jnp.int32, (group * chans, half), 1) > 0
    for start in range(0, rows, group):
        block = plane[:, start : start + group, :].reshape(chans * group, cols)
        parted = matmul(matmul(swap, block).astype(BF16), split)
        odd = parted[:, half:]
        before = jnp.where(inner, pltpu.roll(odd, 1, 1), 0.0)
        views = [view.astype(BF16) for view in (before, parted[:, :half], odd)]
        for at in range(group):
            row = start + at
            lanes = slice(row // 2 * half, (row // 2 + 1) * half)
            for e in range(3):
                lo = base + (3 * (row % 2) + e) * chans
                views_ref[lo : lo + chans, lanes] = views[e][at * chans : (at + 1) * chans]


def own_views_kernel(depth, volume_ref, weight_ref, views_ref, even_ref, odd_ref):
    chans = volume_ref.shape[0]
    channels = weight_ref.shape[2]
    place_views(volume_ref.at[:, 0], views_ref, 0)
    place_views(volume_ref.at[:, 1], views_ref, 6 * chans)
    count = lax.axis_size("chan")
    part = channels // count
    here = lax.axis_index("chan")
    row = lax.broadcasted_iota(jnp.int32, (channels, channels), 0)
    col = lax.broadcasted_iota(jnp.int32, (channels, channels), 1)
    order = jnp.zeros((channels, channels), F32)
    for slot in range(count):
        moved = ((here ^ slot) - slot) * part
        inside = (col >= slot * part) & (col < (slot + 1) * part)
        order = jnp.where(inside & (row == col + moved), 1.0, order)
    ordered = matmul(weight_ref[...].reshape(27 * chans, channels), order.astype(BF16)).astype(BF16)
    beyond = jnp.where(lax.axis_index("depth") == depth - 1, 0.0, 1.0).astype(BF16)
    for k, e in enumerate((1, 2, 0)):
        for b in range(3):
            pick = lambda a: ordered[(9 * a + 3 * b + e) * chans : (9 * a + 3 * b + e + 1) * chans]
            lo = (3 * k + b) * chans
            even_ref[lo : lo + chans, :] = pick(1)
            odd_ref[lo : lo + chans, :] = jnp.concatenate([pick(0) * beyond, pick(2)], axis=1)


def behind_views_kernel(behind_ref, views_ref):
    first = lax.axis_index("depth") == 0

    @pl.when(jnp.logical_not(first))
    def _():
        place_views(behind_ref.at[:, 1], views_ref, 0)

    @pl.when(first)
    def _():
        views_ref[...] = jnp.zeros(views_ref.shape, BF16)


def place_lines(part, out_ref, at, wide_ref):
    outs, _, rows, cols = part.shape
    pitch = rows + 8
    for o in range(outs):
        wide_ref[o * pitch : o * pitch + rows, :] = part[o, 0].astype(F32)
    for row in range(rows):
        line = wide_ref[pl.ds(row, outs, stride=pitch), :].astype(BF16)
        out_ref[at : at + outs, row * cols : (row + 1) * cols] = line


def lines_kernel(*refs):
    *parts, out_ref, wide_ref = refs
    at = 0
    for part in parts:
        place_lines(part, out_ref, at, wide_ref)
        at += part.shape[0]


def weight_kernel(
    outs, cols, chunk, own_ref, behind_ref, *refs
):
    *line_refs, keep_ref, send_ref, terms_ref, placed_ref = refs
    channels = terms_ref.shape[1]
    chans = behind_ref.shape[0] // 6
    cells = own_ref.shape[1]
    contract = (((1,), (1,)), ((), ()))

    def grads(lo, hi):
        return jnp.concatenate([ref[:, lo:hi] for ref in line_refs], axis=0)

    pitch = chans + 8
    sums = None
    for lo in range(0, cells, chunk):
        hi = lo + chunk
        below = grads(lo + cols, min(hi + cols, cells))
        if hi == cells:
            below = jnp.concatenate([below, jnp.zeros((channels, cols), BF16)], axis=1)
        both = jnp.concatenate([grads(lo, hi), below], axis=0)
        views = jnp.concatenate([behind_ref[:, lo:hi], own_ref[:, lo:hi]], axis=0)
        part = lax.dot_general(views, both, contract, preferred_element_type=F32)
        sums = part if sums is None else sums + part
    for a in range(3):
        terms = sums[6 * a * chans : 6 * (a + 1) * chans]
        even, odd = terms[: 3 * chans, :channels], terms[3 * chans :]
        for b, block in enumerate((odd[:, channels:], even, odd[:, :channels])):
            for e in range(3):
                lo = (9 * a + 3 * b + e) * pitch
                terms_ref[lo : lo + chans, :] = block[e * chans : (e + 1) * chans]
    terms_ref[27 * pitch :, :] = jnp.zeros((6 * pitch, channels), F32)
    for c in range(chans):
        placed_ref[32 * c : 32 * c + 32, :] = terms_ref[pl.ds(c, 32, stride=pitch), :]
    turned = placed_ref[...].T
    count = lax.axis_size("chan")
    part = channels // count
    odd_core = lax.axis_index("depth") % 2 == 1
    for slot in range(count):
        start = (lax.axis_index("chan") ^ slot) * (part // 2)
        for at in range(0, part // 2, outs):
            lo = slot * part + 2 * at
            even, odd = turned[lo : lo + outs], turned[lo + outs : lo + 2 * outs]
            place = pl.ds(pl.multiple_of(start + at, outs), outs)
            keep_ref[place, :] = jnp.where(odd_core, odd, even)
            send_ref[place, :] = jnp.where(odd_core, even, odd)


def pair_kernel(keep_ref, other_ref, *out_refs):
    chip = lax.axis_index("depth") // 2
    outs = out_refs[0].shape[0]
    for k, out_ref in enumerate(out_refs):
        place = pl.ds(pl.multiple_of((chip ^ k) * outs, outs), outs)
        out_ref[...] = keep_ref[place, :] + other_ref[place, :]


def input_rows(taps_ref, line_refs, rows_ref, cells_ref, lines_ref, finished):
    chans, rows, cols = rows_ref.shape
    half = cols // 2
    grid_cells = half * rows // 2
    cells_ref[:, grid_cells:] = jnp.zeros((cells_ref.shape[0], half), F32)
    group = 256 // chans

    def compute(start):
        lanes = slice(start // 2 * half, (start + group) // 2 * half)
        grads = jnp.concatenate([ref[:, lanes] for ref in line_refs], axis=0)
        cells_ref[:, lanes] = matmul(taps_ref[...], grads)

    compute(0)
    pitch = chans + 8
    weave = one_hot(cols, cols, lambda row, col: col == 2 * (row & (half - 1)) + row // half)
    inner = lax.broadcasted_iota(jnp.int32, (chans, half), 1) < half - 1

    def cells(kind, b, r):
        lo = (3 * kind + b) * chans
        return cells_ref[lo : lo + chans, r * half : (r + 1) * half]

    for start in range(0, rows, group):
        if start + group < rows:
            compute(start + group)
        pieces = []
        for row in range(start, start + group):
            r = row // 2
            if row % 2 == 0:
                even, odd, next_odd = [cells(kind, 1, r) for kind in range(3)]
            else:
                even, odd, next_odd = [cells(kind, 0, r + 1) + cells(kind, 2, r) for kind in range(3)]
            odd = odd + jnp.where(inner, pltpu.roll(next_odd, half - 1, 1), 0.0)
            pieces.append(jnp.concatenate([even, odd], axis=1).astype(BF16))
        woven = matmul(jnp.concatenate(pieces, axis=0), weave)
        for side in range(2):
            lanes = slice(side * half, (side + 1) * half)
            for at in range(group):
                lines_ref[side, at * pitch : at * pitch + chans] = woven[at * chans : (at + 1) * chans, lanes]
            for c in range(chans):
                line = lines_ref[side, pl.ds(c, group, stride=pitch), :].astype(BF16)
                rows_ref[c, start : start + group, lanes] = line
        finished(start, group)


def even_kernel(taps_ref, *refs):
    *line_refs, rows_ref, cells_ref, lines_ref = refs
    input_rows(taps_ref, line_refs, rows_ref, cells_ref, lines_ref, lambda start, size: None)


def odd_kernel(even_ref, taps_ref, *refs):
    *line_refs, out_ref, cells_ref, lines_ref, rows_ref, even_sem, sems = refs
    copies = [pltpu.make_async_copy(even_ref, out_ref.at[:, 0], even_sem)]
    copies[0].start()

    def finished(start, size):
        place = pl.ds(start, size)
        copy = pltpu.make_async_copy(rows_ref.at[:, place], out_ref.at[:, 1, place], sems.at[start // size])
        copy.start()
        copies.append(copy)

    input_rows(taps_ref, line_refs, rows_ref, cells_ref, lines_ref, finished)
    for copy in copies:
        copy.wait()


def total_kernel(scale, *refs):
    *term_refs, out_ref = refs
    chans, outs, taps = out_ref.shape
    total = term_refs[0][...]
    for ref in term_refs[1:]:
        total = total + ref[...]
    total = total * scale
    for c in range(chans):
        out_ref[c] = total[:, 32 * c : 32 * c + taps]


def from_behind(shard, axis, by):
    count = lax.axis_size(axis)
    pairs = [(i, i + by) for i in range(count) if 0 <= i + by < count]
    return lax.ppermute(shard, axis, pairs)


def upsample(stacked, axis, extended):
    tap_zero, tap_one, tap_two = (stacked[0], stacked[1], stacked[2])
    coord_axis = axis - 1
    length = tap_zero.shape[coord_axis]
    if extended:
        outer = length - 1
        even_cells = lax.slice_in_dim(tap_one, 0, outer, axis=coord_axis)
        odd_cells = lax.slice_in_dim(tap_zero, 1, length, axis=coord_axis) + lax.slice_in_dim(
            tap_two, 0, outer, axis=coord_axis
        )
    else:
        outer = length
        shifted = lax.slice_in_dim(tap_zero, 1, length, axis=coord_axis)
        shifted = jnp.concatenate(
            [shifted, jnp.zeros_like(lax.slice_in_dim(tap_zero, 0, 1, axis=coord_axis))],
            axis=coord_axis,
        )
        even_cells = tap_one
        odd_cells = shifted + tap_two
    paired = jnp.stack([even_cells, odd_cells], axis=coord_axis + 1)
    new_shape = list(even_cells.shape)
    new_shape[coord_axis] = 2 * outer
    return paired.reshape(new_shape)


def phase_grads(weight_rows, grads_ext):
    local_in = weight_rows.shape[0] // 27
    channels_out, planes, rows, cols = grads_ext.shape
    taps_out = jnp.dot(
        weight_rows, grads_ext.reshape(channels_out, -1), preferred_element_type=jnp.float32
    )
    taps_out = taps_out.reshape(3, 3, 3, local_in, planes, rows, cols)
    along_w = upsample(jnp.moveaxis(taps_out, 2, 0), 6, False)
    along_h = upsample(jnp.moveaxis(along_w, 1, 0), 4, False)
    return upsample(along_h, 2, True)


def weight_terms(inputs, grads_ext):
    row_extra = 0
    weight_cube = lax.conv_general_dilated(
        inputs[None],
        grads_ext[:, None],
        (1, 1, 1),
        ((1, 2), (1, row_extra), (1, 0)),
        rhs_dilation=(2, 2, 2),
        dimension_numbers=("CNDHW", "OIDHW", "NCDHW"),
        preferred_element_type=jnp.float32,
    )
    return jnp.transpose(weight_cube, (2, 3, 4, 0, 1)).reshape(
        27, weight_cube.shape[0], weight_cube.shape[1]
    )


def plain_shards(grad_out, volume, weight):
    plane_next = from_behind(grad_out, "depth", -1)
    grads_ext = jnp.concatenate([grad_out, plane_next], axis=1)
    channels_out = weight.shape[2]
    local_in = volume.shape[0]
    every_channel = lax.all_gather(grads_ext, "chan", axis=0, tiled=True)
    own_weight = lax.dynamic_slice_in_dim(weight, lax.axis_index("chan") * local_in, local_in, 1)
    input_part = phase_grads(own_weight.reshape(27 * local_in, channels_out), every_channel)
    weight_part = weight_terms(volume, every_channel)
    input_grad = input_part.astype(jnp.bfloat16)
    summed = lax.psum_scatter(weight_part, "depth", scatter_dimension=2, tiled=True)
    cell_count = grad_out.shape[1] * lax.axis_size("depth") * grad_out.shape[2] * grad_out.shape[3]
    return (input_grad, summed * (1.0 / math.sqrt(cell_count)))


def call(kernel, out_shape, *args, out_spec=VMEM, scratch=(), cost=None):
    flops, moved = cost
    return pl.pallas_call(
        kernel,
        out_shape=out_shape,
        in_specs=[VMEM] * len(args),
        out_specs=jax.tree.map(lambda _: out_spec, out_shape),
        scratch_shapes=scratch,
        compiler_params=pltpu.CompilerParams(vmem_limit_bytes=LIMIT),
        cost_estimate=pl.CostEstimate(flops=flops, bytes_accessed=moved, transcendentals=0),
    )(*args)


def shards(grad_out, volume, weight):
    count = lax.axis_size("chan")
    depth = lax.axis_size("depth")
    own_outs, _, rows, cols = grad_out.shape
    chans = volume.shape[0]
    channels = weight.shape[2]
    cells = rows * cols
    farther = [(i, (i + 1) % depth) for i in range(depth)]
    nearer = [(b, a) for a, b in farther]

    own_weight = lax.dynamic_slice_in_dim(weight, lax.axis_index("chan") * chans, chans, 1)
    views, even_taps, odd_taps = call(
        lambda *refs: own_views_kernel(depth, *refs),
        (
            jax.ShapeDtypeStruct((12 * chans, cells), BF16),
            jax.ShapeDtypeStruct((9 * chans, channels), BF16),
            jax.ShapeDtypeStruct((9 * chans, 2 * channels), BF16),
        ),
        volume,
        own_weight,
        cost=(2 * 2 * 2 * cells * chans * 8 * cols, 4 << 20),
    )
    got = {0: grad_out}
    for mask in sorted(range(1, count), key=lambda mask: (mask & (mask - 1) > 0, -mask)):
        low = mask & -mask
        if mask == 3:
            got[2], views = lax.optimization_barrier((got[2], views))
        got[mask] = lax.ppermute(got[mask - low], "chan", [(i, i ^ low) for i in range(count)])
    lines = lambda *parts: call(
        lines_kernel,
        jax.ShapeDtypeStruct((sum(part.shape[0] for part in parts), cells), BF16),
        *parts,
        scratch=(pltpu.VMEM(((own_outs + 1) * (rows + 8), cols), F32),),
        cost=(1 << 20, 2 << 20),
    )
    behind = lax.ppermute(volume, "depth", farther)
    next_own = lax.ppermute(grad_out, "depth", nearer)
    behind_views = call(
        behind_views_kernel,
        jax.ShapeDtypeStruct((6 * chans, cells), BF16),
        behind,
        cost=(2 * 2 * cells * chans * 8 * cols, 2 << 20),
    )
    first_lines, next_first_lines = lines(grad_out), lines(next_own)
    got[1], views, behind_views, first_lines, next_first_lines = lax.optimization_barrier(
        (got[1], views, behind_views, first_lines, next_first_lines)
    )
    later_lines = [lines(*[got[mask] for mask in range(1, count - 1)]), lines(got[count - 1])]
    own_lines = [first_lines] + later_lines
    next_lines = [next_first_lines] + [lax.ppermute(part, "depth", nearer) for part in later_lines]
    outs = channels // depth
    half_terms = jax.ShapeDtypeStruct((channels // 2, 32 * chans), F32)
    keep, send = call(
        lambda *refs: weight_kernel(outs, cols, 4 * cols, *refs),
        (half_terms, half_terms),
        views,
        behind_views,
        *own_lines,
        scratch=(
            pltpu.VMEM((33 * (chans + 8), channels), F32),
            pltpu.VMEM((32 * chans, channels), F32),
        ),
        cost=(2 * 27 * chans * channels * cells, 8 << 20),
    )
    cells_scratch = (
        pltpu.VMEM((9 * chans, cells + cols), F32),
        pltpu.VMEM((2, (256 // chans + 1) * (chans + 8), cols), F32),
    )
    plane = jax.ShapeDtypeStruct((chans, 2 * rows, 2 * cols), BF16)
    other = lax.ppermute(send, "depth", [(i, i ^ 1) for i in range(depth)])
    even_grad = call(
        even_kernel,
        plane,
        even_taps,
        *own_lines,
        scratch=cells_scratch,
        cost=(2 * 9 * chans * channels * cells, 4 << 20),
    )
    other, even_grad = lax.optimization_barrier((other, even_grad))
    own_terms, *terms = call(
        pair_kernel,
        [jax.ShapeDtypeStruct((outs, 32 * chans), F32)] * (depth // 2),
        keep,
        other,
        cost=(1 << 16, 1 << 19),
    )
    terms = [
        lax.ppermute(terms[k - 1], "depth", [(i, i ^ (2 * k)) for i in range(depth)])
        for k in range(depth // 2 - 1, 0, -1)
    ]
    input_grad = call(
        odd_kernel,
        jax.ShapeDtypeStruct(volume.shape, BF16),
        even_grad,
        odd_taps,
        *next_lines,
        *own_lines,
        out_spec=HBM,
        scratch=cells_scratch
        + (
            pltpu.VMEM(plane.shape, BF16),
            pltpu.SemaphoreType.DMA,
            pltpu.SemaphoreType.DMA((2 * rows * chans // 256,)),
        ),
        cost=(4 * 9 * chans * channels * cells, 4 << 20),
    )
    own_terms, input_grad = lax.optimization_barrier((own_terms, input_grad))
    scale = 1.0 / math.sqrt(depth * cells)
    weight_grad = call(
        functools.partial(total_kernel, scale),
        jax.ShapeDtypeStruct((chans, outs, 27), F32),
        own_terms,
        *terms,
        cost=(1 << 16, 1 << 19),
    )
    return input_grad, jnp.transpose(weight_grad, (2, 0, 1))


def solution(mesh):
    in_specs = (P("chan", "depth", None, None), P("chan", "depth", None, None), P())
    out_specs = (P("chan", "depth", None, None), P(None, "chan", "depth"))
    ring, depth = mesh.shape["chan"], mesh.shape["depth"]

    def either(grad_out, volume, weight):
        fits = (
            grad_out.shape[0] % 32 == 0
            and volume.shape[0] == 16
            and grad_out.shape[1] == 1
            and ring >= 4
            and ring & (ring - 1) == 0
            and depth & (depth - 1) == 0
            and depth % (2 * ring) == 0
        )
        return (shards if fits else plain_shards)(grad_out, volume, weight)

    return jax.shard_map(either, mesh=mesh, in_specs=in_specs, out_specs=out_specs, check_vma=False)
```

```python
import functools
import math

import jax
import jax.numpy as jnp
from jax import lax
from jax.experimental import pallas as pl
from jax.experimental.pallas import tpu as pltpu
from jax.sharding import PartitionSpec as P

F32 = jnp.float32
BF16 = jnp.bfloat16
VMEM = pl.BlockSpec(memory_space=pltpu.VMEM)
HBM = pl.BlockSpec(memory_space=pltpu.HBM)
LIMIT = 48 * 1024 * 1024


def matmul(left, right):
    return jnp.dot(left, right, preferred_element_type=F32)


def one_hot(rows, cols, source):
    row = lax.broadcasted_iota(jnp.int32, (rows, cols), 0)
    col = lax.broadcasted_iota(jnp.int32, (rows, cols), 1)
    return jnp.where(source(row, col), 1.0, 0.0).astype(BF16)


def swap_rows(major, minor):
    bits = minor.bit_length() - 1
    return one_hot(
        major * minor,
        major * minor,
        lambda row, col: col == (row & (minor - 1)) * major + (row >> bits),
    )


def place_views(plane, views_ref, base):
    chans, rows, cols = plane.shape
    half = cols // 2
    group = 256 // chans
    swap = swap_rows(group, chans)
    split = one_hot(cols, cols, lambda row, col: row == 2 * (col & (half - 1)) + col // half)
    inner = lax.broadcasted_iota(jnp.int32, (group * chans, half), 1) > 0
    for start in range(0, rows, group):
        block = plane[:, start : start + group, :].reshape(chans * group, cols)
        parted = matmul(matmul(swap, block).astype(BF16), split)
        odd = parted[:, half:]
        before = jnp.where(inner, pltpu.roll(odd, 1, 1), 0.0)
        views = [view.astype(BF16) for view in (before, parted[:, :half], odd)]
        for at in range(group):
            row = start + at
            lanes = slice(row // 2 * half, (row // 2 + 1) * half)
            for e in range(3):
                lo = base + (3 * (row % 2) + e) * chans
                views_ref[lo : lo + chans, lanes] = views[e][at * chans : (at + 1) * chans]


def own_views_kernel(depth, volume_ref, weight_ref, views_ref, even_ref, odd_ref):
    chans = volume_ref.shape[0]
    channels = weight_ref.shape[2]
    place_views(volume_ref.at[:, 0], views_ref, 0)
    place_views(volume_ref.at[:, 1], views_ref, 6 * chans)
    count = lax.axis_size("chan")
    part = channels // count
    here = lax.axis_index("chan")
    row = lax.broadcasted_iota(jnp.int32, (channels, channels), 0)
    col = lax.broadcasted_iota(jnp.int32, (channels, channels), 1)
    order = jnp.zeros((channels, channels), F32)
    for slot in range(count):
        moved = ((here ^ slot ^ (slot >> 1)) - slot) * part
        inside = (col >= slot * part) & (col < (slot + 1) * part)
        order = jnp.where(inside & (row == col + moved), 1.0, order)
    ordered = matmul(weight_ref[...].reshape(27 * chans, channels), order.astype(BF16)).astype(BF16)
    beyond = jnp.where(lax.axis_index("depth") == depth - 1, 0.0, 1.0).astype(BF16)
    for k, e in enumerate((1, 2, 0)):
        for b in range(3):
            pick = lambda a: ordered[(9 * a + 3 * b + e) * chans : (9 * a + 3 * b + e + 1) * chans]
            lo = (3 * k + b) * chans
            even_ref[lo : lo + chans, :] = pick(1)
            odd_ref[lo : lo + chans, :] = jnp.concatenate([pick(0) * beyond, pick(2)], axis=1)


def behind_views_kernel(behind_ref, views_ref):
    first = lax.axis_index("depth") == 0

    @pl.when(jnp.logical_not(first))
    def _():
        place_views(behind_ref.at[:, 1], views_ref, 0)

    @pl.when(first)
    def _():
        views_ref[...] = jnp.zeros(views_ref.shape, BF16)


def place_lines(part, out_ref, at, wide_ref):
    outs, _, rows, cols = part.shape
    pitch = rows + 8
    for o in range(outs):
        wide_ref[o * pitch : o * pitch + rows, :] = part[o, 0].astype(F32)
    for row in range(rows):
        line = wide_ref[pl.ds(row, outs, stride=pitch), :].astype(BF16)
        out_ref[at : at + outs, row * cols : (row + 1) * cols] = line


def lines_kernel(*refs):
    *parts, out_ref, wide_ref = refs
    at = 0
    for part in parts:
        place_lines(part, out_ref, at, wide_ref)
        at += part.shape[0]


def weight_kernel(
    outs, cols, chunk, own_ref, behind_ref, *refs
):
    *line_refs, keep_ref, send_ref, terms_ref, placed_ref = refs
    channels = terms_ref.shape[1]
    chans = behind_ref.shape[0] // 6
    cells = own_ref.shape[1]
    contract = (((1,), (1,)), ((), ()))

    def grads(lo, hi):
        return jnp.concatenate([ref[:, lo:hi] for ref in line_refs], axis=0)

    pitch = chans + 8
    sums = None
    for lo in range(0, cells, chunk):
        hi = lo + chunk
        below = grads(lo + cols, min(hi + cols, cells))
        if hi == cells:
            below = jnp.concatenate([below, jnp.zeros((channels, cols), BF16)], axis=1)
        both = jnp.concatenate([grads(lo, hi), below], axis=0)
        views = jnp.concatenate([behind_ref[:, lo:hi], own_ref[:, lo:hi]], axis=0)
        part = lax.dot_general(views, both, contract, preferred_element_type=F32)
        sums = part if sums is None else sums + part
    for a in range(3):
        terms = sums[6 * a * chans : 6 * (a + 1) * chans]
        even, odd = terms[: 3 * chans, :channels], terms[3 * chans :]
        for b, block in enumerate((odd[:, channels:], even, odd[:, :channels])):
            for e in range(3):
                lo = (9 * a + 3 * b + e) * pitch
                terms_ref[lo : lo + chans, :] = block[e * chans : (e + 1) * chans]
    terms_ref[27 * pitch :, :] = jnp.zeros((6 * pitch, channels), F32)
    for c in range(chans):
        placed_ref[32 * c : 32 * c + 32, :] = terms_ref[pl.ds(c, 32, stride=pitch), :]
    turned = placed_ref[...].T
    count = lax.axis_size("chan")
    part = channels // count
    odd_core = lax.axis_index("depth") % 2 == 1
    for slot in range(count):
        start = (lax.axis_index("chan") ^ slot ^ (slot >> 1)) * (part // 2)
        for at in range(0, part // 2, outs):
            lo = slot * part + 2 * at
            even, odd = turned[lo : lo + outs], turned[lo + outs : lo + 2 * outs]
            place = pl.ds(pl.multiple_of(start + at, outs), outs)
            keep_ref[place, :] = jnp.where(odd_core, odd, even)
            send_ref[place, :] = jnp.where(odd_core, even, odd)


def pair_kernel(keep_ref, other_ref, *out_refs):
    chip = lax.axis_index("depth") // 2
    outs = out_refs[0].shape[0]
    for k, out_ref in enumerate(out_refs):
        place = pl.ds(pl.multiple_of((chip ^ k) * outs, outs), outs)
        out_ref[...] = keep_ref[place, :] + other_ref[place, :]


def input_rows(taps_ref, line_refs, rows_ref, cells_ref, lines_ref, finished):
    chans, rows, cols = rows_ref.shape
    half = cols // 2
    grid_cells = half * rows // 2
    cells_ref[:, grid_cells:] = jnp.zeros((cells_ref.shape[0], half), F32)
    group = 256 // chans

    def compute(start):
        lanes = slice(start // 2 * half, (start + group) // 2 * half)
        grads = jnp.concatenate([ref[:, lanes] for ref in line_refs], axis=0)
        cells_ref[:, lanes] = matmul(taps_ref[...], grads)

    compute(0)
    pitch = chans + 8
    weave = one_hot(cols, cols, lambda row, col: col == 2 * (row & (half - 1)) + row // half)
    inner = lax.broadcasted_iota(jnp.int32, (chans, half), 1) < half - 1

    def cells(kind, b, r):
        lo = (3 * kind + b) * chans
        return cells_ref[lo : lo + chans, r * half : (r + 1) * half]

    for start in range(0, rows, group):
        if start + group < rows:
            compute(start + group)
        pieces = []
        for row in range(start, start + group):
            r = row // 2
            if row % 2 == 0:
                even, odd, next_odd = [cells(kind, 1, r) for kind in range(3)]
            else:
                even, odd, next_odd = [cells(kind, 0, r + 1) + cells(kind, 2, r) for kind in range(3)]
            odd = odd + jnp.where(inner, pltpu.roll(next_odd, half - 1, 1), 0.0)
            pieces.append(jnp.concatenate([even, odd], axis=1).astype(BF16))
        woven = matmul(jnp.concatenate(pieces, axis=0), weave)
        for side in range(2):
            lanes = slice(side * half, (side + 1) * half)
            for at in range(group):
                lines_ref[side, at * pitch : at * pitch + chans] = woven[at * chans : (at + 1) * chans, lanes]
            for c in range(chans):
                line = lines_ref[side, pl.ds(c, group, stride=pitch), :].astype(BF16)
                rows_ref[c, start : start + group, lanes] = line
        finished(start, group)


def even_kernel(taps_ref, *refs):
    *line_refs, rows_ref, cells_ref, lines_ref = refs
    input_rows(taps_ref, line_refs, rows_ref, cells_ref, lines_ref, lambda start, size: None)


def odd_kernel(even_ref, taps_ref, *refs):
    *line_refs, out_ref, cells_ref, lines_ref, rows_ref, even_sem, sems = refs
    copies = [pltpu.make_async_copy(even_ref, out_ref.at[:, 0], even_sem)]
    copies[0].start()

    def finished(start, size):
        place = pl.ds(start, size)
        copy = pltpu.make_async_copy(rows_ref.at[:, place], out_ref.at[:, 1, place], sems.at[start // size])
        copy.start()
        copies.append(copy)

    input_rows(taps_ref, line_refs, rows_ref, cells_ref, lines_ref, finished)
    for copy in copies:
        copy.wait()


def total_kernel(scale, *refs):
    *term_refs, out_ref = refs
    chans, outs, taps = out_ref.shape
    total = term_refs[0][...]
    for ref in term_refs[1:]:
        total = total + ref[...]
    total = total * scale
    for c in range(chans):
        out_ref[c] = total[:, 32 * c : 32 * c + taps]


def from_behind(shard, axis, by):
    count = lax.axis_size(axis)
    pairs = [(i, i + by) for i in range(count) if 0 <= i + by < count]
    return lax.ppermute(shard, axis, pairs)


def upsample(stacked, axis, extended):
    tap_zero, tap_one, tap_two = (stacked[0], stacked[1], stacked[2])
    coord_axis = axis - 1
    length = tap_zero.shape[coord_axis]
    if extended:
        outer = length - 1
        even_cells = lax.slice_in_dim(tap_one, 0, outer, axis=coord_axis)
        odd_cells = lax.slice_in_dim(tap_zero, 1, length, axis=coord_axis) + lax.slice_in_dim(
            tap_two, 0, outer, axis=coord_axis
        )
    else:
        outer = length
        shifted = lax.slice_in_dim(tap_zero, 1, length, axis=coord_axis)
        shifted = jnp.concatenate(
            [shifted, jnp.zeros_like(lax.slice_in_dim(tap_zero, 0, 1, axis=coord_axis))],
            axis=coord_axis,
        )
        even_cells = tap_one
        odd_cells = shifted + tap_two
    paired = jnp.stack([even_cells, odd_cells], axis=coord_axis + 1)
    new_shape = list(even_cells.shape)
    new_shape[coord_axis] = 2 * outer
    return paired.reshape(new_shape)


def phase_grads(weight_rows, grads_ext):
    local_in = weight_rows.shape[0] // 27
    channels_out, planes, rows, cols = grads_ext.shape
    taps_out = jnp.dot(
        weight_rows, grads_ext.reshape(channels_out, -1), preferred_element_type=jnp.float32
    )
    taps_out = taps_out.reshape(3, 3, 3, local_in, planes, rows, cols)
    along_w = upsample(jnp.moveaxis(taps_out, 2, 0), 6, False)
    along_h = upsample(jnp.moveaxis(along_w, 1, 0), 4, False)
    return upsample(along_h, 2, True)


def weight_terms(inputs, grads_ext):
    row_extra = 0
    weight_cube = lax.conv_general_dilated(
        inputs[None],
        grads_ext[:, None],
        (1, 1, 1),
        ((1, 2), (1, row_extra), (1, 0)),
        rhs_dilation=(2, 2, 2),
        dimension_numbers=("CNDHW", "OIDHW", "NCDHW"),
        preferred_element_type=jnp.float32,
    )
    return jnp.transpose(weight_cube, (2, 3, 4, 0, 1)).reshape(
        27, weight_cube.shape[0], weight_cube.shape[1]
    )


def plain_shards(grad_out, volume, weight):
    plane_next = from_behind(grad_out, "depth", -1)
    grads_ext = jnp.concatenate([grad_out, plane_next], axis=1)
    channels_out = weight.shape[2]
    local_in = volume.shape[0]
    every_channel = lax.all_gather(grads_ext, "chan", axis=0, tiled=True)
    own_weight = lax.dynamic_slice_in_dim(weight, lax.axis_index("chan") * local_in, local_in, 1)
    input_part = phase_grads(own_weight.reshape(27 * local_in, channels_out), every_channel)
    weight_part = weight_terms(volume, every_channel)
    input_grad = input_part.astype(jnp.bfloat16)
    summed = lax.psum_scatter(weight_part, "depth", scatter_dimension=2, tiled=True)
    cell_count = grad_out.shape[1] * lax.axis_size("depth") * grad_out.shape[2] * grad_out.shape[3]
    return (input_grad, summed * (1.0 / math.sqrt(cell_count)))


def call(kernel, out_shape, *args, out_spec=VMEM, scratch=(), cost=None):
    flops, moved = cost
    return pl.pallas_call(
        kernel,
        out_shape=out_shape,
        in_specs=[VMEM] * len(args),
        out_specs=jax.tree.map(lambda _: out_spec, out_shape),
        scratch_shapes=scratch,
        compiler_params=pltpu.CompilerParams(vmem_limit_bytes=LIMIT),
        cost_estimate=pl.CostEstimate(flops=flops, bytes_accessed=moved, transcendentals=0),
    )(*args)


def shards(grad_out, volume, weight):
    count = lax.axis_size("chan")
    depth = lax.axis_size("depth")
    own_outs, _, rows, cols = grad_out.shape
    chans = volume.shape[0]
    channels = weight.shape[2]
    cells = rows * cols
    farther = [(i, (i + 1) % depth) for i in range(depth)]
    nearer = [(b, a) for a, b in farther]

    own_weight = lax.dynamic_slice_in_dim(weight, lax.axis_index("chan") * chans, chans, 1)
    views, even_taps, odd_taps = call(
        lambda *refs: own_views_kernel(depth, *refs),
        (
            jax.ShapeDtypeStruct((12 * chans, cells), BF16),
            jax.ShapeDtypeStruct((9 * chans, channels), BF16),
            jax.ShapeDtypeStruct((9 * chans, 2 * channels), BF16),
        ),
        volume,
        own_weight,
        cost=(2 * 2 * 2 * cells * chans * 8 * cols, 4 << 20),
    )
    pairs = lambda mask: [(i, i ^ mask) for i in range(count)]
    far = lax.ppermute(grad_out, "chan", pairs(3))
    near = lax.ppermute(grad_out, "chan", pairs(1))
    far, views = lax.optimization_barrier((far, views))
    forwarded = lax.ppermute(far, "chan", pairs(1))
    lines = lambda *parts: call(
        lines_kernel,
        jax.ShapeDtypeStruct((sum(part.shape[0] for part in parts), cells), BF16),
        *parts,
        scratch=(pltpu.VMEM(((own_outs + 1) * (rows + 8), cols), F32),),
        cost=(1 << 20, 2 << 20),
    )
    behind = lax.ppermute(volume, "depth", farther)
    next_own = lax.ppermute(grad_out, "depth", nearer)
    behind_views = call(
        behind_views_kernel,
        jax.ShapeDtypeStruct((6 * chans, cells), BF16),
        behind,
        cost=(2 * 2 * cells * chans * 8 * cols, 2 << 20),
    )
    first_lines, next_first_lines = lines(grad_out), lines(next_own)
    near, views, behind_views, first_lines, next_first_lines = lax.optimization_barrier(
        (near, views, behind_views, first_lines, next_first_lines)
    )
    later_lines = [lines(near, far), lines(forwarded)]
    own_lines = [first_lines] + later_lines
    next_lines = [next_first_lines] + [lax.ppermute(part, "depth", nearer) for part in later_lines]
    outs = channels // depth
    half_terms = jax.ShapeDtypeStruct((channels // 2, 32 * chans), F32)
    keep, send = call(
        lambda *refs: weight_kernel(outs, cols, 4 * cols, *refs),
        (half_terms, half_terms),
        views,
        behind_views,
        *own_lines,
        scratch=(
            pltpu.VMEM((33 * (chans + 8), channels), F32),
            pltpu.VMEM((32 * chans, channels), F32),
        ),
        cost=(2 * 27 * chans * channels * cells, 8 << 20),
    )
    cells_scratch = (
        pltpu.VMEM((9 * chans, cells + cols), F32),
        pltpu.VMEM((2, (256 // chans + 1) * (chans + 8), cols), F32),
    )
    plane = jax.ShapeDtypeStruct((chans, 2 * rows, 2 * cols), BF16)
    other = lax.ppermute(send, "depth", [(i, i ^ 1) for i in range(depth)])
    even_grad = call(
        even_kernel,
        plane,
        even_taps,
        *own_lines,
        scratch=cells_scratch,
        cost=(2 * 9 * chans * channels * cells, 4 << 20),
    )
    other, even_grad = lax.optimization_barrier((other, even_grad))
    own_terms, *terms = call(
        pair_kernel,
        [jax.ShapeDtypeStruct((outs, 32 * chans), F32)] * (depth // 2),
        keep,
        other,
        cost=(1 << 16, 1 << 19),
    )
    terms = [
        lax.ppermute(terms[k - 1], "depth", [(i, i ^ (2 * k)) for i in range(depth)])
        for k in range(depth // 2 - 1, 0, -1)
    ]
    input_grad = call(
        odd_kernel,
        jax.ShapeDtypeStruct(volume.shape, BF16),
        even_grad,
        odd_taps,
        *next_lines,
        *own_lines,
        out_spec=HBM,
        scratch=cells_scratch
        + (
            pltpu.VMEM(plane.shape, BF16),
            pltpu.SemaphoreType.DMA,
            pltpu.SemaphoreType.DMA((2 * rows * chans // 256,)),
        ),
        cost=(4 * 9 * chans * channels * cells, 4 << 20),
    )
    own_terms, input_grad = lax.optimization_barrier((own_terms, input_grad))
    scale = 1.0 / math.sqrt(depth * cells)
    weight_grad = call(
        functools.partial(total_kernel, scale),
        jax.ShapeDtypeStruct((chans, outs, 27), F32),
        own_terms,
        *terms,
        cost=(1 << 16, 1 << 19),
    )
    return input_grad, jnp.transpose(weight_grad, (2, 0, 1))


def solution(mesh):
    in_specs = (P("chan", "depth", None, None), P("chan", "depth", None, None), P())
    out_specs = (P("chan", "depth", None, None), P(None, "chan", "depth"))
    ring, depth = mesh.shape["chan"], mesh.shape["depth"]

    def either(grad_out, volume, weight):
        fits = (
            grad_out.shape[0] % 32 == 0
            and volume.shape[0] == 16
            and grad_out.shape[1] == 1
            and ring == 4
            and ring & (ring - 1) == 0
            and depth & (depth - 1) == 0
            and depth % (2 * ring) == 0
        )
        return (shards if fits else plain_shards)(grad_out, volume, weight)

    return jax.shard_map(either, mesh=mesh, in_specs=in_specs, out_specs=out_specs, check_vma=False)
```

```python
import functools
import math

import jax
import jax.numpy as jnp
from jax import lax
from jax.experimental import pallas as pl
from jax.experimental.pallas import tpu as pltpu
from jax.sharding import PartitionSpec as P

F32 = jnp.float32
BF16 = jnp.bfloat16
VMEM = pl.BlockSpec(memory_space=pltpu.VMEM)
HBM = pl.BlockSpec(memory_space=pltpu.HBM)
LIMIT = 48 * 1024 * 1024


def matmul(left, right):
    return jnp.dot(left, right, preferred_element_type=F32)


def one_hot(rows, cols, source):
    row = lax.broadcasted_iota(jnp.int32, (rows, cols), 0)
    col = lax.broadcasted_iota(jnp.int32, (rows, cols), 1)
    return jnp.where(source(row, col), 1.0, 0.0).astype(BF16)


def swap_rows(major, minor):
    bits = minor.bit_length() - 1
    return one_hot(
        major * minor,
        major * minor,
        lambda row, col: col == (row & (minor - 1)) * major + (row >> bits),
    )


def place_views(plane, views_ref, base):
    chans, rows, cols = plane.shape
    half = cols // 2
    group = 256 // chans
    swap = swap_rows(group, chans)
    split = one_hot(cols, cols, lambda row, col: row == 2 * (col & (half - 1)) + col // half)
    inner = lax.broadcasted_iota(jnp.int32, (group * chans, half), 1) > 0
    for start in range(0, rows, group):
        block = plane[:, start : start + group, :].reshape(chans * group, cols)
        parted = matmul(matmul(swap, block).astype(BF16), split)
        odd = parted[:, half:]
        before = jnp.where(inner, pltpu.roll(odd, 1, 1), 0.0)
        views = [view.astype(BF16) for view in (before, parted[:, :half], odd)]
        for at in range(group):
            row = start + at
            lanes = slice(row // 2 * half, (row // 2 + 1) * half)
            for e in range(3):
                lo = base + (3 * (row % 2) + e) * chans
                views_ref[lo : lo + chans, lanes] = views[e][at * chans : (at + 1) * chans]


def own_views_kernel(depth, volume_ref, weight_ref, views_ref, even_ref, odd_ref):
    chans = volume_ref.shape[0]
    channels = weight_ref.shape[2]
    place_views(volume_ref.at[:, 0], views_ref, 0)
    place_views(volume_ref.at[:, 1], views_ref, 6 * chans)
    count = lax.axis_size("chan")
    part = channels // count
    here = lax.axis_index("chan")
    row = lax.broadcasted_iota(jnp.int32, (channels, channels), 0)
    col = lax.broadcasted_iota(jnp.int32, (channels, channels), 1)
    order = jnp.zeros((channels, channels), F32)
    for slot in range(count):
        moved = ((here ^ slot ^ (slot >> 1)) - slot) * part
        inside = (col >= slot * part) & (col < (slot + 1) * part)
        order = jnp.where(inside & (row == col + moved), 1.0, order)
    ordered = matmul(weight_ref[...].reshape(27 * chans, channels), order.astype(BF16)).astype(BF16)
    beyond = jnp.where(lax.axis_index("depth") == depth - 1, 0.0, 1.0).astype(BF16)
    for k, e in enumerate((1, 2, 0)):
        for b in range(3):
            pick = lambda a: ordered[(9 * a + 3 * b + e) * chans : (9 * a + 3 * b + e + 1) * chans]
            lo = (3 * k + b) * chans
            even_ref[lo : lo + chans, :] = pick(1)
            odd_ref[lo : lo + chans, :] = jnp.concatenate([pick(0) * beyond, pick(2)], axis=1)


def behind_views_kernel(behind_ref, views_ref):
    first = lax.axis_index("depth") == 0

    @pl.when(jnp.logical_not(first))
    def _():
        place_views(behind_ref.at[:, 1], views_ref, 0)

    @pl.when(first)
    def _():
        views_ref[...] = jnp.zeros(views_ref.shape, BF16)


def place_lines(part, out_ref, at, wide_ref):
    outs, _, rows, cols = part.shape
    pitch = rows + 8
    for o in range(outs):
        wide_ref[o * pitch : o * pitch + rows, :] = part[o, 0].astype(F32)
    for row in range(rows):
        line = wide_ref[pl.ds(row, outs, stride=pitch), :].astype(BF16)
        out_ref[at : at + outs, row * cols : (row + 1) * cols] = line


def lines_kernel(*refs):
    *parts, out_ref, wide_ref = refs
    at = 0
    for part in parts:
        place_lines(part, out_ref, at, wide_ref)
        at += part.shape[0]


def weight_kernel(
    outs, cols, chunk, own_ref, behind_ref, *refs
):
    *line_refs, keep_ref, send_ref, terms_ref, placed_ref = refs
    channels = terms_ref.shape[1]
    chans = behind_ref.shape[0] // 6
    cells = own_ref.shape[1]
    contract = (((1,), (1,)), ((), ()))

    def grads(lo, hi):
        return jnp.concatenate([ref[:, lo:hi] for ref in line_refs], axis=0)

    pitch = chans + 8
    sums = None
    for lo in range(0, cells, chunk):
        hi = lo + chunk
        below = grads(lo + cols, min(hi + cols, cells))
        if hi == cells:
            below = jnp.concatenate([below, jnp.zeros((channels, cols), BF16)], axis=1)
        both = jnp.concatenate([grads(lo, hi), below], axis=0)
        views = jnp.concatenate([behind_ref[:, lo:hi], own_ref[:, lo:hi]], axis=0)
        part = lax.dot_general(views, both, contract, preferred_element_type=F32)
        sums = part if sums is None else sums + part
    for a in range(3):
        terms = sums[6 * a * chans : 6 * (a + 1) * chans]
        even, odd = terms[: 3 * chans, :channels], terms[3 * chans :]
        for b, block in enumerate((odd[:, channels:], even, odd[:, :channels])):
            for e in range(3):
                lo = (9 * a + 3 * b + e) * pitch
                terms_ref[lo : lo + chans, :] = block[e * chans : (e + 1) * chans]
    terms_ref[27 * pitch :, :] = jnp.zeros((6 * pitch, channels), F32)
    for c in range(chans):
        placed_ref[32 * c : 32 * c + 32, :] = terms_ref[pl.ds(c, 32, stride=pitch), :]
    turned = placed_ref[...].T
    count = lax.axis_size("chan")
    part = channels // count
    odd_core = lax.axis_index("depth") % 2 == 1
    for slot in range(count):
        start = (lax.axis_index("chan") ^ slot ^ (slot >> 1)) * (part // 2)
        for at in range(0, part // 2, outs):
            lo = slot * part + 2 * at
            even, odd = turned[lo : lo + outs], turned[lo + outs : lo + 2 * outs]
            place = pl.ds(pl.multiple_of(start + at, outs), outs)
            keep_ref[place, :] = jnp.where(odd_core, odd, even)
            send_ref[place, :] = jnp.where(odd_core, even, odd)


def pair_kernel(keep_ref, other_ref, *out_refs):
    chip = lax.axis_index("depth") // 2
    outs = out_refs[0].shape[0]
    for k, out_ref in enumerate(out_refs):
        place = pl.ds(pl.multiple_of((chip ^ k) * outs, outs), outs)
        out_ref[...] = keep_ref[place, :] + other_ref[place, :]


def input_rows(taps_ref, line_refs, rows_ref, cells_ref, lines_ref, finished):
    chans, rows, cols = rows_ref.shape
    half = cols // 2
    grid_cells = half * rows // 2
    cells_ref[:, grid_cells:] = jnp.zeros((cells_ref.shape[0], half), F32)
    group = 256 // chans

    def compute(start):
        lanes = slice(start // 2 * half, (start + group) // 2 * half)
        grads = jnp.concatenate([ref[:, lanes] for ref in line_refs], axis=0)
        cells_ref[:, lanes] = matmul(taps_ref[...], grads)

    compute(0)
    pitch = chans + 8
    weave = one_hot(cols, cols, lambda row, col: col == 2 * (row & (half - 1)) + row // half)
    inner = lax.broadcasted_iota(jnp.int32, (chans, half), 1) < half - 1

    def cells(kind, b, r):
        lo = (3 * kind + b) * chans
        return cells_ref[lo : lo + chans, r * half : (r + 1) * half]

    for start in range(0, rows, group):
        if start + group < rows:
            compute(start + group)
        pieces = []
        for row in range(start, start + group):
            r = row // 2
            if row % 2 == 0:
                even, odd, next_odd = [cells(kind, 1, r) for kind in range(3)]
            else:
                even, odd, next_odd = [cells(kind, 0, r + 1) + cells(kind, 2, r) for kind in range(3)]
            odd = odd + jnp.where(inner, pltpu.roll(next_odd, half - 1, 1), 0.0)
            pieces.append(jnp.concatenate([even, odd], axis=1).astype(BF16))
        woven = matmul(jnp.concatenate(pieces, axis=0), weave)
        for side in range(2):
            lanes = slice(side * half, (side + 1) * half)
            for at in range(group):
                lines_ref[side, at * pitch : at * pitch + chans] = woven[at * chans : (at + 1) * chans, lanes]
            for c in range(chans):
                line = lines_ref[side, pl.ds(c, group, stride=pitch), :].astype(BF16)
                rows_ref[c, start : start + group, lanes] = line
        finished(start, group)


def even_kernel(taps_ref, *refs):
    *line_refs, rows_ref, cells_ref, lines_ref = refs
    input_rows(taps_ref, line_refs, rows_ref, cells_ref, lines_ref, lambda start, size: None)


def odd_kernel(even_ref, taps_ref, *refs):
    *line_refs, out_ref, cells_ref, lines_ref, rows_ref, even_sem, sems = refs
    copies = [pltpu.make_async_copy(even_ref, out_ref.at[:, 0], even_sem)]
    copies[0].start()

    def finished(start, size):
        place = pl.ds(start, size)
        copy = pltpu.make_async_copy(rows_ref.at[:, place], out_ref.at[:, 1, place], sems.at[start // size])
        copy.start()
        copies.append(copy)

    input_rows(taps_ref, line_refs, rows_ref, cells_ref, lines_ref, finished)
    for copy in copies:
        copy.wait()


def total_kernel(scale, *refs):
    *term_refs, out_ref = refs
    chans, outs, taps = out_ref.shape
    total = term_refs[0][...]
    for ref in term_refs[1:]:
        total = total + ref[...]
    total = total * scale
    for c in range(chans):
        out_ref[c] = total[:, 32 * c : 32 * c + taps]


def from_behind(shard, axis, by):
    count = lax.axis_size(axis)
    pairs = [(i, i + by) for i in range(count) if 0 <= i + by < count]
    return lax.ppermute(shard, axis, pairs)


def upsample(stacked, axis, extended):
    tap_zero, tap_one, tap_two = (stacked[0], stacked[1], stacked[2])
    coord_axis = axis - 1
    length = tap_zero.shape[coord_axis]
    if extended:
        outer = length - 1
        even_cells = lax.slice_in_dim(tap_one, 0, outer, axis=coord_axis)
        odd_cells = lax.slice_in_dim(tap_zero, 1, length, axis=coord_axis) + lax.slice_in_dim(
            tap_two, 0, outer, axis=coord_axis
        )
    else:
        outer = length
        shifted = lax.slice_in_dim(tap_zero, 1, length, axis=coord_axis)
        shifted = jnp.concatenate(
            [shifted, jnp.zeros_like(lax.slice_in_dim(tap_zero, 0, 1, axis=coord_axis))],
            axis=coord_axis,
        )
        even_cells = tap_one
        odd_cells = shifted + tap_two
    paired = jnp.stack([even_cells, odd_cells], axis=coord_axis + 1)
    new_shape = list(even_cells.shape)
    new_shape[coord_axis] = 2 * outer
    return paired.reshape(new_shape)


def phase_grads(weight_rows, grads_ext):
    local_in = weight_rows.shape[0] // 27
    channels_out, planes, rows, cols = grads_ext.shape
    taps_out = jnp.dot(
        weight_rows, grads_ext.reshape(channels_out, -1), preferred_element_type=jnp.float32
    )
    taps_out = taps_out.reshape(3, 3, 3, local_in, planes, rows, cols)
    along_w = upsample(jnp.moveaxis(taps_out, 2, 0), 6, False)
    along_h = upsample(jnp.moveaxis(along_w, 1, 0), 4, False)
    return upsample(along_h, 2, True)


def weight_terms(inputs, grads_ext):
    row_extra = 0
    weight_cube = lax.conv_general_dilated(
        inputs[None],
        grads_ext[:, None],
        (1, 1, 1),
        ((1, 2), (1, row_extra), (1, 0)),
        rhs_dilation=(2, 2, 2),
        dimension_numbers=("CNDHW", "OIDHW", "NCDHW"),
        preferred_element_type=jnp.float32,
    )
    return jnp.transpose(weight_cube, (2, 3, 4, 0, 1)).reshape(
        27, weight_cube.shape[0], weight_cube.shape[1]
    )


def plain_shards(grad_out, volume, weight):
    plane_next = from_behind(grad_out, "depth", -1)
    grads_ext = jnp.concatenate([grad_out, plane_next], axis=1)
    channels_out = weight.shape[2]
    local_in = volume.shape[0]
    every_channel = lax.all_gather(grads_ext, "chan", axis=0, tiled=True)
    own_weight = lax.dynamic_slice_in_dim(weight, lax.axis_index("chan") * local_in, local_in, 1)
    input_part = phase_grads(own_weight.reshape(27 * local_in, channels_out), every_channel)
    weight_part = weight_terms(volume, every_channel)
    input_grad = input_part.astype(jnp.bfloat16)
    summed = lax.psum_scatter(weight_part, "depth", scatter_dimension=2, tiled=True)
    cell_count = grad_out.shape[1] * lax.axis_size("depth") * grad_out.shape[2] * grad_out.shape[3]
    return (input_grad, summed * (1.0 / math.sqrt(cell_count)))


def call(kernel, out_shape, *args, out_spec=VMEM, scratch=(), cost=None):
    flops, moved = cost
    return pl.pallas_call(
        kernel,
        out_shape=out_shape,
        in_specs=[VMEM] * len(args),
        out_specs=jax.tree.map(lambda _: out_spec, out_shape),
        scratch_shapes=scratch,
        compiler_params=pltpu.CompilerParams(vmem_limit_bytes=LIMIT),
        cost_estimate=pl.CostEstimate(flops=flops, bytes_accessed=moved, transcendentals=0),
    )(*args)


def shards(grad_out, volume, weight):
    count = lax.axis_size("chan")
    depth = lax.axis_size("depth")
    own_outs, _, rows, cols = grad_out.shape
    chans = volume.shape[0]
    channels = weight.shape[2]
    cells = rows * cols
    farther = [(i, (i + 1) % depth) for i in range(depth)]
    nearer = [(b, a) for a, b in farther]

    own_weight = lax.dynamic_slice_in_dim(weight, lax.axis_index("chan") * chans, chans, 1)
    views, even_taps, odd_taps = call(
        lambda *refs: own_views_kernel(depth, *refs),
        (
            jax.ShapeDtypeStruct((12 * chans, cells), BF16),
            jax.ShapeDtypeStruct((9 * chans, channels), BF16),
            jax.ShapeDtypeStruct((9 * chans, 2 * channels), BF16),
        ),
        volume,
        own_weight,
        cost=(2 * 2 * 2 * cells * chans * 8 * cols, 4 << 20),
    )
    pairs = lambda mask: [(i, i ^ mask) for i in range(count)]
    far = lax.ppermute(grad_out, "chan", pairs(3))
    own, views = lax.optimization_barrier((grad_out, views))
    near = lax.ppermute(own, "chan", pairs(1))
    forwarded = lax.ppermute(far, "chan", pairs(1))
    lines = lambda *parts: call(
        lines_kernel,
        jax.ShapeDtypeStruct((sum(part.shape[0] for part in parts), cells), BF16),
        *parts,
        scratch=(pltpu.VMEM(((own_outs + 1) * (rows + 8), cols), F32),),
        cost=(1 << 20, 2 << 20),
    )
    behind = lax.ppermute(volume, "depth", farther)
    next_own = lax.ppermute(own, "depth", nearer)
    behind_views = call(
        behind_views_kernel,
        jax.ShapeDtypeStruct((6 * chans, cells), BF16),
        behind,
        cost=(2 * 2 * cells * chans * 8 * cols, 2 << 20),
    )
    first_lines, next_first_lines = lines(grad_out), lines(next_own)
    near, views, behind_views, first_lines, next_first_lines = lax.optimization_barrier(
        (near, views, behind_views, first_lines, next_first_lines)
    )
    later_lines = [lines(near, far), lines(forwarded)]
    own_lines = [first_lines] + later_lines
    next_lines = [next_first_lines] + [lax.ppermute(part, "depth", nearer) for part in later_lines]
    outs = channels // depth
    half_terms = jax.ShapeDtypeStruct((channels // 2, 32 * chans), F32)
    keep, send = call(
        lambda *refs: weight_kernel(outs, cols, 4 * cols, *refs),
        (half_terms, half_terms),
        views,
        behind_views,
        *own_lines,
        scratch=(
            pltpu.VMEM((33 * (chans + 8), channels), F32),
            pltpu.VMEM((32 * chans, channels), F32),
        ),
        cost=(2 * 27 * chans * channels * cells, 8 << 20),
    )
    cells_scratch = (
        pltpu.VMEM((9 * chans, cells + cols), F32),
        pltpu.VMEM((2, (256 // chans + 1) * (chans + 8), cols), F32),
    )
    plane = jax.ShapeDtypeStruct((chans, 2 * rows, 2 * cols), BF16)
    other = lax.ppermute(send, "depth", [(i, i ^ 1) for i in range(depth)])
    even_grad = call(
        even_kernel,
        plane,
        even_taps,
        *own_lines,
        scratch=cells_scratch,
        cost=(2 * 9 * chans * channels * cells, 4 << 20),
    )
    other, even_grad = lax.optimization_barrier((other, even_grad))
    own_terms, *terms = call(
        pair_kernel,
        [jax.ShapeDtypeStruct((outs, 32 * chans), F32)] * (depth // 2),
        keep,
        other,
        cost=(1 << 16, 1 << 19),
    )
    terms = [
        lax.ppermute(terms[k - 1], "depth", [(i, i ^ (2 * k)) for i in range(depth)])
        for k in range(depth // 2 - 1, 0, -1)
    ]
    input_grad = call(
        odd_kernel,
        jax.ShapeDtypeStruct(volume.shape, BF16),
        even_grad,
        odd_taps,
        *next_lines,
        *own_lines,
        out_spec=HBM,
        scratch=cells_scratch
        + (
            pltpu.VMEM(plane.shape, BF16),
            pltpu.SemaphoreType.DMA,
            pltpu.SemaphoreType.DMA((2 * rows * chans // 256,)),
        ),
        cost=(4 * 9 * chans * channels * cells, 4 << 20),
    )
    own_terms, input_grad = lax.optimization_barrier((own_terms, input_grad))
    scale = 1.0 / math.sqrt(depth * cells)
    weight_grad = call(
        functools.partial(total_kernel, scale),
        jax.ShapeDtypeStruct((chans, outs, 27), F32),
        own_terms,
        *terms,
        cost=(1 << 16, 1 << 19),
    )
    return input_grad, jnp.transpose(weight_grad, (2, 0, 1))


def solution(mesh):
    in_specs = (P("chan", "depth", None, None), P("chan", "depth", None, None), P())
    out_specs = (P("chan", "depth", None, None), P(None, "chan", "depth"))
    ring, depth = mesh.shape["chan"], mesh.shape["depth"]

    def either(grad_out, volume, weight):
        fits = (
            grad_out.shape[0] % 32 == 0
            and volume.shape[0] == 16
            and grad_out.shape[1] == 1
            and ring == 4
            and ring & (ring - 1) == 0
            and depth & (depth - 1) == 0
            and depth % (2 * ring) == 0
        )
        return (shards if fits else plain_shards)(grad_out, volume, weight)

    return jax.shard_map(either, mesh=mesh, in_specs=in_specs, out_specs=out_specs, check_vma=False)
```

```python
import functools
import math

import jax
import jax.numpy as jnp
from jax import lax
from jax.experimental import pallas as pl
from jax.experimental.pallas import tpu as pltpu
from jax.sharding import PartitionSpec as P

F32 = jnp.float32
BF16 = jnp.bfloat16
VMEM = pl.BlockSpec(memory_space=pltpu.VMEM)
HBM = pl.BlockSpec(memory_space=pltpu.HBM)
LIMIT = 48 * 1024 * 1024


def matmul(left, right):
    return jnp.dot(left, right, preferred_element_type=F32)


def one_hot(rows, cols, source):
    row = lax.broadcasted_iota(jnp.int32, (rows, cols), 0)
    col = lax.broadcasted_iota(jnp.int32, (rows, cols), 1)
    return jnp.where(source(row, col), 1.0, 0.0).astype(BF16)


def swap_rows(major, minor):
    bits = minor.bit_length() - 1
    return one_hot(
        major * minor,
        major * minor,
        lambda row, col: col == (row & (minor - 1)) * major + (row >> bits),
    )


def place_views(plane, views_ref, base):
    chans, rows, cols = plane.shape
    half = cols // 2
    group = 256 // chans
    swap = swap_rows(group, chans)
    split = one_hot(cols, cols, lambda row, col: row == 2 * (col & (half - 1)) + col // half)
    inner = lax.broadcasted_iota(jnp.int32, (group * chans, half), 1) > 0
    for start in range(0, rows, group):
        block = plane[:, start : start + group, :].reshape(chans * group, cols)
        parted = matmul(matmul(swap, block).astype(BF16), split)
        odd = parted[:, half:]
        before = jnp.where(inner, pltpu.roll(odd, 1, 1), 0.0)
        views = [view.astype(BF16) for view in (before, parted[:, :half], odd)]
        for at in range(group):
            row = start + at
            lanes = slice(row // 2 * half, (row // 2 + 1) * half)
            for e in range(3):
                lo = base + (3 * (row % 2) + e) * chans
                views_ref[lo : lo + chans, lanes] = views[e][at * chans : (at + 1) * chans]


def own_views_kernel(depth, volume_ref, weight_ref, views_ref, even_ref, odd_ref):
    chans = volume_ref.shape[0]
    channels = weight_ref.shape[2]
    place_views(volume_ref.at[:, 0], views_ref, 0)
    place_views(volume_ref.at[:, 1], views_ref, 6 * chans)
    count = lax.axis_size("chan")
    part = channels // count
    here = lax.axis_index("chan")
    row = lax.broadcasted_iota(jnp.int32, (channels, channels), 0)
    col = lax.broadcasted_iota(jnp.int32, (channels, channels), 1)
    order = jnp.zeros((channels, channels), F32)
    for slot in range(count):
        moved = ((here ^ slot ^ (slot >> 1)) - slot) * part
        inside = (col >= slot * part) & (col < (slot + 1) * part)
        order = jnp.where(inside & (row == col + moved), 1.0, order)
    ordered = matmul(weight_ref[...].reshape(27 * chans, channels), order.astype(BF16)).astype(BF16)
    beyond = jnp.where(lax.axis_index("depth") == depth - 1, 0.0, 1.0).astype(BF16)
    for k, e in enumerate((1, 2, 0)):
        for b in range(3):
            pick = lambda a: ordered[(9 * a + 3 * b + e) * chans : (9 * a + 3 * b + e + 1) * chans]
            lo = (3 * k + b) * chans
            even_ref[lo : lo + chans, :] = pick(1)
            odd_ref[lo : lo + chans, :] = jnp.concatenate([pick(0) * beyond, pick(2)], axis=1)


def behind_views_kernel(behind_ref, views_ref):
    first = lax.axis_index("depth") == 0

    @pl.when(jnp.logical_not(first))
    def _():
        place_views(behind_ref.at[:, 1], views_ref, 0)

    @pl.when(first)
    def _():
        views_ref[...] = jnp.zeros(views_ref.shape, BF16)


def place_lines(part, out_ref, at, wide_ref):
    outs, _, rows, cols = part.shape
    pitch = rows + 8
    for o in range(outs):
        wide_ref[o * pitch : o * pitch + rows, :] = part[o, 0].astype(F32)
    for row in range(rows):
        line = wide_ref[pl.ds(row, outs, stride=pitch), :].astype(BF16)
        out_ref[at : at + outs, row * cols : (row + 1) * cols] = line


def lines_kernel(*refs):
    *parts, out_ref, wide_ref = refs
    at = 0
    for part in parts:
        place_lines(part, out_ref, at, wide_ref)
        at += part.shape[0]


def weight_kernel(
    outs, cols, chunk, own_ref, behind_ref, *refs
):
    *line_refs, keep_ref, send_ref, terms_ref, placed_ref = refs
    channels = terms_ref.shape[1]
    chans = behind_ref.shape[0] // 6
    cells = own_ref.shape[1]
    contract = (((1,), (1,)), ((), ()))

    def grads(lo, hi):
        return jnp.concatenate([ref[:, lo:hi] for ref in line_refs], axis=0)

    pitch = chans + 8
    sums = None
    for lo in range(0, cells, chunk):
        hi = lo + chunk
        below = grads(lo + cols, min(hi + cols, cells))
        if hi == cells:
            below = jnp.concatenate([below, jnp.zeros((channels, cols), BF16)], axis=1)
        both = jnp.concatenate([grads(lo, hi), below], axis=0)
        views = jnp.concatenate([behind_ref[:, lo:hi], own_ref[:, lo:hi]], axis=0)
        part = lax.dot_general(views, both, contract, preferred_element_type=F32)
        sums = part if sums is None else sums + part
    for a in range(3):
        terms = sums[6 * a * chans : 6 * (a + 1) * chans]
        even, odd = terms[: 3 * chans, :channels], terms[3 * chans :]
        for b, block in enumerate((odd[:, channels:], even, odd[:, :channels])):
            for e in range(3):
                lo = (9 * a + 3 * b + e) * pitch
                terms_ref[lo : lo + chans, :] = block[e * chans : (e + 1) * chans]
    terms_ref[27 * pitch :, :] = jnp.zeros((6 * pitch, channels), F32)
    for c in range(chans):
        placed_ref[32 * c : 32 * c + 32, :] = terms_ref[pl.ds(c, 32, stride=pitch), :]
    turned = placed_ref[...].T
    count = lax.axis_size("chan")
    part = channels // count
    odd_core = lax.axis_index("depth") % 2 == 1
    for slot in range(count):
        start = (lax.axis_index("chan") ^ slot ^ (slot >> 1)) * (part // 2)
        for at in range(0, part // 2, outs):
            lo = slot * part + 2 * at
            even, odd = turned[lo : lo + outs], turned[lo + outs : lo + 2 * outs]
            place = pl.ds(pl.multiple_of(start + at, outs), outs)
            keep_ref[place, :] = jnp.where(odd_core, odd, even)
            send_ref[place, :] = jnp.where(odd_core, even, odd)


def pair_kernel(keep_ref, other_ref, *out_refs):
    chip = lax.axis_index("depth") // 2
    outs = out_refs[0].shape[0]
    for k, out_ref in enumerate(out_refs):
        place = pl.ds(pl.multiple_of((chip ^ k) * outs, outs), outs)
        out_ref[...] = keep_ref[place, :] + other_ref[place, :]


def input_rows(taps_ref, line_refs, rows_ref, cells_ref, lines_ref, finished):
    chans, rows, cols = rows_ref.shape
    half = cols // 2
    grid_cells = half * rows // 2
    cells_ref[:, grid_cells:] = jnp.zeros((cells_ref.shape[0], half), F32)
    group = 256 // chans

    def compute(start):
        lanes = slice(start // 2 * half, (start + group) // 2 * half)
        grads = jnp.concatenate([ref[:, lanes] for ref in line_refs], axis=0)
        cells_ref[:, lanes] = matmul(taps_ref[...], grads)

    compute(0)
    pitch = chans + 8
    weave = one_hot(cols, cols, lambda row, col: col == 2 * (row & (half - 1)) + row // half)
    inner = lax.broadcasted_iota(jnp.int32, (chans, half), 1) < half - 1

    def cells(kind, b, r):
        lo = (3 * kind + b) * chans
        return cells_ref[lo : lo + chans, r * half : (r + 1) * half]

    for start in range(0, rows, group):
        if start + group < rows:
            compute(start + group)
        pieces = []
        for row in range(start, start + group):
            r = row // 2
            if row % 2 == 0:
                even, odd, next_odd = [cells(kind, 1, r) for kind in range(3)]
            else:
                even, odd, next_odd = [cells(kind, 0, r + 1) + cells(kind, 2, r) for kind in range(3)]
            odd = odd + jnp.where(inner, pltpu.roll(next_odd, half - 1, 1), 0.0)
            pieces.append(jnp.concatenate([even, odd], axis=1).astype(BF16))
        woven = matmul(jnp.concatenate(pieces, axis=0), weave)
        for side in range(2):
            lanes = slice(side * half, (side + 1) * half)
            for at in range(group):
                lines_ref[side, at * pitch : at * pitch + chans] = woven[at * chans : (at + 1) * chans, lanes]
            for c in range(chans):
                line = lines_ref[side, pl.ds(c, group, stride=pitch), :].astype(BF16)
                rows_ref[c, start : start + group, lanes] = line
        finished(start, group)


def even_kernel(taps_ref, *refs):
    *line_refs, rows_ref, cells_ref, lines_ref = refs
    input_rows(taps_ref, line_refs, rows_ref, cells_ref, lines_ref, lambda start, size: None)


def odd_kernel(even_ref, taps_ref, *refs):
    *line_refs, out_ref, cells_ref, lines_ref, rows_ref, even_sem, sems = refs
    copies = [pltpu.make_async_copy(even_ref, out_ref.at[:, 0], even_sem)]
    copies[0].start()

    def finished(start, size):
        place = pl.ds(start, size)
        copy = pltpu.make_async_copy(rows_ref.at[:, place], out_ref.at[:, 1, place], sems.at[start // size])
        copy.start()
        copies.append(copy)

    input_rows(taps_ref, line_refs, rows_ref, cells_ref, lines_ref, finished)
    for copy in copies:
        copy.wait()


def total_kernel(scale, *refs):
    *term_refs, out_ref = refs
    chans, outs, taps = out_ref.shape
    total = term_refs[0][...]
    for ref in term_refs[1:]:
        total = total + ref[...]
    total = total * scale
    for c in range(chans):
        out_ref[c] = total[:, 32 * c : 32 * c + taps]


def from_behind(shard, axis, by):
    count = lax.axis_size(axis)
    pairs = [(i, i + by) for i in range(count) if 0 <= i + by < count]
    return lax.ppermute(shard, axis, pairs)


def upsample(stacked, axis, extended):
    tap_zero, tap_one, tap_two = (stacked[0], stacked[1], stacked[2])
    coord_axis = axis - 1
    length = tap_zero.shape[coord_axis]
    if extended:
        outer = length - 1
        even_cells = lax.slice_in_dim(tap_one, 0, outer, axis=coord_axis)
        odd_cells = lax.slice_in_dim(tap_zero, 1, length, axis=coord_axis) + lax.slice_in_dim(
            tap_two, 0, outer, axis=coord_axis
        )
    else:
        outer = length
        shifted = lax.slice_in_dim(tap_zero, 1, length, axis=coord_axis)
        shifted = jnp.concatenate(
            [shifted, jnp.zeros_like(lax.slice_in_dim(tap_zero, 0, 1, axis=coord_axis))],
            axis=coord_axis,
        )
        even_cells = tap_one
        odd_cells = shifted + tap_two
    paired = jnp.stack([even_cells, odd_cells], axis=coord_axis + 1)
    new_shape = list(even_cells.shape)
    new_shape[coord_axis] = 2 * outer
    return paired.reshape(new_shape)


def phase_grads(weight_rows, grads_ext):
    local_in = weight_rows.shape[0] // 27
    channels_out, planes, rows, cols = grads_ext.shape
    taps_out = jnp.dot(
        weight_rows, grads_ext.reshape(channels_out, -1), preferred_element_type=jnp.float32
    )
    taps_out = taps_out.reshape(3, 3, 3, local_in, planes, rows, cols)
    along_w = upsample(jnp.moveaxis(taps_out, 2, 0), 6, False)
    along_h = upsample(jnp.moveaxis(along_w, 1, 0), 4, False)
    return upsample(along_h, 2, True)


def weight_terms(inputs, grads_ext):
    row_extra = 0
    weight_cube = lax.conv_general_dilated(
        inputs[None],
        grads_ext[:, None],
        (1, 1, 1),
        ((1, 2), (1, row_extra), (1, 0)),
        rhs_dilation=(2, 2, 2),
        dimension_numbers=("CNDHW", "OIDHW", "NCDHW"),
        preferred_element_type=jnp.float32,
    )
    return jnp.transpose(weight_cube, (2, 3, 4, 0, 1)).reshape(
        27, weight_cube.shape[0], weight_cube.shape[1]
    )


def plain_shards(grad_out, volume, weight):
    plane_next = from_behind(grad_out, "depth", -1)
    grads_ext = jnp.concatenate([grad_out, plane_next], axis=1)
    channels_out = weight.shape[2]
    local_in = volume.shape[0]
    every_channel = lax.all_gather(grads_ext, "chan", axis=0, tiled=True)
    own_weight = lax.dynamic_slice_in_dim(weight, lax.axis_index("chan") * local_in, local_in, 1)
    input_part = phase_grads(own_weight.reshape(27 * local_in, channels_out), every_channel)
    weight_part = weight_terms(volume, every_channel)
    input_grad = input_part.astype(jnp.bfloat16)
    summed = lax.psum_scatter(weight_part, "depth", scatter_dimension=2, tiled=True)
    cell_count = grad_out.shape[1] * lax.axis_size("depth") * grad_out.shape[2] * grad_out.shape[3]
    return (input_grad, summed * (1.0 / math.sqrt(cell_count)))


def call(kernel, out_shape, *args, out_spec=VMEM, scratch=(), cost=None):
    flops, moved = cost
    return pl.pallas_call(
        kernel,
        out_shape=out_shape,
        in_specs=[VMEM] * len(args),
        out_specs=jax.tree.map(lambda _: out_spec, out_shape),
        scratch_shapes=scratch,
        compiler_params=pltpu.CompilerParams(vmem_limit_bytes=LIMIT),
        cost_estimate=pl.CostEstimate(flops=flops, bytes_accessed=moved, transcendentals=0),
    )(*args)


def shards(grad_out, volume, weight):
    count = lax.axis_size("chan")
    depth = lax.axis_size("depth")
    own_outs, _, rows, cols = grad_out.shape
    chans = volume.shape[0]
    channels = weight.shape[2]
    cells = rows * cols
    farther = [(i, (i + 1) % depth) for i in range(depth)]
    nearer = [(b, a) for a, b in farther]

    own_weight = lax.dynamic_slice_in_dim(weight, lax.axis_index("chan") * chans, chans, 1)
    views, even_taps, odd_taps = call(
        lambda *refs: own_views_kernel(depth, *refs),
        (
            jax.ShapeDtypeStruct((12 * chans, cells), BF16),
            jax.ShapeDtypeStruct((9 * chans, channels), BF16),
            jax.ShapeDtypeStruct((9 * chans, 2 * channels), BF16),
        ),
        volume,
        own_weight,
        cost=(2 * 2 * 2 * cells * chans * 8 * cols, 4 << 20),
    )
    pairs = lambda mask: [(i, i ^ mask) for i in range(count)]
    far = lax.ppermute(grad_out, "chan", pairs(3))
    own, views = lax.optimization_barrier((grad_out, views))
    near = lax.ppermute(own, "chan", pairs(1))
    forwarded = lax.ppermute(far, "chan", pairs(1))
    lines = lambda *parts: call(
        lines_kernel,
        jax.ShapeDtypeStruct((sum(part.shape[0] for part in parts), cells), BF16),
        *parts,
        scratch=(pltpu.VMEM(((own_outs + 1) * (rows + 8), cols), F32),),
        cost=(1 << 20, 2 << 20),
    )
    behind = lax.ppermute(volume, "depth", farther)
    next_own = lax.ppermute(own, "depth", nearer)
    behind_views = call(
        behind_views_kernel,
        jax.ShapeDtypeStruct((6 * chans, cells), BF16),
        behind,
        cost=(2 * 2 * cells * chans * 8 * cols, 2 << 20),
    )
    first_lines, next_first_lines = lines(grad_out), lines(next_own)
    near, views, behind_views, first_lines, next_first_lines = lax.optimization_barrier(
        (near, views, behind_views, first_lines, next_first_lines)
    )
    later_lines = [lines(near, far), lines(forwarded)]
    own_lines = [first_lines] + later_lines
    next_lines = [next_first_lines] + [lax.ppermute(part, "depth", nearer) for part in later_lines]
    outs = channels // depth
    half_terms = jax.ShapeDtypeStruct((channels // 2, 32 * chans), F32)
    keep, send = call(
        lambda *refs: weight_kernel(outs, cols, 4 * cols, *refs),
        (half_terms, half_terms),
        views,
        behind_views,
        *own_lines,
        scratch=(
            pltpu.VMEM((33 * (chans + 8), channels), F32),
            pltpu.VMEM((32 * chans, channels), F32),
        ),
        cost=(2 * 27 * chans * channels * cells, 8 << 20),
    )
    cells_scratch = (
        pltpu.VMEM((9 * chans, cells + cols), F32),
        pltpu.VMEM((2, (256 // chans + 1) * (chans + 8), cols), F32),
    )
    plane = jax.ShapeDtypeStruct((chans, 2 * rows, 2 * cols), BF16)
    other = lax.ppermute(send, "depth", [(i, i ^ 1) for i in range(depth)])
    even_grad = call(
        even_kernel,
        plane,
        even_taps,
        *own_lines,
        scratch=cells_scratch,
        cost=(2 * 9 * chans * channels * cells, 4 << 20),
    )
    other, even_grad = lax.optimization_barrier((other, even_grad))
    own_terms, *terms = call(
        pair_kernel,
        [jax.ShapeDtypeStruct((outs, 32 * chans), F32)] * (depth // 2),
        keep,
        other,
        cost=(1 << 16, 1 << 19),
    )
    terms = [
        lax.ppermute(terms[k - 1], "depth", [(i, i ^ (2 * k)) for i in range(depth)])
        for k in [depth // 2 - 1, *range(1, depth // 2 - 1)]
    ]
    input_grad = call(
        odd_kernel,
        jax.ShapeDtypeStruct(volume.shape, BF16),
        even_grad,
        odd_taps,
        *next_lines,
        *own_lines,
        out_spec=HBM,
        scratch=cells_scratch
        + (
            pltpu.VMEM(plane.shape, BF16),
            pltpu.SemaphoreType.DMA,
            pltpu.SemaphoreType.DMA((2 * rows * chans // 256,)),
        ),
        cost=(4 * 9 * chans * channels * cells, 4 << 20),
    )
    own_terms, input_grad = lax.optimization_barrier((own_terms, input_grad))
    scale = 1.0 / math.sqrt(depth * cells)
    weight_grad = call(
        functools.partial(total_kernel, scale),
        jax.ShapeDtypeStruct((chans, outs, 27), F32),
        own_terms,
        *terms,
        cost=(1 << 16, 1 << 19),
    )
    return input_grad, jnp.transpose(weight_grad, (2, 0, 1))


def solution(mesh):
    in_specs = (P("chan", "depth", None, None), P("chan", "depth", None, None), P())
    out_specs = (P("chan", "depth", None, None), P(None, "chan", "depth"))
    ring, depth = mesh.shape["chan"], mesh.shape["depth"]

    def either(grad_out, volume, weight):
        fits = (
            grad_out.shape[0] % 32 == 0
            and volume.shape[0] == 16
            and grad_out.shape[1] == 1
            and ring == 4
            and ring & (ring - 1) == 0
            and depth & (depth - 1) == 0
            and depth % (2 * ring) == 0
        )
        return (shards if fits else plain_shards)(grad_out, volume, weight)

    return jax.shard_map(either, mesh=mesh, in_specs=in_specs, out_specs=out_specs, check_vma=False)
```
